32 devices in a mesh: row: 8 (over z, y), col: 4 (over x, core).
Axes of the slice: x: 2, y: 2, z: 4, core: 2. Of those that a mesh axis runs over, the one named last changes fastest.
Arguments:
- design: float32 [4096, 4096], P('row', 'col'), may hold values from -6 to 6
- sign_bits: int32 [4096], P('row'), may hold values from 0 to 1
- picks: int32 [8, 8, 16], P(None, 'row'), may hold values from 0 to 511
- counts: int32 [8, 8], P(None, 'row'), may hold values from 6 to 16, as said below
- target: float32 [4096], P('row'), may hold values from -6 to 6
- rinv: float32 [4096, 4096], P('col')
Outputs:
- sketch: float32 [1024, 4096], P('row', 'col')
- solution: float32 [4096], P('col')
- basis: float32 [4096], P('row')
The draws below stay inside these ranges and needn't reach their ends.
Inputs may be any that keep to these rules, and one draw needn't show every extreme that they name: `counts`: some owner takes 16 rows from some block.
All inputs are finite; a program needn't handle non-finite values.
Results may differ from the reference program's by a relative error of at most 0.0003.
Values sent between devices are 32-bit elements; how exact they have to be, the bound alone decides.
No kernel may reach another device: no remote copies, remote signals or barrier semaphores. Data moves between devices by JAX's collectives and lax.ppermute only.
A program may use at most 64 MiB of HBM per device.

```python
import jax
import jax.numpy as jnp
from jax import lax

N = 4096
RD = 512
HB = 256
PAIR = 16
ITERS = 2
ROWS = 4096
SK = 1024
N_ROW = 8


def draw_picks(key, part):
    key = jax.random.fold_in(key, 11)
    return jax.random.randint(key, (N_ROW, N_ROW, PAIR), 0, RD, dtype=jnp.int32)


def draw_counts(key, part):
    key = jax.random.fold_in(key, 12)
    first, second, third, fourth = jax.random.split(key, 4)
    lowest_top = max(1, PAIR - PAIR // 4)
    highest = jax.random.randint(first, (N_ROW,), lowest_top, PAIR + 1, dtype=jnp.int32)
    chosen = jax.random.randint(second, (), 0, N_ROW, dtype=jnp.int32)
    highest = jnp.where(jnp.arange(N_ROW, dtype=jnp.int32) == chosen, PAIR, highest)
    floor_count = highest // 2
    fraction = jax.random.randint(third, (N_ROW, N_ROW), 0, 65536, dtype=jnp.int32)
    taken = floor_count[:, None] + fraction * (highest[:, None] - floor_count[:, None] + 1) // 65536
    source = jax.random.randint(fourth, (N_ROW,), 0, N_ROW, dtype=jnp.int32)
    full = jnp.arange(N_ROW, dtype=jnp.int32)[None, :] == source[:, None]
    return jnp.where(full, highest[:, None], taken).astype(jnp.int32)


def draw_rinv(key, part):
    key = jax.random.fold_in(key, 13)
    first, second = jax.random.split(key)
    row_index = jnp.arange(N, dtype=jnp.int32)[:, None]
    col_index = jnp.arange(N, dtype=jnp.int32)[None, :]
    off = jax.random.normal(first, (N, N), jnp.float32) * 0.8 * (1.0 / N) ** 0.5
    diag = jnp.exp(jax.random.uniform(second, (N,), jnp.float32, -0.7, 0.7))
    upper = jnp.where(col_index > row_index, off, 0.0)
    return jnp.where(col_index == row_index, diag[:, None], upper).astype(jnp.float32)


def touch_ends(drawn, own_key, smallest, high):
    extent = drawn.shape
    place = [jax.random.randint(jax.random.fold_in(own_key, axis), (), 0, extent[axis]) for axis in range(len(extent))]
    drawn = drawn.at[tuple(place)].set(smallest)
    longest = extent.index(max(extent))
    place[longest] = (place[longest] + 1) % extent[longest]
    return drawn.at[tuple(place)].set(high)


def block_levels(rng, extent, pieces, least, high):
    loudness, own = 1.0, jax.random.fold_in(rng, 6)
    for dim, blocks in pieces:
        draws = jnp.exp(jax.random.uniform(jax.random.fold_in(own, dim), (blocks,), jnp.float32, least / len(pieces), high / len(pieces)))
        loudness = loudness * jnp.repeat(draws, extent[dim] // blocks).reshape([-1 if axis == dim else 1 for axis in range(len(extent))])
    return loudness


def centred(key, shape, width, limit, pieces=(), kind=jnp.bfloat16):
    level = block_levels(key, shape, pieces, -0.22, 0.18) if pieces else 1.0
    drawn = jax.random.normal(key, shape, jnp.float32) * width * level
    return jnp.minimum(jnp.maximum(drawn, -limit), limit).astype(kind)


def setup_inputs(seed: int = 0) -> dict:
    seeds = jax.random.split(jax.random.key(seed), 7)
    design = centred(seeds[0], (ROWS, N), 1.0, 6.0, ((0, 8), (1, 4)), jnp.float32)
    sign_bits = touch_ends(jax.random.randint(seeds[1], (ROWS,), 0, 2), jax.random.fold_in(seeds[1], 1), 0, 1).astype(jnp.int32)
    picks = draw_picks(jax.random.fold_in(seeds[6], 71), 0)
    counts = draw_counts(jax.random.fold_in(seeds[6], 71), 0)
    target = centred(seeds[4], (ROWS,), 1.0, 6.0, ((0, 8),), jnp.float32)
    rinv = draw_rinv(jax.random.fold_in(seeds[6], 71), 0)
    return {"design": design, "sign_bits": sign_bits, "picks": picks, "counts": counts, "target": target, "rinv": rinv}


HI = lax.Precision.HIGHEST

def walsh(size):
    index = jnp.arange(size, dtype=jnp.int32)
    common = jnp.bitwise_and(index[:, None], index[None, :])
    parity = jnp.zeros((size, size), jnp.int32)
    for shift in range(max(size.bit_length() - 1, 1)):
        parity = parity + jnp.bitwise_and(jnp.right_shift(common, shift), 1)
    return (1 - 2 * (parity % 2)).astype(jnp.float32)

def reference(design, sign_bits, picks, counts, target, rinv):
    signs = (2 * sign_bits - 1).astype(jnp.float32)
    signed = design * signs[:, None]
    blocks = signed.reshape(N_ROW, RD // HB, HB, N)
    mixed = jnp.einsum('bc,pqcn->pqbn', walsh(HB), blocks, precision=HI)
    transformed = jnp.einsum('ps,sqbn->pqbn', walsh(N_ROW), mixed, precision=HI)
    transformed = (transformed / jnp.sqrt(jnp.float32(ROWS))).reshape(ROWS, N)
    block_start = (jnp.arange(N_ROW, dtype=jnp.int32) * RD)[None, :, None]
    rows = (picks + block_start).astype(jnp.int32).reshape(-1)
    taken = jnp.take(transformed, rows, axis=0).reshape(N_ROW, N_ROW, PAIR, N)
    used = jnp.arange(PAIR, dtype=jnp.int32)[None, None, :] < counts[:, :, None]
    sketch = jnp.where(used[..., None], taken, jnp.float32(0.0)).reshape(SK, N)

    def forward(vector):
        return jnp.dot(design, jnp.dot(rinv, vector, precision=HI), precision=HI)

    def backward(vector):
        return jnp.dot(jnp.dot(vector, design, precision=HI), rinv, precision=HI)
    beta = jnp.sqrt(jnp.sum(target * target))
    left = target / beta
    right = backward(left)
    alpha = jnp.sqrt(jnp.sum(right * right))
    right = right / alpha
    search = right
    iterate = jnp.zeros((N,), jnp.float32)
    phibar = beta
    rhobar = alpha
    for step in range(ITERS):
        left = forward(right) - alpha * left
        beta = jnp.sqrt(jnp.sum(left * left))
        left = left / beta
        right = backward(left) - beta * right
        alpha = jnp.sqrt(jnp.sum(right * right))
        right = right / alpha
        rho = jnp.sqrt(rhobar * rhobar + beta * beta)
        cosine = rhobar / rho
        sine = beta / rho
        theta = sine * alpha
        rhobar = -cosine * alpha
        phi = cosine * phibar
        phibar = sine * phibar
        iterate = iterate + phi / rho * search
        search = right - theta / rho * search
    solution = jnp.dot(rinv, iterate, precision=HI)
    return (sketch, solution, left)
```

```python
import functools

import jax
import jax.numpy as jnp
import numpy as np
from jax import lax
from jax.experimental import pallas as pl
from jax.experimental.pallas import tpu as pltpu
from jax.sharding import PartitionSpec as P

HB = 256
PAIR = 16
ITERS = 2
LANE = 128
CHUNKS = 2
F32 = jnp.float32
VMEM = pl.BlockSpec(memory_space=pltpu.VMEM)


def swap(array, axis, mask):
    return lax.ppermute(array, axis, [(i, i ^ mask) for i in range(lax.axis_size(axis))])


def gathered(array, axis):
    return [array] + [swap(array, axis, mask) for mask in range(1, lax.axis_size(axis))]


def tree(values):
    while len(values) > 1:
        values = [values[i] + values[i + 1] for i in range(0, len(values), 2)]
    return values[0]


def walsh(size):
    index = np.arange(size)
    common = index[:, None] & index[None, :]
    parity = np.zeros((size, size), np.int64)
    for shift in range(size.bit_length()):
        parity ^= (common >> shift) & 1
    return (1 - 2 * parity).astype(np.float32)


def call(body, out_shape, *operands, megabytes=24, flops=0, size=0):
    return pl.pallas_call(
        body,
        out_shape=out_shape,
        in_specs=[VMEM] * len(operands),
        out_specs=jax.tree.map(lambda _: VMEM, out_shape),
        compiler_params=pltpu.CompilerParams(vmem_limit_bytes=megabytes << 20),
        cost_estimate=pl.CostEstimate(flops=flops, bytes_accessed=size, transcendentals=0),
    )(*operands)


def fold_rows(block):
    return block.reshape(block.shape[0] // 8, 8, LANE).sum(axis=0)


def total(rows):
    return jnp.sum(jnp.sum(rows, axis=0, keepdims=True), axis=1, keepdims=True)


def splat(scalar):
    return jnp.broadcast_to(scalar, (1, LANE))


def left_product(vector, matrix_ref, out_ref):
    blocks, tiles = matrix_ref.shape[0] // LANE, matrix_ref.shape[1] // LANE
    sums = [jnp.zeros((8, LANE), F32) for _ in range(tiles)]
    for block in range(blocks):
        across = jnp.broadcast_to(vector[block : block + 1, :], (LANE, LANE)).T
        for tile in range(tiles):
            part = matrix_ref[block * LANE : (block + 1) * LANE, tile * LANE : (tile + 1) * LANE]
            sums[tile] = sums[tile] + fold_rows(part * across)
    for tile in range(tiles):
        out_ref[tile : tile + 1, :] = jnp.sum(sums[tile], axis=0, keepdims=True)


def left_product_long(vector_ref, matrix_ref, out_ref):
    blocks, tiles = matrix_ref.shape[0] // LANE, matrix_ref.shape[1] // LANE

    def step(block, sums):
        across = jnp.broadcast_to(vector_ref[pl.ds(block, 1), :], (LANE, LANE)).T
        rows = pl.ds(pl.multiple_of(block * LANE, LANE), LANE)
        return tuple(
            sums[tile] + fold_rows(matrix_ref[rows, tile * LANE : (tile + 1) * LANE] * across)
            for tile in range(tiles)
        )

    sums = lax.fori_loop(0, blocks, step, tuple(jnp.zeros((8, LANE), F32) for _ in range(tiles)))
    for tile in range(tiles):
        out_ref[tile : tile + 1, :] = jnp.sum(sums[tile], axis=0, keepdims=True)


def right_product(matrix_ref, vector, out_ref):
    blocks, tiles = matrix_ref.shape[0] // LANE, matrix_ref.shape[1] // LANE

    def step(block, carry):
        rows = pl.ds(pl.multiple_of(block * LANE, LANE), LANE)
        sums = jnp.zeros((LANE, LANE), F32)
        for tile in range(tiles):
            sums = sums + matrix_ref[rows, tile * LANE : (tile + 1) * LANE] * vector[tile : tile + 1, :]
        out_ref[pl.ds(block, 1), :] = jnp.sum(fold_rows(sums.T), axis=0, keepdims=True)
        return carry

    lax.fori_loop(0, blocks, step, 0)


def pack_width(width):
    return -(-(width // LANE + 1) // 8) * 8


def first_body(design_ref, target_ref, out_ref):
    tiles = design_ref.shape[1] // LANE
    target = target_ref[...]
    out_ref[...] = jnp.zeros_like(out_ref)
    left_product(target, design_ref, out_ref)
    out_ref[tiles : tiles + 1, :] = splat(total(target * target))


def back_body(groups, rinv_ref, *refs):
    parts, (term_ref, beta_ref, scratch) = refs[:groups], refs[groups:]
    summed = tree([ref[...] for ref in parts])
    tiles = rinv_ref.shape[0] // LANE
    beta = jnp.sqrt(summed[tiles : tiles + 1, :])
    beta_ref[...] = beta
    scratch[...] = summed[:tiles, :] / beta
    left_product_long(scratch, rinv_ref, term_ref)


def forward_body(groups, first, rinv_ref, design_ref, *refs):
    parts = refs[:groups]
    if first:
        image_ref, right_ref, held_ref, alpha_ref = refs[groups:]
        right = tree([ref[...] for ref in parts])
    else:
        before_ref, beta_ref, image_ref, right_ref, held_ref, alpha_ref = refs[groups:]
        right = tree([ref[...] for ref in parts]) - beta_ref[...] * before_ref[...]
    alpha = jnp.sqrt(total(right * right))
    alpha_ref[...] = splat(alpha)
    right = right / alpha
    right_ref[...] = right
    right_product(rinv_ref, right, held_ref)
    right_product(design_ref, held_ref[...], image_ref)


def turn_body(groups, last, *refs):
    parts, refs = refs[:groups], refs[groups:]
    before_ref, beta_ref, alpha_ref = refs[:3]
    left = tree([ref[...] for ref in parts]) - alpha_ref[...] * (before_ref[...] / beta_ref[...])
    square = splat(total(left * left))
    if last:
        left_ref, out_ref = refs[3:]
        left_ref[...] = left
        out_ref[...] = jnp.broadcast_to(square, out_ref.shape)
    else:
        design_ref, left_ref, out_ref = refs[3:]
        left_ref[...] = left
        tiles = design_ref.shape[1] // LANE
        out_ref[...] = jnp.zeros_like(out_ref)
        left_product(left, design_ref, out_ref)
        out_ref[tiles : tiles + 1, :] = square


def last_body(groups, *refs):
    parts, refs = refs[:groups], refs[groups:]
    left_ref, refs = refs[0], refs[1:]
    betas = [ref[...] for ref in refs[:ITERS]]
    alphas = [ref[...] for ref in refs[ITERS : 2 * ITERS]]
    held = [ref[...] for ref in refs[2 * ITERS : 3 * ITERS]]
    basis_ref, solution_ref = refs[3 * ITERS :]
    last = jnp.sqrt(tree([ref[...] for ref in parts])[:1, :])
    basis_ref[...] = left_ref[...] / last
    betas.append(last)
    phibar, rhobar = betas[0], alphas[0]
    search, iterate = held[0], jnp.zeros_like(held[0])
    for step in range(ITERS):
        beta = betas[step + 1]
        rho = jnp.sqrt(rhobar * rhobar + beta * beta)
        cosine = rhobar / rho
        sine = beta / rho
        phi = cosine * phibar
        phibar = sine * phibar
        iterate = iterate + phi / rho * search
        if step + 1 < ITERS:
            alpha = alphas[step + 1]
            search = held[step + 1] - sine * alpha / rho * search
            rhobar = -cosine * alpha
    solution_ref[...] = iterate


def shape(*dims):
    return jax.ShapeDtypeStruct(dims, F32)


def least_squares(design, target, rinv):
    rows, width = design.shape
    whole = rinv.shape[1]
    row_groups, col_groups = lax.axis_size("row"), lax.axis_size("col")
    packed = shape(pack_width(width), LANE)
    scalar = shape(1, LANE)
    big, small = rinv.size, design.size
    message = call(
        first_body, packed, design, target.reshape(rows // LANE, LANE), flops=2 * small, size=4 * small
    )
    left, alpha, right = target.reshape(rows // LANE, LANE), None, None
    betas, alphas, held = [], [], []
    for step in range(ITERS):
        parts = gathered(message, "row")
        term, beta = pl.pallas_call(
            functools.partial(back_body, row_groups),
            out_shape=(shape(whole // LANE, LANE), scalar),
            in_specs=[VMEM] * (1 + row_groups),
            out_specs=(VMEM, VMEM),
            scratch_shapes=[pltpu.VMEM((width // LANE, LANE), F32)],
            compiler_params=pltpu.CompilerParams(vmem_limit_bytes=24 << 20),
            cost_estimate=pl.CostEstimate(flops=2 * big, bytes_accessed=4 * big, transcendentals=0),
        )(rinv, *parts)
        betas.append(beta)
        parts = gathered(term, "col")
        extra = () if step == 0 else (right, beta)
        image, right, kept, alpha = call(
            functools.partial(forward_body, col_groups, step == 0),
            (shape(rows // LANE, LANE), shape(whole // LANE, LANE), shape(width // LANE, LANE), scalar),
            rinv,
            design,
            *parts,
            *extra,
            flops=2 * big,
            size=4 * big,
        )
        alphas.append(alpha)
        held.append(kept)
        parts = gathered(image, "col")
        last = step + 1 == ITERS
        extra = () if last else (design,)
        left, message = call(
            functools.partial(turn_body, col_groups, last),
            (shape(rows // LANE, LANE), shape(8, LANE) if last else packed),
            *parts,
            left,
            beta,
            alpha,
            *extra,
            flops=2 * small,
            size=0 if last else 4 * small,
        )
    parts = gathered(message, "row")
    basis, solution = call(
        functools.partial(last_body, row_groups),
        (shape(rows // LANE, LANE), shape(width // LANE, LANE)),
        *parts,
        left,
        *betas,
        *alphas,
        *held,
    )
    return solution.reshape(-1), basis.reshape(-1)


def sample_body(own_ref, other_ref, mix_ref, out_ref):
    flip = 1 - 2 * pl.program_id(0).astype(F32)
    both = own_ref[...] + flip * other_ref[...]
    high = both.astype(jnp.bfloat16)
    low = (both - high.astype(F32)).astype(jnp.bfloat16)
    mix = mix_ref[0]
    out_ref[0] = jnp.dot(mix, high, preferred_element_type=F32) + jnp.dot(mix, low, preferred_element_type=F32)


def sample(own, other, mix):
    slots, rows, width = mix.shape[1], own.shape[0], own.shape[1]
    block = min(slots, 256)
    return pl.pallas_call(
        sample_body,
        grid=(2, slots // block),
        out_shape=shape(2, slots, width),
        in_specs=[
            pl.BlockSpec((rows, width), lambda i, j: (0, 0)),
            pl.BlockSpec((rows, width), lambda i, j: (0, 0)),
            pl.BlockSpec((1, block, rows), lambda i, j: (i, j, 0)),
        ],
        out_specs=pl.BlockSpec((1, block, width), lambda i, j: (i, j, 0)),
        compiler_params=pltpu.CompilerParams(vmem_limit_bytes=16 << 20),
        cost_estimate=pl.CostEstimate(
            flops=8 * slots * rows * width, bytes_accessed=4 * slots * (rows + 2 * width), transcendentals=0
        ),
    )(own, other, mix)


def mixers(picks, counts, rows):
    groups = lax.axis_size("row")
    bits = groups.bit_length() - 1
    me = lax.axis_index("row")
    used = jnp.arange(PAIR, dtype=jnp.int32)[None, :] < counts
    coded = jnp.where(used, picks[:, 0, :], -1).reshape(-1, LANE)
    coded = jnp.stack(gathered(coded, "row")).reshape(groups, groups, PAIR)
    order = jnp.arange(groups, dtype=jnp.int32) ^ me
    coded = coded[order][:, order]
    coded = coded.reshape((groups // 2, 2) + (2,) * bits + (PAIR,))
    at = [2 + bits - 1 - bit for bit in range(bits)]
    owner_order = [at[bit] for bit in range(2, bits)] + [at[0]]
    coded = coded.transpose([at[1], 1] + owner_order + [0, 2 + bits])
    coded = coded.reshape(2, 2, groups // 2, groups // 2, PAIR)
    block = jnp.arange(groups // 2, dtype=jnp.int32)
    parity = jnp.zeros_like(block)
    for bit in range(bits - 1):
        parity = parity ^ (jnp.right_shift(block & jnp.right_shift(me, 1), bit) & 1)
    sign = (1 - 2 * parity).astype(F32)
    low = (1 - 2 * (jnp.arange(2, dtype=jnp.int32) * (me & 1))).astype(F32)
    sign = low[:, None] * sign[None, :]
    sign = jnp.broadcast_to(sign[None, :, None, :, None], coded.shape)
    coded, sign = coded.reshape(-1), sign.reshape(-1)
    chosen = coded[:, None] == jnp.arange(rows, dtype=jnp.int32)[None, :]
    chosen = jnp.where(chosen, sign[:, None], 0.0).astype(jnp.bfloat16).reshape(-1, rows // HB, HB)
    mix = jnp.einsum("sqc,cb->sqb", chosen, jnp.asarray(walsh(HB), jnp.bfloat16), preferred_element_type=F32)
    return mix.astype(jnp.bfloat16).reshape(2, 2, -1, rows)


def sketch_rows(design, sign_bits, picks, counts):
    rows, width = design.shape
    groups = lax.axis_size("row")
    bits = groups.bit_length() - 1
    me = lax.axis_index("row")
    low = me & 1
    signs = (2 * sign_bits - 1).astype(F32)[:, None]
    half = width // 2
    piece = half // CHUNKS if half // CHUNKS >= LANE else half
    mix = mixers(picks, counts, rows)
    done_mine, done_other = [], []
    for start in range(0, half, piece):
        mine = jnp.where(low == 1, design[:, half + start : half + start + piece], design[:, start : start + piece])
        away = jnp.where(low == 1, design[:, start : start + piece], design[:, half + start : half + start + piece])
        mine, away = mine * signs, away * signs
        other = swap(away, "row", 1)
        send = sample(mine, other, mix[1])
        keep = sample(mine, other, mix[0])
        slots = send.shape[1]
        for bit in range(1, bits):
            arrived = swap(send, "row", 1 << bit)
            keep = keep + arrived
            slots //= 2
            send = keep[:, slots:]
            keep = keep[:, :slots]
        arrived = swap(send, "row", 1)
        done_mine.append(keep)
        done_other.append(arrived)
    mine, other = jnp.concatenate(done_mine, axis=2), jnp.concatenate(done_other, axis=2)
    left = jnp.where(low == 1, other, mine)
    right = jnp.where(low == 1, mine, other)
    both = jnp.concatenate([left, right], axis=2).reshape(2, groups // 2, PAIR, width)
    both = both.transpose(1, 0, 2, 3).reshape(groups * PAIR, width)
    return both / jnp.sqrt(jnp.float32(rows * groups))


def shards(design, sign_bits, picks, counts, target, rinv):
    sketch = sketch_rows(design, sign_bits, picks, counts)
    answer, basis = least_squares(design, target, rinv)
    return (sketch, answer, basis)


def solution(mesh):
    placed = (
        P("row", "col"),
        P("row"),
        P(None, "row", None),
        P(None, "row"),
        P("row"),
        P("col", None),
    )
    return jax.shard_map(
        shards,
        mesh=mesh,
        in_specs=placed,
        out_specs=(P("row", "col"), P("col"), P("row")),
        check_vma=False,
    )
```

```python
import functools

import jax
import jax.numpy as jnp
import numpy as np
from jax import lax
from jax.experimental import pallas as pl
from jax.experimental.pallas import tpu as pltpu
from jax.sharding import PartitionSpec as P

HB = 256
PAIR = 16
ITERS = 2
LANE = 128
CHUNKS = 2
F32 = jnp.float32
VMEM = pl.BlockSpec(memory_space=pltpu.VMEM)


def swap(array, axis, mask):
    return lax.ppermute(array, axis, [(i, i ^ mask) for i in range(lax.axis_size(axis))])


def exchange(copies, axis):
    return lax.all_to_all(copies, axis, split_axis=0, concat_axis=0, tiled=True)


def tree(values):
    while len(values) > 1:
        values = [values[i] + values[i + 1] for i in range(0, len(values), 2)]
    return values[0]


def walsh(size):
    index = np.arange(size)
    common = index[:, None] & index[None, :]
    parity = np.zeros((size, size), np.int64)
    for shift in range(size.bit_length()):
        parity ^= (common >> shift) & 1
    return (1 - 2 * parity).astype(np.float32)


def call(body, out_shape, *operands, scratch=(), flops=0, size=0):
    return pl.pallas_call(
        body,
        out_shape=out_shape,
        in_specs=[VMEM] * len(operands),
        out_specs=jax.tree.map(lambda _: VMEM, out_shape),
        scratch_shapes=scratch,
        compiler_params=pltpu.CompilerParams(vmem_limit_bytes=24 << 20),
        cost_estimate=pl.CostEstimate(flops=flops, bytes_accessed=size, transcendentals=0),
    )(*operands)


def fold_rows(block):
    return block.reshape(block.shape[0] // 8, 8, LANE).sum(axis=0)


def total(rows):
    return jnp.sum(jnp.sum(rows, axis=0, keepdims=True), axis=1, keepdims=True)


def splat(scalar):
    return jnp.broadcast_to(scalar, (1, LANE))


def left_product(vector, matrix_ref, out_ref):
    blocks, tiles = matrix_ref.shape[0] // LANE, matrix_ref.shape[1] // LANE
    sums = [jnp.zeros((8, LANE), F32) for _ in range(tiles)]
    for block in range(blocks):
        across = jnp.broadcast_to(vector[block : block + 1, :], (LANE, LANE)).T
        for tile in range(tiles):
            part = matrix_ref[block * LANE : (block + 1) * LANE, tile * LANE : (tile + 1) * LANE]
            sums[tile] = sums[tile] + fold_rows(part * across)
    for tile in range(tiles):
        out_ref[tile : tile + 1, :] = jnp.sum(sums[tile], axis=0, keepdims=True)


def left_product_long(vector_ref, matrix_ref, out_ref):
    blocks, tiles = matrix_ref.shape[0] // LANE, matrix_ref.shape[1] // LANE

    def step(block, sums):
        across = jnp.broadcast_to(vector_ref[pl.ds(block, 1), :], (LANE, LANE)).T
        rows = pl.ds(pl.multiple_of(block * LANE, LANE), LANE)
        return tuple(
            sums[tile] + fold_rows(matrix_ref[rows, tile * LANE : (tile + 1) * LANE] * across)
            for tile in range(tiles)
        )

    sums = lax.fori_loop(0, blocks, step, tuple(jnp.zeros((8, LANE), F32) for _ in range(tiles)))
    for tile in range(tiles):
        out_ref[tile : tile + 1, :] = jnp.sum(sums[tile], axis=0, keepdims=True)


def right_product(matrix_ref, vector, out_ref):
    blocks, tiles = matrix_ref.shape[0] // LANE, matrix_ref.shape[1] // LANE

    def step(block, carry):
        rows = pl.ds(pl.multiple_of(block * LANE, LANE), LANE)
        sums = jnp.zeros((LANE, LANE), F32)
        for tile in range(tiles):
            sums = sums + matrix_ref[rows, tile * LANE : (tile + 1) * LANE] * vector[tile : tile + 1, :]
        out_ref[pl.ds(block, 1), :] = jnp.sum(fold_rows(sums.T), axis=0, keepdims=True)
        return carry

    lax.fori_loop(0, blocks, step, 0)


def rounded(count, unit):
    return -(-count // unit) * unit


def message_rows(width):
    return rounded(width // LANE + 1, 8)


def copy_out(out_ref):
    first = out_ref[0]
    for index in range(1, out_ref.shape[0]):
        out_ref[index] = first


def signs_across(bits_ref, block):
    signs = (2 * bits_ref[block : block + 1, :] - 1).astype(F32)
    return jnp.broadcast_to(signs, (LANE, LANE)).T


def first_body(design_ref, target_ref, bits_ref, picks_ref, counts_ref, out_ref, *away_refs):
    rows, width = design_ref.shape
    tiles = width // LANE
    target = target_ref[...]
    out_ref[0] = jnp.zeros(out_ref.shape[1:], F32)
    left_product(target, design_ref, out_ref.at[0])
    out_ref[0, tiles : tiles + 1, :] = splat(total(target * target))
    slot = lax.broadcasted_iota(jnp.int32, picks_ref.shape, 1)
    coded = jnp.where(slot < counts_ref[...], picks_ref[...], -1).astype(F32)
    start = message_rows(width)
    out_ref[0, start : start + coded.shape[0], : coded.shape[1]] = coded
    copy_out(out_ref)
    low = lax.axis_index("row") & 1
    half = width // 2
    for chunk, away_ref in enumerate(away_refs):
        piece = away_ref.shape[1]
        for block in range(rows // LANE):
            part = pl.ds(block * LANE, LANE)
            signs = signs_across(bits_ref, block)
            for tile in range(0, piece, LANE):
                column = pl.multiple_of((1 - low) * half + chunk * piece + tile, LANE)
                away_ref[part, tile : tile + LANE] = design_ref[part, pl.ds(column, LANE)] * signs


def back_body(rinv_ref, parts_ref, term_ref, beta_ref, scratch):
    tiles = rinv_ref.shape[0] // LANE
    summed = tree([parts_ref[i, : tiles + 1, :] for i in range(parts_ref.shape[0])])
    beta = jnp.sqrt(summed[tiles : tiles + 1, :])
    beta_ref[...] = beta
    scratch[...] = summed[:tiles, :] / beta
    left_product_long(scratch, rinv_ref, term_ref.at[0])
    copy_out(term_ref)


def forward_body(first, rinv_ref, design_ref, parts_ref, *refs):
    right = tree([parts_ref[i] for i in range(parts_ref.shape[0])])
    if not first:
        before_ref, beta_ref, *refs = refs
        right = right - beta_ref[...] * before_ref[...]
    image_ref, right_ref, held_ref, alpha_ref = refs
    alpha = jnp.sqrt(total(right * right))
    alpha_ref[...] = splat(alpha)
    right = right / alpha
    right_ref[...] = right
    right_product(rinv_ref, right, held_ref)
    right_product(design_ref, held_ref[...], image_ref.at[0])
    copy_out(image_ref)


def turn_body(last, parts_ref, before_ref, beta_ref, alpha_ref, *refs):
    left = tree([parts_ref[i] for i in range(parts_ref.shape[0])])
    left = left - alpha_ref[...] * (before_ref[...] / beta_ref[...])
    square = splat(total(left * left))
    if last:
        left_ref, out_ref = refs
        out_ref[...] = jnp.broadcast_to(square, out_ref.shape)
    else:
        design_ref, left_ref, out_ref = refs
        tiles = design_ref.shape[1] // LANE
        out_ref[0] = jnp.zeros(out_ref.shape[1:], F32)
        left_product(left, design_ref, out_ref.at[0])
        out_ref[0, tiles : tiles + 1, :] = square
        copy_out(out_ref)
    left_ref[...] = left


def last_body(parts_ref, left_ref, *refs):
    betas = [ref[...] for ref in refs[:ITERS]]
    alphas = [ref[...] for ref in refs[ITERS : 2 * ITERS]]
    held = [ref[...] for ref in refs[2 * ITERS : 3 * ITERS]]
    basis_ref, solution_ref = refs[3 * ITERS :]
    last = jnp.sqrt(tree([parts_ref[i] for i in range(parts_ref.shape[0])])[:1, :])
    basis_ref[...] = left_ref[...] / last
    betas.append(last)
    phibar, rhobar = betas[0], alphas[0]
    search, iterate = held[0], jnp.zeros_like(held[0])
    for step in range(ITERS):
        beta = betas[step + 1]
        rho = jnp.sqrt(rhobar * rhobar + beta * beta)
        cosine = rhobar / rho
        sine = beta / rho
        phi = cosine * phibar
        phibar = sine * phibar
        iterate = iterate + phi / rho * search
        if step + 1 < ITERS:
            alpha = alphas[step + 1]
            search = held[step + 1] - sine * alpha / rho * search
            rhobar = -cosine * alpha
    solution_ref[...] = iterate


def shape(*dims):
    return jax.ShapeDtypeStruct(dims, F32)


def mix_body(parts_ref, walsh_ref, order_ref, out_ref):
    groups = parts_ref.shape[0]
    rows = out_ref.shape[3]
    bits = groups.bit_length() - 1
    start = parts_ref.shape[1] - rounded(groups, 8)
    me = lax.axis_index("row")
    local = lax.broadcasted_iota(jnp.int32, (PAIR, rows), 1).astype(F32)

    def step(block, carry):
        coded = parts_ref[block, start : start + rounded(groups, 8), :]
        filler = jnp.zeros((LANE - coded.shape[0], LANE), F32)
        coded = jnp.concatenate([coded, filler], axis=0).T
        parity = jnp.int32(0)
        for bit in range(bits):
            parity = parity ^ ((block & me) >> bit)
        sign = (1 - 2 * (parity & 1)).astype(F32)
        chosen = []
        for owner in range(groups):
            match = jnp.broadcast_to(coded[:PAIR, owner : owner + 1], (PAIR, rows)) == local
            chosen.append(jnp.where(match, sign, 0.0))
        chosen = jnp.concatenate(chosen, axis=0).astype(jnp.bfloat16)
        for part in range(rows // HB):
            columns = slice(part * HB, (part + 1) * HB)
            mixed = jnp.dot(chosen[:, columns], walsh_ref[...], preferred_element_type=F32)
            mixed = mixed.astype(jnp.bfloat16)
            for owner in range(groups):
                apart = owner ^ me
                place = jnp.int32(0)
                for bit in list(range(2, bits)) + [0]:
                    place = 2 * place + ((apart >> bit) & 1)
                place = pl.multiple_of((place * (groups // 2) + (block >> 1)) * PAIR, PAIR)
                rows_here = mixed[owner * PAIR : (owner + 1) * PAIR, :]
                out_ref[(apart >> 1) & 1, block & 1, pl.ds(place, PAIR), columns] = rows_here
        return carry

    lax.fori_loop(0, groups, step, 0)


def sample_body(chunk, design_ref, bits_ref, other_ref, mix_ref, order_ref, send_ref, keep_ref, both):
    rows, piece = other_ref.shape
    half = design_ref.shape[1] // 2
    low = lax.axis_index("row") & 1
    column = pl.multiple_of(low * half + chunk * piece, LANE)
    for block in range(rows // LANE):
        part = slice(block * LANE, (block + 1) * LANE)
        signs = signs_across(bits_ref, block)
        signs = jnp.concatenate([signs] * (piece // LANE), axis=1)
        mine = design_ref[part, pl.ds(column, piece)] * signs
        other = other_ref[part, :]
        for index, value in enumerate((mine + other, mine - other)):
            high = value.astype(jnp.bfloat16)
            both[index, 0, part, :] = high
            both[index, 1, part, :] = (value - high.astype(F32)).astype(jnp.bfloat16)
    slots = mix_ref.shape[2]
    block = min(slots, HB)

    def step(place, carry):
        part = pl.ds(pl.multiple_of(place * block, block), block)
        for apart, out_ref in enumerate((keep_ref, send_ref)):
            for index in range(2):
                mix = mix_ref[apart, index, part, :]
                high = jnp.dot(mix, both[index, 0], preferred_element_type=F32)
                low = jnp.dot(mix, both[index, 1], preferred_element_type=F32)
                out_ref[index, part, :] = high + low
        return carry

    if slots == block:
        step(0, 0)
    else:
        lax.fori_loop(0, slots // block, step, 0)


def halve_body(kept_ref, arrived_ref, order_ref, send_ref, keep_ref):
    slots = keep_ref.shape[1]
    keep_ref[...] = kept_ref[:, :slots, :] + arrived_ref[:, :slots, :]
    send_ref[...] = kept_ref[:, slots:, :] + arrived_ref[:, slots:, :]


def assemble_body(chunks, scale, *refs):
    mine, other, out_ref = refs[:chunks], refs[chunks : 2 * chunks], refs[-1]
    low = lax.axis_index("row") & 1
    half = out_ref.shape[1] // 2
    for chunk in range(chunks):
        piece = mine[chunk].shape[2]
        for refs_here, place in ((mine, low), (other, 1 - low)):
            column = pl.ds(pl.multiple_of(place * half + chunk * piece, LANE), piece)
            for block in range(mine[chunk].shape[1] // PAIR):
                for index in range(2):
                    value = refs_here[chunk][index, block * PAIR : (block + 1) * PAIR, :]
                    out_ref[(2 * block + index) * PAIR : (2 * block + index + 1) * PAIR, column] = value / scale


def shape(*dims, dtype=F32):
    return jax.ShapeDtypeStruct(dims, dtype)


def shards(design, sign_bits, picks, counts, target, rinv):
    rows, width = design.shape
    whole = rinv.shape[1]
    row_groups, col_groups = lax.axis_size("row"), lax.axis_size("col")
    bits = row_groups.bit_length() - 1
    lines, half = rows // LANE, width // 2
    chunks = min(CHUNKS, half // LANE)
    piece = half // chunks
    big, small = rinv.size, design.size
    scalar = shape(1, LANE)
    deep = message_rows(width)
    sign_bits = sign_bits.reshape(lines, LANE)
    left = target.reshape(lines, LANE)

    message, *away = call(
        first_body,
        (shape(row_groups, deep + rounded(row_groups, 8), LANE),) + (shape(rows, piece),) * chunks,
        design,
        left,
        sign_bits,
        picks.reshape(row_groups, PAIR),
        counts,
        flops=2 * small,
        size=4 * small,
    )

    def sample(chunk, order):
        slots = row_groups * row_groups * PAIR // 4
        return call(
            functools.partial(sample_body, chunk),
            (shape(2, slots, piece),) * 2,
            design,
            sign_bits,
            arrived[chunk],
            mix,
            order,
            scratch=[pltpu.VMEM((2, 2, rows, piece), jnp.bfloat16)],
            flops=16 * slots * rows * piece,
            size=8 * rows * piece,
        )

    def halve(kept, arrived, order):
        slots = kept.shape[1] // 2
        return call(halve_body, (shape(2, slots, piece),) * 2, kept, arrived, order, size=12 * kept.size)

    def back(message):
        return call(
            back_body,
            (shape(col_groups, whole // LANE, LANE), scalar),
            rinv,
            message,
            scratch=[pltpu.VMEM((width // LANE, LANE), F32)],
            flops=2 * big,
            size=4 * big,
        )

    def forward(terms, *before):
        return call(
            functools.partial(forward_body, not before),
            (
                shape(col_groups, lines, LANE),
                shape(whole // LANE, LANE),
                shape(width // LANE, LANE),
                scalar,
            ),
            rinv,
            design,
            terms,
            *before,
            flops=2 * big,
            size=4 * big,
        )

    def turn(images, left, beta, alpha, last):
        return call(
            functools.partial(turn_body, last),
            (shape(lines, LANE), shape(row_groups, 8 if last else deep, LANE)),
            images,
            left,
            beta,
            alpha,
            *(() if last else (design,)),
            flops=2 * small,
            size=0 if last else 4 * small,
        )

    betas, alphas, held = [], [], []
    message = exchange(message, "row")
    arrived = [swap(part, "row", 1) for part in away]
    mix, sent, kept = None, [], []
    right = None
    for step in range(ITERS):
        term, beta = back(message)
        betas.append(beta)
        if step == 0:
            mix = call(
                mix_body,
                shape(2, 2, row_groups * row_groups * PAIR // 4, rows, dtype=jnp.bfloat16),
                message,
                jnp.asarray(walsh(HB), jnp.bfloat16),
                beta,
                size=4 * small,
            )
        else:
            for chunk in range(1, chunks):
                send, keep = sample(chunk, beta)
                sent.append(swap(send, "row", 2))
                kept.append(keep)
        terms = exchange(term, "col")
        image, right, part, alpha = forward(terms, *(() if step == 0 else (right, beta)))
        alphas.append(alpha)
        held.append(part)
        if step == 0:
            send, keep = sample(0, alpha)
            sent.append(swap(send, "row", 2))
            kept.append(keep)
        images = exchange(image, "col")
        left, message = turn(images, left, beta, alpha, step + 1 == ITERS)
        message = exchange(message, "row")
    basis, answer = call(
        last_body, (shape(lines, LANE), shape(width // LANE, LANE)), message, left, *betas, *alphas, *held
    )
    mine, other = [], []
    for chunk in range(chunks):
        keep, come = kept[chunk], sent[chunk]
        for bit in range(2, bits):
            send, keep = halve(keep, come, alpha)
            come = swap(send, "row", 1 << bit)
        send, keep = halve(keep, come, alpha)
        mine.append(keep)
        other.append(swap(send, "row", 1))
    scale = float(np.sqrt(np.float32(rows * row_groups)))
    sketch = call(
        functools.partial(assemble_body, chunks, scale), shape(row_groups * PAIR, width), *mine, *other
    )
    return (sketch, answer.reshape(-1), basis.reshape(-1))


def solution(mesh):
    placed = (
        P("row", "col"),
        P("row"),
        P(None, "row", None),
        P(None, "row"),
        P("row"),
        P("col", None),
    )
    return jax.shard_map(
        shards,
        mesh=mesh,
        in_specs=placed,
        out_specs=(P("row", "col"), P("col"), P("row")),
        check_vma=False,
    )
```

```python
import functools

import jax
import jax.numpy as jnp
import numpy as np
from jax import lax
from jax.experimental import pallas as pl
from jax.experimental.pallas import tpu as pltpu
from jax.sharding import PartitionSpec as P

HB = 256
PAIR = 16
ITERS = 2
LANE = 128
F32 = jnp.float32
VMEM = pl.BlockSpec(memory_space=pltpu.VMEM)


def exchange(copies, axis):
    return lax.all_to_all(copies, axis, split_axis=0, concat_axis=0, tiled=True)


def direct(array, axis):
    size = lax.axis_size(axis)
    return [array] + [
        lax.ppermute(array, axis, [(i, i ^ mask) for i in range(size)]) for mask in range(1, size)
    ]


def tree(values):
    while len(values) > 1:
        values = [values[i] + values[i + 1] for i in range(0, len(values), 2)]
    return values[0]


def walsh(size):
    index = np.arange(size)
    common = index[:, None] & index[None, :]
    parity = np.zeros((size, size), np.int64)
    for shift in range(size.bit_length()):
        parity ^= (common >> shift) & 1
    return (1 - 2 * parity).astype(np.float32)


def call(body, out_shape, *operands, scratch=(), flops=0, size=0):
    return pl.pallas_call(
        body,
        out_shape=out_shape,
        in_specs=[VMEM] * len(operands),
        out_specs=jax.tree.map(lambda _: VMEM, out_shape),
        scratch_shapes=scratch,
        compiler_params=pltpu.CompilerParams(vmem_limit_bytes=24 << 20),
        cost_estimate=pl.CostEstimate(flops=flops, bytes_accessed=size, transcendentals=0),
    )(*operands)


def fold_rows(block):
    return block.reshape(block.shape[0] // 8, 8, LANE).sum(axis=0)


def total(rows):
    return jnp.sum(jnp.sum(rows, axis=0, keepdims=True), axis=1, keepdims=True)


def splat(scalar):
    return jnp.broadcast_to(scalar, (1, LANE))


def left_product(vector, matrix_ref, out_ref):
    blocks, tiles = matrix_ref.shape[0] // LANE, matrix_ref.shape[1] // LANE
    sums = [jnp.zeros((8, LANE), F32) for _ in range(tiles)]
    for block in range(blocks):
        across = jnp.broadcast_to(vector[block : block + 1, :], (LANE, LANE)).T
        for tile in range(tiles):
            part = matrix_ref[block * LANE : (block + 1) * LANE, tile * LANE : (tile + 1) * LANE]
            sums[tile] = sums[tile] + fold_rows(part * across)
    for tile in range(tiles):
        out_ref[tile : tile + 1, :] = jnp.sum(sums[tile], axis=0, keepdims=True)


def left_product_long(vector_ref, matrix_ref, out_ref):
    blocks, tiles = matrix_ref.shape[0] // LANE, matrix_ref.shape[1] // LANE

    def step(block, sums):
        across = jnp.broadcast_to(vector_ref[pl.ds(block, 1), :], (LANE, LANE)).T
        rows = pl.ds(pl.multiple_of(block * LANE, LANE), LANE)
        return tuple(
            sums[tile] + fold_rows(matrix_ref[rows, tile * LANE : (tile + 1) * LANE] * across)
            for tile in range(tiles)
        )

    sums = lax.fori_loop(0, blocks, step, tuple(jnp.zeros((8, LANE), F32) for _ in range(tiles)))
    for tile in range(tiles):
        out_ref[tile : tile + 1, :] = jnp.sum(sums[tile], axis=0, keepdims=True)


def right_product(matrix_ref, vector, out_ref):
    blocks, tiles = matrix_ref.shape[0] // LANE, matrix_ref.shape[1] // LANE

    def step(block, carry):
        rows = pl.ds(pl.multiple_of(block * LANE, LANE), LANE)
        sums = jnp.zeros((LANE, LANE), F32)
        for tile in range(tiles):
            sums = sums + matrix_ref[rows, tile * LANE : (tile + 1) * LANE] * vector[tile : tile + 1, :]
        out_ref[pl.ds(block, 1), :] = jnp.sum(fold_rows(sums.T), axis=0, keepdims=True)
        return carry

    lax.fori_loop(0, blocks, step, 0)


def rounded(count, unit):
    return -(-count // unit) * unit


def message_rows(width):
    return rounded(width // LANE + 1, 8)


def copy_out(out_ref):
    first = out_ref[0]
    for index in range(1, out_ref.shape[0]):
        out_ref[index] = first


def signs_across(bits_ref, block):
    signs = (2 * bits_ref[block : block + 1, :] - 1).astype(F32)
    return jnp.broadcast_to(signs, (LANE, LANE)).T


def first_body(design_ref, target_ref, picks_ref, counts_ref, out_ref):
    width = design_ref.shape[1]
    tiles = width // LANE
    target = target_ref[...]
    out_ref[0] = jnp.zeros(out_ref.shape[1:], F32)
    left_product(target, design_ref, out_ref.at[0])
    out_ref[0, tiles : tiles + 1, :] = splat(total(target * target))
    slot = lax.broadcasted_iota(jnp.int32, picks_ref.shape, 1)
    coded = jnp.where(slot < counts_ref[...], picks_ref[...], -1).astype(F32)
    start = message_rows(width)
    out_ref[0, start : start + coded.shape[0], : coded.shape[1]] = coded
    copy_out(out_ref)


def back_body(rinv_ref, parts_ref, term_ref, beta_ref, scratch):
    tiles = rinv_ref.shape[0] // LANE
    summed = tree([parts_ref[i, : tiles + 1, :] for i in range(parts_ref.shape[0])])
    beta = jnp.sqrt(summed[tiles : tiles + 1, :])
    beta_ref[...] = beta
    scratch[...] = summed[:tiles, :] / beta
    left_product_long(scratch, rinv_ref, term_ref)


def forward_body(groups, first, rinv_ref, design_ref, *refs):
    right = tree([ref[...] for ref in refs[:groups]])
    refs = refs[groups:]
    if not first:
        before_ref, beta_ref, *refs = refs
        right = right - beta_ref[...] * before_ref[...]
    image_ref, right_ref, held_ref, alpha_ref = refs
    alpha = jnp.sqrt(total(right * right))
    alpha_ref[...] = splat(alpha)
    right = right / alpha
    right_ref[...] = right
    right_product(rinv_ref, right, held_ref)
    right_product(design_ref, held_ref[...], image_ref)


def turn_body(groups, last, *refs):
    left = tree([ref[...] for ref in refs[:groups]])
    before_ref, beta_ref, alpha_ref, *refs = refs[groups:]
    left = left - alpha_ref[...] * (before_ref[...] / beta_ref[...])
    square = splat(total(left * left))
    if last:
        left_ref, out_ref = refs
        out_ref[...] = jnp.broadcast_to(square, out_ref.shape)
    else:
        design_ref, left_ref, out_ref = refs
        tiles = design_ref.shape[1] // LANE
        out_ref[0] = jnp.zeros(out_ref.shape[1:], F32)
        left_product(left, design_ref, out_ref.at[0])
        out_ref[0, tiles : tiles + 1, :] = square
        copy_out(out_ref)
    left_ref[...] = left


def last_body(parts_ref, left_ref, *refs):
    betas = [ref[...] for ref in refs[:ITERS]]
    alphas = [ref[...] for ref in refs[ITERS : 2 * ITERS]]
    held = [ref[...] for ref in refs[2 * ITERS : 3 * ITERS]]
    basis_ref, solution_ref = refs[3 * ITERS :]
    last = jnp.sqrt(tree([parts_ref[i] for i in range(parts_ref.shape[0])])[:1, :])
    basis_ref[...] = left_ref[...] / last
    betas.append(last)
    phibar, rhobar = betas[0], alphas[0]
    search, iterate = held[0], jnp.zeros_like(held[0])
    for step in range(ITERS):
        beta = betas[step + 1]
        rho = jnp.sqrt(rhobar * rhobar + beta * beta)
        cosine = rhobar / rho
        sine = beta / rho
        phi = cosine * phibar
        phibar = sine * phibar
        iterate = iterate + phi / rho * search
        if step + 1 < ITERS:
            alpha = alphas[step + 1]
            search = held[step + 1] - sine * alpha / rho * search
            rhobar = -cosine * alpha
    solution_ref[...] = iterate


def sample_body(scale, parts_ref, walsh_ref, design_ref, bits_ref, order_ref, out_ref, high_ref, low_ref):
    groups = out_ref.shape[0]
    rows, width = design_ref.shape
    spread = rounded(groups, 8)
    start = parts_ref.shape[1] - spread
    me, block = lax.axis_index("row"), pl.program_id(0)

    @pl.when(block == 0)
    def _():
        for line in range(rows // LANE):
            part = slice(line * LANE, (line + 1) * LANE)
            signs = signs_across(bits_ref, line)
            for tile in range(0, width, LANE):
                value = design_ref[part, tile : tile + LANE] * signs
                high = value.astype(jnp.bfloat16)
                high_ref[part, tile : tile + LANE] = high
                low_ref[part, tile : tile + LANE] = (value - high.astype(F32)).astype(jnp.bfloat16)

    coded = parts_ref[block, start : start + spread, :]
    filler = jnp.zeros((LANE - spread, LANE), F32)
    coded = jnp.concatenate([coded, filler], axis=0).T
    parity = jnp.int32(0)
    for bit in range(groups.bit_length() - 1):
        parity = parity ^ ((block & me) >> bit)
    sign = (1 - 2 * (parity & 1)).astype(F32)
    local = lax.broadcasted_iota(jnp.int32, (PAIR, rows), 1).astype(F32)
    chosen = []
    for owner in range(groups):
        match = jnp.broadcast_to(coded[:PAIR, owner : owner + 1], (PAIR, rows)) == local
        chosen.append(jnp.where(match, sign, 0.0))
    chosen = jnp.concatenate(chosen, axis=0).astype(jnp.bfloat16)
    mix = []
    for part in range(rows // HB):
        mixed = jnp.dot(chosen[:, part * HB : (part + 1) * HB], walsh_ref[...], preferred_element_type=F32)
        mix.append(mixed.astype(jnp.bfloat16))
    mix = jnp.concatenate(mix, axis=1)
    value = jnp.dot(mix, high_ref[...], preferred_element_type=F32)
    value = value + jnp.dot(mix, low_ref[...], preferred_element_type=F32)
    out_ref[...] = (value / scale).reshape(out_ref.shape)


def shape(*dims, dtype=F32):
    return jax.ShapeDtypeStruct(dims, dtype)


def shards(design, sign_bits, picks, counts, target, rinv):
    rows, width = design.shape
    whole = rinv.shape[1]
    row_groups, col_groups = lax.axis_size("row"), lax.axis_size("col")
    lines = rows // LANE
    big, small = rinv.size, design.size
    scalar = shape(1, LANE)
    deep = message_rows(width)
    left = target.reshape(lines, LANE)

    message = call(
        first_body,
        shape(row_groups, deep + rounded(row_groups, 8), LANE),
        design,
        left,
        picks.reshape(row_groups, PAIR),
        counts,
        flops=2 * small,
        size=4 * small,
    )

    def sample(message, order):
        scale = float(np.sqrt(np.float32(rows * row_groups)))
        signs = jnp.asarray(walsh(HB), jnp.bfloat16)
        operands = (message, signs, design, sign_bits.reshape(lines, LANE), order)
        return pl.pallas_call(
            functools.partial(sample_body, scale),
            grid=(row_groups,),
            out_shape=shape(row_groups, row_groups, PAIR, width),
            in_specs=[VMEM] * len(operands),
            out_specs=pl.BlockSpec((row_groups, 1, PAIR, width), lambda block: (0, block, 0, 0)),
            scratch_shapes=[pltpu.VMEM((rows, width), jnp.bfloat16)] * 2,
            compiler_params=pltpu.CompilerParams(vmem_limit_bytes=20 << 20),
            cost_estimate=pl.CostEstimate(
                flops=4 * row_groups * row_groups * PAIR * small,
                bytes_accessed=4 * row_groups * row_groups * PAIR * width,
                transcendentals=0,
            ),
        )(*operands)

    def back(message):
        return call(
            back_body,
            (shape(whole // LANE, LANE), scalar),
            rinv,
            message,
            scratch=[pltpu.VMEM((width // LANE, LANE), F32)],
            flops=2 * big,
            size=4 * big,
        )

    def forward(terms, *before):
        return call(
            functools.partial(forward_body, col_groups, not before),
            (shape(lines, LANE), shape(whole // LANE, LANE), shape(width // LANE, LANE), scalar),
            rinv,
            design,
            *terms,
            *before,
            flops=2 * big,
            size=4 * big,
        )

    def turn(images, left, beta, alpha, last):
        return call(
            functools.partial(turn_body, col_groups, last),
            (shape(lines, LANE), shape(row_groups, 8 if last else deep, LANE)),
            *images,
            left,
            beta,
            alpha,
            *(() if last else (design,)),
            flops=2 * small,
            size=0 if last else 4 * small,
        )

    betas, alphas, held = [], [], []
    message = exchange(message, "row")
    for step in range(ITERS):
        term, beta = back(message)
        betas.append(beta)
        if step == 0:
            sampled = sample(message, beta).reshape(row_groups * row_groups * PAIR, width)
            sketch = lax.psum_scatter(sampled, "row", scatter_dimension=0, tiled=True)
        terms = direct(term, "col")
        image, right, part, alpha = forward(terms, *(() if step == 0 else (right, beta)))
        alphas.append(alpha)
        held.append(part)
        images = direct(image, "col")
        left, message = turn(images, left, beta, alpha, step + 1 == ITERS)
        message = exchange(message, "row")
    basis, answer = call(
        last_body, (shape(lines, LANE), shape(width // LANE, LANE)), message, left, *betas, *alphas, *held
    )
    return (sketch, answer.reshape(-1), basis.reshape(-1))


def solution(mesh):
    placed = (
        P("row", "col"),
        P("row"),
        P(None, "row", None),
        P(None, "row"),
        P("row"),
        P("col", None),
    )
    return jax.shard_map(
        shards,
        mesh=mesh,
        in_specs=placed,
        out_specs=(P("row", "col"), P("col"), P("row")),
        check_vma=False,
    )
```

```python
import functools

import jax
import jax.numpy as jnp
import numpy as np
from jax import lax
from jax.experimental import pallas as pl
from jax.experimental.pallas import tpu as pltpu
from jax.sharding import PartitionSpec as P

HB = 256
PAIR = 16
ITERS = 2
LANE = 128
CHUNKS = 2
F32 = jnp.float32
VMEM = pl.BlockSpec(memory_space=pltpu.VMEM)
HBM = pl.BlockSpec(memory_space=pltpu.HBM)


def exchange(copies, axis):
    return lax.all_to_all(copies, axis, split_axis=0, concat_axis=0, tiled=True)


def direct(array, axis):
    size = lax.axis_size(axis)
    return [array] + [
        lax.ppermute(array, axis, [(i, i ^ mask) for i in range(size)]) for mask in range(1, size)
    ]


def tree(values):
    while len(values) > 1:
        values = [values[i] + values[i + 1] for i in range(0, len(values), 2)]
    return values[0]


def walsh(size):
    index = np.arange(size)
    common = index[:, None] & index[None, :]
    parity = np.zeros((size, size), np.int64)
    for shift in range(size.bit_length()):
        parity ^= (common >> shift) & 1
    return (1 - 2 * parity).astype(np.float32)


def call(body, out_shape, *operands, scratch=(), flops=0, size=0):
    return pl.pallas_call(
        body,
        out_shape=out_shape,
        in_specs=[VMEM] * len(operands),
        out_specs=jax.tree.map(lambda _: VMEM, out_shape),
        scratch_shapes=scratch,
        compiler_params=pltpu.CompilerParams(vmem_limit_bytes=24 << 20),
        cost_estimate=pl.CostEstimate(flops=flops, bytes_accessed=size, transcendentals=0),
    )(*operands)


def fold_rows(block):
    return block.reshape(block.shape[0] // 8, 8, LANE).sum(axis=0)


def total(rows):
    return jnp.sum(jnp.sum(rows, axis=0, keepdims=True), axis=1, keepdims=True)


def splat(scalar):
    return jnp.broadcast_to(scalar, (1, LANE))


def left_product(vector, matrix_ref, out_ref):
    blocks, tiles = matrix_ref.shape[0] // LANE, matrix_ref.shape[1] // LANE
    sums = [jnp.zeros((8, LANE), F32) for _ in range(tiles)]
    for block in range(blocks):
        across = jnp.broadcast_to(vector[block : block + 1, :], (LANE, LANE)).T
        for tile in range(tiles):
            part = matrix_ref[block * LANE : (block + 1) * LANE, tile * LANE : (tile + 1) * LANE]
            sums[tile] = sums[tile] + fold_rows(part * across)
    for tile in range(tiles):
        out_ref[tile : tile + 1, :] = jnp.sum(sums[tile], axis=0, keepdims=True)


def left_product_long(vector_ref, matrix_ref, out_ref):
    blocks, tiles = matrix_ref.shape[0] // LANE, matrix_ref.shape[1] // LANE

    def step(block, sums):
        across = jnp.broadcast_to(vector_ref[pl.ds(block, 1), :], (LANE, LANE)).T
        rows = pl.ds(pl.multiple_of(block * LANE, LANE), LANE)
        return tuple(
            sums[tile] + fold_rows(matrix_ref[rows, tile * LANE : (tile + 1) * LANE] * across)
            for tile in range(tiles)
        )

    sums = lax.fori_loop(0, blocks, step, tuple(jnp.zeros((8, LANE), F32) for _ in range(tiles)))
    for tile in range(tiles):
        out_ref[tile : tile + 1, :] = jnp.sum(sums[tile], axis=0, keepdims=True)


def right_product(matrix_ref, vector, out_ref):
    blocks, tiles = matrix_ref.shape[0] // LANE, matrix_ref.shape[1] // LANE

    def step(block, carry):
        rows = pl.ds(pl.multiple_of(block * LANE, LANE), LANE)
        sums = jnp.zeros((LANE, LANE), F32)
        for tile in range(tiles):
            sums = sums + matrix_ref[rows, tile * LANE : (tile + 1) * LANE] * vector[tile : tile + 1, :]
        out_ref[pl.ds(block, 1), :] = jnp.sum(fold_rows(sums.T), axis=0, keepdims=True)
        return carry

    lax.fori_loop(0, blocks, step, 0)


def rounded(count, unit):
    return -(-count // unit) * unit


def message_rows(width):
    return rounded(width // LANE + 1, 8)


def copy_out(out_ref):
    first = out_ref[0]
    for index in range(1, out_ref.shape[0]):
        out_ref[index] = first


def signs_across(bits_ref, block):
    signs = (2 * bits_ref[block : block + 1, :] - 1).astype(F32)
    return jnp.broadcast_to(signs, (LANE, LANE)).T


def first_body(design_ref, target_ref, bits_ref, picks_ref, counts_ref, *refs):
    chunks = len(refs) - 8
    out_ref, away_refs = refs[0], refs[1 : 1 + chunks]
    design, target_here, bits, picks, counts, away, sems = refs[1 + chunks :]
    rows, width = design.shape
    lines, tiles, half = rows // LANE, width // LANE, width // 2
    piece = half // chunks
    small = [
        pltpu.make_async_copy(source, place, sems.at[index])
        for index, (source, place) in enumerate(
            ((target_ref, target_here), (bits_ref, bits), (picks_ref, picks), (counts_ref, counts))
        )
    ]
    parts = [slice(line * LANE, (line + 1) * LANE) for line in range(lines)]
    large = [
        pltpu.make_async_copy(design_ref.at[part, :], design.at[part, :], sems.at[4 + line])
        for line, part in enumerate(parts)
    ]
    for copy in small + large:
        copy.start()
    for copy in small:
        copy.wait()
    low = lax.axis_index("row") & 1
    sums = [jnp.zeros((8, LANE), F32) for _ in range(tiles)]
    back = []
    for line, part in enumerate(parts):
        across = jnp.broadcast_to(target_here[line : line + 1, :], (LANE, LANE)).T
        signs = signs_across(bits, line)
        large[line].wait()
        for tile in range(tiles):
            value = design[part, tile * LANE : (tile + 1) * LANE]
            sums[tile] = sums[tile] + fold_rows(value * across)
        for tile in range(0, half, LANE):
            column = pl.multiple_of((1 - low) * half + tile, LANE)
            away[part, tile : tile + LANE] = design[part, pl.ds(column, LANE)] * signs
        for chunk in range(chunks):
            copy = pltpu.make_async_copy(
                away.at[part, chunk * piece : (chunk + 1) * piece],
                away_refs[chunk].at[part, :],
                sems.at[4 + lines * (1 + chunk) + line],
            )
            copy.start()
            back.append(copy)
    out_ref[0] = jnp.zeros(out_ref.shape[1:], F32)
    for tile in range(tiles):
        out_ref[0, tile : tile + 1, :] = jnp.sum(sums[tile], axis=0, keepdims=True)
    target = target_here[...]
    out_ref[0, tiles : tiles + 1, :] = splat(total(target * target))
    groups = picks.shape[0]
    owner = lax.broadcasted_iota(jnp.int32, (groups, groups), 0)
    same = owner == lax.broadcasted_iota(jnp.int32, (groups, groups), 1)
    limit = jnp.sum(jnp.where(same, counts[...].astype(F32), 0.0), axis=1, keepdims=True)
    slot = lax.broadcasted_iota(jnp.int32, picks.shape, 1).astype(F32)
    coded = jnp.where(slot < limit, picks[...].astype(F32), -1.0)
    start = message_rows(width)
    out_ref[0, start : start + groups, : coded.shape[1]] = coded
    copy_out(out_ref)
    for copy in back:
        copy.wait()


def back_body(rinv_ref, parts_ref, term_ref, beta_ref, scratch):
    tiles = rinv_ref.shape[0] // LANE
    summed = tree([parts_ref[i, : tiles + 1, :] for i in range(parts_ref.shape[0])])
    beta = jnp.sqrt(summed[tiles : tiles + 1, :])
    beta_ref[...] = beta
    scratch[...] = summed[:tiles, :] / beta
    left_product_long(scratch, rinv_ref, term_ref)


def forward_body(groups, first, rinv_ref, design_ref, *refs):
    right = tree([ref[...] for ref in refs[:groups]])
    refs = refs[groups:]
    if not first:
        before_ref, beta_ref, *refs = refs
        right = right - beta_ref[...] * before_ref[...]
    image_ref, right_ref, held_ref, alpha_ref = refs
    alpha = jnp.sqrt(total(right * right))
    alpha_ref[...] = splat(alpha)
    right = right / alpha
    right_ref[...] = right
    right_product(rinv_ref, right, held_ref)
    right_product(design_ref, held_ref[...], image_ref)


def turn_body(groups, last, *refs):
    left = tree([ref[...] for ref in refs[:groups]])
    before_ref, beta_ref, alpha_ref, *refs = refs[groups:]
    left = left - alpha_ref[...] * (before_ref[...] / beta_ref[...])
    square = splat(total(left * left))
    if last:
        left_ref, out_ref = refs
        out_ref[...] = jnp.broadcast_to(square, out_ref.shape)
    else:
        design_ref, left_ref, out_ref = refs
        tiles = design_ref.shape[1] // LANE
        out_ref[0] = jnp.zeros(out_ref.shape[1:], F32)
        left_product(left, design_ref, out_ref.at[0])
        out_ref[0, tiles : tiles + 1, :] = square
        copy_out(out_ref)
    left_ref[...] = left


def last_body(parts_ref, left_ref, *refs):
    betas = [ref[...] for ref in refs[:ITERS]]
    alphas = [ref[...] for ref in refs[ITERS : 2 * ITERS]]
    held = [ref[...] for ref in refs[2 * ITERS : 3 * ITERS]]
    basis_ref, solution_ref = refs[3 * ITERS :]
    last = jnp.sqrt(tree([parts_ref[i] for i in range(parts_ref.shape[0])])[:1, :])
    basis_ref[...] = left_ref[...] / last
    betas.append(last)
    phibar, rhobar = betas[0], alphas[0]
    search, iterate = held[0], jnp.zeros_like(held[0])
    for step in range(ITERS):
        beta = betas[step + 1]
        rho = jnp.sqrt(rhobar * rhobar + beta * beta)
        cosine = rhobar / rho
        sine = beta / rho
        phi = cosine * phibar
        phibar = sine * phibar
        iterate = iterate + phi / rho * search
        if step + 1 < ITERS:
            alpha = alphas[step + 1]
            search = held[step + 1] - sine * alpha / rho * search
            rhobar = -cosine * alpha
    solution_ref[...] = iterate


def sample_body(
    chunk, scale, parts_ref, walsh_ref, design_ref, bits_ref, pair_ref, order_ref, out_ref, both
):
    groups, piece = out_ref.shape[0], out_ref.shape[3]
    rows, width = design_ref.shape
    spread = rounded(groups, 8)
    start = parts_ref.shape[1] - spread
    me, block = lax.axis_index("row"), pl.program_id(0)
    low = me & 1

    @pl.when(block == 0)
    def _():
        for line in range(rows // LANE):
            part = slice(line * LANE, (line + 1) * LANE)
            far = pl.ds(pl.multiple_of((1 - low) * rows + line * LANE, LANE), LANE)
            signs = signs_across(bits_ref, line)
            for tile in range(0, piece, LANE):
                column = pl.multiple_of(low * (width // 2) + chunk * piece + tile, LANE)
                mine = design_ref[part, pl.ds(column, LANE)] * signs
                other = pair_ref[far, tile : tile + LANE]
                for index, value in enumerate((mine + other, mine - other)):
                    high = value.astype(jnp.bfloat16)
                    both[index, 0, part, tile : tile + LANE] = high
                    both[index, 1, part, tile : tile + LANE] = (value - high.astype(F32)).astype(jnp.bfloat16)

    coded = parts_ref[block, start : start + spread, :]
    filler = jnp.zeros((LANE - spread, LANE), F32)
    coded = jnp.concatenate([coded, filler], axis=0).T
    parity = jnp.int32(0)
    for bit in range(groups.bit_length() - 1):
        parity = parity ^ ((block & me) >> bit)
    sign = (1 - 2 * (parity & 1)).astype(F32)
    local = lax.broadcasted_iota(jnp.int32, (PAIR, rows), 1).astype(F32)
    chosen = []
    for owner in range(groups):
        match = jnp.broadcast_to(coded[:PAIR, owner : owner + 1], (PAIR, rows)) == local
        chosen.append(jnp.where(match, sign, 0.0))
    chosen = jnp.concatenate(chosen, axis=0).astype(jnp.bfloat16)
    mix = []
    for part in range(rows // HB):
        mixed = jnp.dot(chosen[:, part * HB : (part + 1) * HB], walsh_ref[...], preferred_element_type=F32)
        mix.append(mixed.astype(jnp.bfloat16))
    mix = jnp.concatenate(mix, axis=1)
    value = jnp.dot(mix, both[block & 1, 0], preferred_element_type=F32)
    value = value + jnp.dot(mix, both[block & 1, 1], preferred_element_type=F32)
    out_ref[...] = (value / scale).reshape(out_ref.shape)


def assemble_body(*refs):
    chunks = len(refs) // 2
    mine, other, out_ref = refs[:chunks], refs[chunks : 2 * chunks], refs[-1]
    low = lax.axis_index("row") & 1
    half = out_ref.shape[1] // 2
    for chunk in range(chunks):
        piece = half // chunks
        for tile in range(0, piece, LANE):
            near = pl.multiple_of(low * half + chunk * piece + tile, LANE)
            far = pl.multiple_of((1 - low) * half + chunk * piece + tile, LANE)
            out_ref[:, pl.ds(near, LANE)] = mine[chunk][:, tile : tile + LANE]
            out_ref[:, pl.ds(far, LANE)] = other[chunk][:, tile : tile + LANE]


def shape(*dims, dtype=F32):
    return jax.ShapeDtypeStruct(dims, dtype)


def shards(design, sign_bits, picks, counts, target, rinv):
    rows, width = design.shape
    whole = rinv.shape[1]
    row_groups, col_groups = lax.axis_size("row"), lax.axis_size("col")
    lines = rows // LANE
    big, small = rinv.size, design.size
    scalar = shape(1, LANE)
    deep = message_rows(width)
    left = target.reshape(lines, LANE)
    bits = sign_bits.reshape(lines, LANE)
    half = width // 2
    chunks = min(CHUNKS, half // LANE)
    piece = half // chunks
    pairs = [[i, i + 1] for i in range(0, row_groups, 2)]
    quads = [list(range(i, row_groups, 2)) for i in range(2)]

    message, *away = pl.pallas_call(
        first_body,
        out_shape=(shape(row_groups, deep + rounded(row_groups, 8), LANE),) + (shape(rows, piece),) * chunks,
        in_specs=[HBM] * 5,
        out_specs=(VMEM,) + (HBM,) * chunks,
        scratch_shapes=[
            pltpu.VMEM((rows, width), F32),
            pltpu.VMEM((lines, LANE), F32),
            pltpu.VMEM((lines, LANE), jnp.int32),
            pltpu.VMEM((row_groups, PAIR), jnp.int32),
            pltpu.VMEM((1, row_groups), jnp.int32),
            pltpu.VMEM((rows, half), F32),
            pltpu.SemaphoreType.DMA((4 + lines * (1 + chunks),)),
        ],
        compiler_params=pltpu.CompilerParams(vmem_limit_bytes=58 << 20),
        cost_estimate=pl.CostEstimate(flops=2 * small, bytes_accessed=6 * small, transcendentals=0),
    )(design, left, bits, picks.reshape(row_groups, PAIR), counts.reshape(1, row_groups))

    def sample(chunk, pair, order):
        scale = float(np.sqrt(np.float32(rows * row_groups)))
        signs = jnp.asarray(walsh(HB), jnp.bfloat16)
        operands = (picked, signs, design, bits, pair, order)
        made = pl.pallas_call(
            functools.partial(sample_body, chunk, scale),
            grid=(row_groups,),
            out_shape=shape(row_groups, row_groups, PAIR, piece),
            in_specs=[VMEM] * len(operands),
            out_specs=pl.BlockSpec((row_groups, 1, PAIR, piece), lambda block: (0, block, 0, 0)),
            scratch_shapes=[pltpu.VMEM((2, 2, rows, piece), jnp.bfloat16)],
            compiler_params=pltpu.CompilerParams(vmem_limit_bytes=20 << 20),
            cost_estimate=pl.CostEstimate(
                flops=8 * row_groups * row_groups * PAIR * rows * piece,
                bytes_accessed=4 * row_groups * row_groups * PAIR * piece,
                transcendentals=0,
            ),
        )(*operands)
        made = made.reshape(row_groups * row_groups * PAIR, piece)
        return lax.psum_scatter(made, "row", scatter_dimension=0, axis_index_groups=quads, tiled=True)

    def finish(summed, order):
        summed, _ = lax.optimization_barrier((summed, order))
        low = lax.axis_index("row") & 1
        summed = summed.reshape(2, row_groups * PAIR, piece)
        mine = lax.dynamic_index_in_dim(summed, low, 0, keepdims=False)
        other = lax.dynamic_index_in_dim(summed, 1 - low, 0, keepdims=False)
        return mine, lax.ppermute(other, "row", [(i, i ^ 1) for i in range(row_groups)])

    def back(message):
        return call(
            back_body,
            (shape(whole // LANE, LANE), scalar),
            rinv,
            message,
            scratch=[pltpu.VMEM((width // LANE, LANE), F32)],
            flops=2 * big,
            size=4 * big,
        )

    def forward(terms, *before):
        return call(
            functools.partial(forward_body, col_groups, not before),
            (shape(lines, LANE), shape(whole // LANE, LANE), shape(width // LANE, LANE), scalar),
            rinv,
            design,
            *terms,
            *before,
            flops=2 * big,
            size=4 * big,
        )

    def turn(images, left, beta, alpha, last):
        return call(
            functools.partial(turn_body, col_groups, last),
            (shape(lines, LANE), shape(row_groups, 8 if last else deep, LANE)),
            *images,
            left,
            beta,
            alpha,
            *(() if last else (design,)),
            flops=2 * small,
            size=0 if last else 4 * small,
        )

    betas, alphas, held, summed = [], [], [], []
    pair = [lax.all_gather(part, "row", axis=0, axis_index_groups=pairs, tiled=True) for part in away]
    message = picked = exchange(message, "row")
    for step in range(ITERS):
        term, beta = back(message)
        betas.append(beta)
        if step == 0:
            summed.append(sample(0, pair[0], beta))
        terms = direct(term, "col")
        image, right, part, alpha = forward(terms, *(() if step == 0 else (right, beta)))
        alphas.append(alpha)
        held.append(part)
        if step == 0:
            summed += [sample(chunk, pair[chunk], alpha) for chunk in range(1, chunks)]
        images = direct(image, "col")
        left, message = turn(images, left, beta, alpha, step + 1 == ITERS)
        message = exchange(message, "row")
    basis, answer = call(
        last_body, (shape(lines, LANE), shape(width // LANE, LANE)), message, left, *betas, *alphas, *held
    )
    mine, other = zip(*[finish(value, message if i else alpha) for i, value in enumerate(summed)])
    sketch = call(assemble_body, shape(row_groups * PAIR, width), *mine, *other)
    return (sketch, answer.reshape(-1), basis.reshape(-1))


def solution(mesh):
    placed = (
        P("row", "col"),
        P("row"),
        P(None, "row", None),
        P(None, "row"),
        P("row"),
        P("col", None),
    )
    return jax.shard_map(
        shards,
        mesh=mesh,
        in_specs=placed,
        out_specs=(P("row", "col"), P("col"), P("row")),
        check_vma=False,
    )
```

```python
import functools

import jax
import jax.numpy as jnp
import numpy as np
from jax import lax
from jax.experimental import pallas as pl
from jax.experimental.pallas import tpu as pltpu
from jax.sharding import PartitionSpec as P

HB = 256
PAIR = 16
ITERS = 2
LANE = 128
NEAR = 4
F32 = jnp.float32
VMEM = pl.BlockSpec(memory_space=pltpu.VMEM)
HBM = pl.BlockSpec(memory_space=pltpu.HBM)


def exchange(copies, axis):
    return lax.all_to_all(copies, axis, split_axis=0, concat_axis=0, tiled=True)


def direct(array, axis):
    size = lax.axis_size(axis)
    return [array] + [
        lax.ppermute(array, axis, [(i, i ^ mask) for i in range(size)]) for mask in range(1, size)
    ]


def tree(values):
    while len(values) > 1:
        values = [values[i] + values[i + 1] for i in range(0, len(values), 2)]
    return values[0]


def walsh(size):
    index = np.arange(size)
    common = index[:, None] & index[None, :]
    parity = np.zeros((size, size), np.int64)
    for shift in range(size.bit_length()):
        parity ^= (common >> shift) & 1
    return (1 - 2 * parity).astype(np.float32)


def call(body, out_shape, *operands, scratch=(), flops=0, size=0):
    return pl.pallas_call(
        body,
        out_shape=out_shape,
        in_specs=[VMEM] * len(operands),
        out_specs=jax.tree.map(lambda _: VMEM, out_shape),
        scratch_shapes=scratch,
        compiler_params=pltpu.CompilerParams(vmem_limit_bytes=24 << 20),
        cost_estimate=pl.CostEstimate(flops=flops, bytes_accessed=size, transcendentals=0),
    )(*operands)


def fold_rows(block):
    return block.reshape(block.shape[0] // 8, 8, LANE).sum(axis=0)


def total(rows):
    return jnp.sum(jnp.sum(rows, axis=0, keepdims=True), axis=1, keepdims=True)


def splat(scalar):
    return jnp.broadcast_to(scalar, (1, LANE))


def left_product(vector, matrix_ref, out_ref):
    blocks, tiles = matrix_ref.shape[0] // LANE, matrix_ref.shape[1] // LANE
    sums = [jnp.zeros((8, LANE), F32) for _ in range(tiles)]
    for block in range(blocks):
        across = jnp.broadcast_to(vector[block : block + 1, :], (LANE, LANE)).T
        for tile in range(tiles):
            part = matrix_ref[block * LANE : (block + 1) * LANE, tile * LANE : (tile + 1) * LANE]
            sums[tile] = sums[tile] + fold_rows(part * across)
    for tile in range(tiles):
        out_ref[tile : tile + 1, :] = jnp.sum(sums[tile], axis=0, keepdims=True)


def left_product_long(vector_ref, matrix_ref, out_ref, copies=()):
    blocks, tiles = matrix_ref.shape[0] // LANE, matrix_ref.shape[1] // LANE

    def step(block, sums):
        across = jnp.broadcast_to(vector_ref[pl.ds(block, 1), :], (LANE, LANE)).T
        rows = pl.ds(pl.multiple_of(block * LANE, LANE), LANE)
        return tuple(
            sums[tile] + fold_rows(matrix_ref[rows, tile * LANE : (tile + 1) * LANE] * across)
            for tile in range(tiles)
        )

    sums = tuple(jnp.zeros((8, LANE), F32) for _ in range(tiles))
    if copies:
        for block, copy in enumerate(copies):
            copy.wait()
            sums = step(block, sums)
    else:
        sums = lax.fori_loop(0, blocks, step, sums)
    for tile in range(tiles):
        out_ref[tile : tile + 1, :] = jnp.sum(sums[tile], axis=0, keepdims=True)


def right_product(matrix_ref, vector, out_ref):
    blocks, tiles = matrix_ref.shape[0] // LANE, matrix_ref.shape[1] // LANE

    def step(block, carry):
        rows = pl.ds(pl.multiple_of(block * LANE, LANE), LANE)
        sums = jnp.zeros((LANE, LANE), F32)
        for tile in range(tiles):
            sums = sums + matrix_ref[rows, tile * LANE : (tile + 1) * LANE] * vector[tile : tile + 1, :]
        out_ref[pl.ds(block, 1), :] = jnp.sum(fold_rows(sums.T), axis=0, keepdims=True)
        return carry

    lax.fori_loop(0, blocks, step, 0)


def rounded(count, unit):
    return -(-count // unit) * unit


def message_rows(width):
    return rounded(width // LANE + 1, 8)


def copy_out(out_ref):
    first = out_ref[0]
    for index in range(1, out_ref.shape[0]):
        out_ref[index] = first


def signs_across(bits_ref, block):
    signs = (2 * bits_ref[block : block + 1, :] - 1).astype(F32)
    return jnp.broadcast_to(signs, (LANE, LANE)).T


def first_body(design_ref, target_ref, bits_ref, picks_ref, counts_ref, *refs):
    out_ref, away_refs = refs[0], refs[1:NEAR]
    design, target_here, bits, picks, counts, away, sems = refs[NEAR:]
    rows, width = design.shape
    lines, tiles, piece = rows // LANE, width // LANE, width // NEAR
    small = [
        pltpu.make_async_copy(source, place, sems.at[index])
        for index, (source, place) in enumerate(
            ((target_ref, target_here), (bits_ref, bits), (picks_ref, picks), (counts_ref, counts))
        )
    ]
    parts = [slice(line * LANE, (line + 1) * LANE) for line in range(lines)]
    large = [
        pltpu.make_async_copy(design_ref.at[part, :], design.at[part, :], sems.at[4 + line])
        for line, part in enumerate(parts)
    ]
    for copy in small + large:
        copy.start()
    for copy in small:
        copy.wait()
    place = lax.axis_index("row") % NEAR
    sums = [jnp.zeros((8, LANE), F32) for _ in range(tiles)]
    back = []
    for line, part in enumerate(parts):
        across = jnp.broadcast_to(target_here[line : line + 1, :], (LANE, LANE)).T
        signs = signs_across(bits, line)
        large[line].wait()
        for tile in range(tiles):
            value = design[part, tile * LANE : (tile + 1) * LANE]
            sums[tile] = sums[tile] + fold_rows(value * across)
        for mask in range(1, NEAR):
            for tile in range(0, piece, LANE):
                column = pl.multiple_of((place ^ mask) * piece + tile, LANE)
                away[mask - 1, part, tile : tile + LANE] = design[part, pl.ds(column, LANE)] * signs
            copy = pltpu.make_async_copy(
                away.at[mask - 1, part, :], away_refs[mask - 1].at[part, :], sems.at[4 + lines * mask + line]
            )
            copy.start()
            back.append(copy)
    out_ref[0] = jnp.zeros(out_ref.shape[1:], F32)
    for tile in range(tiles):
        out_ref[0, tile : tile + 1, :] = jnp.sum(sums[tile], axis=0, keepdims=True)
    target = target_here[...]
    out_ref[0, tiles : tiles + 1, :] = splat(total(target * target))
    groups = picks.shape[0]
    owner = lax.broadcasted_iota(jnp.int32, (groups, groups), 0)
    same = owner == lax.broadcasted_iota(jnp.int32, (groups, groups), 1)
    limit = jnp.sum(jnp.where(same, counts[...].astype(F32), 0.0), axis=1, keepdims=True)
    slot = lax.broadcasted_iota(jnp.int32, picks.shape, 1).astype(F32)
    coded = jnp.where(slot < limit, picks[...].astype(F32), -1.0)
    start = message_rows(width)
    out_ref[0, start : start + groups, : coded.shape[1]] = coded
    copy_out(out_ref)
    for copy in back:
        copy.wait()


def back_body(first, rinv_ref, parts_ref, term_ref, beta_ref, *refs):
    tiles = rinv_ref.shape[0] // LANE
    copies = []
    if first:
        rinv_here, scratch, sems = refs
        for block in range(tiles):
            part = slice(block * LANE, (block + 1) * LANE)
            copies.append(pltpu.make_async_copy(rinv_ref.at[part, :], rinv_here.at[part, :], sems.at[block]))
            copies[-1].start()
    else:
        rinv_here, (scratch,) = rinv_ref, refs
    summed = tree([parts_ref[i, : tiles + 1, :] for i in range(parts_ref.shape[0])])
    beta = jnp.sqrt(summed[tiles : tiles + 1, :])
    beta_ref[...] = beta
    scratch[...] = summed[:tiles, :] / beta
    left_product_long(scratch, rinv_here, term_ref, copies)


def forward_body(groups, first, rinv_ref, design_ref, *refs):
    right = tree([ref[...] for ref in refs[:groups]])
    refs = refs[groups:]
    if not first:
        before_ref, beta_ref, *refs = refs
        right = right - beta_ref[...] * before_ref[...]
    image_ref, right_ref, held_ref, alpha_ref = refs
    alpha = jnp.sqrt(total(right * right))
    alpha_ref[...] = splat(alpha)
    right = right / alpha
    right_ref[...] = right
    right_product(rinv_ref, right, held_ref)
    right_product(design_ref, held_ref[...], image_ref)


def turn_body(groups, last, *refs):
    left = tree([ref[...] for ref in refs[:groups]])
    before_ref, beta_ref, alpha_ref, *refs = refs[groups:]
    left = left - alpha_ref[...] * (before_ref[...] / beta_ref[...])
    square = splat(total(left * left))
    if last:
        left_ref, out_ref = refs
        out_ref[...] = jnp.broadcast_to(square, out_ref.shape)
    else:
        design_ref, left_ref, out_ref = refs
        tiles = design_ref.shape[1] // LANE
        out_ref[0] = jnp.zeros(out_ref.shape[1:], F32)
        left_product(left, design_ref, out_ref.at[0])
        out_ref[0, tiles : tiles + 1, :] = square
        copy_out(out_ref)
    left_ref[...] = left


def last_body(parts_ref, left_ref, *refs):
    betas = [ref[...] for ref in refs[:ITERS]]
    alphas = [ref[...] for ref in refs[ITERS : 2 * ITERS]]
    held = [ref[...] for ref in refs[2 * ITERS : 3 * ITERS]]
    basis_ref, solution_ref = refs[3 * ITERS :]
    last = jnp.sqrt(tree([parts_ref[i] for i in range(parts_ref.shape[0])])[:1, :])
    basis_ref[...] = left_ref[...] / last
    betas.append(last)
    phibar, rhobar = betas[0], alphas[0]
    search, iterate = held[0], jnp.zeros_like(held[0])
    for step in range(ITERS):
        beta = betas[step + 1]
        rho = jnp.sqrt(rhobar * rhobar + beta * beta)
        cosine = rhobar / rho
        sine = beta / rho
        phi = cosine * phibar
        phibar = sine * phibar
        iterate = iterate + phi / rho * search
        if step + 1 < ITERS:
            alpha = alphas[step + 1]
            search = held[step + 1] - sine * alpha / rho * search
            rhobar = -cosine * alpha
    solution_ref[...] = iterate


def mix_body(parts_ref, walsh_ref, order_ref, out_ref):
    groups, _, rows = out_ref.shape
    spread = rounded(groups, 8)
    start = parts_ref.shape[1] - spread
    me = lax.axis_index("row")
    local = lax.broadcasted_iota(jnp.int32, (PAIR, rows), 1).astype(F32)

    def step(block, carry):
        coded = [parts_ref[block, pl.ds(start + (apart ^ me), 1), :] for apart in range(groups)]
        coded = jnp.concatenate(coded + [jnp.zeros((LANE - groups, LANE), F32)], axis=0).T
        parity = jnp.int32(0)
        for bit in range(groups.bit_length() - 1):
            parity = parity ^ ((block & me) >> bit)
        sign = (1 - 2 * (parity & 1)).astype(F32)
        chosen = []
        for apart in range(groups):
            match = jnp.broadcast_to(coded[:PAIR, apart : apart + 1], (PAIR, rows)) == local
            chosen.append(jnp.where(match, sign, 0.0))
        chosen = jnp.concatenate(chosen, axis=0).astype(jnp.bfloat16)
        for part in range(rows // HB):
            columns = slice(part * HB, (part + 1) * HB)
            mixed = jnp.dot(chosen[:, columns], walsh_ref[...], preferred_element_type=F32)
            out_ref[block, :, columns] = mixed.astype(jnp.bfloat16)
        return carry

    if groups <= 8:
        for block in range(groups):
            step(block, 0)
    else:
        lax.fori_loop(0, groups, step, 0)


def sample_body(scale, design_ref, bits_ref, mix_ref, order_ref, *refs):
    near, (keep_ref, send_ref, both) = refs[: NEAR - 1], refs[NEAR - 1 :]
    rows, piece = near[0].shape
    groups = mix_ref.shape[0]
    place = lax.axis_index("row") % NEAR
    for line in range(rows // LANE):
        part = slice(line * LANE, (line + 1) * LANE)
        signs = signs_across(bits_ref, line)
        for tile in range(0, piece, LANE):
            column = pl.multiple_of(place * piece + tile, LANE)
            here = slice(tile, tile + LANE)
            values = [design_ref[part, pl.ds(column, LANE)] * signs] + [ref[part, here] for ref in near]
            apart = 1
            while apart < NEAR:
                for first in range(NEAR):
                    if not first & apart:
                        one, two = values[first], values[first | apart]
                        values[first], values[first | apart] = one + two, one - two
                apart *= 2
            for index, value in enumerate(values):
                high = value.astype(jnp.bfloat16)
                both[index, 0, part, here] = high
                both[index, 1, part, here] = (value - high.astype(F32)).astype(jnp.bfloat16)

    def step(block, carry):
        mix = mix_ref[block]
        value = jnp.dot(mix, both[block % NEAR, 0], preferred_element_type=F32)
        value = value + jnp.dot(mix, both[block % NEAR, 1], preferred_element_type=F32)
        value = value / scale
        slot = pl.ds(block * PAIR, PAIR)
        for apart in range(groups):
            far, low = apart // NEAR, apart % NEAR
            out_ref = send_ref if far >= groups // NEAR // 2 else keep_ref
            out_ref[far % (groups // NEAR // 2), low, slot, :] = value[apart * PAIR : (apart + 1) * PAIR, :]
        return carry

    if groups <= 8:
        for block in range(groups):
            step(block, 0)
    else:
        lax.fori_loop(0, groups, step, 0)


def halve_body(kept_ref, arrived_ref, order_ref, keep_ref, send_ref):
    half = keep_ref.shape[0]
    keep_ref[...] = kept_ref[:half] + arrived_ref[:half]
    send_ref[...] = kept_ref[half:] + arrived_ref[half:]


def split_body(kept_ref, arrived_ref, order_ref, *out_refs):
    for index, out_ref in enumerate(out_refs):
        out_ref[...] = kept_ref[0, index] + arrived_ref[0, index]


def assemble_body(*refs):
    parts, out_ref = refs[:-1], refs[-1]
    place = lax.axis_index("row") % NEAR
    piece = parts[0].shape[1]
    for mask, part_ref in enumerate(parts):
        for tile in range(0, piece, LANE):
            column = pl.multiple_of((place ^ mask) * piece + tile, LANE)
            out_ref[:, pl.ds(column, LANE)] = part_ref[:, tile : tile + LANE]


def shape(*dims, dtype=F32):
    return jax.ShapeDtypeStruct(dims, dtype)


def shards(design, sign_bits, picks, counts, target, rinv):
    rows, width = design.shape
    whole = rinv.shape[1]
    row_groups, col_groups = lax.axis_size("row"), lax.axis_size("col")
    lines = rows // LANE
    big, small = rinv.size, design.size
    scalar = shape(1, LANE)
    deep = message_rows(width)
    left = target.reshape(lines, LANE)
    bits = sign_bits.reshape(lines, LANE)
    piece = width // NEAR
    slots = row_groups * PAIR
    far = row_groups // NEAR

    message, *away = pl.pallas_call(
        first_body,
        out_shape=(shape(row_groups, deep + rounded(row_groups, 8), LANE),) + (shape(rows, piece),) * (NEAR - 1),
        in_specs=[HBM] * 5,
        out_specs=(VMEM,) + (HBM,) * (NEAR - 1),
        scratch_shapes=[
            pltpu.VMEM((rows, width), F32),
            pltpu.VMEM((lines, LANE), F32),
            pltpu.VMEM((lines, LANE), jnp.int32),
            pltpu.VMEM((row_groups, PAIR), jnp.int32),
            pltpu.VMEM((1, row_groups), jnp.int32),
            pltpu.VMEM((NEAR - 1, rows, piece), F32),
            pltpu.SemaphoreType.DMA((4 + lines * NEAR,)),
        ],
        compiler_params=pltpu.CompilerParams(vmem_limit_bytes=58 << 20),
        cost_estimate=pl.CostEstimate(flops=2 * small, bytes_accessed=7 * small, transcendentals=0),
    )(design, left, bits, picks.reshape(row_groups, PAIR), counts.reshape(1, row_groups))

    def swap(array, mask):
        return lax.ppermute(array, "row", [(i, i ^ mask) for i in range(row_groups)])

    def mix(order):
        signs = jnp.asarray(walsh(HB), jnp.bfloat16)
        made = shape(row_groups, slots, rows, dtype=jnp.bfloat16)
        return call(mix_body, made, picked, signs, order, flops=2 * row_groups * slots * rows * HB)

    def sample(near, mixed, order):
        scale = float(np.sqrt(np.float32(rows * row_groups)))
        return call(
            functools.partial(sample_body, scale),
            (shape(far // 2, NEAR, slots, piece),) * 2,
            design,
            bits,
            mixed,
            order,
            *near,
            scratch=[pltpu.VMEM((NEAR, 2, rows, piece), jnp.bfloat16)],
            flops=4 * row_groups * slots * rows * piece,
            size=4 * NEAR * rows * piece,
        )

    def gather_rows(keep, send, order):
        bit = row_groups // 2
        come = swap(send, bit)
        while bit > NEAR:
            bit //= 2
            half = keep.shape[0] // 2
            keep, send = call(halve_body, (shape(half, *keep.shape[1:]),) * 2, keep, come, order)
            come = swap(send, bit)
        return keep, come

    def trade(keep, come, order):
        mine, *others = call(split_body, (shape(slots, piece),) * NEAR, keep, come, order)
        parts = [mine] + [swap(part, mask + 1) for mask, part in enumerate(others)]
        return call(assemble_body, shape(slots, width), *parts, size=8 * slots * width)

    def back(rinv, message, first):
        outs, scratch = (shape(whole // LANE, LANE), scalar), [pltpu.VMEM((width // LANE, LANE), F32)]
        if first:
            outs += (shape(*rinv.shape),)
            scratch += [pltpu.SemaphoreType.DMA((width // LANE,))]
        return pl.pallas_call(
            functools.partial(back_body, first),
            out_shape=outs,
            in_specs=[HBM if first else VMEM, VMEM],
            out_specs=(VMEM,) * len(outs),
            scratch_shapes=scratch,
            compiler_params=pltpu.CompilerParams(vmem_limit_bytes=(34 if first else 24) << 20),
            cost_estimate=pl.CostEstimate(flops=2 * big, bytes_accessed=4 * big, transcendentals=0),
        )(rinv, message)

    def forward(terms, *before):
        return call(
            functools.partial(forward_body, col_groups, not before),
            (shape(lines, LANE), shape(whole // LANE, LANE), shape(width // LANE, LANE), scalar),
            here,
            design,
            *terms,
            *before,
            flops=2 * big,
            size=4 * big,
        )

    def turn(images, left, beta, alpha, last):
        return call(
            functools.partial(turn_body, col_groups, last),
            (shape(lines, LANE), shape(row_groups, 8 if last else deep, LANE)),
            *images,
            left,
            beta,
            alpha,
            *(() if last else (design,)),
            flops=2 * small,
            size=0 if last else 4 * small,
        )

    betas, alphas, held = [], [], []
    message = picked = exchange(message, "row")
    for step in range(ITERS):
        if step == 0:
            term, beta, here = back(rinv, message, True)
            away, _ = lax.optimization_barrier((away, beta))
            near = [swap(part, mask + 1) for mask, part in enumerate(away)]
        else:
            term, beta = back(here, message, False)
            keep, come = gather_rows(*sample(near, mixed, beta), beta)
        betas.append(beta)
        terms = direct(term, "col")
        image, right, part, alpha = forward(terms, *(() if step == 0 else (right, beta)))
        if step == 0:
            mixed = mix(alpha)
        alphas.append(alpha)
        held.append(part)
        images = direct(image, "col")
        left, message = turn(images, left, beta, alpha, step + 1 == ITERS)
        message = exchange(message, "row")
    basis, answer = call(
        last_body, (shape(lines, LANE), shape(width // LANE, LANE)), message, left, *betas, *alphas, *held
    )
    sketch = trade(keep, come, message)
    return (sketch, answer.reshape(-1), basis.reshape(-1))


def solution(mesh):
    placed = (
        P("row", "col"),
        P("row"),
        P(None, "row", None),
        P(None, "row"),
        P("row"),
        P("col", None),
    )
    return jax.shard_map(
        shards,
        mesh=mesh,
        in_specs=placed,
        out_specs=(P("row", "col"), P("col"), P("row")),
        check_vma=False,
    )
```

```python
import functools

import jax
import jax.numpy as jnp
import numpy as np
from jax import lax
from jax.experimental import pallas as pl
from jax.experimental.pallas import tpu as pltpu
from jax.sharding import PartitionSpec as P

HB = 256
PAIR = 16
ITERS = 2
LANE = 128
NEAR = 4
CHUNKS = 2
F32 = jnp.float32
VMEM = pl.BlockSpec(memory_space=pltpu.VMEM)
HBM = pl.BlockSpec(memory_space=pltpu.HBM)


def exchange(copies, axis):
    return lax.all_to_all(copies, axis, split_axis=0, concat_axis=0, tiled=True)


def direct(array, axis):
    size = lax.axis_size(axis)
    return [array] + [
        lax.ppermute(array, axis, [(i, i ^ mask) for i in range(size)]) for mask in range(1, size)
    ]


def tree(values):
    while len(values) > 1:
        values = [values[i] + values[i + 1] for i in range(0, len(values), 2)]
    return values[0]


def walsh(size):
    index = np.arange(size)
    common = index[:, None] & index[None, :]
    parity = np.zeros((size, size), np.int64)
    for shift in range(size.bit_length()):
        parity ^= (common >> shift) & 1
    return (1 - 2 * parity).astype(np.float32)


def call(body, out_shape, *operands, scratch=(), flops=0, size=0):
    return pl.pallas_call(
        body,
        out_shape=out_shape,
        in_specs=[VMEM] * len(operands),
        out_specs=jax.tree.map(lambda _: VMEM, out_shape),
        scratch_shapes=scratch,
        compiler_params=pltpu.CompilerParams(vmem_limit_bytes=24 << 20),
        cost_estimate=pl.CostEstimate(flops=flops, bytes_accessed=size, transcendentals=0),
    )(*operands)


def fold_rows(block):
    return block.reshape(block.shape[0] // 8, 8, LANE).sum(axis=0)


def total(rows):
    return jnp.sum(jnp.sum(rows, axis=0, keepdims=True), axis=1, keepdims=True)


def splat(scalar):
    return jnp.broadcast_to(scalar, (1, LANE))


def left_product(vector, matrix_ref, out_ref):
    blocks, tiles = matrix_ref.shape[0] // LANE, matrix_ref.shape[1] // LANE
    sums = [jnp.zeros((8, LANE), F32) for _ in range(tiles)]
    for block in range(blocks):
        across = jnp.broadcast_to(vector[block : block + 1, :], (LANE, LANE)).T
        for tile in range(tiles):
            part = matrix_ref[block * LANE : (block + 1) * LANE, tile * LANE : (tile + 1) * LANE]
            sums[tile] = sums[tile] + fold_rows(part * across)
    for tile in range(tiles):
        out_ref[tile : tile + 1, :] = jnp.sum(sums[tile], axis=0, keepdims=True)


def left_product_long(vector_ref, matrix_ref, out_ref, copies=()):
    blocks, tiles = matrix_ref.shape[0] // LANE, matrix_ref.shape[1] // LANE

    def step(block, sums):
        across = jnp.broadcast_to(vector_ref[pl.ds(block, 1), :], (LANE, LANE)).T
        rows = pl.ds(pl.multiple_of(block * LANE, LANE), LANE)
        return tuple(
            sums[tile] + fold_rows(matrix_ref[rows, tile * LANE : (tile + 1) * LANE] * across)
            for tile in range(tiles)
        )

    sums = tuple(jnp.zeros((8, LANE), F32) for _ in range(tiles))
    if copies:
        for block, copy in enumerate(copies):
            copy.wait()
            sums = step(block, sums)
    else:
        sums = lax.fori_loop(0, blocks, step, sums)
    for tile in range(tiles):
        out_ref[tile : tile + 1, :] = jnp.sum(sums[tile], axis=0, keepdims=True)


def right_product(matrix_ref, vector, out_ref):
    blocks, tiles = matrix_ref.shape[0] // LANE, matrix_ref.shape[1] // LANE

    def step(block, carry):
        rows = pl.ds(pl.multiple_of(block * LANE, LANE), LANE)
        sums = jnp.zeros((LANE, LANE), F32)
        for tile in range(tiles):
            sums = sums + matrix_ref[rows, tile * LANE : (tile + 1) * LANE] * vector[tile : tile + 1, :]
        out_ref[pl.ds(block, 1), :] = jnp.sum(fold_rows(sums.T), axis=0, keepdims=True)
        return carry

    lax.fori_loop(0, blocks, step, 0)


def rounded(count, unit):
    return -(-count // unit) * unit


def message_rows(width):
    return rounded(width // LANE + 1, 8)


def copy_out(out_ref):
    first = out_ref[0]
    for index in range(1, out_ref.shape[0]):
        out_ref[index] = first


def signs_across(bits_ref, block):
    signs = (2 * bits_ref[block : block + 1, :] - 1).astype(F32)
    return jnp.broadcast_to(signs, (LANE, LANE)).T


def first_body(design_ref, target_ref, bits_ref, picks_ref, counts_ref, *refs):
    out_ref, away_refs = refs[0], refs[1:-7]
    design, target_here, bits, picks, counts, away, sems = refs[-7:]
    chunks = len(away_refs) // (NEAR - 1)
    rows, width = design.shape
    lines, tiles, piece = rows // LANE, width // LANE, width // NEAR
    small = [
        pltpu.make_async_copy(source, place, sems.at[index])
        for index, (source, place) in enumerate(
            ((target_ref, target_here), (bits_ref, bits), (picks_ref, picks), (counts_ref, counts))
        )
    ]
    parts = [slice(line * LANE, (line + 1) * LANE) for line in range(lines)]
    large = [
        pltpu.make_async_copy(design_ref.at[part, :], design.at[part, :], sems.at[4 + line])
        for line, part in enumerate(parts)
    ]
    for copy in small + large:
        copy.start()
    for copy in small:
        copy.wait()
    place = lax.axis_index("row") % NEAR
    sums = [jnp.zeros((8, LANE), F32) for _ in range(tiles)]
    back = []
    for line, part in enumerate(parts):
        across = jnp.broadcast_to(target_here[line : line + 1, :], (LANE, LANE)).T
        signs = signs_across(bits, line)
        large[line].wait()
        for tile in range(tiles):
            value = design[part, tile * LANE : (tile + 1) * LANE]
            sums[tile] = sums[tile] + fold_rows(value * across)
        for mask in range(1, NEAR):
            for tile in range(0, piece, LANE):
                column = pl.multiple_of((place ^ mask) * piece + tile, LANE)
                away[mask - 1, part, tile : tile + LANE] = design[part, pl.ds(column, LANE)] * signs
            for chunk in range(chunks):
                index = chunk * (NEAR - 1) + mask - 1
                columns = slice(chunk * piece // chunks, (chunk + 1) * piece // chunks)
                copy = pltpu.make_async_copy(
                    away.at[mask - 1, part, columns],
                    away_refs[index].at[part, :],
                    sems.at[4 + lines * (index + 1) + line],
                )
                copy.start()
                back.append(copy)
    out_ref[0] = jnp.zeros(out_ref.shape[1:], F32)
    for tile in range(tiles):
        out_ref[0, tile : tile + 1, :] = jnp.sum(sums[tile], axis=0, keepdims=True)
    target = target_here[...]
    out_ref[0, tiles : tiles + 1, :] = splat(total(target * target))
    groups = picks.shape[0]
    owner = lax.broadcasted_iota(jnp.int32, (groups, groups), 0)
    same = owner == lax.broadcasted_iota(jnp.int32, (groups, groups), 1)
    limit = jnp.sum(jnp.where(same, counts[...].astype(F32), 0.0), axis=1, keepdims=True)
    slot = lax.broadcasted_iota(jnp.int32, picks.shape, 1).astype(F32)
    coded = jnp.where(slot < limit, picks[...].astype(F32), -1.0)
    start = message_rows(width)
    out_ref[0, start : start + groups, : coded.shape[1]] = coded
    copy_out(out_ref)
    for copy in back:
        copy.wait()


def back_body(first, rinv_ref, parts_ref, term_ref, beta_ref, *refs):
    tiles = rinv_ref.shape[0] // LANE
    copies = []
    if first:
        rinv_here, scratch, sems = refs
        for block in range(tiles):
            part = slice(block * LANE, (block + 1) * LANE)
            copies.append(pltpu.make_async_copy(rinv_ref.at[part, :], rinv_here.at[part, :], sems.at[block]))
            copies[-1].start()
    else:
        rinv_here, (scratch,) = rinv_ref, refs
    summed = tree([parts_ref[i, : tiles + 1, :] for i in range(parts_ref.shape[0])])
    beta = jnp.sqrt(summed[tiles : tiles + 1, :])
    beta_ref[...] = beta
    scratch[...] = summed[:tiles, :] / beta
    left_product_long(scratch, rinv_here, term_ref, copies)


def forward_body(groups, first, rinv_ref, design_ref, *refs):
    right = tree([ref[...] for ref in refs[:groups]])
    refs = refs[groups:]
    if not first:
        before_ref, beta_ref, *refs = refs
        right = right - beta_ref[...] * before_ref[...]
    image_ref, right_ref, held_ref, alpha_ref = refs
    alpha = jnp.sqrt(total(right * right))
    alpha_ref[...] = splat(alpha)
    right = right / alpha
    right_ref[...] = right
    right_product(rinv_ref, right, held_ref)
    right_product(design_ref, held_ref[...], image_ref)


def turn_body(groups, last, *refs):
    left = tree([ref[...] for ref in refs[:groups]])
    before_ref, beta_ref, alpha_ref, token_ref, *refs = refs[groups:]
    left = left - alpha_ref[...] * (before_ref[...] / beta_ref[...])
    square = splat(total(left * left))
    if last:
        left_ref, out_ref = refs
        out_ref[...] = jnp.broadcast_to(square, out_ref.shape)
    else:
        design_ref, left_ref, out_ref = refs
        tiles = design_ref.shape[1] // LANE
        out_ref[0] = jnp.zeros(out_ref.shape[1:], F32)
        left_product(left, design_ref, out_ref.at[0])
        out_ref[0, tiles : tiles + 1, :] = square
        copy_out(out_ref)
    left_ref[...] = left


def last_body(parts_ref, left_ref, *refs):
    betas = [ref[...] for ref in refs[:ITERS]]
    alphas = [ref[...] for ref in refs[ITERS : 2 * ITERS]]
    held = [ref[...] for ref in refs[2 * ITERS : 3 * ITERS]]
    basis_ref, solution_ref = refs[3 * ITERS :]
    last = jnp.sqrt(tree([parts_ref[i] for i in range(parts_ref.shape[0])])[:1, :])
    basis_ref[...] = left_ref[...] / last
    betas.append(last)
    phibar, rhobar = betas[0], alphas[0]
    search, iterate = held[0], jnp.zeros_like(held[0])
    for step in range(ITERS):
        beta = betas[step + 1]
        rho = jnp.sqrt(rhobar * rhobar + beta * beta)
        cosine = rhobar / rho
        sine = beta / rho
        phi = cosine * phibar
        phibar = sine * phibar
        iterate = iterate + phi / rho * search
        if step + 1 < ITERS:
            alpha = alphas[step + 1]
            search = held[step + 1] - sine * alpha / rho * search
            rhobar = -cosine * alpha
    solution_ref[...] = iterate


def mix_body(parts_ref, walsh_ref, order_ref, out_ref, token_ref):
    token_ref[...] = order_ref[...]
    groups, _, rows = out_ref.shape
    spread = rounded(groups, 8)
    start = parts_ref.shape[1] - spread
    me = lax.axis_index("row")
    local = lax.broadcasted_iota(jnp.int32, (PAIR, rows), 1).astype(F32)

    def step(block, carry):
        coded = [parts_ref[block, pl.ds(start + (apart ^ me), 1), :] for apart in range(groups)]
        coded = jnp.concatenate(coded + [jnp.zeros((LANE - groups, LANE), F32)], axis=0).T
        parity = jnp.int32(0)
        for bit in range(groups.bit_length() - 1):
            parity = parity ^ ((block & me) >> bit)
        sign = (1 - 2 * (parity & 1)).astype(F32)
        chosen = []
        for apart in range(groups):
            match = jnp.broadcast_to(coded[:PAIR, apart : apart + 1], (PAIR, rows)) == local
            chosen.append(jnp.where(match, sign, 0.0))
        chosen = jnp.concatenate(chosen, axis=0).astype(jnp.bfloat16)
        for part in range(rows // HB):
            columns = slice(part * HB, (part + 1) * HB)
            mixed = jnp.dot(chosen[:, columns], walsh_ref[...], preferred_element_type=F32)
            out_ref[block, :, columns] = mixed.astype(jnp.bfloat16)
        return carry

    if groups <= 8:
        for block in range(groups):
            step(block, 0)
    else:
        lax.fori_loop(0, groups, step, 0)


def sample_body(scale, start, design_ref, bits_ref, mix_ref, order_ref, *refs):
    near, (keep_ref, send_ref, token_ref, both) = refs[: NEAR - 1], refs[NEAR - 1 :]
    token_ref[...] = order_ref[...]
    rows, piece = near[0].shape
    quarter = design_ref.shape[1] // NEAR
    groups = mix_ref.shape[0]
    place = lax.axis_index("row") % NEAR
    for line in range(rows // LANE):
        part = slice(line * LANE, (line + 1) * LANE)
        signs = signs_across(bits_ref, line)
        for tile in range(0, piece, LANE):
            column = pl.multiple_of(place * quarter + start + tile, LANE)
            here = slice(tile, tile + LANE)
            values = [design_ref[part, pl.ds(column, LANE)] * signs] + [ref[part, here] for ref in near]
            apart = 1
            while apart < NEAR:
                for first in range(NEAR):
                    if not first & apart:
                        one, two = values[first], values[first | apart]
                        values[first], values[first | apart] = one + two, one - two
                apart *= 2
            for index, value in enumerate(values):
                high = value.astype(jnp.bfloat16)
                both[index, 0, part, here] = high
                both[index, 1, part, here] = (value - high.astype(F32)).astype(jnp.bfloat16)

    def step(block, carry):
        mix = mix_ref[block]
        value = jnp.dot(mix, both[block % NEAR, 0], preferred_element_type=F32)
        value = value + jnp.dot(mix, both[block % NEAR, 1], preferred_element_type=F32)
        value = value / scale
        slot = pl.ds(block * PAIR, PAIR)
        for apart in range(groups):
            far, low = apart // NEAR, apart % NEAR
            out_ref = send_ref if far >= groups // NEAR // 2 else keep_ref
            out_ref[far % (groups // NEAR // 2), low, slot, :] = value[apart * PAIR : (apart + 1) * PAIR, :]
        return carry

    if groups <= 8:
        for block in range(groups):
            step(block, 0)
    else:
        lax.fori_loop(0, groups, step, 0)


def halve_body(kept_ref, arrived_ref, order_ref, keep_ref, send_ref):
    half = keep_ref.shape[0]
    keep_ref[...] = kept_ref[:half] + arrived_ref[:half]
    send_ref[...] = kept_ref[half:] + arrived_ref[half:]


def join_body(kept_ref, arrived_ref, order_ref, out_ref, token_ref):
    token_ref[...] = order_ref[...]
    out_ref[...] = kept_ref[0] + arrived_ref[0]


def split_body(chunks, *refs):
    joined, (kept_ref, arrived_ref, order_ref, token_ref, *out_refs) = refs[: chunks - 1], refs[chunks - 1 :]
    token_ref[...] = order_ref[...]
    piece = kept_ref.shape[3]
    for chunk in range(chunks):
        columns = slice(chunk * piece, (chunk + 1) * piece)
        for index, out_ref in enumerate(out_refs):
            if chunk < chunks - 1:
                out_ref[:, columns] = joined[chunk][index]
            else:
                out_ref[:, columns] = kept_ref[0, index] + arrived_ref[0, index]


def assemble_body(*refs):
    parts, out_ref = refs[:-1], refs[-1]
    place = lax.axis_index("row") % NEAR
    piece = parts[0].shape[1]
    for mask, part_ref in enumerate(parts):
        for tile in range(0, piece, LANE):
            column = pl.multiple_of((place ^ mask) * piece + tile, LANE)
            out_ref[:, pl.ds(column, LANE)] = part_ref[:, tile : tile + LANE]


def shape(*dims, dtype=F32):
    return jax.ShapeDtypeStruct(dims, dtype)


def shards(design, sign_bits, picks, counts, target, rinv):
    rows, width = design.shape
    whole = rinv.shape[1]
    row_groups, col_groups = lax.axis_size("row"), lax.axis_size("col")
    lines = rows // LANE
    big, small = rinv.size, design.size
    scalar = shape(1, LANE)
    deep = message_rows(width)
    left = target.reshape(lines, LANE)
    bits = sign_bits.reshape(lines, LANE)
    chunks = min(CHUNKS, width // NEAR // LANE)
    piece = width // NEAR // chunks
    slots = row_groups * PAIR
    far = row_groups // NEAR

    message, *away = pl.pallas_call(
        first_body,
        out_shape=(shape(row_groups, deep + rounded(row_groups, 8), LANE),)
        + (shape(rows, piece),) * (chunks * (NEAR - 1)),
        in_specs=[HBM] * 5,
        out_specs=(VMEM,) + (HBM,) * (chunks * (NEAR - 1)),
        scratch_shapes=[
            pltpu.VMEM((rows, width), F32),
            pltpu.VMEM((lines, LANE), F32),
            pltpu.VMEM((lines, LANE), jnp.int32),
            pltpu.VMEM((row_groups, PAIR), jnp.int32),
            pltpu.VMEM((1, row_groups), jnp.int32),
            pltpu.VMEM((NEAR - 1, rows, width // NEAR), F32),
            pltpu.SemaphoreType.DMA((4 + lines * (1 + chunks * (NEAR - 1)),)),
        ],
        compiler_params=pltpu.CompilerParams(vmem_limit_bytes=58 << 20),
        cost_estimate=pl.CostEstimate(flops=2 * small, bytes_accessed=7 * small, transcendentals=0),
    )(design, left, bits, picks.reshape(row_groups, PAIR), counts.reshape(1, row_groups))

    def swap(array, mask):
        return lax.ppermute(array, "row", [(i, i ^ mask) for i in range(row_groups)])

    def mix(order):
        signs = jnp.asarray(walsh(HB), jnp.bfloat16)
        made = (shape(row_groups, slots, rows, dtype=jnp.bfloat16), scalar)
        return call(mix_body, made, picked, signs, order, flops=2 * row_groups * slots * rows * HB)

    def sample(chunk, mixed, order):
        scale = float(np.sqrt(np.float32(rows * row_groups)))
        return call(
            functools.partial(sample_body, scale, chunk * piece),
            (shape(far // 2, NEAR, slots, piece),) * 2 + (scalar,),
            design,
            bits,
            mixed,
            order,
            *near[chunk],
            scratch=[pltpu.VMEM((NEAR, 2, rows, piece), jnp.bfloat16)],
            flops=4 * row_groups * slots * rows * piece,
            size=4 * NEAR * rows * piece,
        )

    def halve(keep, come, order):
        bit = row_groups // 2
        while bit > NEAR:
            bit //= 2
            half = keep.shape[0] // 2
            keep, send = call(halve_body, (shape(half, *keep.shape[1:]),) * 2, keep, come, order)
            come = swap(send, bit)
        return keep, come

    def join(keep, come, order):
        keep, come = halve(keep, come, order)
        return call(join_body, (shape(*keep.shape[1:]), scalar), keep, come, order)

    def trade(joined, keep, come, order):
        token, mine, *others = call(
            functools.partial(split_body, chunks),
            (scalar,) + (shape(slots, width // NEAR),) * NEAR,
            *joined,
            *halve(keep, come, order),
            order,
        )
        return [mine] + [swap(part, mask + 1) for mask, part in enumerate(others)], token

    def back(rinv, message, first):
        outs, scratch = (shape(whole // LANE, LANE), scalar), [pltpu.VMEM((width // LANE, LANE), F32)]
        if first:
            outs += (shape(*rinv.shape),)
            scratch += [pltpu.SemaphoreType.DMA((width // LANE,))]
        return pl.pallas_call(
            functools.partial(back_body, first),
            out_shape=outs,
            in_specs=[HBM if first else VMEM, VMEM],
            out_specs=(VMEM,) * len(outs),
            scratch_shapes=scratch,
            compiler_params=pltpu.CompilerParams(vmem_limit_bytes=(34 if first else 24) << 20),
            cost_estimate=pl.CostEstimate(flops=2 * big, bytes_accessed=4 * big, transcendentals=0),
        )(rinv, message)

    def forward(terms, *before):
        return call(
            functools.partial(forward_body, col_groups, not before),
            (shape(lines, LANE), shape(whole // LANE, LANE), shape(width // LANE, LANE), scalar),
            here,
            design,
            *terms,
            *before,
            flops=2 * big,
            size=4 * big,
        )

    def turn(images, left, beta, alpha, token, last):
        return call(
            functools.partial(turn_body, col_groups, last),
            (shape(lines, LANE), shape(row_groups, 8 if last else deep, LANE)),
            *images,
            left,
            beta,
            alpha,
            token,
            *(() if last else (design,)),
            flops=2 * small,
            size=0 if last else 4 * small,
        )

    def spread(chunk, order):
        parts = away[chunk * (NEAR - 1) : (chunk + 1) * (NEAR - 1)]
        parts, _ = lax.optimization_barrier((parts, order))
        return [swap(part, mask + 1) for mask, part in enumerate(parts)]

    betas, alphas, held, joined = [], [], [], []
    message = picked = exchange(message, "row")
    near = [spread(0, message)]
    for step in range(ITERS):
        last = step + 1 == ITERS
        if step == 0:
            term, beta, here = back(rinv, message, True)
            mixed, token = mix(beta)
            near += [spread(chunk, beta) for chunk in range(1, chunks)]
        else:
            term, beta = back(here, message, False)
        betas.append(beta)
        terms = direct(term, "col")
        image, right, kept, alpha = forward(terms, *(() if step == 0 else (right, beta)))
        alphas.append(alpha)
        held.append(kept)
        if step == 0:
            parts = []
            token = alpha
            for chunk in range(chunks):
                keep, send, token = sample(chunk, mixed, token)
                if chunk < chunks - 1:
                    parts.append((keep, swap(send, row_groups // 2)))
            for part in parts:
                part, token = join(*part, token)
                joined.append(part)
        images = direct(image, "col")
        if last:
            quarters, token = trade(joined, keep, come, alpha)
        left, message = turn(images, left, beta, alpha, token, last)
        message = exchange(message, "row")
        if step == 0:
            send, _ = lax.optimization_barrier((send, message))
            come = swap(send, row_groups // 2)
    basis, answer = call(
        last_body, (shape(lines, LANE), shape(width // LANE, LANE)), message, left, *betas, *alphas, *held
    )
    sketch = call(assemble_body, shape(slots, width), *quarters, size=8 * slots * width)
    return (sketch, answer.reshape(-1), basis.reshape(-1))


def solution(mesh):
    placed = (
        P("row", "col"),
        P("row"),
        P(None, "row", None),
        P(None, "row"),
        P("row"),
        P("col", None),
    )
    return jax.shard_map(
        shards,
        mesh=mesh,
        in_specs=placed,
        out_specs=(P("row", "col"), P("col"), P("row")),
        check_vma=False,
    )
```

```python
import functools

import jax
import jax.numpy as jnp
import numpy as np
from jax import lax
from jax.experimental import pallas as pl
from jax.experimental.pallas import tpu as pltpu
from jax.sharding import PartitionSpec as P

HB = 256
PAIR = 16
ITERS = 2
LANE = 128
NEAR = 4
CHUNKS = 2
F32 = jnp.float32
VMEM = pl.BlockSpec(memory_space=pltpu.VMEM)
HBM = pl.BlockSpec(memory_space=pltpu.HBM)


def exchange(copies, axis):
    return lax.all_to_all(copies, axis, split_axis=0, concat_axis=0, tiled=True)


def direct(array, axis):
    size = lax.axis_size(axis)
    return [array] + [
        lax.ppermute(array, axis, [(i, i ^ mask) for i in range(size)]) for mask in range(1, size)
    ]


def tree(values):
    while len(values) > 1:
        values = [values[i] + values[i + 1] for i in range(0, len(values), 2)]
    return values[0]


def walsh(size):
    index = np.arange(size)
    common = index[:, None] & index[None, :]
    parity = np.zeros((size, size), np.int64)
    for shift in range(size.bit_length()):
        parity ^= (common >> shift) & 1
    return (1 - 2 * parity).astype(np.float32)


def call(body, out_shape, *operands, scratch=()):
    return pl.pallas_call(
        body,
        out_shape=out_shape,
        in_specs=[VMEM] * len(operands),
        out_specs=jax.tree.map(lambda _: VMEM, out_shape),
        scratch_shapes=scratch,
        compiler_params=pltpu.CompilerParams(vmem_limit_bytes=24 << 20),
    )(*operands)


def fold_rows(block):
    return block.reshape(block.shape[0] // 8, 8, LANE).sum(axis=0)


def total(rows):
    return jnp.sum(jnp.sum(rows, axis=0, keepdims=True), axis=1, keepdims=True)


def splat(scalar):
    return jnp.broadcast_to(scalar, (1, LANE))


def left_product(vector, matrix_ref, out_ref):
    blocks, tiles = matrix_ref.shape[0] // LANE, matrix_ref.shape[1] // LANE
    sums = [jnp.zeros((8, LANE), F32) for _ in range(tiles)]
    for block in range(blocks):
        weight = across(vector[block : block + 1, :])
        for tile in range(tiles):
            part = matrix_ref[block * LANE : (block + 1) * LANE, tile * LANE : (tile + 1) * LANE]
            sums[tile] = sums[tile] + fold_rows(part * weight)
    for tile in range(tiles):
        out_ref[tile : tile + 1, :] = jnp.sum(sums[tile], axis=0, keepdims=True)


def left_product_long(vector_ref, matrix_ref, out_ref, copies=()):
    blocks, tiles = matrix_ref.shape[0] // LANE, matrix_ref.shape[1] // LANE

    def step(block, sums):
        weight = across(vector_ref[pl.ds(block, 1), :])
        rows = pl.ds(pl.multiple_of(block * LANE, LANE), LANE)
        return tuple(
            sums[tile] + fold_rows(matrix_ref[rows, tile * LANE : (tile + 1) * LANE] * weight)
            for tile in range(tiles)
        )

    sums = tuple(jnp.zeros((8, LANE), F32) for _ in range(tiles))
    if copies:
        for block, copy in enumerate(copies):
            copy.wait()
            sums = step(block, sums)
    else:
        sums = lax.fori_loop(0, blocks, step, sums)
    for tile in range(tiles):
        out_ref[tile : tile + 1, :] = jnp.sum(sums[tile], axis=0, keepdims=True)


def right_product(matrix_ref, vector, out_ref):
    blocks, tiles = matrix_ref.shape[0] // LANE, matrix_ref.shape[1] // LANE

    def step(block, carry):
        rows = pl.ds(pl.multiple_of(block * LANE, LANE), LANE)
        sums = jnp.zeros((LANE, LANE), F32)
        for tile in range(tiles):
            sums = sums + matrix_ref[rows, tile * LANE : (tile + 1) * LANE] * vector[tile : tile + 1, :]
        out_ref[pl.ds(block, 1), :] = jnp.sum(fold_rows(sums.T), axis=0, keepdims=True)
        return carry

    lax.fori_loop(0, blocks, step, 0)


def rounded(count, unit):
    return -(-count // unit) * unit


def message_rows(width):
    return rounded(width // LANE + 1, 8)


def picks_at(width):
    return message_rows(width)


def signs_at(width, groups):
    return message_rows(width) + rounded(groups, 8)


def copy_out(out_ref):
    first = out_ref[0]
    for index in range(1, out_ref.shape[0]):
        out_ref[index] = first


def across(row):
    return jnp.broadcast_to(row, (LANE, LANE)).T


def first_body(design_ref, target_ref, bits_ref, picks_ref, counts_ref, *refs):
    out_ref, away_refs = refs[0], refs[1:-6]
    design, target_here, bits, picks, counts, sems = refs[-6:]
    rows, width = design.shape
    lines, tiles, quarter = rows // LANE, width // LANE, width // NEAR
    small = [
        pltpu.make_async_copy(source, place, sems.at[index])
        for index, (source, place) in enumerate(
            ((target_ref, target_here), (bits_ref, bits), (picks_ref, picks), (counts_ref, counts))
        )
    ]
    parts = [slice(line * LANE, (line + 1) * LANE) for line in range(lines)]
    large = [
        pltpu.make_async_copy(design_ref.at[part, :], design.at[part, :], sems.at[4 + line])
        for line, part in enumerate(parts)
    ]
    place = lax.axis_index("row") % NEAR
    away = []
    for index, away_ref in enumerate(away_refs):
        chunk, mask = index // (NEAR - 1), index % (NEAR - 1) + 1
        piece = away_ref.shape[1]
        column = pl.multiple_of((place ^ mask) * quarter + chunk * piece, LANE)
        source = design_ref.at[:, pl.ds(column, piece)]
        away.append(pltpu.make_async_copy(source, away_ref, sems.at[4 + lines + index]))
    for copy in small + large + away:
        copy.start()
    for copy in small:
        copy.wait()
    out_ref[0] = jnp.zeros(out_ref.shape[1:], F32)
    groups = picks.shape[0]
    owner = lax.broadcasted_iota(jnp.int32, (groups, groups), 0)
    same = owner == lax.broadcasted_iota(jnp.int32, (groups, groups), 1)
    limit = jnp.sum(jnp.where(same, counts[...].astype(F32), 0.0), axis=1, keepdims=True)
    slot = lax.broadcasted_iota(jnp.int32, picks.shape, 1).astype(F32)
    coded = jnp.where(slot < limit, picks[...].astype(F32), -1.0)
    start = picks_at(width)
    out_ref[0, start : start + groups, : coded.shape[1]] = coded
    start = signs_at(width, groups)
    out_ref[0, start : start + lines, :] = (2 * bits[...] - 1).astype(F32)
    target = target_here[...]
    out_ref[0, tiles : tiles + 1, :] = splat(total(target * target))
    sums = [jnp.zeros((8, LANE), F32) for _ in range(tiles)]
    for line, part in enumerate(parts):
        weight = across(target[line : line + 1, :])
        large[line].wait()
        for tile in range(tiles):
            sums[tile] = sums[tile] + fold_rows(design[part, tile * LANE : (tile + 1) * LANE] * weight)
    for tile in range(tiles):
        out_ref[0, tile : tile + 1, :] = jnp.sum(sums[tile], axis=0, keepdims=True)
    copy_out(out_ref)
    for copy in away:
        copy.wait()


def back_body(first, rinv_ref, parts_ref, term_ref, beta_ref, *refs):
    tiles = rinv_ref.shape[0] // LANE
    copies = []
    if first:
        rinv_here, scratch, sems = refs
        for block in range(tiles):
            part = slice(block * LANE, (block + 1) * LANE)
            copies.append(pltpu.make_async_copy(rinv_ref.at[part, :], rinv_here.at[part, :], sems.at[block]))
            copies[-1].start()
    else:
        rinv_here, (scratch,) = rinv_ref, refs
    summed = tree([parts_ref[i, : tiles + 1, :] for i in range(parts_ref.shape[0])])
    beta = jnp.sqrt(summed[tiles : tiles + 1, :])
    beta_ref[...] = beta
    scratch[...] = summed[:tiles, :] / beta
    left_product_long(scratch, rinv_here, term_ref, copies)


def forward_body(groups, first, rinv_ref, design_ref, *refs):
    right = tree([ref[...] for ref in refs[:groups]])
    refs = refs[groups:]
    if not first:
        before_ref, beta_ref, *refs = refs
        right = right - beta_ref[...] * before_ref[...]
    image_ref, right_ref, held_ref, alpha_ref = refs
    alpha = jnp.sqrt(total(right * right))
    alpha_ref[...] = splat(alpha)
    right = right / alpha
    right_ref[...] = right
    right_product(rinv_ref, right, held_ref)
    right_product(design_ref, held_ref[...], image_ref)


def turn_body(groups, last, *refs):
    left = tree([ref[...] for ref in refs[:groups]])
    before_ref, beta_ref, alpha_ref, token_ref, *refs = refs[groups:]
    left = left - alpha_ref[...] * (before_ref[...] / beta_ref[...])
    square = splat(total(left * left))
    if last:
        left_ref, out_ref = refs
        out_ref[...] = jnp.broadcast_to(square, out_ref.shape)
    else:
        design_ref, left_ref, out_ref = refs
        tiles = design_ref.shape[1] // LANE
        out_ref[0] = jnp.zeros(out_ref.shape[1:], F32)
        left_product(left, design_ref, out_ref.at[0])
        out_ref[0, tiles : tiles + 1, :] = square
        copy_out(out_ref)
    left_ref[...] = left


def last_body(parts_ref, left_ref, *refs):
    quarters, sketch_ref, refs = refs[-NEAR - 3 : -3], refs[-1], refs[:-1]
    place = lax.axis_index("row") % NEAR
    piece = quarters[0].shape[1]
    for mask, part_ref in enumerate(quarters):
        for tile in range(0, piece, LANE):
            column = pl.multiple_of((place ^ mask) * piece + tile, LANE)
            sketch_ref[:, pl.ds(column, LANE)] = part_ref[:, tile : tile + LANE]
    betas = [ref[...] for ref in refs[:ITERS]]
    alphas = [ref[...] for ref in refs[ITERS : 2 * ITERS]]
    held = [ref[...] for ref in refs[2 * ITERS : 3 * ITERS]]
    basis_ref, solution_ref = refs[-2:]
    last = jnp.sqrt(tree([parts_ref[i] for i in range(parts_ref.shape[0])])[:1, :])
    basis_ref[...] = left_ref[...] / last
    betas.append(last)
    phibar, rhobar = betas[0], alphas[0]
    search, iterate = held[0], jnp.zeros_like(held[0])
    for step in range(ITERS):
        beta = betas[step + 1]
        rho = jnp.sqrt(rhobar * rhobar + beta * beta)
        cosine = rhobar / rho
        sine = beta / rho
        phi = cosine * phibar
        phibar = sine * phibar
        iterate = iterate + phi / rho * search
        if step + 1 < ITERS:
            alpha = alphas[step + 1]
            search = held[step + 1] - sine * alpha / rho * search
            rhobar = -cosine * alpha
    solution_ref[...] = iterate


def mix_body(start, parts_ref, walsh_ref, order_ref, out_ref, token_ref):
    token_ref[...] = order_ref[...]
    groups, _, rows = out_ref.shape
    me = lax.axis_index("row")
    local = lax.broadcasted_iota(jnp.int32, (PAIR, rows), 1).astype(F32)

    def step(block, carry):
        coded = [parts_ref[block, pl.ds(start + (apart ^ me), 1), :] for apart in range(groups)]
        coded = jnp.concatenate(coded + [jnp.zeros((LANE - groups, LANE), F32)], axis=0).T
        parity = jnp.int32(0)
        for bit in range(groups.bit_length() - 1):
            parity = parity ^ ((block & me) >> bit)
        sign = (1 - 2 * (parity & 1)).astype(F32)
        chosen = []
        for apart in range(groups):
            match = jnp.broadcast_to(coded[:PAIR, apart : apart + 1], (PAIR, rows)) == local
            chosen.append(jnp.where(match, sign, 0.0))
        chosen = jnp.concatenate(chosen, axis=0).astype(jnp.bfloat16)
        for part in range(rows // HB):
            columns = slice(part * HB, (part + 1) * HB)
            mixed = jnp.dot(chosen[:, columns], walsh_ref[...], preferred_element_type=F32)
            out_ref[block, :, columns] = mixed.astype(jnp.bfloat16)
        return carry

    if groups <= 8:
        for block in range(groups):
            step(block, 0)
    else:
        lax.fori_loop(0, groups, step, 0)


def sample_body(scale, start, design_ref, parts_ref, mix_ref, order_ref, *refs):
    near, (keep_ref, send_ref, token_ref, both) = refs[: NEAR - 1], refs[NEAR - 1 :]
    token_ref[...] = order_ref[...]
    rows, piece = near[0].shape
    quarter = design_ref.shape[1] // NEAR
    groups = mix_ref.shape[0]
    me = lax.axis_index("row")
    signs_start = signs_at(design_ref.shape[1], groups)
    for line in range(rows // LANE):
        part = slice(line * LANE, (line + 1) * LANE)
        signs = [across(parts_ref[me ^ mask, signs_start + line : signs_start + line + 1, :]) for mask in range(NEAR)]
        for tile in range(0, piece, LANE):
            column = pl.multiple_of(me % NEAR * quarter + start + tile, LANE)
            here = slice(tile, tile + LANE)
            values = [design_ref[part, pl.ds(column, LANE)]] + [ref[part, here] for ref in near]
            values = [value * sign for value, sign in zip(values, signs)]
            apart = 1
            while apart < NEAR:
                for first in range(NEAR):
                    if not first & apart:
                        one, two = values[first], values[first | apart]
                        values[first], values[first | apart] = one + two, one - two
                apart *= 2
            for index, value in enumerate(values):
                high = value.astype(jnp.bfloat16)
                both[index, 0, part, here] = high
                both[index, 1, part, here] = (value - high.astype(F32)).astype(jnp.bfloat16)

    def step(block, carry):
        mix = mix_ref[block]
        value = jnp.dot(mix, both[block % NEAR, 0], preferred_element_type=F32)
        value = value + jnp.dot(mix, both[block % NEAR, 1], preferred_element_type=F32)
        value = value / scale
        slot = pl.ds(block * PAIR, PAIR)
        for apart in range(groups):
            far, low = apart // NEAR, apart % NEAR
            out_ref = send_ref if far >= groups // NEAR // 2 else keep_ref
            out_ref[far % (groups // NEAR // 2), low, slot, :] = value[apart * PAIR : (apart + 1) * PAIR, :]
        return carry

    if groups <= 8:
        for block in range(groups):
            step(block, 0)
    else:
        lax.fori_loop(0, groups, step, 0)


def halve_body(kept_ref, arrived_ref, order_ref, keep_ref, send_ref):
    half = keep_ref.shape[0]
    keep_ref[...] = kept_ref[:half] + arrived_ref[:half]
    send_ref[...] = kept_ref[half:] + arrived_ref[half:]


def join_body(kept_ref, arrived_ref, order_ref, out_ref, token_ref):
    token_ref[...] = order_ref[...]
    out_ref[...] = kept_ref[0] + arrived_ref[0]


def split_body(chunks, *refs):
    joined, (kept_ref, arrived_ref, order_ref, token_ref, *out_refs) = refs[: chunks - 1], refs[chunks - 1 :]
    token_ref[...] = order_ref[:1, :]
    piece = kept_ref.shape[3]
    for chunk in range(chunks):
        columns = slice(chunk * piece, (chunk + 1) * piece)
        for index, out_ref in enumerate(out_refs):
            if chunk < chunks - 1:
                out_ref[:, columns] = joined[chunk][index]
            else:
                out_ref[:, columns] = kept_ref[0, index] + arrived_ref[0, index]


def shape(*dims, dtype=F32):
    return jax.ShapeDtypeStruct(dims, dtype)


def shards(design, sign_bits, picks, counts, target, rinv):
    rows, width = design.shape
    whole = rinv.shape[1]
    row_groups, col_groups = lax.axis_size("row"), lax.axis_size("col")
    lines = rows // LANE
    scalar = shape(1, LANE)
    deep = message_rows(width)
    left = target.reshape(lines, LANE)
    bits = sign_bits.reshape(lines, LANE)
    chunks = min(CHUNKS, width // NEAR // LANE)
    piece = width // NEAR // chunks
    slots = row_groups * PAIR
    far = row_groups // NEAR

    message, *away = pl.pallas_call(
        first_body,
        out_shape=(shape(row_groups, signs_at(width, row_groups) + rounded(lines, 8), LANE),)
        + (shape(rows, piece),) * (chunks * (NEAR - 1)),
        in_specs=[HBM] * 5,
        out_specs=(VMEM,) + (HBM,) * (chunks * (NEAR - 1)),
        scratch_shapes=[
            pltpu.VMEM((rows, width), F32),
            pltpu.VMEM((lines, LANE), F32),
            pltpu.VMEM((lines, LANE), jnp.int32),
            pltpu.VMEM((row_groups, PAIR), jnp.int32),
            pltpu.VMEM((1, row_groups), jnp.int32),
            pltpu.SemaphoreType.DMA((4 + lines + chunks * (NEAR - 1),)),
        ],
        compiler_params=pltpu.CompilerParams(vmem_limit_bytes=58 << 20),
    )(design, left, bits, picks.reshape(row_groups, PAIR), counts.reshape(1, row_groups))

    def swap(array, mask):
        return lax.ppermute(array, "row", [(i, i ^ mask) for i in range(row_groups)])

    def mix(order):
        signs = jnp.asarray(walsh(HB), jnp.bfloat16)
        made = (shape(row_groups, slots, rows, dtype=jnp.bfloat16), scalar)
        return call(functools.partial(mix_body, picks_at(width)), made, picked, signs, order)

    def sample(chunk, mixed, order):
        scale = float(np.sqrt(np.float32(rows * row_groups)))
        return call(
            functools.partial(sample_body, scale, chunk * piece),
            (shape(far // 2, NEAR, slots, piece),) * 2 + (scalar,),
            design,
            picked,
            mixed,
            order,
            *near[chunk],
            scratch=[pltpu.VMEM((NEAR, 2, rows, piece), jnp.bfloat16)],
        )

    def halve(keep, come, order):
        bit = row_groups // 2
        while bit > NEAR:
            bit //= 2
            half = keep.shape[0] // 2
            keep, send = call(halve_body, (shape(half, *keep.shape[1:]),) * 2, keep, come, order)
            come = swap(send, bit)
        return keep, come

    def join(keep, come, order):
        keep, come = halve(keep, come, order)
        return call(join_body, (shape(*keep.shape[1:]), scalar), keep, come, order)

    def trade(joined, keep, come, order):
        token, mine, *others = call(
            functools.partial(split_body, chunks),
            (scalar,) + (shape(slots, width // NEAR),) * NEAR,
            *joined,
            *halve(keep, come, order),
            order,
        )
        return [mine] + [swap(part, mask + 1) for mask, part in enumerate(others)], token

    def back(rinv, message, first):
        outs, scratch = (shape(whole // LANE, LANE), scalar), [pltpu.VMEM((width // LANE, LANE), F32)]
        if first:
            outs += (shape(*rinv.shape),)
            scratch += [pltpu.SemaphoreType.DMA((width // LANE,))]
        return pl.pallas_call(
            functools.partial(back_body, first),
            out_shape=outs,
            in_specs=[HBM if first else VMEM, VMEM],
            out_specs=(VMEM,) * len(outs),
            scratch_shapes=scratch,
            compiler_params=pltpu.CompilerParams(vmem_limit_bytes=(34 if first else 24) << 20),
            )(rinv, message)

    def forward(terms, *before):
        return call(
            functools.partial(forward_body, col_groups, not before),
            (shape(lines, LANE), shape(whole // LANE, LANE), shape(width // LANE, LANE), scalar),
            here,
            design,
            *terms,
            *before,
        )

    def turn(images, left, beta, alpha, token, last):
        return call(
            functools.partial(turn_body, col_groups, last),
            (shape(lines, LANE), shape(row_groups, 8 if last else deep, LANE)),
            *images,
            left,
            beta,
            alpha,
            token,
            *(() if last else (design,)),
        )

    def spread(chunk, order):
        parts = away[chunk * (NEAR - 1) : (chunk + 1) * (NEAR - 1)]
        parts, _ = lax.optimization_barrier((parts, order))
        return [swap(part, mask + 1) for mask, part in enumerate(parts)]

    betas, alphas, held, joined = [], [], [], []
    message = picked = exchange(message, "row")
    near = [spread(0, message)]
    for step in range(ITERS):
        last = step + 1 == ITERS
        if step == 0:
            term, beta, here = back(rinv, message, True)
            mixed, token = mix(beta)
            near += [spread(chunk, beta) for chunk in range(1, chunks)]
        else:
            term, beta = back(here, message, False)
        betas.append(beta)
        terms = direct(term, "col")
        image, right, kept, alpha = forward(terms, *(() if step == 0 else (right, beta)))
        alphas.append(alpha)
        held.append(kept)
        if step == 0:
            parts = []
            for chunk in range(chunks):
                keep, send, token = sample(chunk, mixed, token if chunk == 0 else alpha)
                if chunk < chunks - 1:
                    parts.append((keep, swap(send, row_groups // 2)))
            for part in parts:
                part, token = join(*part, token)
                joined.append(part)
        images = direct(image, "col")
        if last:
            quarters, token = trade(joined, keep, come, images[1])
        left, message = turn(images, left, beta, alpha, token, last)
        message = exchange(message, "row")
        if step == 0:
            send, _ = lax.optimization_barrier((send, message))
            come = swap(send, row_groups // 2)
    basis, answer, sketch = call(
        last_body,
        (shape(lines, LANE), shape(width // LANE, LANE), shape(slots, width)),
        message,
        left,
        *betas,
        *alphas,
        *held,
        *quarters,
    )
    return (sketch, answer.reshape(-1), basis.reshape(-1))


def solution(mesh):
    placed = (
        P("row", "col"),
        P("row"),
        P(None, "row", None),
        P(None, "row"),
        P("row"),
        P("col", None),
    )
    return jax.shard_map(
        shards,
        mesh=mesh,
        in_specs=placed,
        out_specs=(P("row", "col"), P("col"), P("row")),
        check_vma=False,
    )
```

```python
import functools

import jax
import jax.numpy as jnp
import numpy as np
from jax import lax
from jax.experimental import pallas as pl
from jax.experimental.pallas import tpu as pltpu
from jax.sharding import PartitionSpec as P

HB = 256
PAIR = 16
ITERS = 2
LANE = 128
NEAR = 4
CHUNKS = 2
F32 = jnp.float32
VMEM = pl.BlockSpec(memory_space=pltpu.VMEM)
HBM = pl.BlockSpec(memory_space=pltpu.HBM)


def exchange(copies, axis):
    return lax.all_to_all(copies, axis, split_axis=0, concat_axis=0, tiled=True)


def paired(array, axis):
    size = lax.axis_size(axis)
    mask = 1
    while True:
        come = lax.ppermute(array, axis, [(i, i ^ mask) for i in range(size)])
        mask *= 2
        if mask == size:
            return [array, come]
        array = array + come


def tree(values):
    while len(values) > 1:
        values = [values[i] + values[i + 1] for i in range(0, len(values), 2)]
    return values[0]


def walsh(size):
    index = np.arange(size)
    common = index[:, None] & index[None, :]
    parity = np.zeros((size, size), np.int64)
    for shift in range(size.bit_length()):
        parity ^= (common >> shift) & 1
    return (1 - 2 * parity).astype(np.float32)


def call(body, out_shape, *operands, scratch=()):
    return pl.pallas_call(
        body,
        out_shape=out_shape,
        in_specs=[VMEM] * len(operands),
        out_specs=jax.tree.map(lambda _: VMEM, out_shape),
        scratch_shapes=scratch,
        compiler_params=pltpu.CompilerParams(vmem_limit_bytes=24 << 20),
    )(*operands)


def fold_rows(block):
    return block.reshape(block.shape[0] // 8, 8, LANE).sum(axis=0)


def total(rows):
    return jnp.sum(jnp.sum(rows, axis=0, keepdims=True), axis=1, keepdims=True)


def splat(scalar):
    return jnp.broadcast_to(scalar, (1, LANE))


def left_product(vector, matrix_ref, out_ref):
    blocks, tiles = matrix_ref.shape[0] // LANE, matrix_ref.shape[1] // LANE
    sums = [jnp.zeros((8, LANE), F32) for _ in range(tiles)]
    for block in range(blocks):
        weight = across(vector[block : block + 1, :])
        for tile in range(tiles):
            part = matrix_ref[block * LANE : (block + 1) * LANE, tile * LANE : (tile + 1) * LANE]
            sums[tile] = sums[tile] + fold_rows(part * weight)
    for tile in range(tiles):
        out_ref[tile : tile + 1, :] = jnp.sum(sums[tile], axis=0, keepdims=True)


def left_product_long(vector_ref, matrix_ref, out_ref, copies=()):
    blocks, tiles = matrix_ref.shape[0] // LANE, matrix_ref.shape[1] // LANE

    def step(block, sums):
        weight = across(vector_ref[pl.ds(block, 1), :])
        rows = pl.ds(pl.multiple_of(block * LANE, LANE), LANE)
        return tuple(
            sums[tile] + fold_rows(matrix_ref[rows, tile * LANE : (tile + 1) * LANE] * weight)
            for tile in range(tiles)
        )

    sums = tuple(jnp.zeros((8, LANE), F32) for _ in range(tiles))
    if copies:
        for block, copy in enumerate(copies):
            copy.wait()
            sums = step(block, sums)
    else:
        sums = lax.fori_loop(0, blocks, step, sums)
    for tile in range(tiles):
        out_ref[tile : tile + 1, :] = jnp.sum(sums[tile], axis=0, keepdims=True)


def right_product(matrix_ref, vector, out_ref):
    blocks, tiles = matrix_ref.shape[0] // LANE, matrix_ref.shape[1] // LANE

    def step(block, carry):
        rows = pl.ds(pl.multiple_of(block * LANE, LANE), LANE)
        sums = jnp.zeros((LANE, LANE), F32)
        for tile in range(tiles):
            sums = sums + matrix_ref[rows, tile * LANE : (tile + 1) * LANE] * vector[tile : tile + 1, :]
        out_ref[pl.ds(block, 1), :] = jnp.sum(fold_rows(sums.T), axis=0, keepdims=True)
        return carry

    lax.fori_loop(0, blocks, step, 0)


def rounded(count, unit):
    return -(-count // unit) * unit


def message_rows(width):
    return rounded(width // LANE + 1, 8)


def picks_at(width):
    return message_rows(width)


def signs_at(width, groups):
    return message_rows(width) + rounded(groups, 8)


def copy_out(out_ref):
    first = out_ref[0]
    for index in range(1, out_ref.shape[0]):
        out_ref[index] = first


def across(row):
    return jnp.broadcast_to(row, (LANE, LANE)).T


def first_body(design_ref, target_ref, bits_ref, picks_ref, counts_ref, *refs):
    out_ref, away_refs = refs[0], refs[1:-6]
    design, target_here, bits, picks, counts, sems = refs[-6:]
    rows, width = design.shape
    lines, tiles, quarter = rows // LANE, width // LANE, width // NEAR
    small = [
        pltpu.make_async_copy(source, place, sems.at[index])
        for index, (source, place) in enumerate(
            ((target_ref, target_here), (bits_ref, bits), (picks_ref, picks), (counts_ref, counts))
        )
    ]
    parts = [slice(line * LANE, (line + 1) * LANE) for line in range(lines)]
    large = [
        pltpu.make_async_copy(design_ref.at[part, :], design.at[part, :], sems.at[4 + line])
        for line, part in enumerate(parts)
    ]
    place = lax.axis_index("row") % NEAR
    away = []
    for index, away_ref in enumerate(away_refs):
        chunk, mask = index // (NEAR - 1), index % (NEAR - 1) + 1
        piece = away_ref.shape[1]
        column = pl.multiple_of((place ^ mask) * quarter + chunk * piece, LANE)
        source = design.at[:, pl.ds(column, piece)]
        away.append(pltpu.make_async_copy(source, away_ref, sems.at[4 + lines + index]))
    for copy in small + large:
        copy.start()
    for copy in small:
        copy.wait()
    out_ref[0] = jnp.zeros(out_ref.shape[1:], F32)
    groups = picks.shape[0]
    owner = lax.broadcasted_iota(jnp.int32, (groups, groups), 0)
    same = owner == lax.broadcasted_iota(jnp.int32, (groups, groups), 1)
    limit = jnp.sum(jnp.where(same, counts[...].astype(F32), 0.0), axis=1, keepdims=True)
    slot = lax.broadcasted_iota(jnp.int32, picks.shape, 1).astype(F32)
    coded = jnp.where(slot < limit, picks[...].astype(F32), -1.0)
    start = picks_at(width)
    out_ref[0, start : start + groups, : coded.shape[1]] = coded
    start = signs_at(width, groups)
    out_ref[0, start : start + lines, :] = (2 * bits[...] - 1).astype(F32)
    target = target_here[...]
    out_ref[0, tiles : tiles + 1, :] = splat(total(target * target))
    sums = [jnp.zeros((8, LANE), F32) for _ in range(tiles)]
    for line, part in enumerate(parts):
        weight = across(target[line : line + 1, :])
        large[line].wait()
        if line == lines - 1:
            for copy in away:
                copy.start()
        for tile in range(tiles):
            sums[tile] = sums[tile] + fold_rows(design[part, tile * LANE : (tile + 1) * LANE] * weight)
    for tile in range(tiles):
        out_ref[0, tile : tile + 1, :] = jnp.sum(sums[tile], axis=0, keepdims=True)
    copy_out(out_ref)
    for copy in away:
        copy.wait()


def back_body(first, rinv_ref, parts_ref, term_ref, beta_ref, *refs):
    tiles = rinv_ref.shape[0] // LANE
    copies = []
    if first:
        rinv_here, scratch, sems = refs
        for block in range(tiles):
            part = slice(block * LANE, (block + 1) * LANE)
            copies.append(pltpu.make_async_copy(rinv_ref.at[part, :], rinv_here.at[part, :], sems.at[block]))
            copies[-1].start()
    else:
        rinv_here, (scratch,) = rinv_ref, refs
    summed = tree([parts_ref[i, : tiles + 1, :] for i in range(parts_ref.shape[0])])
    beta = jnp.sqrt(summed[tiles : tiles + 1, :])
    beta_ref[...] = beta
    scratch[...] = summed[:tiles, :] / beta
    left_product_long(scratch, rinv_here, term_ref, copies)


def forward_body(groups, first, rinv_ref, design_ref, *refs):
    right = tree([ref[...] for ref in refs[:groups]])
    refs = refs[groups:]
    if not first:
        before_ref, beta_ref, *refs = refs
        right = right - beta_ref[...] * before_ref[...]
    image_ref, right_ref, held_ref, alpha_ref = refs
    alpha = jnp.sqrt(total(right * right))
    alpha_ref[...] = splat(alpha)
    right = right / alpha
    right_ref[...] = right
    right_product(rinv_ref, right, held_ref)
    right_product(design_ref, held_ref[...], image_ref)


def turn_body(groups, last, *refs):
    left = tree([ref[...] for ref in refs[:groups]])
    before_ref, beta_ref, alpha_ref, token_ref, *refs = refs[groups:]
    left = left - alpha_ref[...] * (before_ref[...] / beta_ref[...])
    square = splat(total(left * left))
    if last:
        left_ref, out_ref = refs
        out_ref[...] = jnp.broadcast_to(square, out_ref.shape)
    else:
        design_ref, left_ref, out_ref = refs
        tiles = design_ref.shape[1] // LANE
        out_ref[0] = jnp.zeros(out_ref.shape[1:], F32)
        left_product(left, design_ref, out_ref.at[0])
        out_ref[0, tiles : tiles + 1, :] = square
        copy_out(out_ref)
    left_ref[...] = left


def last_body(parts_ref, left_ref, *refs):
    quarters, sketch_ref, refs = refs[-NEAR - 3 : -3], refs[-1], refs[:-1]
    place = lax.axis_index("row") % NEAR
    piece = quarters[0].shape[1]
    for mask, part_ref in enumerate(quarters):
        for tile in range(0, piece, LANE):
            column = pl.multiple_of((place ^ mask) * piece + tile, LANE)
            sketch_ref[:, pl.ds(column, LANE)] = part_ref[:, tile : tile + LANE]
    betas = [ref[...] for ref in refs[:ITERS]]
    alphas = [ref[...] for ref in refs[ITERS : 2 * ITERS]]
    held = [ref[...] for ref in refs[2 * ITERS : 3 * ITERS]]
    basis_ref, solution_ref = refs[-2:]
    last = jnp.sqrt(tree([parts_ref[i] for i in range(parts_ref.shape[0])])[:1, :])
    basis_ref[...] = left_ref[...] / last
    betas.append(last)
    phibar, rhobar = betas[0], alphas[0]
    search, iterate = held[0], jnp.zeros_like(held[0])
    for step in range(ITERS):
        beta = betas[step + 1]
        rho = jnp.sqrt(rhobar * rhobar + beta * beta)
        cosine = rhobar / rho
        sine = beta / rho
        phi = cosine * phibar
        phibar = sine * phibar
        iterate = iterate + phi / rho * search
        if step + 1 < ITERS:
            alpha = alphas[step + 1]
            search = held[step + 1] - sine * alpha / rho * search
            rhobar = -cosine * alpha
    solution_ref[...] = iterate


def mix_body(start, parts_ref, walsh_ref, order_ref, out_ref, token_ref):
    token_ref[...] = order_ref[...]
    groups, _, rows = out_ref.shape
    me = lax.axis_index("row")
    local = lax.broadcasted_iota(jnp.int32, (PAIR, rows), 1).astype(F32)

    def step(block, carry):
        coded = [parts_ref[block, pl.ds(start + (apart ^ me), 1), :] for apart in range(groups)]
        coded = jnp.concatenate(coded + [jnp.zeros((LANE - groups, LANE), F32)], axis=0).T
        parity = jnp.int32(0)
        for bit in range(groups.bit_length() - 1):
            parity = parity ^ ((block & me) >> bit)
        sign = (1 - 2 * (parity & 1)).astype(F32)
        chosen = []
        for apart in range(groups):
            match = jnp.broadcast_to(coded[:PAIR, apart : apart + 1], (PAIR, rows)) == local
            chosen.append(jnp.where(match, sign, 0.0))
        chosen = jnp.concatenate(chosen, axis=0).astype(jnp.bfloat16)
        for part in range(rows // HB):
            columns = slice(part * HB, (part + 1) * HB)
            mixed = jnp.dot(chosen[:, columns], walsh_ref[...], preferred_element_type=F32)
            out_ref[block, :, columns] = mixed.astype(jnp.bfloat16)
        return carry

    if groups <= 8:
        for block in range(groups):
            step(block, 0)
    else:
        lax.fori_loop(0, groups, step, 0)


def sample_body(scale, start, design_ref, parts_ref, mix_ref, order_ref, *refs):
    near, (keep_ref, send_ref, token_ref, both) = refs[: NEAR - 1], refs[NEAR - 1 :]
    token_ref[...] = order_ref[...]
    rows, piece = near[0].shape
    quarter = design_ref.shape[1] // NEAR
    groups = mix_ref.shape[0]
    me = lax.axis_index("row")
    signs_start = signs_at(design_ref.shape[1], groups)
    for line in range(rows // LANE):
        part = slice(line * LANE, (line + 1) * LANE)
        signs = [across(parts_ref[me ^ mask, signs_start + line : signs_start + line + 1, :]) for mask in range(NEAR)]
        for tile in range(0, piece, LANE):
            column = pl.multiple_of(me % NEAR * quarter + start + tile, LANE)
            here = slice(tile, tile + LANE)
            values = [design_ref[part, pl.ds(column, LANE)]] + [ref[part, here] for ref in near]
            values = [value * sign for value, sign in zip(values, signs)]
            apart = 1
            while apart < NEAR:
                for first in range(NEAR):
                    if not first & apart:
                        one, two = values[first], values[first | apart]
                        values[first], values[first | apart] = one + two, one - two
                apart *= 2
            for index, value in enumerate(values):
                high = value.astype(jnp.bfloat16)
                both[index, 0, part, here] = high
                both[index, 1, part, here] = (value - high.astype(F32)).astype(jnp.bfloat16)

    def step(block, carry):
        mix = mix_ref[block]
        value = jnp.dot(mix, both[block % NEAR, 0], preferred_element_type=F32)
        value = value + jnp.dot(mix, both[block % NEAR, 1], preferred_element_type=F32)
        value = value / scale
        slot = pl.ds(block * PAIR, PAIR)
        for apart in range(groups):
            far, low = apart // NEAR, apart % NEAR
            out_ref = send_ref if far >= groups // NEAR // 2 else keep_ref
            out_ref[far % (groups // NEAR // 2), low, slot, :] = value[apart * PAIR : (apart + 1) * PAIR, :]
        return carry

    if groups <= 8:
        for block in range(groups):
            step(block, 0)
    else:
        lax.fori_loop(0, groups, step, 0)


def halve_body(kept_ref, arrived_ref, order_ref, keep_ref, send_ref):
    half = keep_ref.shape[0]
    keep_ref[...] = kept_ref[:half] + arrived_ref[:half]
    send_ref[...] = kept_ref[half:] + arrived_ref[half:]


def join_body(kept_ref, arrived_ref, order_ref, out_ref, token_ref):
    token_ref[...] = order_ref[...]
    out_ref[...] = kept_ref[0] + arrived_ref[0]


def split_body(chunks, *refs):
    joined, (kept_ref, arrived_ref, order_ref, token_ref, *out_refs) = refs[: chunks - 1], refs[chunks - 1 :]
    token_ref[...] = order_ref[:1, :]
    piece = kept_ref.shape[3]
    for chunk in range(chunks):
        columns = slice(chunk * piece, (chunk + 1) * piece)
        for index, out_ref in enumerate(out_refs):
            if chunk < chunks - 1:
                out_ref[:, columns] = joined[chunk][index]
            else:
                out_ref[:, columns] = kept_ref[0, index] + arrived_ref[0, index]


def shape(*dims, dtype=F32):
    return jax.ShapeDtypeStruct(dims, dtype)


def shards(design, sign_bits, picks, counts, target, rinv):
    rows, width = design.shape
    whole = rinv.shape[1]
    row_groups = lax.axis_size("row")
    lines = rows // LANE
    scalar = shape(1, LANE)
    deep = message_rows(width)
    left = target.reshape(lines, LANE)
    bits = sign_bits.reshape(lines, LANE)
    chunks = min(CHUNKS, width // NEAR // LANE)
    piece = width // NEAR // chunks
    slots = row_groups * PAIR
    far = row_groups // NEAR

    message, *away = pl.pallas_call(
        first_body,
        out_shape=(shape(row_groups, signs_at(width, row_groups) + rounded(lines, 8), LANE),)
        + (shape(rows, piece),) * (chunks * (NEAR - 1)),
        in_specs=[HBM] * 5,
        out_specs=(VMEM,) + (HBM,) * (chunks * (NEAR - 1)),
        scratch_shapes=[
            pltpu.VMEM((rows, width), F32),
            pltpu.VMEM((lines, LANE), F32),
            pltpu.VMEM((lines, LANE), jnp.int32),
            pltpu.VMEM((row_groups, PAIR), jnp.int32),
            pltpu.VMEM((1, row_groups), jnp.int32),
            pltpu.SemaphoreType.DMA((4 + lines + chunks * (NEAR - 1),)),
        ],
        compiler_params=pltpu.CompilerParams(vmem_limit_bytes=58 << 20),
    )(design, left, bits, picks.reshape(row_groups, PAIR), counts.reshape(1, row_groups))

    def swap(array, mask):
        return lax.ppermute(array, "row", [(i, i ^ mask) for i in range(row_groups)])

    def mix(order):
        signs = jnp.asarray(walsh(HB), jnp.bfloat16)
        made = (shape(row_groups, slots, rows, dtype=jnp.bfloat16), scalar)
        return call(functools.partial(mix_body, picks_at(width)), made, picked, signs, order)

    def sample(chunk, mixed, order):
        scale = float(np.sqrt(np.float32(rows * row_groups)))
        return call(
            functools.partial(sample_body, scale, chunk * piece),
            (shape(far // 2, NEAR, slots, piece),) * 2 + (scalar,),
            design,
            picked,
            mixed,
            order,
            *near[chunk],
            scratch=[pltpu.VMEM((NEAR, 2, rows, piece), jnp.bfloat16)],
        )

    def halve(keep, come, order):
        bit = row_groups // 2
        while bit > NEAR:
            bit //= 2
            half = keep.shape[0] // 2
            keep, send = call(halve_body, (shape(half, *keep.shape[1:]),) * 2, keep, come, order)
            come = swap(send, bit)
        return keep, come

    def join(keep, come, order):
        keep, come = halve(keep, come, order)
        return call(join_body, (shape(*keep.shape[1:]), scalar), keep, come, order)

    def trade(joined, keep, come, order):
        token, mine, *others = call(
            functools.partial(split_body, chunks),
            (scalar,) + (shape(slots, width // NEAR),) * NEAR,
            *joined,
            *halve(keep, come, order),
            order,
        )
        return [mine] + [swap(part, mask + 1) for mask, part in enumerate(others)], token

    def back(rinv, message, first):
        outs, scratch = (shape(whole // LANE, LANE), scalar), [pltpu.VMEM((width // LANE, LANE), F32)]
        if first:
            outs += (shape(*rinv.shape),)
            scratch += [pltpu.SemaphoreType.DMA((width // LANE,))]
        return pl.pallas_call(
            functools.partial(back_body, first),
            out_shape=outs,
            in_specs=[HBM if first else VMEM, VMEM],
            out_specs=(VMEM,) * len(outs),
            scratch_shapes=scratch,
            compiler_params=pltpu.CompilerParams(vmem_limit_bytes=(34 if first else 24) << 20),
            )(rinv, message)

    def forward(terms, *before):
        return call(
            functools.partial(forward_body, 2, not before),
            (shape(lines, LANE), shape(whole // LANE, LANE), shape(width // LANE, LANE), scalar),
            here,
            design,
            *terms,
            *before,
        )

    def turn(images, left, beta, alpha, token, last):
        return call(
            functools.partial(turn_body, 2, last),
            (shape(lines, LANE), shape(row_groups, 8 if last else deep, LANE)),
            *images,
            left,
            beta,
            alpha,
            token,
            *(() if last else (design,)),
        )

    def spread(chunk, order):
        parts = away[chunk * (NEAR - 1) : (chunk + 1) * (NEAR - 1)]
        parts, _ = lax.optimization_barrier((parts, order))
        return [swap(part, mask + 1) for mask, part in enumerate(parts)]

    betas, alphas, held, joined = [], [], [], []
    message = picked = exchange(message, "row")
    near = [spread(0, message)]
    for step in range(ITERS):
        last = step + 1 == ITERS
        if step == 0:
            term, beta, here = back(rinv, message, True)
            mixed, token = mix(beta)
            near += [spread(chunk, beta) for chunk in range(1, chunks)]
        else:
            term, beta = back(here, message, False)
        betas.append(beta)
        terms = paired(term, "col")
        image, right, kept, alpha = forward(terms, *(() if step == 0 else (right, beta)))
        alphas.append(alpha)
        held.append(kept)
        if step == 0:
            parts = []
            for chunk in range(chunks):
                keep, send, token = sample(chunk, mixed, token if chunk == 0 else alpha)
                if chunk < chunks - 1:
                    parts.append((keep, swap(send, row_groups // 2)))
            for part in parts:
                part, token = join(*part, token)
                joined.append(part)
        images = paired(image, "col")
        if last:
            quarters, token = trade(joined, keep, come, images[1])
        left, message = turn(images, left, beta, alpha, token, last)
        message = exchange(message, "row")
        if step == 0:
            send, _ = lax.optimization_barrier((send, message))
            come = swap(send, row_groups // 2)
    basis, answer, sketch = call(
        last_body,
        (shape(lines, LANE), shape(width // LANE, LANE), shape(slots, width)),
        message,
        left,
        *betas,
        *alphas,
        *held,
        *quarters,
    )
    return (sketch, answer.reshape(-1), basis.reshape(-1))


def solution(mesh):
    placed = (
        P("row", "col"),
        P("row"),
        P(None, "row", None),
        P(None, "row"),
        P("row"),
        P("col", None),
    )
    return jax.shard_map(
        shards,
        mesh=mesh,
        in_specs=placed,
        out_specs=(P("row", "col"), P("col"), P("row")),
        check_vma=False,
    )
```

```python
import functools

import jax
import jax.numpy as jnp
import numpy as np
from jax import lax
from jax.experimental import pallas as pl
from jax.experimental.pallas import tpu as pltpu
from jax.sharding import PartitionSpec as P

HB = 256
PAIR = 16
ITERS = 2
LANE = 128
NEAR = 4
CHUNKS = 2
F32 = jnp.float32
VMEM = pl.BlockSpec(memory_space=pltpu.VMEM)
HBM = pl.BlockSpec(memory_space=pltpu.HBM)


def exchange(copies, axis):
    return lax.all_to_all(copies, axis, split_axis=0, concat_axis=0, tiled=True)


def paired(array, axis):
    size = lax.axis_size(axis)
    mask = 1
    while True:
        come = lax.ppermute(array, axis, [(i, i ^ mask) for i in range(size)])
        mask *= 2
        if mask == size:
            return [array, come]
        array = array + come


def tree(values):
    while len(values) > 1:
        values = [values[i] + values[i + 1] for i in range(0, len(values), 2)]
    return values[0]


def walsh(size):
    index = np.arange(size)
    common = index[:, None] & index[None, :]
    parity = np.zeros((size, size), np.int64)
    for shift in range(size.bit_length()):
        parity ^= (common >> shift) & 1
    return (1 - 2 * parity).astype(np.float32)


def call(body, out_shape, *operands, scratch=()):
    return pl.pallas_call(
        body,
        out_shape=out_shape,
        in_specs=[VMEM] * len(operands),
        out_specs=jax.tree.map(lambda _: VMEM, out_shape),
        scratch_shapes=scratch,
        compiler_params=pltpu.CompilerParams(vmem_limit_bytes=24 << 20),
    )(*operands)


def fold_rows(block):
    return block.reshape(block.shape[0] // 8, 8, LANE).sum(axis=0)


def total(rows):
    return jnp.sum(jnp.sum(rows, axis=0, keepdims=True), axis=1, keepdims=True)


def splat(scalar):
    return jnp.broadcast_to(scalar, (1, LANE))


def left_product(vector, matrix_ref, out_ref):
    blocks, tiles = matrix_ref.shape[0] // LANE, matrix_ref.shape[1] // LANE
    sums = [jnp.zeros((8, LANE), F32) for _ in range(tiles)]
    for block in range(blocks):
        weight = across(vector[block : block + 1, :])
        for tile in range(tiles):
            part = matrix_ref[block * LANE : (block + 1) * LANE, tile * LANE : (tile + 1) * LANE]
            sums[tile] = sums[tile] + fold_rows(part * weight)
    for tile in range(tiles):
        out_ref[tile : tile + 1, :] = jnp.sum(sums[tile], axis=0, keepdims=True)


def left_product_long(vector_ref, matrix_ref, out_ref, copies=()):
    blocks, tiles = matrix_ref.shape[0] // LANE, matrix_ref.shape[1] // LANE

    def step(block, sums):
        weight = across(vector_ref[pl.ds(block, 1), :])
        rows = pl.ds(pl.multiple_of(block * LANE, LANE), LANE)
        return tuple(
            sums[tile] + fold_rows(matrix_ref[rows, tile * LANE : (tile + 1) * LANE] * weight)
            for tile in range(tiles)
        )

    sums = tuple(jnp.zeros((8, LANE), F32) for _ in range(tiles))
    if copies:
        for block, copy in enumerate(copies):
            copy.wait()
            sums = step(block, sums)
    else:
        sums = lax.fori_loop(0, blocks, step, sums)
    for tile in range(tiles):
        out_ref[tile : tile + 1, :] = jnp.sum(sums[tile], axis=0, keepdims=True)


def right_product(matrix_ref, vector, out_ref):
    blocks, tiles = matrix_ref.shape[0] // LANE, matrix_ref.shape[1] // LANE

    def step(block, carry):
        rows = pl.ds(pl.multiple_of(block * LANE, LANE), LANE)
        sums = jnp.zeros((LANE, LANE), F32)
        for tile in range(tiles):
            sums = sums + matrix_ref[rows, tile * LANE : (tile + 1) * LANE] * vector[tile : tile + 1, :]
        out_ref[pl.ds(block, 1), :] = jnp.sum(fold_rows(sums.T), axis=0, keepdims=True)
        return carry

    lax.fori_loop(0, blocks, step, 0)


def rounded(count, unit):
    return -(-count // unit) * unit


def message_rows(width):
    return rounded(width // LANE + 1, 8)


def picks_at(width):
    return message_rows(width)


def signs_at(width, groups):
    return message_rows(width) + rounded(groups, 8)


def copy_out(out_ref):
    first = out_ref[0]
    for index in range(1, out_ref.shape[0]):
        out_ref[index] = first


def across(row):
    return jnp.broadcast_to(row, (LANE, LANE)).T


def first_body(design_ref, target_ref, bits_ref, picks_ref, counts_ref, *refs):
    out_ref, away_refs = refs[0], refs[1:-6]
    design, target_here, bits, picks, counts, sems = refs[-6:]
    rows, width = design.shape
    lines, tiles, quarter = rows // LANE, width // LANE, width // NEAR
    small = [
        pltpu.make_async_copy(source, place, sems.at[index])
        for index, (source, place) in enumerate(
            ((target_ref, target_here), (bits_ref, bits), (picks_ref, picks), (counts_ref, counts))
        )
    ]
    parts = [slice(line * LANE, (line + 1) * LANE) for line in range(lines)]
    large = [
        pltpu.make_async_copy(design_ref.at[part, :], design.at[part, :], sems.at[4 + line])
        for line, part in enumerate(parts)
    ]
    place = lax.axis_index("row") % NEAR
    away = []
    for index, away_ref in enumerate(away_refs):
        piece = away_ref.shape[1]
        mask = min(index + 1, NEAR - 1)
        column = pl.multiple_of((place ^ mask) * quarter + (index + 1 - mask) * piece, LANE)
        source = design.at[:, pl.ds(column, piece)]
        away.append(pltpu.make_async_copy(source, away_ref, sems.at[4 + lines + index]))
    for copy in small + large:
        copy.start()
    for copy in small:
        copy.wait()
    out_ref[0] = jnp.zeros(out_ref.shape[1:], F32)
    groups = picks.shape[0]
    owner = lax.broadcasted_iota(jnp.int32, (groups, groups), 0)
    same = owner == lax.broadcasted_iota(jnp.int32, (groups, groups), 1)
    limit = jnp.sum(jnp.where(same, counts[...].astype(F32), 0.0), axis=1, keepdims=True)
    slot = lax.broadcasted_iota(jnp.int32, picks.shape, 1).astype(F32)
    coded = jnp.where(slot < limit, picks[...].astype(F32), -1.0)
    start = picks_at(width)
    out_ref[0, start : start + groups, : coded.shape[1]] = coded
    start = signs_at(width, groups)
    out_ref[0, start : start + lines, :] = (2 * bits[...] - 1).astype(F32)
    target = target_here[...]
    out_ref[0, tiles : tiles + 1, :] = splat(total(target * target))
    sums = [jnp.zeros((8, LANE), F32) for _ in range(tiles)]
    for line, part in enumerate(parts):
        weight = across(target[line : line + 1, :])
        large[line].wait()
        if line == lines - 1:
            for copy in away:
                copy.start()
        for tile in range(tiles):
            sums[tile] = sums[tile] + fold_rows(design[part, tile * LANE : (tile + 1) * LANE] * weight)
    for tile in range(tiles):
        out_ref[0, tile : tile + 1, :] = jnp.sum(sums[tile], axis=0, keepdims=True)
    copy_out(out_ref)
    for copy in away:
        copy.wait()


def back_body(first, rinv_ref, parts_ref, term_ref, beta_ref, *refs):
    tiles = rinv_ref.shape[0] // LANE
    copies = []
    if first:
        rinv_here, scratch, sems = refs
        for block in range(tiles):
            part = slice(block * LANE, (block + 1) * LANE)
            copies.append(pltpu.make_async_copy(rinv_ref.at[part, :], rinv_here.at[part, :], sems.at[block]))
            copies[-1].start()
    else:
        rinv_here, (scratch,) = rinv_ref, refs
    summed = tree([parts_ref[i, : tiles + 1, :] for i in range(parts_ref.shape[0])])
    beta = jnp.sqrt(summed[tiles : tiles + 1, :])
    beta_ref[...] = beta
    scratch[...] = summed[:tiles, :] / beta
    left_product_long(scratch, rinv_here, term_ref, copies)


def forward_body(groups, first, rinv_ref, design_ref, *refs):
    right = tree([ref[...] for ref in refs[:groups]])
    refs = refs[groups:]
    if not first:
        before_ref, beta_ref, *refs = refs
        right = right - beta_ref[...] * before_ref[...]
    image_ref, right_ref, held_ref, alpha_ref = refs
    alpha = jnp.sqrt(total(right * right))
    alpha_ref[...] = splat(alpha)
    right = right / alpha
    right_ref[...] = right
    right_product(rinv_ref, right, held_ref)
    right_product(design_ref, held_ref[...], image_ref)


def turn_body(groups, last, *refs):
    left = tree([ref[...] for ref in refs[:groups]])
    before_ref, beta_ref, alpha_ref, token_ref, *refs = refs[groups:]
    left = left - alpha_ref[...] * (before_ref[...] / beta_ref[...])
    square = splat(total(left * left))
    if last:
        left_ref, out_ref = refs
        out_ref[...] = jnp.broadcast_to(square, out_ref.shape)
    else:
        design_ref, left_ref, out_ref = refs
        tiles = design_ref.shape[1] // LANE
        out_ref[0] = jnp.zeros(out_ref.shape[1:], F32)
        left_product(left, design_ref, out_ref.at[0])
        out_ref[0, tiles : tiles + 1, :] = square
        copy_out(out_ref)
    left_ref[...] = left


def last_body(parts_ref, left_ref, *refs):
    quarters, sketch_ref, refs = refs[-NEAR - 3 : -3], refs[-1], refs[:-1]
    place = lax.axis_index("row") % NEAR
    piece = quarters[0].shape[1]
    for mask, part_ref in enumerate(quarters):
        for tile in range(0, piece, LANE):
            column = pl.multiple_of((place ^ mask) * piece + tile, LANE)
            sketch_ref[:, pl.ds(column, LANE)] = part_ref[:, tile : tile + LANE]
    betas = [ref[...] for ref in refs[:ITERS]]
    alphas = [ref[...] for ref in refs[ITERS : 2 * ITERS]]
    held = [ref[...] for ref in refs[2 * ITERS : 3 * ITERS]]
    basis_ref, solution_ref = refs[-2:]
    last = jnp.sqrt(tree([parts_ref[i] for i in range(parts_ref.shape[0])])[:1, :])
    basis_ref[...] = left_ref[...] / last
    betas.append(last)
    phibar, rhobar = betas[0], alphas[0]
    search, iterate = held[0], jnp.zeros_like(held[0])
    for step in range(ITERS):
        beta = betas[step + 1]
        rho = jnp.sqrt(rhobar * rhobar + beta * beta)
        cosine = rhobar / rho
        sine = beta / rho
        phi = cosine * phibar
        phibar = sine * phibar
        iterate = iterate + phi / rho * search
        if step + 1 < ITERS:
            alpha = alphas[step + 1]
            search = held[step + 1] - sine * alpha / rho * search
            rhobar = -cosine * alpha
    solution_ref[...] = iterate


def mix_body(start, parts_ref, walsh_ref, order_ref, out_ref, token_ref):
    token_ref[...] = order_ref[...]
    groups, _, rows = out_ref.shape
    me = lax.axis_index("row")
    local = lax.broadcasted_iota(jnp.int32, (PAIR, rows), 1).astype(F32)

    def step(block, carry):
        coded = [parts_ref[block, pl.ds(start + (apart ^ me), 1), :] for apart in range(groups)]
        coded = jnp.concatenate(coded + [jnp.zeros((LANE - groups, LANE), F32)], axis=0).T
        parity = jnp.int32(0)
        for bit in range(groups.bit_length() - 1):
            parity = parity ^ ((block & me) >> bit)
        sign = (1 - 2 * (parity & 1)).astype(F32)
        chosen = []
        for apart in range(groups):
            match = jnp.broadcast_to(coded[:PAIR, apart : apart + 1], (PAIR, rows)) == local
            chosen.append(jnp.where(match, sign, 0.0))
        chosen = jnp.concatenate(chosen, axis=0).astype(jnp.bfloat16)
        for part in range(rows // HB):
            columns = slice(part * HB, (part + 1) * HB)
            mixed = jnp.dot(chosen[:, columns], walsh_ref[...], preferred_element_type=F32)
            out_ref[block, :, columns] = mixed.astype(jnp.bfloat16)
        return carry

    if groups <= 8:
        for block in range(groups):
            step(block, 0)
    else:
        lax.fori_loop(0, groups, step, 0)


def sample_body(scale, start, design_ref, parts_ref, mix_ref, order_ref, *refs):
    near, (keep_ref, send_ref, token_ref, both) = refs[: NEAR - 1], refs[NEAR - 1 :]
    token_ref[...] = order_ref[...]
    rows, piece = near[-1].shape
    quarter = design_ref.shape[1] // NEAR
    groups = mix_ref.shape[0]
    me = lax.axis_index("row")
    signs_start = signs_at(design_ref.shape[1], groups)
    for line in range(rows // LANE):
        part = slice(line * LANE, (line + 1) * LANE)
        signs = [across(parts_ref[me ^ mask, signs_start + line : signs_start + line + 1, :]) for mask in range(NEAR)]
        for tile in range(0, piece, LANE):
            column = pl.multiple_of(me % NEAR * quarter + start + tile, LANE)
            here = slice(tile, tile + LANE)
            there = slice(start + tile, start + tile + LANE)
            values = [design_ref[part, pl.ds(column, LANE)]] + [ref[part, there] for ref in near[:-1]]
            values.append(near[-1][part, here])
            values = [value * sign for value, sign in zip(values, signs)]
            apart = 1
            while apart < NEAR:
                for first in range(NEAR):
                    if not first & apart:
                        one, two = values[first], values[first | apart]
                        values[first], values[first | apart] = one + two, one - two
                apart *= 2
            for index, value in enumerate(values):
                high = value.astype(jnp.bfloat16)
                both[index, 0, part, here] = high
                both[index, 1, part, here] = (value - high.astype(F32)).astype(jnp.bfloat16)

    def step(block, carry):
        mix = mix_ref[block]
        value = jnp.dot(mix, both[block % NEAR, 0], preferred_element_type=F32)
        value = value + jnp.dot(mix, both[block % NEAR, 1], preferred_element_type=F32)
        value = value / scale
        slot = pl.ds(block * PAIR, PAIR)
        for apart in range(groups):
            far, low = apart // NEAR, apart % NEAR
            out_ref = send_ref if far >= groups // NEAR // 2 else keep_ref
            out_ref[far % (groups // NEAR // 2), low, slot, :] = value[apart * PAIR : (apart + 1) * PAIR, :]
        return carry

    if groups <= 8:
        for block in range(groups):
            step(block, 0)
    else:
        lax.fori_loop(0, groups, step, 0)


def halve_body(kept_ref, arrived_ref, order_ref, keep_ref, send_ref):
    half = keep_ref.shape[0]
    keep_ref[...] = kept_ref[:half] + arrived_ref[:half]
    send_ref[...] = kept_ref[half:] + arrived_ref[half:]


def join_body(kept_ref, arrived_ref, order_ref, out_ref, token_ref):
    token_ref[...] = order_ref[...]
    out_ref[...] = kept_ref[0] + arrived_ref[0]


def split_body(chunks, *refs):
    joined, (kept_ref, arrived_ref, order_ref, token_ref, *out_refs) = refs[: chunks - 1], refs[chunks - 1 :]
    token_ref[...] = order_ref[:1, :]
    piece = kept_ref.shape[3]
    for chunk in range(chunks):
        columns = slice(chunk * piece, (chunk + 1) * piece)
        for index, out_ref in enumerate(out_refs):
            if chunk < chunks - 1:
                out_ref[:, columns] = joined[chunk][index]
            else:
                out_ref[:, columns] = kept_ref[0, index] + arrived_ref[0, index]


def shape(*dims, dtype=F32):
    return jax.ShapeDtypeStruct(dims, dtype)


def shards(design, sign_bits, picks, counts, target, rinv):
    rows, width = design.shape
    whole = rinv.shape[1]
    row_groups = lax.axis_size("row")
    lines = rows // LANE
    scalar = shape(1, LANE)
    deep = message_rows(width)
    left = target.reshape(lines, LANE)
    bits = sign_bits.reshape(lines, LANE)
    chunks = min(CHUNKS, width // NEAR // LANE)
    piece = width // NEAR // chunks
    slots = row_groups * PAIR
    far = row_groups // NEAR

    message, *away = pl.pallas_call(
        first_body,
        out_shape=(shape(row_groups, signs_at(width, row_groups) + rounded(lines, 8), LANE),)
        + (shape(rows, width // NEAR),) * (NEAR - 2)
        + (shape(rows, piece),) * chunks,
        in_specs=[HBM] * 5,
        out_specs=(VMEM,) + (HBM,) * (NEAR - 2 + chunks),
        scratch_shapes=[
            pltpu.VMEM((rows, width), F32),
            pltpu.VMEM((lines, LANE), F32),
            pltpu.VMEM((lines, LANE), jnp.int32),
            pltpu.VMEM((row_groups, PAIR), jnp.int32),
            pltpu.VMEM((1, row_groups), jnp.int32),
            pltpu.SemaphoreType.DMA((4 + lines + NEAR - 2 + chunks,)),
        ],
        compiler_params=pltpu.CompilerParams(vmem_limit_bytes=58 << 20),
    )(design, left, bits, picks.reshape(row_groups, PAIR), counts.reshape(1, row_groups))

    def swap(array, mask):
        return lax.ppermute(array, "row", [(i, i ^ mask) for i in range(row_groups)])

    def mix(order):
        signs = jnp.asarray(walsh(HB), jnp.bfloat16)
        made = (shape(row_groups, slots, rows, dtype=jnp.bfloat16), scalar)
        return call(functools.partial(mix_body, picks_at(width)), made, picked, signs, order)

    def sample(chunk, mixed, order):
        scale = float(np.sqrt(np.float32(rows * row_groups)))
        return call(
            functools.partial(sample_body, scale, chunk * piece),
            (shape(far // 2, NEAR, slots, piece),) * 2 + (scalar,),
            design,
            picked,
            mixed,
            order,
            *near[: NEAR - 2],
            near[NEAR - 2 + chunk],
            scratch=[pltpu.VMEM((NEAR, 2, rows, piece), jnp.bfloat16)],
        )

    def halve(keep, come, order):
        bit = row_groups // 2
        while bit > NEAR:
            bit //= 2
            half = keep.shape[0] // 2
            keep, send = call(halve_body, (shape(half, *keep.shape[1:]),) * 2, keep, come, order)
            come = swap(send, bit)
        return keep, come

    def join(keep, come, order):
        keep, come = halve(keep, come, order)
        return call(join_body, (shape(*keep.shape[1:]), scalar), keep, come, order)

    def trade(joined, keep, come, order):
        token, mine, *others = call(
            functools.partial(split_body, chunks),
            (scalar,) + (shape(slots, width // NEAR),) * NEAR,
            *joined,
            *halve(keep, come, order),
            order,
        )
        return [mine] + [swap(part, mask + 1) for mask, part in enumerate(others)], token

    def back(rinv, message, first):
        outs, scratch = (shape(whole // LANE, LANE), scalar), [pltpu.VMEM((width // LANE, LANE), F32)]
        if first:
            outs += (shape(*rinv.shape),)
            scratch += [pltpu.SemaphoreType.DMA((width // LANE,))]
        return pl.pallas_call(
            functools.partial(back_body, first),
            out_shape=outs,
            in_specs=[HBM if first else VMEM, VMEM],
            out_specs=(VMEM,) * len(outs),
            scratch_shapes=scratch,
            compiler_params=pltpu.CompilerParams(vmem_limit_bytes=(34 if first else 24) << 20),
            )(rinv, message)

    def forward(terms, *before):
        return call(
            functools.partial(forward_body, 2, not before),
            (shape(lines, LANE), shape(whole // LANE, LANE), shape(width // LANE, LANE), scalar),
            here,
            design,
            *terms,
            *before,
        )

    def turn(images, left, beta, alpha, token, last):
        return call(
            functools.partial(turn_body, 2, last),
            (shape(lines, LANE), shape(row_groups, 8 if last else deep, LANE)),
            *images,
            left,
            beta,
            alpha,
            token,
            *(() if last else (design,)),
        )

    betas, alphas, held, joined = [], [], [], []
    message = picked = exchange(message, "row")
    away, _ = lax.optimization_barrier((away, message))
    near = [swap(part, min(index + 1, NEAR - 1)) for index, part in enumerate(away)]
    for step in range(ITERS):
        last = step + 1 == ITERS
        if step == 0:
            term, beta, here = back(rinv, message, True)
            mixed, token = mix(beta)
        else:
            term, beta = back(here, message, False)
        betas.append(beta)
        terms = paired(term, "col")
        image, right, kept, alpha = forward(terms, *(() if step == 0 else (right, beta)))
        alphas.append(alpha)
        held.append(kept)
        if step == 0:
            parts = []
            for chunk in range(chunks):
                keep, send, token = sample(chunk, mixed, alpha)
                if chunk < chunks - 1:
                    parts.append((keep, swap(send, row_groups // 2)))
            for part in parts:
                part, token = join(*part, token)
                joined.append(part)
        images = paired(image, "col")
        if last:
            quarters, token = trade(joined, keep, come, images[0])
        left, message = turn(images, left, beta, alpha, token, last)
        message = exchange(message, "row")
        if step == 0:
            send, _ = lax.optimization_barrier((send, message))
            come = swap(send, row_groups // 2)
    basis, answer, sketch = call(
        last_body,
        (shape(lines, LANE), shape(width // LANE, LANE), shape(slots, width)),
        message,
        left,
        *betas,
        *alphas,
        *held,
        *quarters,
    )
    return (sketch, answer.reshape(-1), basis.reshape(-1))


def solution(mesh):
    placed = (
        P("row", "col"),
        P("row"),
        P(None, "row", None),
        P(None, "row"),
        P("row"),
        P("col", None),
    )
    return jax.shard_map(
        shards,
        mesh=mesh,
        in_specs=placed,
        out_specs=(P("row", "col"), P("col"), P("row")),
        check_vma=False,
    )
```

```python
import functools

import jax
import jax.numpy as jnp
import numpy as np
from jax import lax
from jax.experimental import pallas as pl
from jax.experimental.pallas import tpu as pltpu
from jax.sharding import PartitionSpec as P

HB = 256
PAIR = 16
ITERS = 2
LANE = 128
NEAR = 4
F32 = jnp.float32
VMEM = pl.BlockSpec(memory_space=pltpu.VMEM)
HBM = pl.BlockSpec(memory_space=pltpu.HBM)


def exchange(copies, axis):
    return lax.all_to_all(copies, axis, split_axis=0, concat_axis=0, tiled=True)


def paired(array, axis):
    size = lax.axis_size(axis)
    mask = 1
    while True:
        come = lax.ppermute(array, axis, [(i, i ^ mask) for i in range(size)])
        mask *= 2
        if mask == size:
            return [array, come]
        array = array + come


def tree(values):
    while len(values) > 1:
        values = [values[i] + values[i + 1] for i in range(0, len(values), 2)]
    return values[0]


def walsh(size):
    index = np.arange(size)
    common = index[:, None] & index[None, :]
    parity = np.zeros((size, size), np.int64)
    for shift in range(size.bit_length()):
        parity ^= (common >> shift) & 1
    return (1 - 2 * parity).astype(np.float32)


def call(body, out_shape, *operands, scratch=()):
    return pl.pallas_call(
        body,
        out_shape=out_shape,
        in_specs=[VMEM] * len(operands),
        out_specs=jax.tree.map(lambda _: VMEM, out_shape),
        scratch_shapes=scratch,
        compiler_params=pltpu.CompilerParams(vmem_limit_bytes=24 << 20),
    )(*operands)


def fold_rows(block):
    return block.reshape(block.shape[0] // 8, 8, LANE).sum(axis=0)


def total(rows):
    return jnp.sum(jnp.sum(rows, axis=0, keepdims=True), axis=1, keepdims=True)


def splat(scalar):
    return jnp.broadcast_to(scalar, (1, LANE))


def left_product(vector, matrix_ref, out_ref):
    blocks, tiles = matrix_ref.shape[0] // LANE, matrix_ref.shape[1] // LANE
    sums = [jnp.zeros((8, LANE), F32) for _ in range(tiles)]
    for block in range(blocks):
        weight = across(vector[block : block + 1, :])
        for tile in range(tiles):
            part = matrix_ref[block * LANE : (block + 1) * LANE, tile * LANE : (tile + 1) * LANE]
            sums[tile] = sums[tile] + fold_rows(part * weight)
    for tile in range(tiles):
        out_ref[tile : tile + 1, :] = jnp.sum(sums[tile], axis=0, keepdims=True)


def left_product_long(vector_ref, matrix_ref, out_ref, copies=()):
    blocks, tiles = matrix_ref.shape[0] // LANE, matrix_ref.shape[1] // LANE

    def step(block, sums):
        weight = across(vector_ref[pl.ds(block, 1), :])
        rows = pl.ds(pl.multiple_of(block * LANE, LANE), LANE)
        return tuple(
            sums[tile] + fold_rows(matrix_ref[rows, tile * LANE : (tile + 1) * LANE] * weight)
            for tile in range(tiles)
        )

    sums = tuple(jnp.zeros((8, LANE), F32) for _ in range(tiles))
    if copies:
        for block, copy in enumerate(copies):
            copy.wait()
            sums = step(block, sums)
    else:
        sums = lax.fori_loop(0, blocks, step, sums)
    for tile in range(tiles):
        out_ref[tile : tile + 1, :] = jnp.sum(sums[tile], axis=0, keepdims=True)


def right_product(matrix_ref, vector, out_ref):
    blocks, tiles = matrix_ref.shape[0] // LANE, matrix_ref.shape[1] // LANE

    def step(block, carry):
        rows = pl.ds(pl.multiple_of(block * LANE, LANE), LANE)
        sums = jnp.zeros((LANE, LANE), F32)
        for tile in range(tiles):
            sums = sums + matrix_ref[rows, tile * LANE : (tile + 1) * LANE] * vector[tile : tile + 1, :]
        out_ref[pl.ds(block, 1), :] = jnp.sum(fold_rows(sums.T), axis=0, keepdims=True)
        return carry

    lax.fori_loop(0, blocks, step, 0)


def rounded(count, unit):
    return -(-count // unit) * unit


def message_rows(width):
    return rounded(width // LANE + 1, 8)


def picks_at(width):
    return message_rows(width)


def signs_at(width, groups):
    return message_rows(width) + rounded(groups, 8)


def columns_traded(width):
    unit = NEAR * LANE
    return max(unit, width // 2 // unit * unit)


def copy_out(out_ref):
    first = out_ref[0]
    for index in range(1, out_ref.shape[0]):
        out_ref[index] = first


def across(row):
    return jnp.broadcast_to(row, (LANE, LANE)).T


def first_body(design_ref, target_ref, bits_ref, picks_ref, counts_ref, *refs):
    out_ref, away_refs = refs[0], refs[1:-6]
    design, target_here, bits, picks, counts, sems = refs[-6:]
    rows, width = design.shape
    lines, tiles = rows // LANE, width // LANE
    small = [
        pltpu.make_async_copy(source, place, sems.at[index])
        for index, (source, place) in enumerate(
            ((target_ref, target_here), (bits_ref, bits), (picks_ref, picks), (counts_ref, counts))
        )
    ]
    parts = [slice(line * LANE, (line + 1) * LANE) for line in range(lines)]
    large = [
        pltpu.make_async_copy(design_ref.at[part, :], design.at[part, :], sems.at[4 + line])
        for line, part in enumerate(parts)
    ]
    place = lax.axis_index("row") % NEAR
    away = []
    for index, away_ref in enumerate(away_refs):
        piece = away_ref.shape[1]
        column = pl.multiple_of(width - NEAR * piece + (place ^ (index + 1)) * piece, LANE)
        source = design.at[:, pl.ds(column, piece)]
        away.append(pltpu.make_async_copy(source, away_ref, sems.at[4 + lines + index]))
    for copy in small + large:
        copy.start()
    for copy in small:
        copy.wait()
    out_ref[0] = jnp.zeros(out_ref.shape[1:], F32)
    groups = picks.shape[0]
    owner = lax.broadcasted_iota(jnp.int32, (groups, groups), 0)
    same = owner == lax.broadcasted_iota(jnp.int32, (groups, groups), 1)
    limit = jnp.sum(jnp.where(same, counts[...].astype(F32), 0.0), axis=1, keepdims=True)
    slot = lax.broadcasted_iota(jnp.int32, picks.shape, 1).astype(F32)
    coded = jnp.where(slot < limit, picks[...].astype(F32), -1.0)
    start = picks_at(width)
    out_ref[0, start : start + groups, : coded.shape[1]] = coded
    start = signs_at(width, groups)
    out_ref[0, start : start + lines, :] = (2 * bits[...] - 1).astype(F32)
    target = target_here[...]
    out_ref[0, tiles : tiles + 1, :] = splat(total(target * target))
    sums = [jnp.zeros((8, LANE), F32) for _ in range(tiles)]
    for line, part in enumerate(parts):
        weight = across(target[line : line + 1, :])
        large[line].wait()
        if line == lines - 1:
            for copy in away:
                copy.start()
        for tile in range(tiles):
            sums[tile] = sums[tile] + fold_rows(design[part, tile * LANE : (tile + 1) * LANE] * weight)
    for tile in range(tiles):
        out_ref[0, tile : tile + 1, :] = jnp.sum(sums[tile], axis=0, keepdims=True)
    copy_out(out_ref)
    for copy in away:
        copy.wait()


def back_body(first, rinv_ref, parts_ref, order_ref, term_ref, beta_ref, *refs):
    tiles = rinv_ref.shape[0] // LANE
    copies = []
    if first:
        rinv_here, scratch, sems = refs
        for block in range(tiles):
            part = slice(block * LANE, (block + 1) * LANE)
            copies.append(pltpu.make_async_copy(rinv_ref.at[part, :], rinv_here.at[part, :], sems.at[block]))
            copies[-1].start()
    else:
        rinv_here, (scratch,) = rinv_ref, refs
    summed = tree([parts_ref[i, : tiles + 1, :] for i in range(parts_ref.shape[0])])
    beta = jnp.sqrt(summed[tiles : tiles + 1, :])
    beta_ref[...] = beta
    scratch[...] = summed[:tiles, :] / beta
    left_product_long(scratch, rinv_here, term_ref, copies)


def forward_body(groups, first, rinv_ref, design_ref, *refs):
    right = tree([ref[...] for ref in refs[:groups]])
    refs = refs[groups:]
    if not first:
        before_ref, beta_ref, *refs = refs
        right = right - beta_ref[...] * before_ref[...]
    image_ref, right_ref, held_ref, alpha_ref = refs
    alpha = jnp.sqrt(total(right * right))
    alpha_ref[...] = splat(alpha)
    right = right / alpha
    right_ref[...] = right
    right_product(rinv_ref, right, held_ref)
    right_product(design_ref, held_ref[...], image_ref)


def turn_body(groups, last, *refs):
    left = tree([ref[...] for ref in refs[:groups]])
    before_ref, beta_ref, alpha_ref, *refs = refs[groups:]
    left = left - alpha_ref[...] * (before_ref[...] / beta_ref[...])
    square = splat(total(left * left))
    if last:
        left_ref, out_ref = refs
        out_ref[...] = jnp.broadcast_to(square, out_ref.shape)
    else:
        design_ref, left_ref, out_ref = refs
        tiles = design_ref.shape[1] // LANE
        out_ref[0] = jnp.zeros(out_ref.shape[1:], F32)
        left_product(left, design_ref, out_ref.at[0])
        out_ref[0, tiles : tiles + 1, :] = square
        copy_out(out_ref)
    left_ref[...] = left


def pieces(value):
    high = value.astype(jnp.bfloat16)
    return high, (value - high.astype(F32)).astype(jnp.bfloat16)


def weigh(mix, high, low):
    return jnp.dot(mix, high, preferred_element_type=F32) + jnp.dot(mix, low, preferred_element_type=F32)


def for_blocks(groups, step):
    if groups <= 8:
        for block in range(groups):
            step(block, 0)
    else:
        lax.fori_loop(0, groups, step, 0)


def mix_rows(parts_ref, walsh_ref, width, block, groups, rows):
    me = lax.axis_index("row")
    start = picks_at(width)
    local = lax.broadcasted_iota(jnp.int32, (PAIR, rows), 1).astype(F32)
    coded = [parts_ref[block, pl.ds(start + (apart ^ me), 1), :] for apart in range(groups)]
    coded = jnp.concatenate(coded + [jnp.zeros((LANE - groups, LANE), F32)], axis=0).T
    parity = jnp.int32(0)
    for bit in range(groups.bit_length() - 1):
        parity = parity ^ ((block & me) >> bit)
    sign = (1 - 2 * (parity & 1)).astype(F32)
    chosen = []
    for apart in range(groups):
        match = jnp.broadcast_to(coded[:PAIR, apart : apart + 1], (PAIR, rows)) == local
        chosen.append(jnp.where(match, sign, 0.0))
    chosen = jnp.concatenate(chosen, axis=0).astype(jnp.bfloat16)
    mixed = []
    for part in range(rows // HB):
        mix = jnp.dot(chosen[:, part * HB : (part + 1) * HB], walsh_ref[...], preferred_element_type=F32)
        mixed.append(mix.astype(jnp.bfloat16))
    return jnp.concatenate(mixed, axis=1)


def mix_body(width, parts_ref, walsh_ref, mix_ref, token_ref):
    token_ref[...] = parts_ref[0, :1, :]
    groups, _, rows = mix_ref.shape

    def step(block, carry):
        mix_ref[block] = mix_rows(parts_ref, walsh_ref, width, block, groups, rows)
        return carry

    for_blocks(groups, step)


def share_body(scale, parts_ref, walsh_ref, design_ref, mix_ref, token_ref, out_ref, here, both, share, sems):
    token_ref[...] = parts_ref[0, :1, :]
    groups, _, columns = share.shape
    rows, width = design_ref.shape
    fetch = pltpu.make_async_copy(design_ref.at[:, pl.ds(0, columns)], here, sems.at[groups])
    fetch.start()
    me = lax.axis_index("row")

    def mix(block, carry):
        mix_ref[block] = mix_rows(parts_ref, walsh_ref, width, block, groups, rows)
        return carry

    for_blocks(groups, mix)
    fetch.wait()
    start = signs_at(width, groups)
    for line in range(rows // LANE):
        part = slice(line * LANE, (line + 1) * LANE)
        sign = across(parts_ref[me, start + line : start + line + 1, :])
        for tile in range(0, columns, LANE):
            place = slice(tile, tile + LANE)
            both[0, part, place], both[1, part, place] = pieces(here[part, place] * sign)

    def out_copy(block):
        slot = pl.ds(block * PAIR, PAIR)
        return pltpu.make_async_copy(share.at[:, slot, :], out_ref.at[:, slot, :], sems.at[block])

    def step(block, carry):
        value = weigh(mix_ref[block], both[0], both[1]) / scale
        for apart in range(groups):
            share[apart ^ me, pl.ds(block * PAIR, PAIR), :] = value[apart * PAIR : (apart + 1) * PAIR, :]
        out_copy(block).start()
        return carry

    def finish(block, carry):
        out_copy(block).wait()
        return carry

    for_blocks(groups, step)
    for_blocks(groups, finish)


def sample_body(scale, design_ref, parts_ref, mix_ref, order_ref, *refs):
    near, (keep_ref, send_ref, both) = refs[: NEAR - 1], refs[NEAR - 1 :]
    rows, piece = near[0].shape
    width = design_ref.shape[1]
    groups = mix_ref.shape[0]
    me = lax.axis_index("row")
    signs_start = signs_at(width, groups)
    for line in range(rows // LANE):
        part = slice(line * LANE, (line + 1) * LANE)
        signs = [across(parts_ref[me ^ mask, signs_start + line : signs_start + line + 1, :]) for mask in range(NEAR)]
        for tile in range(0, piece, LANE):
            column = pl.multiple_of(width - NEAR * piece + me % NEAR * piece + tile, LANE)
            here = slice(tile, tile + LANE)
            values = [design_ref[part, pl.ds(column, LANE)]] + [ref[part, here] for ref in near]
            values = [value * sign for value, sign in zip(values, signs)]
            apart = 1
            while apart < NEAR:
                for first in range(NEAR):
                    if not first & apart:
                        one, two = values[first], values[first | apart]
                        values[first], values[first | apart] = one + two, one - two
                apart *= 2
            for index, value in enumerate(values):
                both[index, 0, part, here], both[index, 1, part, here] = pieces(value)

    def step(block, carry):
        value = weigh(mix_ref[block], both[block % NEAR, 0], both[block % NEAR, 1]) / scale
        slot = pl.ds(block * PAIR, PAIR)
        for apart in range(groups):
            far, low = apart // NEAR, apart % NEAR
            out_ref = send_ref if far >= groups // NEAR // 2 else keep_ref
            out_ref[far % (groups // NEAR // 2), low, slot, :] = value[apart * PAIR : (apart + 1) * PAIR, :]
        return carry

    for_blocks(groups, step)


def halve_body(kept_ref, arrived_ref, order_ref, keep_ref, send_ref):
    half = keep_ref.shape[0]
    keep_ref[...] = kept_ref[:half] + arrived_ref[:half]
    send_ref[...] = kept_ref[half:] + arrived_ref[half:]


def split_body(kept_ref, arrived_ref, order_ref, *out_refs):
    for index, out_ref in enumerate(out_refs):
        out_ref[...] = kept_ref[0, index] + arrived_ref[0, index]


def last_body(parts_ref, left_ref, *refs):
    basis_ref, solution_ref, sketch_ref = refs[-3:]
    quarters, summed = refs[3 * ITERS : 3 * ITERS + NEAR], refs[3 * ITERS + NEAR : -3]
    place = lax.axis_index("row") % NEAR
    piece = quarters[0].shape[1]
    width = sketch_ref.shape[1]
    for ref in summed:
        sketch_ref[:, : width - NEAR * piece] = ref[...]
    for mask, part_ref in enumerate(quarters):
        for tile in range(0, piece, LANE):
            column = pl.multiple_of(width - NEAR * piece + (place ^ mask) * piece + tile, LANE)
            sketch_ref[:, pl.ds(column, LANE)] = part_ref[:, tile : tile + LANE]
    betas = [ref[...] for ref in refs[:ITERS]]
    alphas = [ref[...] for ref in refs[ITERS : 2 * ITERS]]
    held = [ref[...] for ref in refs[2 * ITERS : 3 * ITERS]]
    last = jnp.sqrt(tree([parts_ref[i] for i in range(parts_ref.shape[0])])[:1, :])
    basis_ref[...] = left_ref[...] / last
    betas.append(last)
    phibar, rhobar = betas[0], alphas[0]
    search, iterate = held[0], jnp.zeros_like(held[0])
    for step in range(ITERS):
        beta = betas[step + 1]
        rho = jnp.sqrt(rhobar * rhobar + beta * beta)
        cosine = rhobar / rho
        sine = beta / rho
        phi = cosine * phibar
        phibar = sine * phibar
        iterate = iterate + phi / rho * search
        if step + 1 < ITERS:
            alpha = alphas[step + 1]
            search = held[step + 1] - sine * alpha / rho * search
            rhobar = -cosine * alpha
    solution_ref[...] = iterate


def shape(*dims, dtype=F32):
    return jax.ShapeDtypeStruct(dims, dtype)


def shards(design, sign_bits, picks, counts, target, rinv):
    rows, width = design.shape
    whole = rinv.shape[1]
    row_groups = lax.axis_size("row")
    lines = rows // LANE
    scalar = shape(1, LANE)
    deep = message_rows(width)
    left = target.reshape(lines, LANE)
    bits = sign_bits.reshape(lines, LANE)
    piece = columns_traded(width) // NEAR
    rest = width - NEAR * piece
    scale = float(np.sqrt(np.float32(rows * row_groups)))
    slots = row_groups * PAIR
    far = row_groups // NEAR

    message, *away = pl.pallas_call(
        first_body,
        out_shape=(shape(row_groups, signs_at(width, row_groups) + rounded(lines, 8), LANE),)
        + (shape(rows, piece),) * (NEAR - 1),
        in_specs=[HBM] * 5,
        out_specs=(VMEM,) + (HBM,) * (NEAR - 1),
        scratch_shapes=[
            pltpu.VMEM((rows, width), F32),
            pltpu.VMEM((lines, LANE), F32),
            pltpu.VMEM((lines, LANE), jnp.int32),
            pltpu.VMEM((row_groups, PAIR), jnp.int32),
            pltpu.VMEM((1, row_groups), jnp.int32),
            pltpu.SemaphoreType.DMA((4 + lines + NEAR - 1,)),
        ],
        compiler_params=pltpu.CompilerParams(vmem_limit_bytes=58 << 20),
    )(design, left, bits, picks.reshape(row_groups, PAIR), counts.reshape(1, row_groups))

    def swap(array, mask):
        return lax.ppermute(array, "row", [(i, i ^ mask) for i in range(row_groups)])

    signs = jnp.asarray(walsh(HB), jnp.bfloat16)
    made = (shape(row_groups, slots, rows, dtype=jnp.bfloat16), scalar)

    def mix(message):
        return call(functools.partial(mix_body, width), made, message, signs)

    def share(message):
        return pl.pallas_call(
            functools.partial(share_body, scale),
            out_shape=made + (shape(row_groups, slots, rest),),
            in_specs=[VMEM, VMEM, HBM],
            out_specs=(VMEM, VMEM, HBM),
            scratch_shapes=[
                pltpu.VMEM((rows, rest), F32),
                pltpu.VMEM((2, rows, rest), jnp.bfloat16),
                pltpu.VMEM((row_groups, slots, rest), F32),
                pltpu.SemaphoreType.DMA((row_groups + 1,)),
            ],
            compiler_params=pltpu.CompilerParams(vmem_limit_bytes=57 << 20),
        )(message, signs, design)

    def sample(mixed, order):
        return call(
            functools.partial(sample_body, scale),
            (shape(far // 2, NEAR, slots, piece),) * 2,
            design,
            picked,
            mixed,
            order,
            *near,
            scratch=[pltpu.VMEM((NEAR, 2, rows, piece), jnp.bfloat16)],
        )

    def halve(keep, come, order):
        bit = row_groups // 2
        while bit > NEAR:
            bit //= 2
            half = keep.shape[0] // 2
            keep, send = call(halve_body, (shape(half, *keep.shape[1:]),) * 2, keep, come, order)
            come = swap(send, bit)
        return keep, come

    def trade(keep, come, order):
        mine, *others = call(split_body, (shape(slots, piece),) * NEAR, *halve(keep, come, order), order)
        return [mine] + [swap(part, mask + 1) for mask, part in enumerate(others)]

    def back(rinv, message, order, first):
        outs, scratch = (shape(whole // LANE, LANE), scalar), [pltpu.VMEM((width // LANE, LANE), F32)]
        if first:
            outs += (shape(*rinv.shape),)
            scratch += [pltpu.SemaphoreType.DMA((width // LANE,))]
        return pl.pallas_call(
            functools.partial(back_body, first),
            out_shape=outs,
            in_specs=[HBM if first else VMEM, VMEM, VMEM],
            out_specs=(VMEM,) * len(outs),
            scratch_shapes=scratch,
            compiler_params=pltpu.CompilerParams(vmem_limit_bytes=(34 if first else 24) << 20),
            )(rinv, message, order)

    def forward(terms, *before):
        return call(
            functools.partial(forward_body, 2, not before),
            (shape(lines, LANE), shape(whole // LANE, LANE), shape(width // LANE, LANE), scalar),
            here,
            design,
            *terms,
            *before,
        )

    def turn(images, left, beta, alpha, last):
        return call(
            functools.partial(turn_body, 2, last),
            (shape(lines, LANE), shape(row_groups, 8 if last else deep, LANE)),
            *images,
            left,
            beta,
            alpha,
            *(() if last else (design,)),
        )

    betas, alphas, held, summed = [], [], [], []
    message = picked = exchange(message, "row")
    away, _ = lax.optimization_barrier((away, message))
    near = [swap(part, mask + 1) for mask, part in enumerate(away)]
    if rest == 0:
        mixed, token = mix(message)
    else:
        mixed, token, shared = share(message)
        shared = shared.reshape(row_groups * slots, rest)
        summed.append(lax.psum_scatter(shared, "row", scatter_dimension=0, tiled=True))
    for step in range(ITERS):
        last = step + 1 == ITERS
        if step == 0:
            term, beta, here = back(rinv, message, token, True)
        else:
            term, beta = back(here, message, token, False)
            quarters = trade(keep, come, beta)
        betas.append(beta)
        terms = paired(term, "col")
        if step == 0:
            keep, send = sample(mixed, terms[1])
            come = swap(send, row_groups // 2)
        image, right, kept, alpha = forward(terms, *(() if step == 0 else (right, beta)))
        alphas.append(alpha)
        held.append(kept)
        images = paired(image, "col")
        left, message = turn(images, left, beta, alpha, last)
        message = exchange(message, "row")
    basis, answer, sketch = call(
        last_body,
        (shape(lines, LANE), shape(width // LANE, LANE), shape(slots, width)),
        message,
        left,
        *betas,
        *alphas,
        *held,
        *quarters,
        *summed,
    )
    return (sketch, answer.reshape(-1), basis.reshape(-1))


def solution(mesh):
    placed = (
        P("row", "col"),
        P("row"),
        P(None, "row", None),
        P(None, "row"),
        P("row"),
        P("col", None),
    )
    return jax.shard_map(
        shards,
        mesh=mesh,
        in_specs=placed,
        out_specs=(P("row", "col"), P("col"), P("row")),
        check_vma=False,
    )
```

```python
import functools

import jax
import jax.numpy as jnp
import numpy as np
from jax import lax
from jax.experimental import pallas as pl
from jax.experimental.pallas import tpu as pltpu
from jax.sharding import PartitionSpec as P

HB = 256
PAIR = 16
ITERS = 2
LANE = 128
NEAR = 4
CHUNKS = 2
F32 = jnp.float32
VMEM = pl.BlockSpec(memory_space=pltpu.VMEM)
HBM = pl.BlockSpec(memory_space=pltpu.HBM)
ANY = pl.BlockSpec(memory_space=pl.ANY)


def exchange(copies, axis):
    return lax.all_to_all(copies, axis, split_axis=0, concat_axis=0, tiled=True)


def paired(array, axis):
    size = lax.axis_size(axis)
    mask = 1
    while True:
        come = lax.ppermute(array, axis, [(i, i ^ mask) for i in range(size)])
        mask *= 2
        if mask == size:
            return [array, come]
        array = array + come


def tree(values):
    while len(values) > 1:
        values = [values[i] + values[i + 1] for i in range(0, len(values), 2)]
    return values[0]


def walsh(size):
    index = np.arange(size)
    common = index[:, None] & index[None, :]
    parity = np.zeros((size, size), np.int64)
    for shift in range(size.bit_length()):
        parity ^= (common >> shift) & 1
    return (1 - 2 * parity).astype(np.float32)


def call(body, out_shape, *operands, scratch=()):
    return pl.pallas_call(
        body,
        out_shape=out_shape,
        in_specs=[VMEM] * len(operands),
        out_specs=jax.tree.map(lambda _: VMEM, out_shape),
        scratch_shapes=scratch,
        compiler_params=pltpu.CompilerParams(vmem_limit_bytes=24 << 20),
    )(*operands)


def fold_rows(block):
    return block.reshape(block.shape[0] // 8, 8, LANE).sum(axis=0)


def total(rows):
    return jnp.sum(jnp.sum(rows, axis=0, keepdims=True), axis=1, keepdims=True)


def splat(scalar):
    return jnp.broadcast_to(scalar, (1, LANE))


def left_product(vector, matrix_ref, out_ref):
    blocks, tiles = matrix_ref.shape[0] // LANE, matrix_ref.shape[1] // LANE
    sums = [jnp.zeros((8, LANE), F32) for _ in range(tiles)]
    for block in range(blocks):
        weight = across(vector[block : block + 1, :])
        for tile in range(tiles):
            part = matrix_ref[block * LANE : (block + 1) * LANE, tile * LANE : (tile + 1) * LANE]
            sums[tile] = sums[tile] + fold_rows(part * weight)
    for tile in range(tiles):
        out_ref[tile : tile + 1, :] = jnp.sum(sums[tile], axis=0, keepdims=True)


def left_product_long(vector_ref, matrix_ref, out_ref, copies=()):
    blocks, tiles = matrix_ref.shape[0] // LANE, matrix_ref.shape[1] // LANE

    def step(block, sums):
        weight = across(vector_ref[pl.ds(block, 1), :])
        rows = pl.ds(pl.multiple_of(block * LANE, LANE), LANE)
        return tuple(
            sums[tile] + fold_rows(matrix_ref[rows, tile * LANE : (tile + 1) * LANE] * weight)
            for tile in range(tiles)
        )

    sums = tuple(jnp.zeros((8, LANE), F32) for _ in range(tiles))
    if copies:
        for block, copy in enumerate(copies):
            copy.wait()
            sums = step(block, sums)
    else:
        sums = lax.fori_loop(0, blocks, step, sums)
    for tile in range(tiles):
        out_ref[tile : tile + 1, :] = jnp.sum(sums[tile], axis=0, keepdims=True)


def right_product(matrix_ref, vector, out_ref):
    blocks, tiles = matrix_ref.shape[0] // LANE, matrix_ref.shape[1] // LANE

    def step(block, carry):
        rows = pl.ds(pl.multiple_of(block * LANE, LANE), LANE)
        sums = jnp.zeros((LANE, LANE), F32)
        for tile in range(tiles):
            sums = sums + matrix_ref[rows, tile * LANE : (tile + 1) * LANE] * vector[tile : tile + 1, :]
        out_ref[pl.ds(block, 1), :] = jnp.sum(fold_rows(sums.T), axis=0, keepdims=True)
        return carry

    lax.fori_loop(0, blocks, step, 0)


def rounded(count, unit):
    return -(-count // unit) * unit


def message_rows(width):
    return rounded(width // LANE + 1, 8)


def picks_at(width):
    return width // LANE + 1


def signs_at(width, groups):
    return picks_at(width) + groups * PAIR // LANE


def copy_out(out_ref):
    first = out_ref[0]
    for index in range(1, out_ref.shape[0]):
        out_ref[index] = first


def across(row):
    return jnp.broadcast_to(row, (LANE, LANE)).T


def first_body(design_ref, target_ref, bits_ref, picks_ref, counts_ref, *refs):
    out_ref, away_refs = refs[0], refs[1:-6]
    design, target_here, bits, picks, counts, sems = refs[-6:]
    rows, width = design.shape
    lines, tiles = rows // LANE, width // LANE
    small = [
        pltpu.make_async_copy(source, place, sems.at[index])
        for index, (source, place) in enumerate(
            ((target_ref, target_here), (bits_ref, bits), (picks_ref, picks), (counts_ref, counts))
        )
    ]
    parts = [slice(line * LANE, (line + 1) * LANE) for line in range(lines)]
    large = [
        pltpu.make_async_copy(design_ref.at[part, :], design.at[part, :], sems.at[4 + line])
        for line, part in enumerate(parts)
    ]
    place = lax.axis_index("row") % NEAR
    away = []
    for index, away_ref in enumerate(away_refs):
        piece = away_ref.shape[1]
        chunk, mask = index // (NEAR - 1), index % (NEAR - 1) + 1
        column = pl.multiple_of((place ^ mask) * (width // NEAR) + chunk * piece, LANE)
        source = design.at[:, pl.ds(column, piece)]
        away.append(pltpu.make_async_copy(source, away_ref, sems.at[4 + lines + index]))
    for copy in small + large:
        copy.start()
    for copy in small:
        copy.wait()
    out_ref[0] = jnp.zeros(out_ref.shape[1:], F32)
    groups = picks.shape[0]
    owner = lax.broadcasted_iota(jnp.int32, (groups, groups), 0)
    same = owner == lax.broadcasted_iota(jnp.int32, (groups, groups), 1)
    limit = jnp.sum(jnp.where(same, counts[...].astype(F32), 0.0), axis=1, keepdims=True)
    slot = lax.broadcasted_iota(jnp.int32, picks.shape, 1).astype(F32)
    coded = jnp.where(slot < limit, picks[...].astype(F32), -1.0)
    start = picks_at(width)
    for owner in range(0, groups, LANE // PAIR):
        line = jnp.concatenate([coded[i : i + 1, :] for i in range(owner, owner + LANE // PAIR)], axis=1)
        out_ref[0, start + owner * PAIR // LANE : start + owner * PAIR // LANE + 1, :] = line
    start = signs_at(width, groups)
    out_ref[0, start : start + lines, :] = (2 * bits[...] - 1).astype(F32)
    target = target_here[...]
    out_ref[0, tiles : tiles + 1, :] = splat(total(target * target))
    sums = [jnp.zeros((8, LANE), F32) for _ in range(tiles)]
    for line, part in enumerate(parts):
        weight = across(target[line : line + 1, :])
        large[line].wait()
        if line == lines - 1:
            for copy in away:
                copy.start()
        for tile in range(tiles):
            sums[tile] = sums[tile] + fold_rows(design[part, tile * LANE : (tile + 1) * LANE] * weight)
    for tile in range(tiles):
        out_ref[0, tile : tile + 1, :] = jnp.sum(sums[tile], axis=0, keepdims=True)
    copy_out(out_ref)
    for copy in away:
        copy.wait()


def back_body(first, rinv_ref, parts_ref, term_ref, beta_ref, *refs):
    tiles = rinv_ref.shape[0] // LANE
    copies = []
    if first:
        rinv_here, scratch, sems = refs
        for block in range(tiles):
            part = slice(block * LANE, (block + 1) * LANE)
            copies.append(pltpu.make_async_copy(rinv_ref.at[part, :], rinv_here.at[part, :], sems.at[block]))
            copies[-1].start()
    else:
        rinv_here, (scratch,) = rinv_ref, refs
    summed = tree([parts_ref[i, : tiles + 1, :] for i in range(parts_ref.shape[0])])
    beta = jnp.sqrt(summed[tiles : tiles + 1, :])
    beta_ref[...] = beta
    scratch[...] = summed[:tiles, :] / beta
    left_product_long(scratch, rinv_here, term_ref, copies)


def forward_body(groups, first, last, rinv_ref, design_ref, *refs):
    right = tree([ref[...] for ref in refs[:groups]])
    refs = refs[groups:]
    if not first:
        before_ref, beta_ref, *refs = refs
        right = right - beta_ref[...] * before_ref[...]
    image_ref, held_ref, alpha_ref, *right_refs = refs
    alpha = jnp.sqrt(total(right * right))
    alpha_ref[...] = splat(alpha)
    right = right / alpha
    if not last:
        right_refs[0][...] = right
    right_product(rinv_ref, right, held_ref)
    right_product(design_ref, held_ref[...], image_ref)


def turn_body(groups, last, *refs):
    left = tree([ref[...] for ref in refs[:groups]])
    before_ref, beta_ref, alpha_ref, token_ref, *refs = refs[groups:]
    left = left - alpha_ref[...] * (before_ref[...] / beta_ref[...])
    square = splat(total(left * left))
    if last:
        left_ref, out_ref = refs
        out_ref[...] = jnp.broadcast_to(square, out_ref.shape)
    else:
        design_ref, left_ref, out_ref = refs
        tiles = design_ref.shape[1] // LANE
        out_ref[0] = jnp.zeros(out_ref.shape[1:], F32)
        left_product(left, design_ref, out_ref.at[0])
        out_ref[0, tiles : tiles + 1, :] = square
        copy_out(out_ref)
    left_ref[...] = left


def pieces(value):
    high = value.astype(jnp.bfloat16)
    return high, (value - high.astype(F32)).astype(jnp.bfloat16)


def weigh(mix, high, low):
    return jnp.dot(mix, high, preferred_element_type=F32) + jnp.dot(mix, low, preferred_element_type=F32)


def for_blocks(groups, step):
    if groups <= 8:
        for block in range(groups):
            step(block, 0)
    else:
        lax.fori_loop(0, groups, step, 0)


def mix_body(width, parts_ref, walsh_ref, mix_ref):
    groups, _, rows = mix_ref.shape
    me = lax.axis_index("row")
    local = lax.broadcasted_iota(jnp.int32, (LANE, rows), 1).astype(F32)
    per = LANE // PAIR

    def step(block, carry):
        parity = jnp.int32(0)
        for bit in range(groups.bit_length() - 1):
            parity = parity ^ ((block & me) >> bit)
        sign = (1 - 2 * (parity & 1)).astype(F32)
        for line in range(groups // per):
            start = picks_at(width) + line
            coded = across(parts_ref[block, start : start + 1, :])
            match = jnp.concatenate([coded] * (rows // LANE), axis=1) == local
            chosen = jnp.where(match, sign, 0.0).astype(jnp.bfloat16)
            for part in range(rows // HB):
                columns = slice(part * HB, (part + 1) * HB)
                mixed = jnp.dot(chosen[:, columns], walsh_ref[...], preferred_element_type=F32).astype(jnp.bfloat16)
                for index in range(per):
                    place = pl.multiple_of(((line * per + index) ^ me) * PAIR, PAIR)
                    mix_ref[block, pl.ds(place, PAIR), columns] = mixed[index * PAIR : (index + 1) * PAIR, :]
        return carry

    for_blocks(groups, step)


def sample_body(scale, start, design_ref, parts_ref, mix_ref, order_ref, *refs):
    near, (keep_ref, send_ref, both) = refs[: NEAR - 1], refs[NEAR - 1 :]
    rows, piece = near[0].shape
    width = design_ref.shape[1]
    groups = mix_ref.shape[0]
    me = lax.axis_index("row")
    signs_start = signs_at(width, groups)
    for line in range(rows // LANE):
        part = slice(line * LANE, (line + 1) * LANE)
        signs = [across(parts_ref[me ^ mask, signs_start + line : signs_start + line + 1, :]) for mask in range(NEAR)]
        for tile in range(0, piece, LANE):
            column = pl.multiple_of(me % NEAR * (width // NEAR) + start + tile, LANE)
            here = slice(tile, tile + LANE)
            values = [design_ref[part, pl.ds(column, LANE)]] + [ref[part, here] for ref in near]
            values = [value * sign for value, sign in zip(values, signs)]
            apart = 1
            while apart < NEAR:
                for first in range(NEAR):
                    if not first & apart:
                        one, two = values[first], values[first | apart]
                        values[first], values[first | apart] = one + two, one - two
                apart *= 2
            for index, value in enumerate(values):
                both[index, 0, part, here], both[index, 1, part, here] = pieces(value)

    def step(block, carry):
        value = weigh(mix_ref[block], both[block % NEAR, 0], both[block % NEAR, 1]) / scale
        slot = pl.ds(block * PAIR, PAIR)
        for apart in range(groups):
            far, low = apart // NEAR, apart % NEAR
            out_ref = send_ref if far >= groups // NEAR // 2 else keep_ref
            out_ref[far % (groups // NEAR // 2), low, slot, :] = value[apart * PAIR : (apart + 1) * PAIR, :]
        return carry

    for_blocks(groups, step)


def halve_body(kept_ref, arrived_ref, order_ref, keep_ref, send_ref):
    half = keep_ref.shape[0]
    keep_ref[...] = kept_ref[:half] + arrived_ref[:half]
    send_ref[...] = kept_ref[half:] + arrived_ref[half:]


def join_body(kept_ref, arrived_ref, order_ref, out_ref, token_ref):
    token_ref[...] = order_ref[:1, :]
    out_ref[...] = kept_ref[0] + arrived_ref[0]


def touch_body(*refs):
    order_ref, token_ref = refs[-2:]
    token_ref[...] = order_ref[:1, :]


def split_body(chunks, *refs):
    joined, (kept_ref, arrived_ref, order_ref, token_ref, *out_refs) = refs[: chunks - 1], refs[chunks - 1 :]
    token_ref[...] = order_ref[:1, :]
    piece = kept_ref.shape[3]
    for chunk in range(chunks):
        columns = slice(chunk * piece, (chunk + 1) * piece)
        for index, out_ref in enumerate(out_refs):
            if chunk < chunks - 1:
                out_ref[:, columns] = joined[chunk][index]
            else:
                out_ref[:, columns] = kept_ref[0, index] + arrived_ref[0, index]


def last_body(parts_ref, left_ref, *refs):
    basis_ref, solution_ref, sketch_ref = refs[-3:]
    quarters = refs[3 * ITERS : 3 * ITERS + NEAR]
    place = lax.axis_index("row") % NEAR
    piece = quarters[0].shape[1]
    for mask, part_ref in enumerate(quarters):
        for tile in range(0, piece, LANE):
            column = pl.multiple_of((place ^ mask) * piece + tile, LANE)
            sketch_ref[:, pl.ds(column, LANE)] = part_ref[:, tile : tile + LANE]
    betas = [ref[...] for ref in refs[:ITERS]]
    alphas = [ref[...] for ref in refs[ITERS : 2 * ITERS]]
    held = [ref[...] for ref in refs[2 * ITERS : 3 * ITERS]]
    last = jnp.sqrt(tree([parts_ref[i] for i in range(parts_ref.shape[0])])[:1, :])
    basis_ref[...] = left_ref[...] / last
    betas.append(last)
    phibar, rhobar = betas[0], alphas[0]
    search, iterate = held[0], jnp.zeros_like(held[0])
    for step in range(ITERS):
        beta = betas[step + 1]
        rho = jnp.sqrt(rhobar * rhobar + beta * beta)
        cosine = rhobar / rho
        sine = beta / rho
        phi = cosine * phibar
        phibar = sine * phibar
        iterate = iterate + phi / rho * search
        if step + 1 < ITERS:
            alpha = alphas[step + 1]
            search = held[step + 1] - sine * alpha / rho * search
            rhobar = -cosine * alpha
    solution_ref[...] = iterate


def shape(*dims, dtype=F32):
    return jax.ShapeDtypeStruct(dims, dtype)


def shards(design, sign_bits, picks, counts, target, rinv):
    rows, width = design.shape
    whole = rinv.shape[1]
    row_groups = lax.axis_size("row")
    lines = rows // LANE
    scalar = shape(1, LANE)
    deep = message_rows(width)
    left = target.reshape(lines, LANE)
    bits = sign_bits.reshape(lines, LANE)
    chunks = min(CHUNKS, width // NEAR // LANE)
    piece = width // NEAR // chunks
    scale = float(np.sqrt(np.float32(rows * row_groups)))
    slots = row_groups * PAIR
    far = row_groups // NEAR

    message, *away = pl.pallas_call(
        first_body,
        out_shape=(shape(row_groups, rounded(signs_at(width, row_groups) + lines, 8), LANE),)
        + (shape(rows, piece),) * (chunks * (NEAR - 1)),
        in_specs=[HBM] * 5,
        out_specs=(VMEM,) + (HBM,) * (chunks * (NEAR - 1)),
        scratch_shapes=[
            pltpu.VMEM((rows, width), F32),
            pltpu.VMEM((lines, LANE), F32),
            pltpu.VMEM((lines, LANE), jnp.int32),
            pltpu.VMEM((row_groups, PAIR), jnp.int32),
            pltpu.VMEM((1, row_groups), jnp.int32),
            pltpu.SemaphoreType.DMA((4 + lines + chunks * (NEAR - 1),)),
        ],
        compiler_params=pltpu.CompilerParams(vmem_limit_bytes=58 << 20),
    )(design, left, bits, picks.reshape(row_groups, PAIR), counts.reshape(1, row_groups))

    def swap(array, mask):
        return lax.ppermute(array, "row", [(i, i ^ mask) for i in range(row_groups)])

    def mix(message):
        made = shape(row_groups, slots, rows, dtype=jnp.bfloat16)
        return call(functools.partial(mix_body, width), made, message, jnp.asarray(walsh(HB), jnp.bfloat16))

    def sample(chunk, mixed, order):
        return call(
            functools.partial(sample_body, scale, chunk * piece),
            (shape(far // 2, NEAR, slots, piece),) * 2,
            design,
            picked,
            mixed,
            order,
            *near[chunk],
            scratch=[pltpu.VMEM((NEAR, 2, rows, piece), jnp.bfloat16)],
        )

    def spread(chunk, masks, order):
        parts = [away[chunk * (NEAR - 1) + mask - 1] for mask in masks]
        parts, _ = lax.optimization_barrier((parts, order))
        return [swap(part, mask) for mask, part in zip(masks, parts)]

    def halve(keep, come, order):
        bit = row_groups // 2
        while bit > NEAR:
            bit //= 2
            half = keep.shape[0] // 2
            keep, send = call(halve_body, (shape(half, *keep.shape[1:]),) * 2, keep, come, order)
            come = swap(send, bit)
        return keep, come

    def join(keep, come, order):
        keep, come = halve(keep, come, order)
        return call(join_body, (shape(*keep.shape[1:]), scalar), keep, come, order)

    def trade(joined, keep, come, order):
        token, mine, *others = call(
            functools.partial(split_body, chunks),
            (scalar,) + (shape(slots, width // NEAR),) * NEAR,
            *joined,
            *halve(keep, come, order),
            order,
        )
        return [mine] + [swap(part, mask + 1) for mask, part in enumerate(others)], token

    def back(rinv, message, first):
        outs, scratch = (shape(whole // LANE, LANE), scalar), [pltpu.VMEM((width // LANE, LANE), F32)]
        if first:
            outs += (shape(*rinv.shape),)
            scratch += [pltpu.SemaphoreType.DMA((width // LANE,))]
        return pl.pallas_call(
            functools.partial(back_body, first),
            out_shape=outs,
            in_specs=[HBM if first else VMEM, VMEM],
            out_specs=(VMEM,) * len(outs),
            scratch_shapes=scratch,
            compiler_params=pltpu.CompilerParams(vmem_limit_bytes=(34 if first else 24) << 20),
            )(rinv, message)

    def forward(terms, last, *before):
        return call(
            functools.partial(forward_body, len(terms), not before, last),
            (shape(lines, LANE), shape(width // LANE, LANE), scalar)
            + (() if last else (shape(whole // LANE, LANE),)),
            here,
            design,
            *terms,
            *before,
        )

    def turn(images, left, beta, alpha, token, last):
        return call(
            functools.partial(turn_body, 2, last),
            (shape(lines, LANE), shape(row_groups, 8 if last else deep, LANE)),
            *images,
            left,
            beta,
            alpha,
            token,
            *(() if last else (design,)),
        )

    betas, alphas, held, joined = [], [], [], []
    message = picked = exchange(message, "row")
    near = [spread(0, (1, 2, 3), message)]
    right = []
    for step in range(ITERS):
        last = step + 1 == ITERS
        if step == 0:
            term, beta, here = back(rinv, message, True)
            mixed = mix(message)
        else:
            term, beta = back(here, message, False)
        betas.append(beta)
        terms = paired(term, "col")
        if step == 0:
            near += [spread(chunk, (1, 2), terms[1]) for chunk in range(1, chunks)]
            keep, send = sample(0, mixed, terms[1])
            come = swap(send, row_groups // 2)
        elif chunks > 1:
            keep, send = sample(1, mixed, terms[1])
            come = swap(send, row_groups // 2)
        image, kept, alpha, *right = forward(terms, last, *right, *betas[1:])
        alphas.append(alpha)
        held.append(kept)
        images = paired(image, "col")
        token = alpha
        if chunks > 1 and step == 0:
            part, token = join(keep, come, alpha)
            joined.append(part)
            there = [array for arrays in near[1:] for array in arrays]
            token = pl.pallas_call(
                touch_body,
                out_shape=scalar,
                in_specs=[ANY] * len(there) + [VMEM],
                out_specs=VMEM,
            )(*there, token)
        if last:
            quarters, token = trade(joined, keep, come, alpha)
        left, message = turn(images, left, beta, alpha, token, last)
        message = exchange(message, "row")
        if step == 0:
            for chunk in range(1, chunks):
                near[chunk] += spread(chunk, (3,), message)
    basis, answer, sketch = call(
        last_body,
        (shape(lines, LANE), shape(width // LANE, LANE), shape(slots, width)),
        message,
        left,
        *betas,
        *alphas,
        *held,
        *quarters,
    )
    return (sketch, answer.reshape(-1), basis.reshape(-1))


def solution(mesh):
    placed = (
        P("row", "col"),
        P("row"),
        P(None, "row", None),
        P(None, "row"),
        P("row"),
        P("col", None),
    )
    return jax.shard_map(
        shards,
        mesh=mesh,
        in_specs=placed,
        out_specs=(P("row", "col"), P("col"), P("row")),
        check_vma=False,
    )
```

```python
import functools

import jax
import jax.numpy as jnp
import numpy as np
from jax import lax
from jax.experimental import pallas as pl
from jax.experimental.pallas import tpu as pltpu
from jax.sharding import PartitionSpec as P

HB = 256
PAIR = 16
ITERS = 2
LANE = 128
NEAR = 4
CHUNKS = 2
F32 = jnp.float32
VMEM = pl.BlockSpec(memory_space=pltpu.VMEM)
HBM = pl.BlockSpec(memory_space=pltpu.HBM)
ANY = pl.BlockSpec(memory_space=pl.ANY)


def exchange(copies, axis):
    return lax.all_to_all(copies, axis, split_axis=0, concat_axis=0, tiled=True)


def paired(array, axis):
    size = lax.axis_size(axis)
    mask = 1
    while True:
        come = lax.ppermute(array, axis, [(i, i ^ mask) for i in range(size)])
        mask *= 2
        if mask == size:
            return [array, come]
        array = array + come


def direct(array, axis):
    size = lax.axis_size(axis)
    return [array] + [
        lax.ppermute(array, axis, [(i, i ^ mask) for i in range(size)]) for mask in range(1, size)
    ]


def tree(values):
    while len(values) > 1:
        values = [values[i] + values[i + 1] for i in range(0, len(values), 2)]
    return values[0]


def walsh(size):
    index = np.arange(size)
    common = index[:, None] & index[None, :]
    parity = np.zeros((size, size), np.int64)
    for shift in range(size.bit_length()):
        parity ^= (common >> shift) & 1
    return (1 - 2 * parity).astype(np.float32)


def call(body, out_shape, *operands, scratch=()):
    return pl.pallas_call(
        body,
        out_shape=out_shape,
        in_specs=[VMEM] * len(operands),
        out_specs=jax.tree.map(lambda _: VMEM, out_shape),
        scratch_shapes=scratch,
        compiler_params=pltpu.CompilerParams(vmem_limit_bytes=24 << 20),
    )(*operands)


def fold_rows(block):
    return block.reshape(block.shape[0] // 8, 8, LANE).sum(axis=0)


def total(rows):
    return jnp.sum(jnp.sum(rows, axis=0, keepdims=True), axis=1, keepdims=True)


def splat(scalar):
    return jnp.broadcast_to(scalar, (1, LANE))


def left_product(vector, matrix_ref, out_ref):
    blocks, tiles = matrix_ref.shape[0] // LANE, matrix_ref.shape[1] // LANE
    sums = [jnp.zeros((8, LANE), F32) for _ in range(tiles)]
    for block in range(blocks):
        weight = across(vector[block : block + 1, :])
        for tile in range(tiles):
            part = matrix_ref[block * LANE : (block + 1) * LANE, tile * LANE : (tile + 1) * LANE]
            sums[tile] = sums[tile] + fold_rows(part * weight)
    for tile in range(tiles):
        out_ref[tile : tile + 1, :] = jnp.sum(sums[tile], axis=0, keepdims=True)


def left_product_long(vector_ref, matrix_ref, out_ref, copies=()):
    blocks, tiles = matrix_ref.shape[0] // LANE, matrix_ref.shape[1] // LANE

    def step(block, sums):
        weight = across(vector_ref[pl.ds(block, 1), :])
        rows = pl.ds(pl.multiple_of(block * LANE, LANE), LANE)
        return tuple(
            sums[tile] + fold_rows(matrix_ref[rows, tile * LANE : (tile + 1) * LANE] * weight)
            for tile in range(tiles)
        )

    sums = tuple(jnp.zeros((8, LANE), F32) for _ in range(tiles))
    if copies:
        for block, copy in enumerate(copies):
            copy.wait()
            sums = step(block, sums)
    else:
        sums = lax.fori_loop(0, blocks, step, sums)
    for tile in range(tiles):
        out_ref[tile : tile + 1, :] = jnp.sum(sums[tile], axis=0, keepdims=True)


def right_product(matrix_ref, vector, out_ref):
    blocks, tiles = matrix_ref.shape[0] // LANE, matrix_ref.shape[1] // LANE

    def step(block, carry):
        rows = pl.ds(pl.multiple_of(block * LANE, LANE), LANE)
        sums = jnp.zeros((LANE, LANE), F32)
        for tile in range(tiles):
            sums = sums + matrix_ref[rows, tile * LANE : (tile + 1) * LANE] * vector[tile : tile + 1, :]
        out_ref[pl.ds(block, 1), :] = jnp.sum(fold_rows(sums.T), axis=0, keepdims=True)
        return carry

    lax.fori_loop(0, blocks, step, 0)


def rounded(count, unit):
    return -(-count // unit) * unit


def message_rows(width):
    return rounded(width // LANE + 1, 8)


def picks_at(width):
    return width // LANE + 1


def signs_at(width, groups):
    return picks_at(width) + groups * PAIR // LANE


def copy_out(out_ref):
    first = out_ref[0]
    for index in range(1, out_ref.shape[0]):
        out_ref[index] = first


def across(row):
    return jnp.broadcast_to(row, (LANE, LANE)).T


def first_body(design_ref, target_ref, bits_ref, picks_ref, counts_ref, *refs):
    out_ref, away_refs = refs[0], refs[1:-6]
    design, target_here, bits, picks, counts, sems = refs[-6:]
    rows, width = design.shape
    lines, tiles = rows // LANE, width // LANE
    small = [
        pltpu.make_async_copy(source, place, sems.at[index])
        for index, (source, place) in enumerate(
            ((target_ref, target_here), (bits_ref, bits), (picks_ref, picks), (counts_ref, counts))
        )
    ]
    parts = [slice(line * LANE, (line + 1) * LANE) for line in range(lines)]
    large = [
        pltpu.make_async_copy(design_ref.at[part, :], design.at[part, :], sems.at[4 + line])
        for line, part in enumerate(parts)
    ]
    place = lax.axis_index("row") % NEAR
    away = []
    for index, away_ref in enumerate(away_refs):
        piece = away_ref.shape[1]
        chunk, mask = index // (NEAR - 1), index % (NEAR - 1) + 1
        column = pl.multiple_of((place ^ mask) * (width // NEAR) + chunk * piece, LANE)
        source = design.at[:, pl.ds(column, piece)]
        away.append(pltpu.make_async_copy(source, away_ref, sems.at[4 + lines + index]))
    for copy in small + large:
        copy.start()
    for copy in small:
        copy.wait()
    out_ref[0] = jnp.zeros(out_ref.shape[1:], F32)
    groups = picks.shape[0]
    owner = lax.broadcasted_iota(jnp.int32, (groups, groups), 0)
    same = owner == lax.broadcasted_iota(jnp.int32, (groups, groups), 1)
    limit = jnp.sum(jnp.where(same, counts[...].astype(F32), 0.0), axis=1, keepdims=True)
    slot = lax.broadcasted_iota(jnp.int32, picks.shape, 1).astype(F32)
    coded = jnp.where(slot < limit, picks[...].astype(F32), -1.0)
    start = picks_at(width)
    for owner in range(0, groups, LANE // PAIR):
        line = jnp.concatenate([coded[i : i + 1, :] for i in range(owner, owner + LANE // PAIR)], axis=1)
        out_ref[0, start + owner * PAIR // LANE : start + owner * PAIR // LANE + 1, :] = line
    start = signs_at(width, groups)
    out_ref[0, start : start + lines, :] = (2 * bits[...] - 1).astype(F32)
    target = target_here[...]
    out_ref[0, tiles : tiles + 1, :] = splat(total(target * target))
    sums = [jnp.zeros((8, LANE), F32) for _ in range(tiles)]
    for line, part in enumerate(parts):
        weight = across(target[line : line + 1, :])
        large[line].wait()
        if line == lines - 1:
            for copy in away:
                copy.start()
        for tile in range(tiles):
            sums[tile] = sums[tile] + fold_rows(design[part, tile * LANE : (tile + 1) * LANE] * weight)
    for tile in range(tiles):
        out_ref[0, tile : tile + 1, :] = jnp.sum(sums[tile], axis=0, keepdims=True)
    copy_out(out_ref)
    for copy in away:
        copy.wait()


def back_body(first, rinv_ref, parts_ref, term_ref, beta_ref, *refs):
    tiles = rinv_ref.shape[0] // LANE
    copies = []
    if first:
        rinv_here, scratch, sems = refs
        for block in range(tiles):
            part = slice(block * LANE, (block + 1) * LANE)
            copies.append(pltpu.make_async_copy(rinv_ref.at[part, :], rinv_here.at[part, :], sems.at[block]))
            copies[-1].start()
    else:
        rinv_here, (scratch,) = rinv_ref, refs
    summed = tree([parts_ref[i, : tiles + 1, :] for i in range(parts_ref.shape[0])])
    beta = jnp.sqrt(summed[tiles : tiles + 1, :])
    beta_ref[...] = beta
    scratch[...] = summed[:tiles, :] / beta
    left_product_long(scratch, rinv_here, term_ref, copies)


def forward_body(groups, first, last, rinv_ref, design_ref, *refs):
    right = tree([ref[...] for ref in refs[:groups]])
    refs = refs[groups:]
    if not first:
        before_ref, beta_ref, *refs = refs
        right = right - beta_ref[...] * before_ref[...]
    image_ref, held_ref, alpha_ref, *right_refs = refs
    alpha = jnp.sqrt(total(right * right))
    alpha_ref[...] = splat(alpha)
    right = right / alpha
    if not last:
        right_refs[0][...] = right
    right_product(rinv_ref, right, held_ref)
    right_product(design_ref, held_ref[...], image_ref)


def turn_body(groups, last, *refs):
    left = tree([ref[...] for ref in refs[:groups]])
    before_ref, beta_ref, alpha_ref, token_ref, *refs = refs[groups:]
    left = left - alpha_ref[...] * (before_ref[...] / beta_ref[...])
    square = splat(total(left * left))
    if last:
        left_ref, out_ref = refs
        out_ref[...] = jnp.broadcast_to(square, out_ref.shape)
    else:
        design_ref, left_ref, out_ref = refs
        tiles = design_ref.shape[1] // LANE
        out_ref[0] = jnp.zeros(out_ref.shape[1:], F32)
        left_product(left, design_ref, out_ref.at[0])
        out_ref[0, tiles : tiles + 1, :] = square
        copy_out(out_ref)
    left_ref[...] = left


def pieces(value):
    high = value.astype(jnp.bfloat16)
    return high, (value - high.astype(F32)).astype(jnp.bfloat16)


def weigh(mix, high, low):
    return jnp.dot(mix, high, preferred_element_type=F32) + jnp.dot(mix, low, preferred_element_type=F32)


def for_blocks(groups, step):
    if groups <= 8:
        for block in range(groups):
            step(block, 0)
    else:
        lax.fori_loop(0, groups, step, 0)


def mix_body(width, parts_ref, walsh_ref, mix_ref):
    groups, _, rows = mix_ref.shape
    me = lax.axis_index("row")
    local = lax.broadcasted_iota(jnp.int32, (LANE, rows), 1).astype(F32)
    per = LANE // PAIR

    def step(block, carry):
        parity = jnp.int32(0)
        for bit in range(groups.bit_length() - 1):
            parity = parity ^ ((block & me) >> bit)
        sign = (1 - 2 * (parity & 1)).astype(F32)
        for line in range(groups // per):
            start = picks_at(width) + line
            coded = across(parts_ref[block, start : start + 1, :])
            match = jnp.concatenate([coded] * (rows // LANE), axis=1) == local
            chosen = jnp.where(match, sign, 0.0).astype(jnp.bfloat16)
            for part in range(rows // HB):
                columns = slice(part * HB, (part + 1) * HB)
                mixed = jnp.dot(chosen[:, columns], walsh_ref[...], preferred_element_type=F32).astype(jnp.bfloat16)
                for index in range(per):
                    place = pl.multiple_of(((line * per + index) ^ me) * PAIR, PAIR)
                    mix_ref[block, pl.ds(place, PAIR), columns] = mixed[index * PAIR : (index + 1) * PAIR, :]
        return carry

    for_blocks(groups, step)


def sample_body(scale, start, design_ref, parts_ref, mix_ref, order_ref, *refs):
    near, (keep_ref, send_ref, both) = refs[: NEAR - 1], refs[NEAR - 1 :]
    rows, piece = near[0].shape
    width = design_ref.shape[1]
    groups = mix_ref.shape[0]
    me = lax.axis_index("row")
    signs_start = signs_at(width, groups)
    for line in range(rows // LANE):
        part = slice(line * LANE, (line + 1) * LANE)
        signs = [across(parts_ref[me ^ mask, signs_start + line : signs_start + line + 1, :]) for mask in range(NEAR)]
        for tile in range(0, piece, LANE):
            column = pl.multiple_of(me % NEAR * (width // NEAR) + start + tile, LANE)
            here = slice(tile, tile + LANE)
            values = [design_ref[part, pl.ds(column, LANE)]] + [ref[part, here] for ref in near]
            values = [value * sign for value, sign in zip(values, signs)]
            apart = 1
            while apart < NEAR:
                for first in range(NEAR):
                    if not first & apart:
                        one, two = values[first], values[first | apart]
                        values[first], values[first | apart] = one + two, one - two
                apart *= 2
            for index, value in enumerate(values):
                both[index, 0, part, here], both[index, 1, part, here] = pieces(value)

    def step(block, carry):
        value = weigh(mix_ref[block], both[block % NEAR, 0], both[block % NEAR, 1]) / scale
        slot = pl.ds(block * PAIR, PAIR)
        for apart in range(groups):
            far, low = apart // NEAR, apart % NEAR
            out_ref = send_ref if far >= groups // NEAR // 2 else keep_ref
            out_ref[far % (groups // NEAR // 2), low, slot, :] = value[apart * PAIR : (apart + 1) * PAIR, :]
        return carry

    for_blocks(groups, step)


def halve_body(kept_ref, arrived_ref, order_ref, keep_ref, send_ref):
    half = keep_ref.shape[0]
    keep_ref[...] = kept_ref[:half] + arrived_ref[:half]
    send_ref[...] = kept_ref[half:] + arrived_ref[half:]


def join_body(kept_ref, arrived_ref, order_ref, out_ref, token_ref):
    token_ref[...] = order_ref[:1, :]
    out_ref[...] = kept_ref[0] + arrived_ref[0]


def touch_body(*refs):
    order_ref, token_ref = refs[-2:]
    token_ref[...] = order_ref[:1, :]


def split_body(chunks, *refs):
    joined, (kept_ref, arrived_ref, order_ref, *out_refs) = refs[: chunks - 1], refs[chunks - 1 :]
    piece = kept_ref.shape[3]
    for chunk in range(chunks):
        columns = slice(chunk * piece, (chunk + 1) * piece)
        for index, out_ref in enumerate(out_refs):
            if chunk < chunks - 1:
                out_ref[:, columns] = joined[chunk][index]
            else:
                out_ref[:, columns] = kept_ref[0, index] + arrived_ref[0, index]


def assemble_body(*refs):
    quarters, sketch_ref = refs[:-1], refs[-1]
    place = lax.axis_index("row") % NEAR
    piece = quarters[0].shape[1]
    for mask, part_ref in enumerate(quarters):
        for tile in range(0, piece, LANE):
            column = pl.multiple_of((place ^ mask) * piece + tile, LANE)
            sketch_ref[:, pl.ds(column, LANE)] = part_ref[:, tile : tile + LANE]


def last_body(parts_ref, left_ref, *refs):
    basis_ref, solution_ref = refs[-2:]
    betas = [ref[...] for ref in refs[:ITERS]]
    alphas = [ref[...] for ref in refs[ITERS : 2 * ITERS]]
    held = [ref[...] for ref in refs[2 * ITERS : 3 * ITERS]]
    last = jnp.sqrt(tree([parts_ref[i] for i in range(parts_ref.shape[0])])[:1, :])
    basis_ref[...] = left_ref[...] / last
    betas.append(last)
    phibar, rhobar = betas[0], alphas[0]
    search, iterate = held[0], jnp.zeros_like(held[0])
    for step in range(ITERS):
        beta = betas[step + 1]
        rho = jnp.sqrt(rhobar * rhobar + beta * beta)
        cosine = rhobar / rho
        sine = beta / rho
        phi = cosine * phibar
        phibar = sine * phibar
        iterate = iterate + phi / rho * search
        if step + 1 < ITERS:
            alpha = alphas[step + 1]
            search = held[step + 1] - sine * alpha / rho * search
            rhobar = -cosine * alpha
    solution_ref[...] = iterate


def shape(*dims, dtype=F32):
    return jax.ShapeDtypeStruct(dims, dtype)


def shards(design, sign_bits, picks, counts, target, rinv):
    rows, width = design.shape
    whole = rinv.shape[1]
    row_groups = lax.axis_size("row")
    lines = rows // LANE
    scalar = shape(1, LANE)
    deep = message_rows(width)
    left = target.reshape(lines, LANE)
    bits = sign_bits.reshape(lines, LANE)
    chunks = min(CHUNKS, width // NEAR // LANE)
    piece = width // NEAR // chunks
    scale = float(np.sqrt(np.float32(rows * row_groups)))
    slots = row_groups * PAIR
    far = row_groups // NEAR

    message, *away = pl.pallas_call(
        first_body,
        out_shape=(shape(row_groups, rounded(signs_at(width, row_groups) + lines, 8), LANE),)
        + (shape(rows, piece),) * (chunks * (NEAR - 1)),
        in_specs=[HBM] * 5,
        out_specs=(VMEM,) + (HBM,) * (chunks * (NEAR - 1)),
        scratch_shapes=[
            pltpu.VMEM((rows, width), F32),
            pltpu.VMEM((lines, LANE), F32),
            pltpu.VMEM((lines, LANE), jnp.int32),
            pltpu.VMEM((row_groups, PAIR), jnp.int32),
            pltpu.VMEM((1, row_groups), jnp.int32),
            pltpu.SemaphoreType.DMA((4 + lines + chunks * (NEAR - 1),)),
        ],
        compiler_params=pltpu.CompilerParams(vmem_limit_bytes=58 << 20),
    )(design, left, bits, picks.reshape(row_groups, PAIR), counts.reshape(1, row_groups))

    def swap(array, mask):
        return lax.ppermute(array, "row", [(i, i ^ mask) for i in range(row_groups)])

    def mix(message):
        made = shape(row_groups, slots, rows, dtype=jnp.bfloat16)
        return call(functools.partial(mix_body, width), made, message, jnp.asarray(walsh(HB), jnp.bfloat16))

    def sample(chunk, mixed, order):
        return call(
            functools.partial(sample_body, scale, chunk * piece),
            (shape(far // 2, NEAR, slots, piece),) * 2,
            design,
            picked,
            mixed,
            order,
            *near[chunk],
            scratch=[pltpu.VMEM((NEAR, 2, rows, piece), jnp.bfloat16)],
        )

    def spread(chunk, masks, order):
        parts = [away[chunk * (NEAR - 1) + mask - 1] for mask in masks]
        parts, _ = lax.optimization_barrier((parts, order))
        return [swap(part, mask) for mask, part in zip(masks, parts)]

    def halve(keep, come, order):
        bit = row_groups // 2
        while bit > NEAR:
            bit //= 2
            half = keep.shape[0] // 2
            keep, send = call(halve_body, (shape(half, *keep.shape[1:]),) * 2, keep, come, order)
            come = swap(send, bit)
        return keep, come

    def join(keep, come, order):
        keep, come = halve(keep, come, order)
        return call(join_body, (shape(*keep.shape[1:]), scalar), keep, come, order)

    def trade(joined, keep, come, order):
        mine, *others = call(
            functools.partial(split_body, chunks),
            (shape(slots, width // NEAR),) * NEAR,
            *joined,
            *halve(keep, come, order),
            order,
        )
        return [mine] + [swap(part, mask + 1) for mask, part in enumerate(others)]

    def back(rinv, message, first):
        outs, scratch = (shape(whole // LANE, LANE), scalar), [pltpu.VMEM((width // LANE, LANE), F32)]
        if first:
            outs += (shape(*rinv.shape),)
            scratch += [pltpu.SemaphoreType.DMA((width // LANE,))]
        return pl.pallas_call(
            functools.partial(back_body, first),
            out_shape=outs,
            in_specs=[HBM if first else VMEM, VMEM],
            out_specs=(VMEM,) * len(outs),
            scratch_shapes=scratch,
            compiler_params=pltpu.CompilerParams(vmem_limit_bytes=(34 if first else 24) << 20),
            )(rinv, message)

    def forward(terms, last, *before):
        return call(
            functools.partial(forward_body, len(terms), not before, last),
            (shape(lines, LANE), shape(width // LANE, LANE), scalar)
            + (() if last else (shape(whole // LANE, LANE),)),
            here,
            design,
            *terms,
            *before,
        )

    def turn(images, left, beta, alpha, token, last):
        return call(
            functools.partial(turn_body, len(images), last),
            (shape(lines, LANE), shape(row_groups, 8 if last else deep, LANE)),
            *images,
            left,
            beta,
            alpha,
            token,
            *(() if last else (design,)),
        )

    betas, alphas, held, joined = [], [], [], []
    message = picked = exchange(message, "row")
    near = [spread(0, (1, 2, 3), message)]
    right = []
    for step in range(ITERS):
        last = step + 1 == ITERS
        if step == 0:
            term, beta, here = back(rinv, message, True)
            mixed = mix(message)
        else:
            term, beta = back(here, message, False)
        betas.append(beta)
        spare = chunks > 1 and step > 0
        terms = direct(term, "col") if spare else paired(term, "col")
        if step == 0:
            near += [spread(chunk, (1, 2), terms[1]) for chunk in range(1, chunks)]
            keep, send = sample(0, mixed, terms[1])
            come = swap(send, row_groups // 2)
        image, kept, alpha, *right = forward(terms, last, *right, *betas[1:])
        alphas.append(alpha)
        held.append(kept)
        if spare:
            keep, send = sample(1, mixed, alpha)
            come = swap(send, row_groups // 2)
        images = direct(image, "col") if spare else paired(image, "col")
        token = alpha
        if chunks > 1 and step == 0:
            part, token = join(keep, come, alpha)
            joined.append(part)
            there = [array for arrays in near[1:] for array in arrays]
            token = pl.pallas_call(
                touch_body,
                out_shape=scalar,
                in_specs=[ANY] * len(there) + [VMEM],
                out_specs=VMEM,
                compiler_params=pltpu.CompilerParams(vmem_limit_bytes=2 << 20),
            )(*there, token)
        left, message = turn(images, left, beta, alpha, token, last)
        message = exchange(message, "row")
        if step == 0:
            for chunk in range(1, chunks):
                near[chunk] += spread(chunk, (3,), message)
    basis, answer = call(
        last_body,
        (shape(lines, LANE), shape(width // LANE, LANE)),
        message,
        left,
        *betas,
        *alphas,
        *held,
    )
    sketch = call(assemble_body, shape(slots, width), *trade(joined, keep, come, message))
    return (sketch, answer.reshape(-1), basis.reshape(-1))


def solution(mesh):
    placed = (
        P("row", "col"),
        P("row"),
        P(None, "row", None),
        P(None, "row"),
        P("row"),
        P("col", None),
    )
    return jax.shard_map(
        shards,
        mesh=mesh,
        in_specs=placed,
        out_specs=(P("row", "col"), P("col"), P("row")),
        check_vma=False,
    )
```

```python
import functools

import jax
import jax.numpy as jnp
import numpy as np
from jax import lax
from jax.experimental import pallas as pl
from jax.experimental.pallas import tpu as pltpu
from jax.sharding import PartitionSpec as P

HB = 256
PAIR = 16
ITERS = 2
LANE = 128
NEAR = 4
CHUNKS = 2
F32 = jnp.float32
VMEM = pl.BlockSpec(memory_space=pltpu.VMEM)
HBM = pl.BlockSpec(memory_space=pltpu.HBM)


def exchange(copies, axis):
    return lax.all_to_all(copies, axis, split_axis=0, concat_axis=0, tiled=True)


def paired(array, axis):
    size = lax.axis_size(axis)
    mask = 1
    while True:
        come = lax.ppermute(array, axis, [(i, i ^ mask) for i in range(size)])
        mask *= 2
        if mask == size:
            return [array, come]
        array = array + come


def direct(array, axis):
    size = lax.axis_size(axis)
    return [array] + [
        lax.ppermute(array, axis, [(i, i ^ mask) for i in range(size)]) for mask in range(1, size)
    ]


def tree(values):
    while len(values) > 1:
        values = [values[i] + values[i + 1] for i in range(0, len(values), 2)]
    return values[0]


def walsh(size):
    index = np.arange(size)
    common = index[:, None] & index[None, :]
    parity = np.zeros((size, size), np.int64)
    for shift in range(size.bit_length()):
        parity ^= (common >> shift) & 1
    return (1 - 2 * parity).astype(np.float32)


def call(body, out_shape, *operands, scratch=()):
    return pl.pallas_call(
        body,
        out_shape=out_shape,
        in_specs=[VMEM] * len(operands),
        out_specs=jax.tree.map(lambda _: VMEM, out_shape),
        scratch_shapes=scratch,
        compiler_params=pltpu.CompilerParams(vmem_limit_bytes=24 << 20),
    )(*operands)


def fold_rows(block):
    return block.reshape(block.shape[0] // 8, 8, LANE).sum(axis=0)


def total(rows):
    return jnp.sum(jnp.sum(rows, axis=0, keepdims=True), axis=1, keepdims=True)


def splat(scalar):
    return jnp.broadcast_to(scalar, (1, LANE))


def left_product(vector, matrix_ref, out_ref):
    blocks, tiles = matrix_ref.shape[0] // LANE, matrix_ref.shape[1] // LANE
    sums = [jnp.zeros((8, LANE), F32) for _ in range(tiles)]
    for block in range(blocks):
        weight = across(vector[block : block + 1, :])
        for tile in range(tiles):
            part = matrix_ref[block * LANE : (block + 1) * LANE, tile * LANE : (tile + 1) * LANE]
            sums[tile] = sums[tile] + fold_rows(part * weight)
    for tile in range(tiles):
        out_ref[tile : tile + 1, :] = jnp.sum(sums[tile], axis=0, keepdims=True)


def left_product_long(vector_ref, matrix_ref, out_ref, copies=()):
    blocks, tiles = matrix_ref.shape[0] // LANE, matrix_ref.shape[1] // LANE

    def step(block, sums):
        weight = across(vector_ref[pl.ds(block, 1), :])
        rows = pl.ds(pl.multiple_of(block * LANE, LANE), LANE)
        return tuple(
            sums[tile] + fold_rows(matrix_ref[rows, tile * LANE : (tile + 1) * LANE] * weight)
            for tile in range(tiles)
        )

    sums = tuple(jnp.zeros((8, LANE), F32) for _ in range(tiles))
    if copies:
        for block, copy in enumerate(copies):
            copy.wait()
            sums = step(block, sums)
    else:
        sums = lax.fori_loop(0, blocks, step, sums)
    for tile in range(tiles):
        out_ref[tile : tile + 1, :] = jnp.sum(sums[tile], axis=0, keepdims=True)


def right_product(matrix_ref, vector, out_ref):
    blocks, tiles = matrix_ref.shape[0] // LANE, matrix_ref.shape[1] // LANE

    def step(block, carry):
        rows = pl.ds(pl.multiple_of(block * LANE, LANE), LANE)
        sums = jnp.zeros((LANE, LANE), F32)
        for tile in range(tiles):
            sums = sums + matrix_ref[rows, tile * LANE : (tile + 1) * LANE] * vector[tile : tile + 1, :]
        out_ref[pl.ds(block, 1), :] = jnp.sum(fold_rows(sums.T), axis=0, keepdims=True)
        return carry

    lax.fori_loop(0, blocks, step, 0)


def rounded(count, unit):
    return -(-count // unit) * unit


def message_rows(width):
    return rounded(width // LANE + 1, 8)


def picks_at(width):
    return width // LANE + 1


def signs_at(width, groups):
    return picks_at(width) + groups * PAIR // LANE


def copy_out(out_ref):
    first = out_ref[0]
    for index in range(1, out_ref.shape[0]):
        out_ref[index] = first


def across(row):
    return jnp.broadcast_to(row, (LANE, LANE)).T


def first_body(sent, design_ref, target_ref, bits_ref, picks_ref, counts_ref, *refs):
    out_ref, away_refs = refs[0], refs[1:-6]
    design, target_here, bits, picks, counts, sems = refs[-6:]
    rows, width = design.shape
    lines, tiles = rows // LANE, width // LANE
    small = [
        pltpu.make_async_copy(source, place, sems.at[index])
        for index, (source, place) in enumerate(
            ((target_ref, target_here), (bits_ref, bits), (picks_ref, picks), (counts_ref, counts))
        )
    ]
    parts = [slice(line * LANE, (line + 1) * LANE) for line in range(lines)]
    large = [
        pltpu.make_async_copy(design_ref.at[part, :], design.at[part, :], sems.at[4 + line])
        for line, part in enumerate(parts)
    ]
    place = lax.axis_index("row") % NEAR
    away = []
    for index, away_ref in enumerate(away_refs):
        piece = away_ref.shape[1]
        mask, start = sent[index]
        column = pl.multiple_of((place ^ mask) * (width // NEAR) + start, LANE)
        source = design.at[:, pl.ds(column, piece)]
        away.append(pltpu.make_async_copy(source, away_ref, sems.at[4 + lines + index]))
    for copy in small + large:
        copy.start()
    for copy in small:
        copy.wait()
    out_ref[0] = jnp.zeros(out_ref.shape[1:], F32)
    groups = picks.shape[0]
    owner = lax.broadcasted_iota(jnp.int32, (groups, groups), 0)
    same = owner == lax.broadcasted_iota(jnp.int32, (groups, groups), 1)
    limit = jnp.sum(jnp.where(same, counts[...].astype(F32), 0.0), axis=1, keepdims=True)
    slot = lax.broadcasted_iota(jnp.int32, picks.shape, 1).astype(F32)
    coded = jnp.where(slot < limit, picks[...].astype(F32), -1.0)
    start = picks_at(width)
    for owner in range(0, groups, LANE // PAIR):
        line = jnp.concatenate([coded[i : i + 1, :] for i in range(owner, owner + LANE // PAIR)], axis=1)
        out_ref[0, start + owner * PAIR // LANE : start + owner * PAIR // LANE + 1, :] = line
    start = signs_at(width, groups)
    out_ref[0, start : start + lines, :] = (2 * bits[...] - 1).astype(F32)
    target = target_here[...]
    out_ref[0, tiles : tiles + 1, :] = splat(total(target * target))
    sums = [jnp.zeros((8, LANE), F32) for _ in range(tiles)]
    for line, part in enumerate(parts):
        weight = across(target[line : line + 1, :])
        large[line].wait()
        if line == lines - 1:
            for copy in away:
                copy.start()
        for tile in range(tiles):
            sums[tile] = sums[tile] + fold_rows(design[part, tile * LANE : (tile + 1) * LANE] * weight)
    for tile in range(tiles):
        out_ref[0, tile : tile + 1, :] = jnp.sum(sums[tile], axis=0, keepdims=True)
    copy_out(out_ref)
    for copy in away:
        copy.wait()


def back_body(first, rinv_ref, parts_ref, term_ref, beta_ref, *refs):
    tiles = rinv_ref.shape[0] // LANE
    copies = []
    if first:
        rinv_here, scratch, sems = refs
        for block in range(tiles):
            part = slice(block * LANE, (block + 1) * LANE)
            copies.append(pltpu.make_async_copy(rinv_ref.at[part, :], rinv_here.at[part, :], sems.at[block]))
            copies[-1].start()
    else:
        rinv_here, (scratch,) = rinv_ref, refs
    summed = tree([parts_ref[i, : tiles + 1, :] for i in range(parts_ref.shape[0])])
    beta = jnp.sqrt(summed[tiles : tiles + 1, :])
    beta_ref[...] = beta
    scratch[...] = summed[:tiles, :] / beta
    left_product_long(scratch, rinv_here, term_ref, copies)


def forward_body(groups, first, last, rinv_ref, design_ref, token_ref, *refs):
    right = tree([ref[...] for ref in refs[:groups]])
    refs = refs[groups:]
    if not first:
        before_ref, beta_ref, *refs = refs
        right = right - beta_ref[...] * before_ref[...]
    image_ref, held_ref, alpha_ref, *right_refs = refs
    alpha = jnp.sqrt(total(right * right))
    alpha_ref[...] = splat(alpha)
    right = right / alpha
    if not last:
        right_refs[0][...] = right
    right_product(rinv_ref, right, held_ref)
    right_product(design_ref, held_ref[...], image_ref)


def turn_body(groups, last, *refs):
    left = tree([ref[...] for ref in refs[:groups]])
    before_ref, beta_ref, alpha_ref, *refs = refs[groups:]
    left = left - alpha_ref[...] * (before_ref[...] / beta_ref[...])
    square = splat(total(left * left))
    if last:
        left_ref, out_ref = refs
        out_ref[...] = jnp.broadcast_to(square, out_ref.shape)
    else:
        design_ref, left_ref, out_ref = refs
        tiles = design_ref.shape[1] // LANE
        out_ref[0] = jnp.zeros(out_ref.shape[1:], F32)
        left_product(left, design_ref, out_ref.at[0])
        out_ref[0, tiles : tiles + 1, :] = square
        copy_out(out_ref)
    left_ref[...] = left


def pieces(value):
    high = value.astype(jnp.bfloat16)
    return high, (value - high.astype(F32)).astype(jnp.bfloat16)


def weigh(mix, high, low):
    return jnp.dot(mix, high, preferred_element_type=F32) + jnp.dot(mix, low, preferred_element_type=F32)


def for_blocks(groups, step):
    if groups <= 8:
        for block in range(groups):
            step(block, 0)
    else:
        lax.fori_loop(0, groups, step, 0)


def mix_body(width, parts_ref, walsh_ref, mix_ref):
    groups, _, rows = mix_ref.shape
    me = lax.axis_index("row")
    local = lax.broadcasted_iota(jnp.int32, (LANE, rows), 1).astype(F32)
    per = LANE // PAIR

    def step(block, carry):
        parity = jnp.int32(0)
        for bit in range(groups.bit_length() - 1):
            parity = parity ^ ((block & me) >> bit)
        sign = (1 - 2 * (parity & 1)).astype(F32)
        for line in range(groups // per):
            start = picks_at(width) + line
            coded = across(parts_ref[block, start : start + 1, :])
            match = jnp.concatenate([coded] * (rows // LANE), axis=1) == local
            chosen = jnp.where(match, sign, 0.0).astype(jnp.bfloat16)
            for part in range(rows // HB):
                columns = slice(part * HB, (part + 1) * HB)
                mixed = jnp.dot(chosen[:, columns], walsh_ref[...], preferred_element_type=F32).astype(jnp.bfloat16)
                for index in range(per):
                    place = pl.multiple_of(((line * per + index) ^ me) * PAIR, PAIR)
                    mix_ref[block, pl.ds(place, PAIR), columns] = mixed[index * PAIR : (index + 1) * PAIR, :]
        return carry

    for_blocks(groups, step)


def sample_body(scale, start, design_ref, parts_ref, mix_ref, order_ref, *refs):
    near, (keep_ref, send_ref, token_ref, both) = refs[: NEAR - 1], refs[NEAR - 1 :]
    token_ref[...] = order_ref[:1, :]
    rows, piece = near[-1].shape
    width = design_ref.shape[1]
    groups = mix_ref.shape[0]
    me = lax.axis_index("row")
    signs_start = signs_at(width, groups)
    for line in range(rows // LANE):
        part = slice(line * LANE, (line + 1) * LANE)
        signs = [across(parts_ref[me ^ mask, signs_start + line : signs_start + line + 1, :]) for mask in range(NEAR)]
        for tile in range(0, piece, LANE):
            column = pl.multiple_of(me % NEAR * (width // NEAR) + start + tile, LANE)
            here = slice(tile, tile + LANE)
            there = slice(start + tile, start + tile + LANE)
            values = [design_ref[part, pl.ds(column, LANE)], near[0][part, there]]
            values += [ref[part, here] for ref in near[1:]]
            values = [value * sign for value, sign in zip(values, signs)]
            apart = 1
            while apart < NEAR:
                for first in range(NEAR):
                    if not first & apart:
                        one, two = values[first], values[first | apart]
                        values[first], values[first | apart] = one + two, one - two
                apart *= 2
            for index, value in enumerate(values):
                both[index, 0, part, here], both[index, 1, part, here] = pieces(value)

    def step(block, carry):
        value = weigh(mix_ref[block], both[block % NEAR, 0], both[block % NEAR, 1]) / scale
        slot = pl.ds(block * PAIR, PAIR)
        for apart in range(groups):
            far, low = apart // NEAR, apart % NEAR
            out_ref = send_ref if far >= groups // NEAR // 2 else keep_ref
            out_ref[far % (groups // NEAR // 2), low, slot, :] = value[apart * PAIR : (apart + 1) * PAIR, :]
        return carry

    for_blocks(groups, step)


def halve_body(kept_ref, arrived_ref, order_ref, keep_ref, send_ref):
    half = keep_ref.shape[0]
    keep_ref[...] = kept_ref[:half] + arrived_ref[:half]
    send_ref[...] = kept_ref[half:] + arrived_ref[half:]


def join_body(kept_ref, arrived_ref, order_ref, out_ref, token_ref):
    token_ref[...] = order_ref[:1, :]
    out_ref[...] = kept_ref[0] + arrived_ref[0]


def split_body(chunks, *refs):
    joined, (kept_ref, arrived_ref, order_ref, token_ref, *out_refs) = refs[: chunks - 1], refs[chunks - 1 :]
    token_ref[...] = order_ref[:1, :]
    piece = kept_ref.shape[3]
    for chunk in range(chunks):
        columns = slice(chunk * piece, (chunk + 1) * piece)
        for index, out_ref in enumerate(out_refs):
            if chunk < chunks - 1:
                out_ref[:, columns] = joined[chunk][index]
            else:
                out_ref[:, columns] = kept_ref[0, index] + arrived_ref[0, index]


def assemble_body(*refs):
    quarters, sketch_ref = refs[:-1], refs[-1]
    place = lax.axis_index("row") % NEAR
    piece = quarters[0].shape[1]
    for mask, part_ref in enumerate(quarters):
        for tile in range(0, piece, LANE):
            column = pl.multiple_of((place ^ mask) * piece + tile, LANE)
            sketch_ref[:, pl.ds(column, LANE)] = part_ref[:, tile : tile + LANE]


def last_body(parts_ref, left_ref, *refs):
    basis_ref, solution_ref = refs[-2:]
    betas = [ref[...] for ref in refs[:ITERS]]
    alphas = [ref[...] for ref in refs[ITERS : 2 * ITERS]]
    held = [ref[...] for ref in refs[2 * ITERS : 3 * ITERS]]
    last = jnp.sqrt(tree([parts_ref[i] for i in range(parts_ref.shape[0])])[:1, :])
    basis_ref[...] = left_ref[...] / last
    betas.append(last)
    phibar, rhobar = betas[0], alphas[0]
    search, iterate = held[0], jnp.zeros_like(held[0])
    for step in range(ITERS):
        beta = betas[step + 1]
        rho = jnp.sqrt(rhobar * rhobar + beta * beta)
        cosine = rhobar / rho
        sine = beta / rho
        phi = cosine * phibar
        phibar = sine * phibar
        iterate = iterate + phi / rho * search
        if step + 1 < ITERS:
            alpha = alphas[step + 1]
            search = held[step + 1] - sine * alpha / rho * search
            rhobar = -cosine * alpha
    solution_ref[...] = iterate


def shape(*dims, dtype=F32):
    return jax.ShapeDtypeStruct(dims, dtype)


def shards(design, sign_bits, picks, counts, target, rinv):
    rows, width = design.shape
    whole = rinv.shape[1]
    row_groups = lax.axis_size("row")
    lines = rows // LANE
    scalar = shape(1, LANE)
    deep = message_rows(width)
    left = target.reshape(lines, LANE)
    bits = sign_bits.reshape(lines, LANE)
    chunks = min(CHUNKS, width // NEAR // LANE)
    piece = width // NEAR // chunks
    scale = float(np.sqrt(np.float32(rows * row_groups)))
    slots = row_groups * PAIR
    far = row_groups // NEAR

    sent = [(1, 0)] + [(mask, chunk * piece) for mask in range(2, NEAR) for chunk in range(chunks)]
    sizes = [piece * chunks] + [piece] * (chunks * (NEAR - 2))

    message, *away = pl.pallas_call(
        functools.partial(first_body, sent),
        out_shape=(shape(row_groups, rounded(signs_at(width, row_groups) + lines, 8), LANE),)
        + tuple(shape(rows, size) for size in sizes),
        in_specs=[HBM] * 5,
        out_specs=(VMEM,) + (HBM,) * len(sent),
        scratch_shapes=[
            pltpu.VMEM((rows, width), F32),
            pltpu.VMEM((lines, LANE), F32),
            pltpu.VMEM((lines, LANE), jnp.int32),
            pltpu.VMEM((row_groups, PAIR), jnp.int32),
            pltpu.VMEM((1, row_groups), jnp.int32),
            pltpu.SemaphoreType.DMA((4 + lines + len(sent),)),
        ],
        compiler_params=pltpu.CompilerParams(vmem_limit_bytes=58 << 20),
    )(design, left, bits, picks.reshape(row_groups, PAIR), counts.reshape(1, row_groups))

    def swap(array, mask):
        return lax.ppermute(array, "row", [(i, i ^ mask) for i in range(row_groups)])

    def mix(message):
        made = shape(row_groups, slots, rows, dtype=jnp.bfloat16)
        return call(functools.partial(mix_body, width), made, message, jnp.asarray(walsh(HB), jnp.bfloat16))

    def sample(chunk, mixed, order):
        return call(
            functools.partial(sample_body, scale, chunk * piece),
            (shape(far // 2, NEAR, slots, piece),) * 2 + (scalar,),
            design,
            picked,
            mixed,
            order,
            *(near[index] for index, (mask, start) in enumerate(sent) if mask == 1 or start == chunk * piece),
            scratch=[pltpu.VMEM((NEAR, 2, rows, piece), jnp.bfloat16)],
        )

    def spread(indices, order):
        parts, _ = lax.optimization_barrier(([away[index] for index in indices], order))
        return [swap(part, sent[index][0]) for index, part in zip(indices, parts)]

    def halve(keep, come, order):
        bit = row_groups // 2
        while bit > NEAR:
            bit //= 2
            half = keep.shape[0] // 2
            keep, send = call(halve_body, (shape(half, *keep.shape[1:]),) * 2, keep, come, order)
            come = swap(send, bit)
        return keep, come

    def join(keep, come, order):
        keep, come = halve(keep, come, order)
        return call(join_body, (shape(*keep.shape[1:]), scalar), keep, come, order)

    def trade(joined, keep, come, order):
        token, mine, *others = call(
            functools.partial(split_body, chunks),
            (scalar,) + (shape(slots, width // NEAR),) * NEAR,
            *joined,
            *halve(keep, come, order),
            order,
        )
        return [mine] + [swap(part, mask + 1) for mask, part in enumerate(others)], token

    def back(rinv, message, first):
        outs, scratch = (shape(whole // LANE, LANE), scalar), [pltpu.VMEM((width // LANE, LANE), F32)]
        if first:
            outs += (shape(*rinv.shape),)
            scratch += [pltpu.SemaphoreType.DMA((width // LANE,))]
        return pl.pallas_call(
            functools.partial(back_body, first),
            out_shape=outs,
            in_specs=[HBM if first else VMEM, VMEM],
            out_specs=(VMEM,) * len(outs),
            scratch_shapes=scratch,
            compiler_params=pltpu.CompilerParams(vmem_limit_bytes=(34 if first else 24) << 20),
            )(rinv, message)

    def forward(terms, token, last, *before):
        return call(
            functools.partial(forward_body, len(terms), not before, last),
            (shape(lines, LANE), shape(width // LANE, LANE), scalar)
            + (() if last else (shape(whole // LANE, LANE),)),
            here,
            design,
            token,
            *terms,
            *before,
        )

    def turn(images, left, beta, alpha, last):
        return call(
            functools.partial(turn_body, len(images), last),
            (shape(lines, LANE), shape(row_groups, 8 if last else deep, LANE)),
            *images,
            left,
            beta,
            alpha,
            *(() if last else (design,)),
        )

    betas, alphas, held, joined, right = [], [], [], [], []
    message = picked = exchange(message, "row")
    late = len(sent) - 1 if chunks > 1 else len(sent)
    near = spread(range(late), message)
    for step in range(ITERS):
        last = step + 1 == ITERS
        if step == 0:
            term, beta, here = back(rinv, message, True)
            mixed = mix(message)
        else:
            term, beta = back(here, message, False)
            token = beta
            if chunks > 1:
                part, token = join(keep, come, beta)
                joined.append(part)
                keep, send, token = sample(1, mixed, token)
                come = swap(send, row_groups // 2)
        betas.append(beta)
        spare = chunks > 1 and step > 0
        terms = direct(term, "col") if spare else paired(term, "col")
        if step == 0:
            near += spread(range(late, len(sent)), terms[1])
            keep, send, token = sample(0, mixed, terms[1])
            come = swap(send, row_groups // 2)
        image, kept, alpha, *right = forward(terms, token, last, *right, *betas[1:])
        alphas.append(alpha)
        held.append(kept)
        images = direct(image, "col") if spare else paired(image, "col")
        left, message = turn(images, left, beta, alpha, last)
        if last:
            quarters, token = trade(joined, keep, come, left)
            message, _ = lax.optimization_barrier((message, token))
        message = exchange(message, "row")
    basis, answer = call(
        last_body,
        (shape(lines, LANE), shape(width // LANE, LANE)),
        message,
        left,
        *betas,
        *alphas,
        *held,
    )
    sketch = call(assemble_body, shape(slots, width), *quarters)
    return (sketch, answer.reshape(-1), basis.reshape(-1))


def solution(mesh):
    placed = (
        P("row", "col"),
        P("row"),
        P(None, "row", None),
        P(None, "row"),
        P("row"),
        P("col", None),
    )
    return jax.shard_map(
        shards,
        mesh=mesh,
        in_specs=placed,
        out_specs=(P("row", "col"), P("col"), P("row")),
        check_vma=False,
    )
```

```python
import functools

import jax
import jax.numpy as jnp
import numpy as np
from jax import lax
from jax.experimental import pallas as pl
from jax.experimental.pallas import tpu as pltpu
from jax.sharding import PartitionSpec as P

HB = 256
PAIR = 16
ITERS = 2
LANE = 128
NEAR = 4
CHUNKS = 2
F32 = jnp.float32
VMEM = pl.BlockSpec(memory_space=pltpu.VMEM)
HBM = pl.BlockSpec(memory_space=pltpu.HBM)


def exchange(copies, axis):
    return lax.all_to_all(copies, axis, split_axis=0, concat_axis=0, tiled=True)


def paired(array, axis):
    size = lax.axis_size(axis)
    mask = 1
    while True:
        come = lax.ppermute(array, axis, [(i, i ^ mask) for i in range(size)])
        mask *= 2
        if mask == size:
            return [array, come]
        array = array + come


def direct(array, axis):
    size = lax.axis_size(axis)
    return [array] + [
        lax.ppermute(array, axis, [(i, i ^ mask) for i in range(size)]) for mask in range(1, size)
    ]


def tree(values):
    while len(values) > 1:
        values = [values[i] + values[i + 1] for i in range(0, len(values), 2)]
    return values[0]


def walsh(size):
    index = np.arange(size)
    common = index[:, None] & index[None, :]
    parity = np.zeros((size, size), np.int64)
    for shift in range(size.bit_length()):
        parity ^= (common >> shift) & 1
    return (1 - 2 * parity).astype(np.float32)


def call(body, out_shape, *operands, scratch=()):
    return pl.pallas_call(
        body,
        out_shape=out_shape,
        in_specs=[VMEM] * len(operands),
        out_specs=jax.tree.map(lambda _: VMEM, out_shape),
        scratch_shapes=scratch,
        compiler_params=pltpu.CompilerParams(vmem_limit_bytes=24 << 20),
    )(*operands)


def fold_rows(block):
    return block.reshape(block.shape[0] // 8, 8, LANE).sum(axis=0)


def total(rows):
    return jnp.sum(jnp.sum(rows, axis=0, keepdims=True), axis=1, keepdims=True)


def splat(scalar):
    return jnp.broadcast_to(scalar, (1, LANE))


def left_product(vector, matrix_ref, out_ref):
    blocks, tiles = matrix_ref.shape[0] // LANE, matrix_ref.shape[1] // LANE
    sums = [jnp.zeros((8, LANE), F32) for _ in range(tiles)]
    for block in range(blocks):
        weight = across(vector[block : block + 1, :])
        for tile in range(tiles):
            part = matrix_ref[block * LANE : (block + 1) * LANE, tile * LANE : (tile + 1) * LANE]
            sums[tile] = sums[tile] + fold_rows(part * weight)
    for tile in range(tiles):
        out_ref[tile : tile + 1, :] = jnp.sum(sums[tile], axis=0, keepdims=True)


def left_product_long(vector_ref, matrix_ref, out_ref, copies=()):
    blocks, tiles = matrix_ref.shape[0] // LANE, matrix_ref.shape[1] // LANE

    def step(block, sums):
        weight = across(vector_ref[pl.ds(block, 1), :])
        rows = pl.ds(pl.multiple_of(block * LANE, LANE), LANE)
        return tuple(
            sums[tile] + fold_rows(matrix_ref[rows, tile * LANE : (tile + 1) * LANE] * weight)
            for tile in range(tiles)
        )

    sums = tuple(jnp.zeros((8, LANE), F32) for _ in range(tiles))
    if copies:
        for block, copy in enumerate(copies):
            copy.wait()
            sums = step(block, sums)
    else:
        sums = lax.fori_loop(0, blocks, step, sums)
    for tile in range(tiles):
        out_ref[tile : tile + 1, :] = jnp.sum(sums[tile], axis=0, keepdims=True)


def right_product(matrix_ref, vector, out_ref):
    blocks, tiles = matrix_ref.shape[0] // LANE, matrix_ref.shape[1] // LANE

    def step(block, carry):
        rows = pl.ds(pl.multiple_of(block * LANE, LANE), LANE)
        sums = jnp.zeros((LANE, LANE), F32)
        for tile in range(tiles):
            sums = sums + matrix_ref[rows, tile * LANE : (tile + 1) * LANE] * vector[tile : tile + 1, :]
        out_ref[pl.ds(block, 1), :] = jnp.sum(fold_rows(sums.T), axis=0, keepdims=True)
        return carry

    lax.fori_loop(0, blocks, step, 0)


def rounded(count, unit):
    return -(-count // unit) * unit


def message_rows(width):
    return rounded(width // LANE + 1, 8)


def picks_at(width):
    return width // LANE + 1


def signs_at(width, groups):
    return picks_at(width) + groups * PAIR // LANE


def copy_out(out_ref):
    first = out_ref[0]
    for index in range(1, out_ref.shape[0]):
        out_ref[index] = first


def across(row):
    return jnp.broadcast_to(row, (LANE, LANE)).T


def first_body(sent, design_ref, target_ref, bits_ref, picks_ref, counts_ref, *refs):
    out_ref, away_refs = refs[0], refs[1:-6]
    design, target_here, bits, picks, counts, sems = refs[-6:]
    rows, width = design.shape
    lines, tiles = rows // LANE, width // LANE
    small = [
        pltpu.make_async_copy(source, place, sems.at[index])
        for index, (source, place) in enumerate(
            ((target_ref, target_here), (bits_ref, bits), (picks_ref, picks), (counts_ref, counts))
        )
    ]
    parts = [slice(line * LANE, (line + 1) * LANE) for line in range(lines)]
    large = [
        pltpu.make_async_copy(design_ref.at[part, :], design.at[part, :], sems.at[4 + line])
        for line, part in enumerate(parts)
    ]
    place = lax.axis_index("row") % NEAR
    away = []
    for index, away_ref in enumerate(away_refs):
        piece = away_ref.shape[1]
        mask, start = sent[index]
        column = pl.multiple_of((place ^ mask) * (width // NEAR) + start, LANE)
        source = design.at[:, pl.ds(column, piece)]
        away.append(pltpu.make_async_copy(source, away_ref, sems.at[4 + lines + index]))
    for copy in small + large:
        copy.start()
    for copy in small:
        copy.wait()
    out_ref[0] = jnp.zeros(out_ref.shape[1:], F32)
    groups = picks.shape[0]
    owner = lax.broadcasted_iota(jnp.int32, (groups, groups), 0)
    same = owner == lax.broadcasted_iota(jnp.int32, (groups, groups), 1)
    limit = jnp.sum(jnp.where(same, counts[...].astype(F32), 0.0), axis=1, keepdims=True)
    slot = lax.broadcasted_iota(jnp.int32, picks.shape, 1).astype(F32)
    coded = jnp.where(slot < limit, picks[...].astype(F32), -1.0)
    start = picks_at(width)
    for owner in range(0, groups, LANE // PAIR):
        line = jnp.concatenate([coded[i : i + 1, :] for i in range(owner, owner + LANE // PAIR)], axis=1)
        out_ref[0, start + owner * PAIR // LANE : start + owner * PAIR // LANE + 1, :] = line
    start = signs_at(width, groups)
    out_ref[0, start : start + lines, :] = (2 * bits[...] - 1).astype(F32)
    target = target_here[...]
    out_ref[0, tiles : tiles + 1, :] = splat(total(target * target))
    sums = [jnp.zeros((8, LANE), F32) for _ in range(tiles)]
    for line, part in enumerate(parts):
        weight = across(target[line : line + 1, :])
        large[line].wait()
        if line == lines - 1:
            for copy in away:
                copy.start()
        for tile in range(tiles):
            sums[tile] = sums[tile] + fold_rows(design[part, tile * LANE : (tile + 1) * LANE] * weight)
    for tile in range(tiles):
        out_ref[0, tile : tile + 1, :] = jnp.sum(sums[tile], axis=0, keepdims=True)
    copy_out(out_ref)
    for copy in away:
        copy.wait()


def back_body(first, rinv_ref, parts_ref, term_ref, beta_ref, *refs):
    tiles = rinv_ref.shape[0] // LANE
    copies = []
    if first:
        rinv_here, scratch, sems = refs
        for block in range(tiles):
            part = slice(block * LANE, (block + 1) * LANE)
            copies.append(pltpu.make_async_copy(rinv_ref.at[part, :], rinv_here.at[part, :], sems.at[block]))
            copies[-1].start()
    else:
        rinv_here, (scratch,) = rinv_ref, refs
    summed = tree([parts_ref[i, : tiles + 1, :] for i in range(parts_ref.shape[0])])
    beta = jnp.sqrt(summed[tiles : tiles + 1, :])
    beta_ref[...] = beta
    scratch[...] = summed[:tiles, :] / beta
    left_product_long(scratch, rinv_here, term_ref, copies)


def forward_body(groups, first, last, rinv_ref, design_ref, token_ref, *refs):
    right = tree([ref[...] for ref in refs[:groups]])
    refs = refs[groups:]
    if not first:
        before_ref, beta_ref, *refs = refs
        right = right - beta_ref[...] * before_ref[...]
    image_ref, held_ref, alpha_ref, *right_refs = refs
    alpha = jnp.sqrt(total(right * right))
    alpha_ref[...] = splat(alpha)
    right = right / alpha
    if not last:
        right_refs[0][...] = right
    right_product(rinv_ref, right, held_ref)
    right_product(design_ref, held_ref[...], image_ref)


def turn_body(groups, last, *refs):
    left = tree([ref[...] for ref in refs[:groups]])
    before_ref, beta_ref, alpha_ref, *refs = refs[groups:]
    left = left - alpha_ref[...] * (before_ref[...] / beta_ref[...])
    square = splat(total(left * left))
    if last:
        *parts, left_ref, out_ref = refs[: -NEAR]
        out_refs = refs[-NEAR:]
        out_ref[...] = jnp.broadcast_to(square, out_ref.shape)
        *joined, kept_ref, arrived_ref = parts
        piece = kept_ref.shape[3]
        for index, rows_ref in enumerate(out_refs):
            for chunk, part_ref in enumerate(joined):
                rows_ref[:, chunk * piece : (chunk + 1) * piece] = part_ref[index]
            rows_ref[:, len(joined) * piece :] = kept_ref[0, index] + arrived_ref[0, index]
    else:
        design_ref, left_ref, out_ref = refs
        tiles = design_ref.shape[1] // LANE
        out_ref[0] = jnp.zeros(out_ref.shape[1:], F32)
        left_product(left, design_ref, out_ref.at[0])
        out_ref[0, tiles : tiles + 1, :] = square
        copy_out(out_ref)
    left_ref[...] = left


def pieces(value):
    high = value.astype(jnp.bfloat16)
    return high, (value - high.astype(F32)).astype(jnp.bfloat16)


def weigh(mix, high, low):
    return jnp.dot(mix, high, preferred_element_type=F32) + jnp.dot(mix, low, preferred_element_type=F32)


def for_blocks(groups, step):
    if groups <= 8:
        for block in range(groups):
            step(block, 0)
    else:
        lax.fori_loop(0, groups, step, 0)


def mix_body(width, parts_ref, walsh_ref, mix_ref):
    groups, _, rows = mix_ref.shape
    me = lax.axis_index("row")
    local = lax.broadcasted_iota(jnp.int32, (LANE, rows), 1).astype(F32)
    per = LANE // PAIR

    def step(block, carry):
        parity = jnp.int32(0)
        for bit in range(groups.bit_length() - 1):
            parity = parity ^ ((block & me) >> bit)
        sign = (1 - 2 * (parity & 1)).astype(F32)
        for line in range(groups // per):
            start = picks_at(width) + line
            coded = across(parts_ref[block, start : start + 1, :])
            match = jnp.concatenate([coded] * (rows // LANE), axis=1) == local
            chosen = jnp.where(match, sign, 0.0).astype(jnp.bfloat16)
            for part in range(rows // HB):
                columns = slice(part * HB, (part + 1) * HB)
                mixed = jnp.dot(chosen[:, columns], walsh_ref[...], preferred_element_type=F32).astype(jnp.bfloat16)
                for index in range(per):
                    place = pl.multiple_of(((line * per + index) ^ me) * PAIR, PAIR)
                    mix_ref[block, pl.ds(place, PAIR), columns] = mixed[index * PAIR : (index + 1) * PAIR, :]
        return carry

    for_blocks(groups, step)


def sample_body(scale, start, design_ref, parts_ref, mix_ref, order_ref, *refs):
    near, (keep_ref, send_ref, token_ref, both) = refs[: NEAR - 1], refs[NEAR - 1 :]
    token_ref[...] = order_ref[:1, :]
    rows, piece = near[-1].shape
    width = design_ref.shape[1]
    groups = mix_ref.shape[0]
    me = lax.axis_index("row")
    signs_start = signs_at(width, groups)
    for line in range(rows // LANE):
        part = slice(line * LANE, (line + 1) * LANE)
        signs = [across(parts_ref[me ^ mask, signs_start + line : signs_start + line + 1, :]) for mask in range(NEAR)]
        for tile in range(0, piece, LANE):
            column = pl.multiple_of(me % NEAR * (width // NEAR) + start + tile, LANE)
            here = slice(tile, tile + LANE)
            there = slice(start + tile, start + tile + LANE)
            values = [design_ref[part, pl.ds(column, LANE)], near[0][part, there]]
            values += [ref[part, here] for ref in near[1:]]
            values = [value * sign for value, sign in zip(values, signs)]
            apart = 1
            while apart < NEAR:
                for first in range(NEAR):
                    if not first & apart:
                        one, two = values[first], values[first | apart]
                        values[first], values[first | apart] = one + two, one - two
                apart *= 2
            for index, value in enumerate(values):
                both[index, 0, part, here], both[index, 1, part, here] = pieces(value)

    def step(block, carry):
        value = weigh(mix_ref[block], both[block % NEAR, 0], both[block % NEAR, 1]) / scale
        slot = pl.ds(block * PAIR, PAIR)
        for apart in range(groups):
            far, low = apart // NEAR, apart % NEAR
            out_ref = send_ref if far >= groups // NEAR // 2 else keep_ref
            out_ref[far % (groups // NEAR // 2), low, slot, :] = value[apart * PAIR : (apart + 1) * PAIR, :]
        return carry

    for_blocks(groups, step)


def halve_body(kept_ref, arrived_ref, order_ref, keep_ref, send_ref):
    half = keep_ref.shape[0]
    keep_ref[...] = kept_ref[:half] + arrived_ref[:half]
    send_ref[...] = kept_ref[half:] + arrived_ref[half:]


def join_body(kept_ref, arrived_ref, order_ref, out_ref, token_ref):
    token_ref[...] = order_ref[:1, :]
    out_ref[...] = kept_ref[0] + arrived_ref[0]


def last_body(parts_ref, left_ref, *refs):
    basis_ref, solution_ref, sketch_ref = refs[-3:]
    quarters = refs[3 * ITERS : 3 * ITERS + NEAR]
    place = lax.axis_index("row") % NEAR
    piece = quarters[0].shape[1]
    for mask, part_ref in enumerate(quarters):
        for tile in range(0, piece, LANE):
            column = pl.multiple_of((place ^ mask) * piece + tile, LANE)
            sketch_ref[:, pl.ds(column, LANE)] = part_ref[:, tile : tile + LANE]
    betas = [ref[...] for ref in refs[:ITERS]]
    alphas = [ref[...] for ref in refs[ITERS : 2 * ITERS]]
    held = [ref[...] for ref in refs[2 * ITERS : 3 * ITERS]]
    last = jnp.sqrt(tree([parts_ref[i] for i in range(parts_ref.shape[0])])[:1, :])
    basis_ref[...] = left_ref[...] / last
    betas.append(last)
    phibar, rhobar = betas[0], alphas[0]
    search, iterate = held[0], jnp.zeros_like(held[0])
    for step in range(ITERS):
        beta = betas[step + 1]
        rho = jnp.sqrt(rhobar * rhobar + beta * beta)
        cosine = rhobar / rho
        sine = beta / rho
        phi = cosine * phibar
        phibar = sine * phibar
        iterate = iterate + phi / rho * search
        if step + 1 < ITERS:
            alpha = alphas[step + 1]
            search = held[step + 1] - sine * alpha / rho * search
            rhobar = -cosine * alpha
    solution_ref[...] = iterate


def shape(*dims, dtype=F32):
    return jax.ShapeDtypeStruct(dims, dtype)


def shards(design, sign_bits, picks, counts, target, rinv):
    rows, width = design.shape
    whole = rinv.shape[1]
    row_groups = lax.axis_size("row")
    lines = rows // LANE
    scalar = shape(1, LANE)
    deep = message_rows(width)
    left = target.reshape(lines, LANE)
    bits = sign_bits.reshape(lines, LANE)
    chunks = min(CHUNKS, width // NEAR // LANE)
    piece = width // NEAR // chunks
    scale = float(np.sqrt(np.float32(rows * row_groups)))
    slots = row_groups * PAIR
    far = row_groups // NEAR

    sent = [(1, 0)] + [(mask, chunk * piece) for mask in range(2, NEAR) for chunk in range(chunks)]
    sizes = [piece * chunks] + [piece] * (chunks * (NEAR - 2))

    message, *away = pl.pallas_call(
        functools.partial(first_body, sent),
        out_shape=(shape(row_groups, rounded(signs_at(width, row_groups) + lines, 8), LANE),)
        + tuple(shape(rows, size) for size in sizes),
        in_specs=[HBM] * 5,
        out_specs=(VMEM,) + (HBM,) * len(sent),
        scratch_shapes=[
            pltpu.VMEM((rows, width), F32),
            pltpu.VMEM((lines, LANE), F32),
            pltpu.VMEM((lines, LANE), jnp.int32),
            pltpu.VMEM((row_groups, PAIR), jnp.int32),
            pltpu.VMEM((1, row_groups), jnp.int32),
            pltpu.SemaphoreType.DMA((4 + lines + len(sent),)),
        ],
        compiler_params=pltpu.CompilerParams(vmem_limit_bytes=58 << 20),
    )(design, left, bits, picks.reshape(row_groups, PAIR), counts.reshape(1, row_groups))

    def swap(array, mask):
        return lax.ppermute(array, "row", [(i, i ^ mask) for i in range(row_groups)])

    def mix(message):
        made = shape(row_groups, slots, rows, dtype=jnp.bfloat16)
        return call(functools.partial(mix_body, width), made, message, jnp.asarray(walsh(HB), jnp.bfloat16))

    def sample(chunk, mixed, order):
        return call(
            functools.partial(sample_body, scale, chunk * piece),
            (shape(far // 2, NEAR, slots, piece),) * 2 + (scalar,),
            design,
            picked,
            mixed,
            order,
            *(near[index] for index, (mask, start) in enumerate(sent) if mask == 1 or start == chunk * piece),
            scratch=[pltpu.VMEM((NEAR, 2, rows, piece), jnp.bfloat16)],
        )

    def spread(indices, order):
        parts, _ = lax.optimization_barrier(([away[index] for index in indices], order))
        return [swap(part, sent[index][0]) for index, part in zip(indices, parts)]

    def halve(keep, come, order):
        bit = row_groups // 2
        while bit > NEAR:
            bit //= 2
            half = keep.shape[0] // 2
            keep, send = call(halve_body, (shape(half, *keep.shape[1:]),) * 2, keep, come, order)
            come = swap(send, bit)
        return keep, come

    def join(keep, come, order):
        keep, come = halve(keep, come, order)
        return call(join_body, (shape(*keep.shape[1:]), scalar), keep, come, order)

    def back(rinv, message, first):
        outs, scratch = (shape(whole // LANE, LANE), scalar), [pltpu.VMEM((width // LANE, LANE), F32)]
        if first:
            outs += (shape(*rinv.shape),)
            scratch += [pltpu.SemaphoreType.DMA((width // LANE,))]
        return pl.pallas_call(
            functools.partial(back_body, first),
            out_shape=outs,
            in_specs=[HBM if first else VMEM, VMEM],
            out_specs=(VMEM,) * len(outs),
            scratch_shapes=scratch,
            compiler_params=pltpu.CompilerParams(vmem_limit_bytes=(34 if first else 24) << 20),
            )(rinv, message)

    def forward(terms, token, last, *before):
        return call(
            functools.partial(forward_body, len(terms), not before, last),
            (shape(lines, LANE), shape(width // LANE, LANE), scalar)
            + (() if last else (shape(whole // LANE, LANE),)),
            here,
            design,
            token,
            *terms,
            *before,
        )

    def turn(images, left, beta, alpha, parts):
        return call(
            functools.partial(turn_body, len(images), bool(parts)),
            (shape(lines, LANE), shape(row_groups, 8 if parts else deep, LANE))
            + (shape(slots, width // NEAR),) * (NEAR if parts else 0),
            *images,
            left,
            beta,
            alpha,
            *(parts or (design,)),
        )

    betas, alphas, held, joined, right = [], [], [], [], []
    message = picked = exchange(message, "row")
    late = len(sent) - 1 if chunks > 1 else len(sent)
    near = spread(range(late), message)
    for step in range(ITERS):
        last = step + 1 == ITERS
        if step == 0:
            term, beta, here = back(rinv, message, True)
            mixed = mix(message)
        else:
            term, beta = back(here, message, False)
            token = beta
            if chunks > 1:
                part, token = join(keep, come, beta)
                joined.append(part)
                keep, send, token = sample(1, mixed, token)
                come = swap(send, row_groups // 2)
        betas.append(beta)
        spare = chunks > 1 and step > 0
        terms = direct(term, "col") if spare else paired(term, "col")
        if step == 0:
            near += spread(range(late, len(sent)), terms[1])
            keep, send, token = sample(0, mixed, terms[1])
            come = swap(send, row_groups // 2)
        image, kept, alpha, *right = forward(terms, token, last, *right, *betas[1:])
        alphas.append(alpha)
        held.append(kept)
        images = direct(image, "col") if spare else paired(image, "col")
        parts = (*joined, *halve(keep, come, beta)) if last else ()
        left, message, *quarters = turn(images, left, beta, alpha, parts)
        message = exchange(message, "row")
    mine, *others = quarters
    basis, answer, sketch = call(
        last_body,
        (shape(lines, LANE), shape(width // LANE, LANE), shape(slots, width)),
        message,
        left,
        *betas,
        *alphas,
        *held,
        mine,
        *(swap(part, mask + 1) for mask, part in enumerate(others)),
    )
    return (sketch, answer.reshape(-1), basis.reshape(-1))


def solution(mesh):
    placed = (
        P("row", "col"),
        P("row"),
        P(None, "row", None),
        P(None, "row"),
        P("row"),
        P("col", None),
    )
    return jax.shard_map(
        shards,
        mesh=mesh,
        in_specs=placed,
        out_specs=(P("row", "col"), P("col"), P("row")),
        check_vma=False,
    )
```

```python
import functools

import jax
import jax.numpy as jnp
import numpy as np
from jax import lax
from jax.experimental import pallas as pl
from jax.experimental.pallas import tpu as pltpu
from jax.sharding import PartitionSpec as P

HB = 256
PAIR = 16
ITERS = 2
LANE = 128
NEAR = 4
CHUNKS = 2
F32 = jnp.float32
VMEM = pl.BlockSpec(memory_space=pltpu.VMEM)
HBM = pl.BlockSpec(memory_space=pltpu.HBM)
ANY = pl.BlockSpec(memory_space=pl.ANY)


def exchange(copies, axis):
    return lax.all_to_all(copies, axis, split_axis=0, concat_axis=0, tiled=True)


def paired(array, axis):
    size = lax.axis_size(axis)
    mask = 1
    while True:
        come = lax.ppermute(array, axis, [(i, i ^ mask) for i in range(size)])
        mask *= 2
        if mask == size:
            return [array, come]
        array = array + come


def direct(array, axis):
    size = lax.axis_size(axis)
    return [array] + [
        lax.ppermute(array, axis, [(i, i ^ mask) for i in range(size)]) for mask in range(1, size)
    ]


def tree(values):
    while len(values) > 1:
        values = [values[i] + values[i + 1] for i in range(0, len(values), 2)]
    return values[0]


def walsh(size):
    index = np.arange(size)
    common = index[:, None] & index[None, :]
    parity = np.zeros((size, size), np.int64)
    for shift in range(size.bit_length()):
        parity ^= (common >> shift) & 1
    return (1 - 2 * parity).astype(np.float32)


def call(body, out_shape, *operands, scratch=()):
    return pl.pallas_call(
        body,
        out_shape=out_shape,
        in_specs=[VMEM] * len(operands),
        out_specs=jax.tree.map(lambda _: VMEM, out_shape),
        scratch_shapes=scratch,
        compiler_params=pltpu.CompilerParams(vmem_limit_bytes=24 << 20),
    )(*operands)


def fold_rows(block):
    return block.reshape(block.shape[0] // 8, 8, LANE).sum(axis=0)


def total(rows):
    return jnp.sum(jnp.sum(rows, axis=0, keepdims=True), axis=1, keepdims=True)


def splat(scalar):
    return jnp.broadcast_to(scalar, (1, LANE))


def left_product(vector, matrix_ref, out_ref):
    blocks, tiles = matrix_ref.shape[0] // LANE, matrix_ref.shape[1] // LANE
    sums = [jnp.zeros((8, LANE), F32) for _ in range(tiles)]
    for block in range(blocks):
        weight = across(vector[block : block + 1, :])
        for tile in range(tiles):
            part = matrix_ref[block * LANE : (block + 1) * LANE, tile * LANE : (tile + 1) * LANE]
            sums[tile] = sums[tile] + fold_rows(part * weight)
    for tile in range(tiles):
        out_ref[tile : tile + 1, :] = jnp.sum(sums[tile], axis=0, keepdims=True)


def left_product_long(vector_ref, matrix_ref, out_ref, copies=()):
    blocks, tiles = matrix_ref.shape[0] // LANE, matrix_ref.shape[1] // LANE

    def step(block, sums):
        weight = across(vector_ref[pl.ds(block, 1), :])
        rows = pl.ds(pl.multiple_of(block * LANE, LANE), LANE)
        return tuple(
            sums[tile] + fold_rows(matrix_ref[rows, tile * LANE : (tile + 1) * LANE] * weight)
            for tile in range(tiles)
        )

    sums = tuple(jnp.zeros((8, LANE), F32) for _ in range(tiles))
    if copies:
        for block, copy in enumerate(copies):
            copy.wait()
            sums = step(block, sums)
    else:
        sums = lax.fori_loop(0, blocks, step, sums)
    for tile in range(tiles):
        out_ref[tile : tile + 1, :] = jnp.sum(sums[tile], axis=0, keepdims=True)


def right_product(matrix_ref, vector, out_ref):
    blocks, tiles = matrix_ref.shape[0] // LANE, matrix_ref.shape[1] // LANE

    def step(block, carry):
        rows = pl.ds(pl.multiple_of(block * LANE, LANE), LANE)
        sums = jnp.zeros((LANE, LANE), F32)
        for tile in range(tiles):
            sums = sums + matrix_ref[rows, tile * LANE : (tile + 1) * LANE] * vector[tile : tile + 1, :]
        out_ref[pl.ds(block, 1), :] = jnp.sum(fold_rows(sums.T), axis=0, keepdims=True)
        return carry

    lax.fori_loop(0, blocks, step, 0)


def rounded(count, unit):
    return -(-count // unit) * unit


def message_rows(width):
    return rounded(width // LANE + 1, 8)


def picks_at(width):
    return width // LANE + 1


def signs_at(width, groups):
    return picks_at(width) + groups * PAIR // LANE


def copy_out(out_ref):
    first = out_ref[0]
    for index in range(1, out_ref.shape[0]):
        out_ref[index] = first


def across(row):
    return jnp.broadcast_to(row, (LANE, LANE)).T


def first_body(sent, design_ref, target_ref, bits_ref, picks_ref, counts_ref, *refs):
    out_ref, away_refs = refs[0], refs[1:-6]
    design, target_here, bits, picks, counts, sems = refs[-6:]
    rows, width = design.shape
    lines, tiles = rows // LANE, width // LANE
    small = [
        pltpu.make_async_copy(source, place, sems.at[index])
        for index, (source, place) in enumerate(
            ((target_ref, target_here), (bits_ref, bits), (picks_ref, picks), (counts_ref, counts))
        )
    ]
    parts = [slice(line * LANE, (line + 1) * LANE) for line in range(lines)]
    large = [
        pltpu.make_async_copy(design_ref.at[part, :], design.at[part, :], sems.at[4 + line])
        for line, part in enumerate(parts)
    ]
    place = lax.axis_index("row") % NEAR
    away = []
    for index, away_ref in enumerate(away_refs):
        piece = away_ref.shape[1]
        mask, start = sent[index]
        column = pl.multiple_of((place ^ mask) * (width // NEAR) + start, LANE)
        source = design.at[:, pl.ds(column, piece)]
        away.append(pltpu.make_async_copy(source, away_ref, sems.at[4 + lines + index]))
    for copy in small + large:
        copy.start()
    for copy in small:
        copy.wait()
    out_ref[0] = jnp.zeros(out_ref.shape[1:], F32)
    groups = picks.shape[0]
    owner = lax.broadcasted_iota(jnp.int32, (groups, groups), 0)
    same = owner == lax.broadcasted_iota(jnp.int32, (groups, groups), 1)
    limit = jnp.sum(jnp.where(same, counts[...].astype(F32), 0.0), axis=1, keepdims=True)
    slot = lax.broadcasted_iota(jnp.int32, picks.shape, 1).astype(F32)
    coded = jnp.where(slot < limit, picks[...].astype(F32), -1.0)
    start = picks_at(width)
    for owner in range(0, groups, LANE // PAIR):
        line = jnp.concatenate([coded[i : i + 1, :] for i in range(owner, owner + LANE // PAIR)], axis=1)
        out_ref[0, start + owner * PAIR // LANE : start + owner * PAIR // LANE + 1, :] = line
    start = signs_at(width, groups)
    out_ref[0, start : start + lines, :] = (2 * bits[...] - 1).astype(F32)
    target = target_here[...]
    out_ref[0, tiles : tiles + 1, :] = splat(total(target * target))
    sums = [jnp.zeros((8, LANE), F32) for _ in range(tiles)]
    for line, part in enumerate(parts):
        weight = across(target[line : line + 1, :])
        large[line].wait()
        if line == lines - 1:
            for copy in away:
                copy.start()
        for tile in range(tiles):
            sums[tile] = sums[tile] + fold_rows(design[part, tile * LANE : (tile + 1) * LANE] * weight)
    for tile in range(tiles):
        out_ref[0, tile : tile + 1, :] = jnp.sum(sums[tile], axis=0, keepdims=True)
    copy_out(out_ref)
    for copy in away:
        copy.wait()


def back_body(first, rinv_ref, parts_ref, order_ref, term_ref, beta_ref, *refs):
    tiles = rinv_ref.shape[0] // LANE
    copies = []
    if first:
        rinv_here, scratch, sems = refs
        for block in range(tiles):
            part = slice(block * LANE, (block + 1) * LANE)
            copies.append(pltpu.make_async_copy(rinv_ref.at[part, :], rinv_here.at[part, :], sems.at[block]))
            copies[-1].start()
    else:
        rinv_here, (scratch,) = rinv_ref, refs
    summed = tree([parts_ref[i, : tiles + 1, :] for i in range(parts_ref.shape[0])])
    beta = jnp.sqrt(summed[tiles : tiles + 1, :])
    beta_ref[...] = beta
    scratch[...] = summed[:tiles, :] / beta
    left_product_long(scratch, rinv_here, term_ref, copies)


def forward_body(groups, first, last, rinv_ref, design_ref, token_ref, *refs):
    right = tree([ref[...] for ref in refs[:groups]])
    refs = refs[groups:]
    if not first:
        before_ref, beta_ref, *refs = refs
        right = right - beta_ref[...] * before_ref[...]
    image_ref, held_ref, alpha_ref, *right_refs = refs
    alpha = jnp.sqrt(total(right * right))
    alpha_ref[...] = splat(alpha)
    right = right / alpha
    if not last:
        right_refs[0][...] = right
    right_product(rinv_ref, right, held_ref)
    right_product(design_ref, held_ref[...], image_ref)


def turn_body(groups, last, *refs):
    left = tree([ref[...] for ref in refs[:groups]])
    before_ref, beta_ref, alpha_ref, *refs = refs[groups:]
    left = left - alpha_ref[...] * (before_ref[...] / beta_ref[...])
    square = splat(total(left * left))
    if last:
        *parts, left_ref, out_ref = refs[: -NEAR]
        out_refs = refs[-NEAR:]
        out_ref[...] = jnp.broadcast_to(square, out_ref.shape)
        *joined, kept_ref, arrived_ref = parts
        piece = kept_ref.shape[3]
        for index, rows_ref in enumerate(out_refs):
            for chunk, part_ref in enumerate(joined):
                rows_ref[:, chunk * piece : (chunk + 1) * piece] = part_ref[index]
            rows_ref[:, len(joined) * piece :] = kept_ref[0, index] + arrived_ref[0, index]
    else:
        design_ref, left_ref, out_ref = refs
        tiles = design_ref.shape[1] // LANE
        out_ref[0] = jnp.zeros(out_ref.shape[1:], F32)
        left_product(left, design_ref, out_ref.at[0])
        out_ref[0, tiles : tiles + 1, :] = square
        copy_out(out_ref)
    left_ref[...] = left


def pieces(value):
    high = value.astype(jnp.bfloat16)
    return high, (value - high.astype(F32)).astype(jnp.bfloat16)


def weigh(mix, high, low):
    return jnp.dot(mix, high, preferred_element_type=F32) + jnp.dot(mix, low, preferred_element_type=F32)


def for_blocks(groups, step):
    if groups <= 8:
        for block in range(groups):
            step(block, 0)
    else:
        lax.fori_loop(0, groups, step, 0)


def mix_body(width, parts_ref, walsh_ref, mix_ref):
    groups, _, rows = mix_ref.shape
    me = lax.axis_index("row")
    local = lax.broadcasted_iota(jnp.int32, (LANE, rows), 1).astype(F32)
    per = LANE // PAIR

    def step(block, carry):
        parity = jnp.int32(0)
        for bit in range(groups.bit_length() - 1):
            parity = parity ^ ((block & me) >> bit)
        sign = (1 - 2 * (parity & 1)).astype(F32)
        for line in range(groups // per):
            start = picks_at(width) + line
            coded = across(parts_ref[block, start : start + 1, :])
            match = jnp.concatenate([coded] * (rows // LANE), axis=1) == local
            chosen = jnp.where(match, sign, 0.0).astype(jnp.bfloat16)
            for part in range(rows // HB):
                columns = slice(part * HB, (part + 1) * HB)
                mixed = jnp.dot(chosen[:, columns], walsh_ref[...], preferred_element_type=F32).astype(jnp.bfloat16)
                for index in range(per):
                    place = pl.multiple_of(((line * per + index) ^ me) * PAIR, PAIR)
                    mix_ref[block, pl.ds(place, PAIR), columns] = mixed[index * PAIR : (index + 1) * PAIR, :]
        return carry

    for_blocks(groups, step)


def sample_body(scale, start, design_ref, parts_ref, mix_ref, order_ref, *refs):
    near, (keep_ref, send_ref, token_ref, both) = refs[: NEAR - 1], refs[NEAR - 1 :]
    token_ref[...] = order_ref[:1, :]
    rows, piece = near[-1].shape
    width = design_ref.shape[1]
    groups = mix_ref.shape[0]
    me = lax.axis_index("row")
    signs_start = signs_at(width, groups)
    for line in range(rows // LANE):
        part = slice(line * LANE, (line + 1) * LANE)
        signs = [across(parts_ref[me ^ mask, signs_start + line : signs_start + line + 1, :]) for mask in range(NEAR)]
        for tile in range(0, piece, LANE):
            column = pl.multiple_of(me % NEAR * (width // NEAR) + start + tile, LANE)
            here = slice(tile, tile + LANE)
            values = [design_ref[part, pl.ds(column, LANE)]] + [ref[part, here] for ref in near]
            values = [value * sign for value, sign in zip(values, signs)]
            apart = 1
            while apart < NEAR:
                for first in range(NEAR):
                    if not first & apart:
                        one, two = values[first], values[first | apart]
                        values[first], values[first | apart] = one + two, one - two
                apart *= 2
            for index, value in enumerate(values):
                both[index, 0, part, here], both[index, 1, part, here] = pieces(value)

    def step(block, carry):
        value = weigh(mix_ref[block], both[block % NEAR, 0], both[block % NEAR, 1]) / scale
        slot = pl.ds(block * PAIR, PAIR)
        for apart in range(groups):
            far, low = apart // NEAR, apart % NEAR
            out_ref = send_ref if far >= groups // NEAR // 2 else keep_ref
            out_ref[far % (groups // NEAR // 2), low, slot, :] = value[apart * PAIR : (apart + 1) * PAIR, :]
        return carry

    for_blocks(groups, step)


def halve_body(kept_ref, arrived_ref, order_ref, keep_ref, send_ref):
    half = keep_ref.shape[0]
    keep_ref[...] = kept_ref[:half] + arrived_ref[:half]
    send_ref[...] = kept_ref[half:] + arrived_ref[half:]


def join_body(kept_ref, arrived_ref, order_ref, out_ref, token_ref):
    token_ref[...] = order_ref[:1, :]
    out_ref[...] = kept_ref[0] + arrived_ref[0]


def touch_body(*refs):
    order_ref, token_ref = refs[-2:]
    token_ref[...] = order_ref[0, :1, :]


def last_body(parts_ref, left_ref, *refs):
    basis_ref, solution_ref, sketch_ref = refs[-3:]
    quarters = refs[3 * ITERS : 3 * ITERS + NEAR]
    place = lax.axis_index("row") % NEAR
    piece = quarters[0].shape[1]
    for mask, part_ref in enumerate(quarters):
        for tile in range(0, piece, LANE):
            column = pl.multiple_of((place ^ mask) * piece + tile, LANE)
            sketch_ref[:, pl.ds(column, LANE)] = part_ref[:, tile : tile + LANE]
    betas = [ref[...] for ref in refs[:ITERS]]
    alphas = [ref[...] for ref in refs[ITERS : 2 * ITERS]]
    held = [ref[...] for ref in refs[2 * ITERS : 3 * ITERS]]
    last = jnp.sqrt(tree([parts_ref[i] for i in range(parts_ref.shape[0])])[:1, :])
    basis_ref[...] = left_ref[...] / last
    betas.append(last)
    phibar, rhobar = betas[0], alphas[0]
    search, iterate = held[0], jnp.zeros_like(held[0])
    for step in range(ITERS):
        beta = betas[step + 1]
        rho = jnp.sqrt(rhobar * rhobar + beta * beta)
        cosine = rhobar / rho
        sine = beta / rho
        phi = cosine * phibar
        phibar = sine * phibar
        iterate = iterate + phi / rho * search
        if step + 1 < ITERS:
            alpha = alphas[step + 1]
            search = held[step + 1] - sine * alpha / rho * search
            rhobar = -cosine * alpha
    solution_ref[...] = iterate


def shape(*dims, dtype=F32):
    return jax.ShapeDtypeStruct(dims, dtype)


def shards(design, sign_bits, picks, counts, target, rinv):
    rows, width = design.shape
    whole = rinv.shape[1]
    row_groups = lax.axis_size("row")
    lines = rows // LANE
    scalar = shape(1, LANE)
    deep = message_rows(width)
    left = target.reshape(lines, LANE)
    bits = sign_bits.reshape(lines, LANE)
    chunks = min(CHUNKS, width // NEAR // LANE)
    piece = width // NEAR // chunks
    scale = float(np.sqrt(np.float32(rows * row_groups)))
    slots = row_groups * PAIR
    far = row_groups // NEAR

    sent = [(mask, chunk * piece) for chunk in range(chunks) for mask in range(1, NEAR)]

    message, *away = pl.pallas_call(
        functools.partial(first_body, sent),
        out_shape=(shape(row_groups, rounded(signs_at(width, row_groups) + lines, 8), LANE),)
        + (shape(rows, piece),) * len(sent),
        in_specs=[HBM] * 5,
        out_specs=(VMEM,) + (HBM,) * len(sent),
        scratch_shapes=[
            pltpu.VMEM((rows, width), F32),
            pltpu.VMEM((lines, LANE), F32),
            pltpu.VMEM((lines, LANE), jnp.int32),
            pltpu.VMEM((row_groups, PAIR), jnp.int32),
            pltpu.VMEM((1, row_groups), jnp.int32),
            pltpu.SemaphoreType.DMA((4 + lines + len(sent),)),
        ],
        compiler_params=pltpu.CompilerParams(vmem_limit_bytes=58 << 20),
    )(design, left, bits, picks.reshape(row_groups, PAIR), counts.reshape(1, row_groups))

    def swap(array, mask):
        return lax.ppermute(array, "row", [(i, i ^ mask) for i in range(row_groups)])

    def mix(message):
        made = shape(row_groups, slots, rows, dtype=jnp.bfloat16)
        return call(functools.partial(mix_body, width), made, message, jnp.asarray(walsh(HB), jnp.bfloat16))

    def sample(chunk, mixed, order):
        return call(
            functools.partial(sample_body, scale, chunk * piece),
            (shape(far // 2, NEAR, slots, piece),) * 2 + (scalar,),
            design,
            picked,
            mixed,
            order,
            *near[chunk * (NEAR - 1) : (chunk + 1) * (NEAR - 1)],
            scratch=[pltpu.VMEM((NEAR, 2, rows, piece), jnp.bfloat16)],
        )

    def spread(indices, order):
        parts = [away[index] for index in indices]
        if order is not None:
            parts, _ = lax.optimization_barrier((parts, order))
        return [swap(part, sent[index][0]) for index, part in zip(indices, parts)]

    def halve(keep, come, order):
        bit = row_groups // 2
        while bit > NEAR:
            bit //= 2
            half = keep.shape[0] // 2
            keep, send = call(halve_body, (shape(half, *keep.shape[1:]),) * 2, keep, come, order)
            come = swap(send, bit)
        return keep, come

    def join(keep, come, order):
        keep, come = halve(keep, come, order)
        return call(join_body, (shape(*keep.shape[1:]), scalar), keep, come, order)

    def back(rinv, message, order, first):
        outs, scratch = (shape(whole // LANE, LANE), scalar), [pltpu.VMEM((width // LANE, LANE), F32)]
        if first:
            outs += (shape(*rinv.shape),)
            scratch += [pltpu.SemaphoreType.DMA((width // LANE,))]
        return pl.pallas_call(
            functools.partial(back_body, first),
            out_shape=outs,
            in_specs=[HBM if first else VMEM, VMEM, VMEM],
            out_specs=(VMEM,) * len(outs),
            scratch_shapes=scratch,
            compiler_params=pltpu.CompilerParams(vmem_limit_bytes=(34 if first else 24) << 20),
            )(rinv, message, order)

    def forward(terms, token, last, *before):
        return call(
            functools.partial(forward_body, len(terms), not before, last),
            (shape(lines, LANE), shape(width // LANE, LANE), scalar)
            + (() if last else (shape(whole // LANE, LANE),)),
            here,
            design,
            token,
            *terms,
            *before,
        )

    def turn(images, left, beta, alpha, parts):
        return call(
            functools.partial(turn_body, len(images), bool(parts)),
            (shape(lines, LANE), shape(row_groups, 8 if parts else deep, LANE))
            + (shape(slots, width // NEAR),) * (NEAR if parts else 0),
            *images,
            left,
            beta,
            alpha,
            *(parts or (design,)),
        )

    betas, alphas, held, joined, right = [], [], [], [], []
    near = spread(range(NEAR - 2), None)
    message = picked = exchange(message, "row")
    token = pl.pallas_call(
        touch_body,
        out_shape=scalar,
        in_specs=[ANY] * len(near) + [VMEM],
        out_specs=VMEM,
        compiler_params=pltpu.CompilerParams(vmem_limit_bytes=2 << 20),
    )(*near, message)
    late = len(sent) - (chunks > 1)
    near += spread(range(NEAR - 2, late), message)
    for step in range(ITERS):
        last = step + 1 == ITERS
        if step == 0:
            term, beta, here = back(rinv, message, token, True)
            mixed = mix(message)
        else:
            term, beta = back(here, message, alpha, False)
            token = beta
            if chunks > 1:
                part, token = join(keep, come, beta)
                joined.append(part)
                keep, send, token = sample(1, mixed, token)
                come = swap(send, row_groups // 2)
        betas.append(beta)
        spare = chunks > 1 and step > 0
        terms = direct(term, "col") if spare else paired(term, "col")
        if step == 0:
            near += spread(range(late, len(sent)), terms[1])
            keep, send, token = sample(0, mixed, beta)
            come = swap(send, row_groups // 2)
        image, kept, alpha, *right = forward(terms, token, last, *right, *betas[1:])
        alphas.append(alpha)
        held.append(kept)
        images = direct(image, "col") if spare else paired(image, "col")
        parts = (*joined, *halve(keep, come, beta)) if last else ()
        left, message, *quarters = turn(images, left, beta, alpha, parts)
        message = exchange(message, "row")
    mine, *others = quarters
    basis, answer, sketch = call(
        last_body,
        (shape(lines, LANE), shape(width // LANE, LANE), shape(slots, width)),
        message,
        left,
        *betas,
        *alphas,
        *held,
        mine,
        *(swap(part, mask + 1) for mask, part in enumerate(others)),
    )
    return (sketch, answer.reshape(-1), basis.reshape(-1))


def solution(mesh):
    placed = (
        P("row", "col"),
        P("row"),
        P(None, "row", None),
        P(None, "row"),
        P("row"),
        P("col", None),
    )
    return jax.shard_map(
        shards,
        mesh=mesh,
        in_specs=placed,
        out_specs=(P("row", "col"), P("col"), P("row")),
        check_vma=False,
    )
```

```python
import functools

import jax
import jax.numpy as jnp
import numpy as np
from jax import lax
from jax.experimental import pallas as pl
from jax.experimental.pallas import tpu as pltpu
from jax.sharding import PartitionSpec as P

HB = 256
PAIR = 16
ITERS = 2
LANE = 128
NEAR = 4
CHUNKS = 2
F32 = jnp.float32
VMEM = pl.BlockSpec(memory_space=pltpu.VMEM)
HBM = pl.BlockSpec(memory_space=pltpu.HBM)
ANY = pl.BlockSpec(memory_space=pl.ANY)


def exchange(copies, axis):
    return lax.all_to_all(copies, axis, split_axis=0, concat_axis=0, tiled=True)


def paired(array, axis):
    size = lax.axis_size(axis)
    mask = 1
    while True:
        come = lax.ppermute(array, axis, [(i, i ^ mask) for i in range(size)])
        mask *= 2
        if mask == size:
            return [array, come]
        array = array + come


def direct(array, axis):
    size = lax.axis_size(axis)
    return [array] + [
        lax.ppermute(array, axis, [(i, i ^ mask) for i in range(size)]) for mask in range(1, size)
    ]


def tree(values):
    while len(values) > 1:
        values = [values[i] + values[i + 1] for i in range(0, len(values), 2)]
    return values[0]


def walsh(size):
    index = np.arange(size)
    common = index[:, None] & index[None, :]
    parity = np.zeros((size, size), np.int64)
    for shift in range(size.bit_length()):
        parity ^= (common >> shift) & 1
    return (1 - 2 * parity).astype(np.float32)


def call(body, out_shape, *operands, scratch=()):
    return pl.pallas_call(
        body,
        out_shape=out_shape,
        in_specs=[VMEM] * len(operands),
        out_specs=jax.tree.map(lambda _: VMEM, out_shape),
        scratch_shapes=scratch,
        compiler_params=pltpu.CompilerParams(vmem_limit_bytes=24 << 20),
    )(*operands)


def fold_rows(block):
    return block.reshape(block.shape[0] // 8, 8, LANE).sum(axis=0)


def total(rows):
    return jnp.sum(jnp.sum(rows, axis=0, keepdims=True), axis=1, keepdims=True)


def splat(scalar):
    return jnp.broadcast_to(scalar, (1, LANE))


def left_product(vector, matrix_ref, out_ref):
    blocks, tiles = matrix_ref.shape[0] // LANE, matrix_ref.shape[1] // LANE
    sums = [jnp.zeros((8, LANE), F32) for _ in range(tiles)]
    for block in range(blocks):
        weight = across(vector[block : block + 1, :])
        for tile in range(tiles):
            part = matrix_ref[block * LANE : (block + 1) * LANE, tile * LANE : (tile + 1) * LANE]
            sums[tile] = sums[tile] + fold_rows(part * weight)
    for tile in range(tiles):
        out_ref[tile : tile + 1, :] = jnp.sum(sums[tile], axis=0, keepdims=True)


def left_product_long(vector_ref, matrix_ref, out_ref, copies=()):
    blocks, tiles = matrix_ref.shape[0] // LANE, matrix_ref.shape[1] // LANE

    def step(block, sums):
        weight = across(vector_ref[pl.ds(block, 1), :])
        rows = pl.ds(pl.multiple_of(block * LANE, LANE), LANE)
        return tuple(
            sums[tile] + fold_rows(matrix_ref[rows, tile * LANE : (tile + 1) * LANE] * weight)
            for tile in range(tiles)
        )

    sums = tuple(jnp.zeros((8, LANE), F32) for _ in range(tiles))
    if copies:
        for block, copy in enumerate(copies):
            copy.wait()
            sums = step(block, sums)
    else:
        sums = lax.fori_loop(0, blocks, step, sums)
    for tile in range(tiles):
        out_ref[tile : tile + 1, :] = jnp.sum(sums[tile], axis=0, keepdims=True)


def right_product(matrix_ref, vector, out_ref):
    blocks, tiles = matrix_ref.shape[0] // LANE, matrix_ref.shape[1] // LANE

    def step(block, carry):
        rows = pl.ds(pl.multiple_of(block * LANE, LANE), LANE)
        sums = jnp.zeros((LANE, LANE), F32)
        for tile in range(tiles):
            sums = sums + matrix_ref[rows, tile * LANE : (tile + 1) * LANE] * vector[tile : tile + 1, :]
        out_ref[pl.ds(block, 1), :] = jnp.sum(fold_rows(sums.T), axis=0, keepdims=True)
        return carry

    lax.fori_loop(0, blocks, step, 0)


def rounded(count, unit):
    return -(-count // unit) * unit


def message_rows(width):
    return rounded(width // LANE + 1, 8)


def picks_at(width):
    return width // LANE + 1


def signs_at(width, groups):
    return picks_at(width) + groups * PAIR // LANE


def copy_out(out_ref):
    first = out_ref[0]
    for index in range(1, out_ref.shape[0]):
        out_ref[index] = first


def across(row):
    return jnp.broadcast_to(row, (LANE, LANE)).T


def first_body(sent, design_ref, target_ref, bits_ref, picks_ref, counts_ref, *refs):
    out_ref, away_refs = refs[0], refs[1:-6]
    design, target_here, bits, picks, counts, sems = refs[-6:]
    rows, width = design.shape
    lines, tiles = rows // LANE, width // LANE
    small = [
        pltpu.make_async_copy(source, place, sems.at[index])
        for index, (source, place) in enumerate(
            ((target_ref, target_here), (bits_ref, bits), (picks_ref, picks), (counts_ref, counts))
        )
    ]
    parts = [slice(line * LANE, (line + 1) * LANE) for line in range(lines)]
    large = [
        pltpu.make_async_copy(design_ref.at[part, :], design.at[part, :], sems.at[4 + line])
        for line, part in enumerate(parts)
    ]
    place = lax.axis_index("row") % NEAR
    away = []
    for index, away_ref in enumerate(away_refs):
        piece = away_ref.shape[1]
        mask, start = sent[index]
        column = pl.multiple_of((place ^ mask) * (width // NEAR) + start, LANE)
        source = design.at[:, pl.ds(column, piece)]
        away.append(pltpu.make_async_copy(source, away_ref, sems.at[4 + lines + index]))
    for copy in small + large:
        copy.start()
    for copy in small:
        copy.wait()
    out_ref[0] = jnp.zeros(out_ref.shape[1:], F32)
    groups = picks.shape[0]
    owner = lax.broadcasted_iota(jnp.int32, (groups, groups), 0)
    same = owner == lax.broadcasted_iota(jnp.int32, (groups, groups), 1)
    limit = jnp.sum(jnp.where(same, counts[...].astype(F32), 0.0), axis=1, keepdims=True)
    slot = lax.broadcasted_iota(jnp.int32, picks.shape, 1).astype(F32)
    coded = jnp.where(slot < limit, picks[...].astype(F32), -1.0)
    start = picks_at(width)
    for owner in range(0, groups, LANE // PAIR):
        line = jnp.concatenate([coded[i : i + 1, :] for i in range(owner, owner + LANE // PAIR)], axis=1)
        out_ref[0, start + owner * PAIR // LANE : start + owner * PAIR // LANE + 1, :] = line
    start = signs_at(width, groups)
    out_ref[0, start : start + lines, :] = (2 * bits[...] - 1).astype(F32)
    target = target_here[...]
    out_ref[0, tiles : tiles + 1, :] = splat(total(target * target))
    sums = [jnp.zeros((8, LANE), F32) for _ in range(tiles)]
    for line, part in enumerate(parts):
        weight = across(target[line : line + 1, :])
        large[line].wait()
        if line == lines - 1:
            for copy in away:
                copy.start()
        for tile in range(tiles):
            sums[tile] = sums[tile] + fold_rows(design[part, tile * LANE : (tile + 1) * LANE] * weight)
    for tile in range(tiles):
        out_ref[0, tile : tile + 1, :] = jnp.sum(sums[tile], axis=0, keepdims=True)
    copy_out(out_ref)
    for copy in away:
        copy.wait()


def back_body(first, rinv_ref, parts_ref, order_ref, term_ref, beta_ref, *refs):
    tiles = rinv_ref.shape[0] // LANE
    copies = []
    if first:
        rinv_here, scratch, sems = refs
        for block in range(tiles):
            part = slice(block * LANE, (block + 1) * LANE)
            copies.append(pltpu.make_async_copy(rinv_ref.at[part, :], rinv_here.at[part, :], sems.at[block]))
            copies[-1].start()
    else:
        rinv_here, (scratch,) = rinv_ref, refs
    summed = tree([parts_ref[i, : tiles + 1, :] for i in range(parts_ref.shape[0])])
    beta = jnp.sqrt(summed[tiles : tiles + 1, :])
    beta_ref[...] = beta
    scratch[...] = summed[:tiles, :] / beta
    left_product_long(scratch, rinv_here, term_ref, copies)


def forward_body(groups, first, last, rinv_ref, design_ref, token_ref, *refs):
    right = tree([ref[...] for ref in refs[:groups]])
    refs = refs[groups:]
    if not first:
        before_ref, beta_ref, *refs = refs
        right = right - beta_ref[...] * before_ref[...]
    image_ref, held_ref, alpha_ref, *right_refs = refs
    alpha = jnp.sqrt(total(right * right))
    alpha_ref[...] = splat(alpha)
    right = right / alpha
    if not last:
        right_refs[0][...] = right
    right_product(rinv_ref, right, held_ref)
    right_product(design_ref, held_ref[...], image_ref)


def turn_body(groups, last, *refs):
    left = tree([ref[...] for ref in refs[:groups]])
    before_ref, beta_ref, alpha_ref, *refs = refs[groups:]
    left = left - alpha_ref[...] * (before_ref[...] / beta_ref[...])
    square = splat(total(left * left))
    if last:
        left_ref, out_ref = refs
        out_ref[...] = jnp.broadcast_to(square, out_ref.shape)
    else:
        design_ref, left_ref, out_ref = refs
        tiles = design_ref.shape[1] // LANE
        out_ref[0] = jnp.zeros(out_ref.shape[1:], F32)
        left_product(left, design_ref, out_ref.at[0])
        out_ref[0, tiles : tiles + 1, :] = square
        copy_out(out_ref)
    left_ref[...] = left


def pieces(value):
    high = value.astype(jnp.bfloat16)
    return high, (value - high.astype(F32)).astype(jnp.bfloat16)


def weigh(mix, high, low):
    return jnp.dot(mix, high, preferred_element_type=F32) + jnp.dot(mix, low, preferred_element_type=F32)


def for_blocks(groups, step):
    if groups <= 8:
        for block in range(groups):
            step(block, 0)
    else:
        lax.fori_loop(0, groups, step, 0)


def mix_body(width, parts_ref, walsh_ref, mix_ref):
    groups, _, rows = mix_ref.shape
    me = lax.axis_index("row")
    local = lax.broadcasted_iota(jnp.int32, (LANE, rows), 1).astype(F32)
    per = LANE // PAIR

    def step(block, carry):
        parity = jnp.int32(0)
        for bit in range(groups.bit_length() - 1):
            parity = parity ^ ((block & me) >> bit)
        sign = (1 - 2 * (parity & 1)).astype(F32)
        for line in range(groups // per):
            start = picks_at(width) + line
            coded = across(parts_ref[block, start : start + 1, :])
            match = jnp.concatenate([coded] * (rows // LANE), axis=1) == local
            chosen = jnp.where(match, sign, 0.0).astype(jnp.bfloat16)
            for part in range(rows // HB):
                columns = slice(part * HB, (part + 1) * HB)
                mixed = jnp.dot(chosen[:, columns], walsh_ref[...], preferred_element_type=F32).astype(jnp.bfloat16)
                for index in range(per):
                    place = pl.multiple_of(((line * per + index) ^ me) * PAIR, PAIR)
                    mix_ref[block, pl.ds(place, PAIR), columns] = mixed[index * PAIR : (index + 1) * PAIR, :]
        return carry

    for_blocks(groups, step)


def sample_body(scale, start, design_ref, parts_ref, mix_ref, order_ref, *refs):
    near, (keep_ref, send_ref, token_ref, both) = refs[: NEAR - 1], refs[NEAR - 1 :]
    token_ref[...] = order_ref[:1, :]
    rows, piece = near[-1].shape
    width = design_ref.shape[1]
    groups = mix_ref.shape[0]
    me = lax.axis_index("row")
    signs_start = signs_at(width, groups)
    for line in range(rows // LANE):
        part = slice(line * LANE, (line + 1) * LANE)
        signs = [across(parts_ref[me ^ mask, signs_start + line : signs_start + line + 1, :]) for mask in range(NEAR)]
        for tile in range(0, piece, LANE):
            column = pl.multiple_of(me % NEAR * (width // NEAR) + start + tile, LANE)
            here = slice(tile, tile + LANE)
            values = [design_ref[part, pl.ds(column, LANE)]] + [ref[part, here] for ref in near]
            values = [value * sign for value, sign in zip(values, signs)]
            apart = 1
            while apart < NEAR:
                for first in range(NEAR):
                    if not first & apart:
                        one, two = values[first], values[first | apart]
                        values[first], values[first | apart] = one + two, one - two
                apart *= 2
            for index, value in enumerate(values):
                both[index, 0, part, here], both[index, 1, part, here] = pieces(value)

    def step(block, carry):
        value = weigh(mix_ref[block], both[block % NEAR, 0], both[block % NEAR, 1]) / scale
        slot = pl.ds(block * PAIR, PAIR)
        for apart in range(groups):
            far, low = apart // NEAR, apart % NEAR
            out_ref = send_ref if far >= groups // NEAR // 2 else keep_ref
            out_ref[far % (groups // NEAR // 2), low, slot, :] = value[apart * PAIR : (apart + 1) * PAIR, :]
        return carry

    for_blocks(groups, step)


def halve_body(kept_ref, arrived_ref, order_ref, keep_ref, send_ref):
    half = keep_ref.shape[0]
    keep_ref[...] = kept_ref[:half] + arrived_ref[:half]
    send_ref[...] = kept_ref[half:] + arrived_ref[half:]


def join_body(kept_ref, arrived_ref, order_ref, out_ref, token_ref):
    token_ref[...] = order_ref[:1, :]
    out_ref[...] = kept_ref[0] + arrived_ref[0]


def split_body(*refs):
    *joined, kept_ref, arrived_ref, order_ref = refs[:-NEAR]
    piece = kept_ref.shape[3]
    for index, rows_ref in enumerate(refs[-NEAR:]):
        for chunk, part_ref in enumerate(joined):
            rows_ref[:, chunk * piece : (chunk + 1) * piece] = part_ref[index]
        rows_ref[:, len(joined) * piece :] = kept_ref[0, index] + arrived_ref[0, index]


def touch_body(*refs):
    order_ref, token_ref = refs[-2:]
    token_ref[...] = order_ref[0, :1, :]


def last_body(parts_ref, left_ref, *refs):
    basis_ref, solution_ref, sketch_ref = refs[-3:]
    quarters = refs[3 * ITERS : 3 * ITERS + NEAR]
    place = lax.axis_index("row") % NEAR
    piece = quarters[0].shape[1]
    for mask, part_ref in enumerate(quarters):
        for tile in range(0, piece, LANE):
            column = pl.multiple_of((place ^ mask) * piece + tile, LANE)
            sketch_ref[:, pl.ds(column, LANE)] = part_ref[:, tile : tile + LANE]
    betas = [ref[...] for ref in refs[:ITERS]]
    alphas = [ref[...] for ref in refs[ITERS : 2 * ITERS]]
    held = [ref[...] for ref in refs[2 * ITERS : 3 * ITERS]]
    last = jnp.sqrt(tree([parts_ref[i] for i in range(parts_ref.shape[0])])[:1, :])
    basis_ref[...] = left_ref[...] / last
    betas.append(last)
    phibar, rhobar = betas[0], alphas[0]
    search, iterate = held[0], jnp.zeros_like(held[0])
    for step in range(ITERS):
        beta = betas[step + 1]
        rho = jnp.sqrt(rhobar * rhobar + beta * beta)
        cosine = rhobar / rho
        sine = beta / rho
        phi = cosine * phibar
        phibar = sine * phibar
        iterate = iterate + phi / rho * search
        if step + 1 < ITERS:
            alpha = alphas[step + 1]
            search = held[step + 1] - sine * alpha / rho * search
            rhobar = -cosine * alpha
    solution_ref[...] = iterate


def shape(*dims, dtype=F32):
    return jax.ShapeDtypeStruct(dims, dtype)


def shards(design, sign_bits, picks, counts, target, rinv):
    rows, width = design.shape
    whole = rinv.shape[1]
    row_groups = lax.axis_size("row")
    lines = rows // LANE
    scalar = shape(1, LANE)
    deep = message_rows(width)
    left = target.reshape(lines, LANE)
    bits = sign_bits.reshape(lines, LANE)
    chunks = min(CHUNKS, width // NEAR // LANE)
    piece = width // NEAR // chunks
    scale = float(np.sqrt(np.float32(rows * row_groups)))
    slots = row_groups * PAIR
    far = row_groups // NEAR

    sent = [(mask, chunk * piece) for chunk in range(chunks) for mask in range(1, NEAR)]

    message, *away = pl.pallas_call(
        functools.partial(first_body, sent),
        out_shape=(shape(row_groups, rounded(signs_at(width, row_groups) + lines, 8), LANE),)
        + (shape(rows, piece),) * len(sent),
        in_specs=[HBM] * 5,
        out_specs=(VMEM,) + (HBM,) * len(sent),
        scratch_shapes=[
            pltpu.VMEM((rows, width), F32),
            pltpu.VMEM((lines, LANE), F32),
            pltpu.VMEM((lines, LANE), jnp.int32),
            pltpu.VMEM((row_groups, PAIR), jnp.int32),
            pltpu.VMEM((1, row_groups), jnp.int32),
            pltpu.SemaphoreType.DMA((4 + lines + len(sent),)),
        ],
        compiler_params=pltpu.CompilerParams(vmem_limit_bytes=58 << 20),
    )(design, left, bits, picks.reshape(row_groups, PAIR), counts.reshape(1, row_groups))

    def swap(array, mask):
        return lax.ppermute(array, "row", [(i, i ^ mask) for i in range(row_groups)])

    def mix(message):
        made = shape(row_groups, slots, rows, dtype=jnp.bfloat16)
        return call(functools.partial(mix_body, width), made, message, jnp.asarray(walsh(HB), jnp.bfloat16))

    def sample(chunk, mixed, order):
        return call(
            functools.partial(sample_body, scale, chunk * piece),
            (shape(far // 2, NEAR, slots, piece),) * 2 + (scalar,),
            design,
            picked,
            mixed,
            order,
            *near[chunk * (NEAR - 1) : (chunk + 1) * (NEAR - 1)],
            scratch=[pltpu.VMEM((NEAR, 2, rows, piece), jnp.bfloat16)],
        )

    def spread(indices, order):
        parts = [away[index] for index in indices]
        if order is not None:
            parts, _ = lax.optimization_barrier((parts, order))
        return [swap(part, sent[index][0]) for index, part in zip(indices, parts)]

    def halve(keep, come, order):
        bit = row_groups // 2
        while bit > NEAR:
            bit //= 2
            half = keep.shape[0] // 2
            keep, send = call(halve_body, (shape(half, *keep.shape[1:]),) * 2, keep, come, order)
            come = swap(send, bit)
        return keep, come

    def join(keep, come, order):
        keep, come = halve(keep, come, order)
        return call(join_body, (shape(*keep.shape[1:]), scalar), keep, come, order)

    def back(rinv, message, order, first):
        outs, scratch = (shape(whole // LANE, LANE), scalar), [pltpu.VMEM((width // LANE, LANE), F32)]
        if first:
            outs += (shape(*rinv.shape),)
            scratch += [pltpu.SemaphoreType.DMA((width // LANE,))]
        return pl.pallas_call(
            functools.partial(back_body, first),
            out_shape=outs,
            in_specs=[HBM if first else VMEM, VMEM, VMEM],
            out_specs=(VMEM,) * len(outs),
            scratch_shapes=scratch,
            compiler_params=pltpu.CompilerParams(vmem_limit_bytes=(34 if first else 24) << 20),
            )(rinv, message, order)

    def forward(terms, token, last, *before):
        return call(
            functools.partial(forward_body, len(terms), not before, last),
            (shape(lines, LANE), shape(width // LANE, LANE), scalar)
            + (() if last else (shape(whole // LANE, LANE),)),
            here,
            design,
            token,
            *terms,
            *before,
        )

    def turn(images, left, beta, alpha, last):
        return call(
            functools.partial(turn_body, len(images), last),
            (shape(lines, LANE), shape(row_groups, 8 if last else deep, LANE)),
            *images,
            left,
            beta,
            alpha,
            *(() if last else (design,)),
        )

    betas, alphas, held, joined, right = [], [], [], [], []
    near = spread(range(1), None)
    message = picked = exchange(message, "row")
    token = pl.pallas_call(
        touch_body,
        out_shape=scalar,
        in_specs=[ANY] * len(near) + [VMEM],
        out_specs=VMEM,
        compiler_params=pltpu.CompilerParams(vmem_limit_bytes=2 << 20),
    )(*near, message)
    late = len(sent) - (chunks > 1)
    near += spread(range(1, late), message)
    for step in range(ITERS):
        last = step + 1 == ITERS
        if step == 0:
            term, beta, here = back(rinv, message, token, True)
            mixed = mix(message)
        else:
            term, beta = back(here, message, alpha, False)
            token = beta
            if chunks > 1:
                part, token = join(keep, come, beta)
                joined.append(part)
                keep, send, token = sample(1, mixed, token)
                come = swap(send, row_groups // 2)
        betas.append(beta)
        spare = chunks > 1 and step > 0
        terms = direct(term, "col") if spare else paired(term, "col")
        if step == 0:
            near += spread(range(late, len(sent)), terms[1])
            keep, send, token = sample(0, mixed, beta)
            come = swap(send, row_groups // 2)
        image, kept, alpha, *right = forward(terms, token, last, *right, *betas[1:])
        alphas.append(alpha)
        held.append(kept)
        images = direct(image, "col") if spare else paired(image, "col")
        left, message = turn(images, left, beta, alpha, last)
        message = exchange(message, "row")
    quarters = (shape(slots, width // NEAR),) * NEAR
    mine, *others = call(split_body, quarters, *joined, *halve(keep, come, beta), left)
    basis, answer, sketch = call(
        last_body,
        (shape(lines, LANE), shape(width // LANE, LANE), shape(slots, width)),
        message,
        left,
        *betas,
        *alphas,
        *held,
        mine,
        *(swap(part, mask + 1) for mask, part in enumerate(others)),
    )
    return (sketch, answer.reshape(-1), basis.reshape(-1))


def solution(mesh):
    placed = (
        P("row", "col"),
        P("row"),
        P(None, "row", None),
        P(None, "row"),
        P("row"),
        P("col", None),
    )
    return jax.shard_map(
        shards,
        mesh=mesh,
        in_specs=placed,
        out_specs=(P("row", "col"), P("col"), P("row")),
        check_vma=False,
    )
```

```python
import functools

import jax
import jax.numpy as jnp
import numpy as np
from jax import lax
from jax.experimental import pallas as pl
from jax.experimental.pallas import tpu as pltpu
from jax.sharding import PartitionSpec as P

HB = 256
PAIR = 16
ITERS = 2
LANE = 128
NEAR = 4
CHUNKS = 2
F32 = jnp.float32
VMEM = pl.BlockSpec(memory_space=pltpu.VMEM)
HBM = pl.BlockSpec(memory_space=pltpu.HBM)
ANY = pl.BlockSpec(memory_space=pl.ANY)


def exchange(copies, axis):
    return lax.all_to_all(copies, axis, split_axis=0, concat_axis=0, tiled=True)


def paired(array, axis):
    size = lax.axis_size(axis)
    mask = 1
    while True:
        come = lax.ppermute(array, axis, [(i, i ^ mask) for i in range(size)])
        mask *= 2
        if mask == size:
            return [array, come]
        array = array + come


def direct(array, axis):
    size = lax.axis_size(axis)
    return [array] + [
        lax.ppermute(array, axis, [(i, i ^ mask) for i in range(size)]) for mask in range(1, size)
    ]


def tree(values):
    while len(values) > 1:
        values = [values[i] + values[i + 1] for i in range(0, len(values), 2)]
    return values[0]


def walsh(size):
    index = np.arange(size)
    common = index[:, None] & index[None, :]
    parity = np.zeros((size, size), np.int64)
    for shift in range(size.bit_length()):
        parity ^= (common >> shift) & 1
    return (1 - 2 * parity).astype(np.float32)


def call(body, out_shape, *operands, scratch=()):
    return pl.pallas_call(
        body,
        out_shape=out_shape,
        in_specs=[VMEM] * len(operands),
        out_specs=jax.tree.map(lambda _: VMEM, out_shape),
        scratch_shapes=scratch,
        compiler_params=pltpu.CompilerParams(vmem_limit_bytes=24 << 20),
    )(*operands)


def fold_rows(block):
    return block.reshape(block.shape[0] // 8, 8, LANE).sum(axis=0)


def total(rows):
    return jnp.sum(jnp.sum(rows, axis=0, keepdims=True), axis=1, keepdims=True)


def splat(scalar):
    return jnp.broadcast_to(scalar, (1, LANE))


def left_product(vector, matrix_ref, out_ref):
    blocks, tiles = matrix_ref.shape[0] // LANE, matrix_ref.shape[1] // LANE
    sums = [jnp.zeros((8, LANE), F32) for _ in range(tiles)]
    for block in range(blocks):
        weight = across(vector[block : block + 1, :])
        for tile in range(tiles):
            part = matrix_ref[block * LANE : (block + 1) * LANE, tile * LANE : (tile + 1) * LANE]
            sums[tile] = sums[tile] + fold_rows(part * weight)
    for tile in range(tiles):
        out_ref[tile : tile + 1, :] = jnp.sum(sums[tile], axis=0, keepdims=True)


def left_product_upper(vector_ref, matrix_ref, out_ref, copies=()):
    blocks, tiles = matrix_ref.shape[0] // LANE, matrix_ref.shape[1] // LANE
    sums = [jnp.zeros((8, LANE), F32) for _ in range(tiles)]
    for block in range(blocks):
        if copies:
            copies[block].wait()
        weight = across(vector_ref[block : block + 1, :])
        for tile in range(block, tiles):
            part = matrix_ref[block * LANE : (block + 1) * LANE, tile * LANE : (tile + 1) * LANE]
            sums[tile] = sums[tile] + fold_rows(part * weight)
    for tile in range(tiles):
        out_ref[tile : tile + 1, :] = jnp.sum(sums[tile], axis=0, keepdims=True)


def right_product(matrix_ref, vector, out_ref):
    blocks, tiles = matrix_ref.shape[0] // LANE, matrix_ref.shape[1] // LANE

    def step(block, carry):
        rows = pl.ds(pl.multiple_of(block * LANE, LANE), LANE)
        sums = jnp.zeros((LANE, LANE), F32)
        for tile in range(tiles):
            sums = sums + matrix_ref[rows, tile * LANE : (tile + 1) * LANE] * vector[tile : tile + 1, :]
        out_ref[pl.ds(block, 1), :] = jnp.sum(fold_rows(sums.T), axis=0, keepdims=True)
        return carry

    lax.fori_loop(0, blocks, step, 0)


def right_product_upper(matrix_ref, vector, out_ref):
    blocks, tiles = matrix_ref.shape[0] // LANE, matrix_ref.shape[1] // LANE
    for block in range(blocks):
        rows = slice(block * LANE, (block + 1) * LANE)
        sums = jnp.zeros((LANE, LANE), F32)
        for tile in range(block, tiles):
            sums = sums + matrix_ref[rows, tile * LANE : (tile + 1) * LANE] * vector[tile : tile + 1, :]
        out_ref[block : block + 1, :] = jnp.sum(fold_rows(sums.T), axis=0, keepdims=True)


def rounded(count, unit):
    return -(-count // unit) * unit


def message_rows(width):
    return rounded(width // LANE + 1, 8)


def picks_at(width):
    return width // LANE + 1


def signs_at(width, groups):
    return picks_at(width) + groups * PAIR // LANE


def copy_out(out_ref):
    first = out_ref[0]
    for index in range(1, out_ref.shape[0]):
        out_ref[index] = first


def across(row):
    return jnp.broadcast_to(row, (LANE, LANE)).T


def first_body(sent, design_ref, target_ref, bits_ref, picks_ref, counts_ref, *refs):
    out_ref, away_refs = refs[0], refs[1:-6]
    design, target_here, bits, picks, counts, sems = refs[-6:]
    rows, width = design.shape
    lines, tiles = rows // LANE, width // LANE
    small = [
        pltpu.make_async_copy(source, place, sems.at[index])
        for index, (source, place) in enumerate(
            ((target_ref, target_here), (bits_ref, bits), (picks_ref, picks), (counts_ref, counts))
        )
    ]
    parts = [slice(line * LANE, (line + 1) * LANE) for line in range(lines)]
    large = [
        pltpu.make_async_copy(design_ref.at[part, :], design.at[part, :], sems.at[4 + line])
        for line, part in enumerate(parts)
    ]
    place = lax.axis_index("row") % NEAR
    away = []
    for index, away_ref in enumerate(away_refs):
        piece = away_ref.shape[1]
        mask, start = sent[index]
        column = pl.multiple_of((place ^ mask) * (width // NEAR) + start, LANE)
        for line, part in enumerate(parts):
            source = design.at[part, pl.ds(column, piece)]
            away.append(pltpu.make_async_copy(source, away_ref.at[part, :], sems.at[4 + lines * (index + 1) + line]))
    for copy in small + large:
        copy.start()
    for copy in small:
        copy.wait()
    out_ref[0] = jnp.zeros(out_ref.shape[1:], F32)
    groups = picks.shape[0]
    owner = lax.broadcasted_iota(jnp.int32, (groups, groups), 0)
    same = owner == lax.broadcasted_iota(jnp.int32, (groups, groups), 1)
    limit = jnp.sum(jnp.where(same, counts[...].astype(F32), 0.0), axis=1, keepdims=True)
    slot = lax.broadcasted_iota(jnp.int32, picks.shape, 1).astype(F32)
    coded = jnp.where(slot < limit, picks[...].astype(F32), -1.0)
    start = picks_at(width)
    for owner in range(0, groups, LANE // PAIR):
        line = jnp.concatenate([coded[i : i + 1, :] for i in range(owner, owner + LANE // PAIR)], axis=1)
        out_ref[0, start + owner * PAIR // LANE : start + owner * PAIR // LANE + 1, :] = line
    start = signs_at(width, groups)
    out_ref[0, start : start + lines, :] = (2 * bits[...] - 1).astype(F32)
    target = target_here[...]
    out_ref[0, tiles : tiles + 1, :] = splat(total(target * target))
    sums = [jnp.zeros((8, LANE), F32) for _ in range(tiles)]
    for line, part in enumerate(parts):
        weight = across(target[line : line + 1, :])
        large[line].wait()
        for copy in away[line::lines]:
            copy.start()
        for tile in range(tiles):
            sums[tile] = sums[tile] + fold_rows(design[part, tile * LANE : (tile + 1) * LANE] * weight)
    for tile in range(tiles):
        out_ref[0, tile : tile + 1, :] = jnp.sum(sums[tile], axis=0, keepdims=True)
    copy_out(out_ref)
    for copy in away:
        copy.wait()


def back_body(first, rinv_ref, parts_ref, term_ref, beta_ref, *refs):
    tiles = rinv_ref.shape[0] // LANE
    copies = []
    if first:
        rinv_here, scratch, sems = refs
        for block in range(tiles):
            part, right = slice(block * LANE, (block + 1) * LANE), slice(block * LANE, rinv_ref.shape[1])
            copies.append(pltpu.make_async_copy(rinv_ref.at[part, right], rinv_here.at[part, right], sems.at[block]))
            copies[-1].start()
    else:
        rinv_here, (scratch,) = rinv_ref, refs
    summed = tree([parts_ref[i, : tiles + 1, :] for i in range(parts_ref.shape[0])])
    beta = jnp.sqrt(summed[tiles : tiles + 1, :])
    beta_ref[...] = beta
    scratch[...] = summed[:tiles, :] / beta
    left_product_upper(scratch, rinv_here, term_ref, copies)


def forward_body(groups, first, last, rinv_ref, design_ref, token_ref, *refs):
    right = tree([ref[...] for ref in refs[:groups]])
    refs = refs[groups:]
    if not first:
        before_ref, beta_ref, *refs = refs
        right = right - beta_ref[...] * before_ref[...]
    image_ref, held_ref, alpha_ref, *right_refs = refs
    alpha = jnp.sqrt(total(right * right))
    alpha_ref[...] = splat(alpha)
    right = right / alpha
    if not last:
        right_refs[0][...] = right
    right_product_upper(rinv_ref, right, held_ref)
    right_product(design_ref, held_ref[...], image_ref)


def turn_body(groups, last, *refs):
    left = tree([ref[...] for ref in refs[:groups]])
    before_ref, beta_ref, alpha_ref, *refs = refs[groups:]
    left = left - alpha_ref[...] * (before_ref[...] / beta_ref[...])
    square = splat(total(left * left))
    if last:
        left_ref, out_ref = refs
        out_ref[...] = jnp.broadcast_to(square, out_ref.shape)
    else:
        design_ref, left_ref, out_ref = refs
        tiles = design_ref.shape[1] // LANE
        out_ref[0] = jnp.zeros(out_ref.shape[1:], F32)
        left_product(left, design_ref, out_ref.at[0])
        out_ref[0, tiles : tiles + 1, :] = square
        copy_out(out_ref)
    left_ref[...] = left


def pieces(value):
    high = value.astype(jnp.bfloat16)
    return high, (value - high.astype(F32)).astype(jnp.bfloat16)


def weigh(mix, high, low):
    return jnp.dot(mix, high, preferred_element_type=F32) + jnp.dot(mix, low, preferred_element_type=F32)


def for_blocks(groups, step):
    if groups <= 8:
        for block in range(groups):
            step(block, 0)
    else:
        lax.fori_loop(0, groups, step, 0)


def mix_body(width, parts_ref, walsh_ref, mix_ref):
    groups, _, rows = mix_ref.shape
    me = lax.axis_index("row")
    local = lax.broadcasted_iota(jnp.int32, (LANE, rows), 1).astype(F32)
    per = LANE // PAIR

    def step(block, carry):
        parity = jnp.int32(0)
        for bit in range(groups.bit_length() - 1):
            parity = parity ^ ((block & me) >> bit)
        sign = (1 - 2 * (parity & 1)).astype(F32)
        for line in range(groups // per):
            start = picks_at(width) + line
            coded = across(parts_ref[block, start : start + 1, :])
            match = jnp.concatenate([coded] * (rows // LANE), axis=1) == local
            chosen = jnp.where(match, sign, 0.0).astype(jnp.bfloat16)
            for part in range(rows // HB):
                columns = slice(part * HB, (part + 1) * HB)
                mixed = jnp.dot(chosen[:, columns], walsh_ref[...], preferred_element_type=F32).astype(jnp.bfloat16)
                for index in range(per):
                    place = pl.multiple_of(((line * per + index) ^ me) * PAIR, PAIR)
                    mix_ref[block, pl.ds(place, PAIR), columns] = mixed[index * PAIR : (index + 1) * PAIR, :]
        return carry

    for_blocks(groups, step)


def sample_body(scale, start, design_ref, parts_ref, mix_ref, order_ref, *refs):
    near, (keep_ref, send_ref, token_ref, both) = refs[: NEAR - 1], refs[NEAR - 1 :]
    token_ref[...] = order_ref[:1, :]
    rows, piece = near[-1].shape
    width = design_ref.shape[1]
    groups = mix_ref.shape[0]
    me = lax.axis_index("row")
    signs_start = signs_at(width, groups)
    for line in range(rows // LANE):
        part = slice(line * LANE, (line + 1) * LANE)
        signs = [across(parts_ref[me ^ mask, signs_start + line : signs_start + line + 1, :]) for mask in range(NEAR)]
        for tile in range(0, piece, LANE):
            column = pl.multiple_of(me % NEAR * (width // NEAR) + start + tile, LANE)
            here = slice(tile, tile + LANE)
            values = [design_ref[part, pl.ds(column, LANE)]] + [ref[part, here] for ref in near]
            values = [value * sign for value, sign in zip(values, signs)]
            apart = 1
            while apart < NEAR:
                for first in range(NEAR):
                    if not first & apart:
                        one, two = values[first], values[first | apart]
                        values[first], values[first | apart] = one + two, one - two
                apart *= 2
            for index, value in enumerate(values):
                both[index, 0, part, here], both[index, 1, part, here] = pieces(value)

    def step(block, carry):
        value = weigh(mix_ref[block], both[block % NEAR, 0], both[block % NEAR, 1]) / scale
        slot = pl.ds(block * PAIR, PAIR)
        for apart in range(groups):
            far, low = apart // NEAR, apart % NEAR
            out_ref = send_ref if far >= groups // NEAR // 2 else keep_ref
            out_ref[far % (groups // NEAR // 2), low, slot, :] = value[apart * PAIR : (apart + 1) * PAIR, :]
        return carry

    for_blocks(groups, step)


def halve_body(kept_ref, arrived_ref, order_ref, keep_ref, send_ref):
    half = keep_ref.shape[0]
    keep_ref[...] = kept_ref[:half] + arrived_ref[:half]
    send_ref[...] = kept_ref[half:] + arrived_ref[half:]


def join_body(kept_ref, arrived_ref, order_ref, out_ref, token_ref):
    token_ref[...] = order_ref[:1, :]
    out_ref[...] = kept_ref[0] + arrived_ref[0]


def split_body(*refs):
    *joined, kept_ref, arrived_ref, order_ref = refs[:-NEAR]
    piece = kept_ref.shape[3]
    for index, rows_ref in enumerate(refs[-NEAR:]):
        for chunk, part_ref in enumerate(joined):
            rows_ref[:, chunk * piece : (chunk + 1) * piece] = part_ref[index]
        rows_ref[:, len(joined) * piece :] = kept_ref[0, index] + arrived_ref[0, index]


def pass_body(*refs):
    refs[-1][...] = refs[-2][...]


def last_body(parts_ref, left_ref, *refs):
    basis_ref, solution_ref, sketch_ref = refs[-3:]
    quarters = refs[3 * ITERS : 3 * ITERS + NEAR]
    place = lax.axis_index("row") % NEAR
    piece = quarters[0].shape[1]
    for mask, part_ref in enumerate(quarters):
        for tile in range(0, piece, LANE):
            column = pl.multiple_of((place ^ mask) * piece + tile, LANE)
            sketch_ref[:, pl.ds(column, LANE)] = part_ref[:, tile : tile + LANE]
    betas = [ref[...] for ref in refs[:ITERS]]
    alphas = [ref[...] for ref in refs[ITERS : 2 * ITERS]]
    held = [ref[...] for ref in refs[2 * ITERS : 3 * ITERS]]
    last = jnp.sqrt(tree([parts_ref[i] for i in range(parts_ref.shape[0])])[:1, :])
    basis_ref[...] = left_ref[...] / last
    betas.append(last)
    phibar, rhobar = betas[0], alphas[0]
    search, iterate = held[0], jnp.zeros_like(held[0])
    for step in range(ITERS):
        beta = betas[step + 1]
        rho = jnp.sqrt(rhobar * rhobar + beta * beta)
        cosine = rhobar / rho
        sine = beta / rho
        phi = cosine * phibar
        phibar = sine * phibar
        iterate = iterate + phi / rho * search
        if step + 1 < ITERS:
            alpha = alphas[step + 1]
            search = held[step + 1] - sine * alpha / rho * search
            rhobar = -cosine * alpha
    solution_ref[...] = iterate


def shape(*dims, dtype=F32):
    return jax.ShapeDtypeStruct(dims, dtype)


def shards(design, sign_bits, picks, counts, target, rinv):
    rows, width = design.shape
    whole = rinv.shape[1]
    row_groups = lax.axis_size("row")
    lines = rows // LANE
    scalar = shape(1, LANE)
    deep = message_rows(width)
    left = target.reshape(lines, LANE)
    bits = sign_bits.reshape(lines, LANE)
    chunks = min(CHUNKS, width // NEAR // LANE)
    piece = width // NEAR // chunks
    scale = float(np.sqrt(np.float32(rows * row_groups)))
    slots = row_groups * PAIR
    far = row_groups // NEAR

    sent = [(mask, chunk * piece) for chunk in range(chunks) for mask in range(1, NEAR)]

    message, *away = pl.pallas_call(
        functools.partial(first_body, sent),
        out_shape=(shape(row_groups, rounded(signs_at(width, row_groups) + lines, 8), LANE),)
        + (shape(rows, piece),) * len(sent),
        in_specs=[HBM] * 5,
        out_specs=(VMEM,) + (HBM,) * len(sent),
        scratch_shapes=[
            pltpu.VMEM((rows, width), F32),
            pltpu.VMEM((lines, LANE), F32),
            pltpu.VMEM((lines, LANE), jnp.int32),
            pltpu.VMEM((row_groups, PAIR), jnp.int32),
            pltpu.VMEM((1, row_groups), jnp.int32),
            pltpu.SemaphoreType.DMA((4 + lines * (1 + len(sent)),)),
        ],
        compiler_params=pltpu.CompilerParams(vmem_limit_bytes=58 << 20),
    )(design, left, bits, picks.reshape(row_groups, PAIR), counts.reshape(1, row_groups))

    def swap(array, mask):
        return lax.ppermute(array, "row", [(i, i ^ mask) for i in range(row_groups)])

    def mix(message):
        made = shape(row_groups, slots, rows, dtype=jnp.bfloat16)
        return call(functools.partial(mix_body, width), made, message, jnp.asarray(walsh(HB), jnp.bfloat16))

    def sample(chunk, mixed, order):
        return call(
            functools.partial(sample_body, scale, chunk * piece),
            (shape(far // 2, NEAR, slots, piece),) * 2 + (scalar,),
            design,
            picked,
            mixed,
            order,
            *near[chunk * (NEAR - 1) : (chunk + 1) * (NEAR - 1)],
            scratch=[pltpu.VMEM((NEAR, 2, rows, piece), jnp.bfloat16)],
        )

    def spread(indices, order):
        parts = [away[index] for index in indices]
        if order is not None:
            parts, _ = lax.optimization_barrier((parts, order))
        return [swap(part, sent[index][0]) for index, part in zip(indices, parts)]

    def halve(keep, come, order):
        bit = row_groups // 2
        while bit > NEAR:
            bit //= 2
            half = keep.shape[0] // 2
            keep, send = call(halve_body, (shape(half, *keep.shape[1:]),) * 2, keep, come, order)
            come = swap(send, bit)
        return keep, come

    def join(keep, come, order):
        keep, come = halve(keep, come, order)
        return call(join_body, (shape(*keep.shape[1:]), scalar), keep, come, order)

    def back(rinv, message, first):
        outs, scratch = (shape(whole // LANE, LANE), scalar), [pltpu.VMEM((width // LANE, LANE), F32)]
        if first:
            outs += (shape(*rinv.shape),)
            scratch += [pltpu.SemaphoreType.DMA((width // LANE,))]
        return pl.pallas_call(
            functools.partial(back_body, first),
            out_shape=outs,
            in_specs=[HBM if first else VMEM, VMEM],
            out_specs=(VMEM,) * len(outs),
            scratch_shapes=scratch,
            compiler_params=pltpu.CompilerParams(vmem_limit_bytes=(34 if first else 24) << 20),
            )(rinv, message)

    def forward(terms, token, last, *before):
        return call(
            functools.partial(forward_body, len(terms), not before, last),
            (shape(lines, LANE), shape(width // LANE, LANE), scalar)
            + (() if last else (shape(whole // LANE, LANE),)),
            here,
            design,
            token,
            *terms,
            *before,
        )

    def turn(images, left, beta, alpha, last):
        return call(
            functools.partial(turn_body, len(images), last),
            (shape(lines, LANE), shape(row_groups, 8 if last else deep, LANE)),
            *images,
            left,
            beta,
            alpha,
            *(() if last else (design,)),
        )

    betas, alphas, held, joined, right = [], [], [], [], []
    near = spread(range(1), None)
    message = picked = exchange(message, "row")
    late = len(sent) - (chunks > 1)
    near += spread(range(1, late), message)
    for step in range(ITERS):
        last = step + 1 == ITERS
        if step == 0:
            term, beta, here = back(rinv, message, True)
            term = pl.pallas_call(
                pass_body,
                out_shape=shape(*term.shape),
                in_specs=[ANY, VMEM],
                out_specs=VMEM,
                compiler_params=pltpu.CompilerParams(vmem_limit_bytes=2 << 20),
            )(near[0], term)
            mixed = mix(message)
        else:
            term, beta = back(here, message, False)
            token = beta
            if chunks > 1:
                part, token = join(keep, come, beta)
                joined.append(part)
                keep, send, token = sample(1, mixed, token)
                come = swap(send, row_groups // 2)
        betas.append(beta)
        spare = chunks > 1 and step > 0
        terms = direct(term, "col") if spare else paired(term, "col")
        if step == 0:
            near += spread(range(late, len(sent)), terms[1])
            keep, send, token = sample(0, mixed, beta)
            come = swap(send, row_groups // 2)
        image, kept, alpha, *right = forward(terms, token, last, *right, *betas[1:])
        alphas.append(alpha)
        held.append(kept)
        images = direct(image, "col") if spare else paired(image, "col")
        left, message = turn(images, left, beta, alpha, last)
        message = exchange(message, "row")
    quarters = (shape(slots, width // NEAR),) * NEAR
    mine, *others = call(split_body, quarters, *joined, *halve(keep, come, beta), left)
    basis, answer, sketch = call(
        last_body,
        (shape(lines, LANE), shape(width // LANE, LANE), shape(slots, width)),
        message,
        left,
        *betas,
        *alphas,
        *held,
        mine,
        *(swap(part, mask + 1) for mask, part in enumerate(others)),
    )
    return (sketch, answer.reshape(-1), basis.reshape(-1))


def solution(mesh):
    placed = (
        P("row", "col"),
        P("row"),
        P(None, "row", None),
        P(None, "row"),
        P("row"),
        P("col", None),
    )
    return jax.shard_map(
        shards,
        mesh=mesh,
        in_specs=placed,
        out_specs=(P("row", "col"), P("col"), P("row")),
        check_vma=False,
    )
```

```python
import functools

import jax
import jax.numpy as jnp
import numpy as np
from jax import lax
from jax.experimental import pallas as pl
from jax.experimental.pallas import tpu as pltpu
from jax.sharding import PartitionSpec as P

HB = 256
PAIR = 16
ITERS = 2
LANE = 128
NEAR = 4
CHUNKS = 2
F32 = jnp.float32
VMEM = pl.BlockSpec(memory_space=pltpu.VMEM)
HBM = pl.BlockSpec(memory_space=pltpu.HBM)
ANY = pl.BlockSpec(memory_space=pl.ANY)


def exchange(copies, axis):
    return lax.all_to_all(copies, axis, split_axis=0, concat_axis=0, tiled=True)


def paired(array, axis):
    size = lax.axis_size(axis)
    mask = 1
    while True:
        come = lax.ppermute(array, axis, [(i, i ^ mask) for i in range(size)])
        mask *= 2
        if mask == size:
            return [array, come]
        array = array + come


def direct(array, axis):
    size = lax.axis_size(axis)
    return [array] + [
        lax.ppermute(array, axis, [(i, i ^ mask) for i in range(size)]) for mask in range(1, size)
    ]


def tree(values):
    while len(values) > 1:
        values = [values[i] + values[i + 1] for i in range(0, len(values), 2)]
    return values[0]


def walsh(size):
    index = np.arange(size)
    common = index[:, None] & index[None, :]
    parity = np.zeros((size, size), np.int64)
    for shift in range(size.bit_length()):
        parity ^= (common >> shift) & 1
    return (1 - 2 * parity).astype(np.float32)


def call(body, out_shape, *operands, scratch=()):
    return pl.pallas_call(
        body,
        out_shape=out_shape,
        in_specs=[VMEM] * len(operands),
        out_specs=jax.tree.map(lambda _: VMEM, out_shape),
        scratch_shapes=scratch,
        compiler_params=pltpu.CompilerParams(vmem_limit_bytes=24 << 20),
    )(*operands)


def fold_rows(block):
    return block.reshape(block.shape[0] // 8, 8, LANE).sum(axis=0)


def total(rows):
    return jnp.sum(jnp.sum(rows, axis=0, keepdims=True), axis=1, keepdims=True)


def splat(scalar):
    return jnp.broadcast_to(scalar, (1, LANE))


def left_product(vector, matrix_ref, out_ref):
    blocks, tiles = matrix_ref.shape[0] // LANE, matrix_ref.shape[1] // LANE
    sums = [jnp.zeros((8, LANE), F32) for _ in range(tiles)]
    for block in range(blocks):
        weight = across(vector[block : block + 1, :])
        for tile in range(tiles):
            part = matrix_ref[block * LANE : (block + 1) * LANE, tile * LANE : (tile + 1) * LANE]
            sums[tile] = sums[tile] + fold_rows(part * weight)
    for tile in range(tiles):
        out_ref[tile : tile + 1, :] = jnp.sum(sums[tile], axis=0, keepdims=True)


def left_product_upper(vector_ref, matrix_ref, out_ref, copies=()):
    blocks, tiles = matrix_ref.shape[0] // LANE, matrix_ref.shape[1] // LANE
    sums = [jnp.zeros((8, LANE), F32) for _ in range(tiles)]
    for block in range(blocks):
        if copies:
            copies[block].wait()
        weight = across(vector_ref[block : block + 1, :])
        for tile in range(block, tiles):
            part = matrix_ref[block * LANE : (block + 1) * LANE, tile * LANE : (tile + 1) * LANE]
            sums[tile] = sums[tile] + fold_rows(part * weight)
    for tile in range(tiles):
        out_ref[tile : tile + 1, :] = jnp.sum(sums[tile], axis=0, keepdims=True)


def right_product(matrix_ref, vector, out_ref):
    blocks, tiles = matrix_ref.shape[0] // LANE, matrix_ref.shape[1] // LANE

    def step(block, carry):
        rows = pl.ds(pl.multiple_of(block * LANE, LANE), LANE)
        sums = jnp.zeros((LANE, LANE), F32)
        for tile in range(tiles):
            sums = sums + matrix_ref[rows, tile * LANE : (tile + 1) * LANE] * vector[tile : tile + 1, :]
        out_ref[pl.ds(block, 1), :] = jnp.sum(fold_rows(sums.T), axis=0, keepdims=True)
        return carry

    lax.fori_loop(0, blocks, step, 0)


def right_product_upper(matrix_ref, vector, out_ref):
    blocks, tiles = matrix_ref.shape[0] // LANE, matrix_ref.shape[1] // LANE
    for block in range(blocks):
        rows = slice(block * LANE, (block + 1) * LANE)
        sums = jnp.zeros((LANE, LANE), F32)
        for tile in range(block, tiles):
            sums = sums + matrix_ref[rows, tile * LANE : (tile + 1) * LANE] * vector[tile : tile + 1, :]
        out_ref[block : block + 1, :] = jnp.sum(fold_rows(sums.T), axis=0, keepdims=True)


def rounded(count, unit):
    return -(-count // unit) * unit


def message_rows(width):
    return rounded(width // LANE + 1, 8)


def picks_at(width):
    return width // LANE + 1


def signs_at(width, groups):
    return picks_at(width) + groups * PAIR // LANE


def copy_out(out_ref):
    first = out_ref[0]
    for index in range(1, out_ref.shape[0]):
        out_ref[index] = first


def across(row):
    return jnp.broadcast_to(row, (LANE, LANE)).T


def first_body(sent, design_ref, target_ref, bits_ref, picks_ref, counts_ref, *refs):
    out_ref, away_refs = refs[0], refs[1:-6]
    design, target_here, bits, picks, counts, sems = refs[-6:]
    rows, width = design.shape
    lines, tiles = rows // LANE, width // LANE
    small = [
        pltpu.make_async_copy(source, place, sems.at[index])
        for index, (source, place) in enumerate(
            ((target_ref, target_here), (bits_ref, bits), (picks_ref, picks), (counts_ref, counts))
        )
    ]
    parts = [slice(line * LANE, (line + 1) * LANE) for line in range(lines)]
    large = [
        pltpu.make_async_copy(design_ref.at[part, :], design.at[part, :], sems.at[4 + line])
        for line, part in enumerate(parts)
    ]
    place = lax.axis_index("row") % NEAR
    away = []
    for index, away_ref in enumerate(away_refs):
        piece = away_ref.shape[1]
        mask, start = sent[index]
        column = pl.multiple_of((place ^ mask) * (width // NEAR) + start, LANE)
        for line, part in enumerate(parts):
            source = design.at[part, pl.ds(column, piece)]
            away.append(pltpu.make_async_copy(source, away_ref.at[part, :], sems.at[4 + lines * (index + 1) + line]))
    for copy in small + large:
        copy.start()
    for copy in small:
        copy.wait()
    out_ref[0] = jnp.zeros(out_ref.shape[1:], F32)
    groups = picks.shape[0]
    owner = lax.broadcasted_iota(jnp.int32, (groups, groups), 0)
    same = owner == lax.broadcasted_iota(jnp.int32, (groups, groups), 1)
    limit = jnp.sum(jnp.where(same, counts[...].astype(F32), 0.0), axis=1, keepdims=True)
    slot = lax.broadcasted_iota(jnp.int32, picks.shape, 1).astype(F32)
    coded = jnp.where(slot < limit, picks[...].astype(F32), -1.0)
    start = picks_at(width)
    for owner in range(0, groups, LANE // PAIR):
        line = jnp.concatenate([coded[i : i + 1, :] for i in range(owner, owner + LANE // PAIR)], axis=1)
        out_ref[0, start + owner * PAIR // LANE : start + owner * PAIR // LANE + 1, :] = line
    start = signs_at(width, groups)
    out_ref[0, start : start + lines, :] = (2 * bits[...] - 1).astype(F32)
    target = target_here[...]
    out_ref[0, tiles : tiles + 1, :] = splat(total(target * target))
    sums = [jnp.zeros((8, LANE), F32) for _ in range(tiles)]
    for line, part in enumerate(parts):
        weight = across(target[line : line + 1, :])
        large[line].wait()
        for copy in away[line::lines]:
            copy.start()
        for tile in range(tiles):
            sums[tile] = sums[tile] + fold_rows(design[part, tile * LANE : (tile + 1) * LANE] * weight)
    for tile in range(tiles):
        out_ref[0, tile : tile + 1, :] = jnp.sum(sums[tile], axis=0, keepdims=True)
    copy_out(out_ref)
    for copy in away:
        copy.wait()


def back_body(first, rinv_ref, parts_ref, term_ref, beta_ref, *refs):
    tiles = rinv_ref.shape[0] // LANE
    copies = []
    if first:
        rinv_here, scratch, sems = refs
        for block in range(tiles):
            part, right = slice(block * LANE, (block + 1) * LANE), slice(block * LANE, rinv_ref.shape[1])
            copies.append(pltpu.make_async_copy(rinv_ref.at[part, right], rinv_here.at[part, right], sems.at[block]))
            copies[-1].start()
    else:
        rinv_here, (scratch,) = rinv_ref, refs
    summed = tree([parts_ref[i, : tiles + 1, :] for i in range(parts_ref.shape[0])])
    beta = jnp.sqrt(summed[tiles : tiles + 1, :])
    beta_ref[...] = beta
    scratch[...] = summed[:tiles, :] / beta
    left_product_upper(scratch, rinv_here, term_ref, copies)


def forward_body(groups, first, last, rinv_ref, design_ref, token_ref, *refs):
    right = tree([ref[...] for ref in refs[:groups]])
    refs = refs[groups:]
    if not first:
        before_ref, beta_ref, *refs = refs
        right = right - beta_ref[...] * before_ref[...]
    image_ref, held_ref, alpha_ref, *right_refs = refs
    alpha = jnp.sqrt(total(right * right))
    alpha_ref[...] = splat(alpha)
    right = right / alpha
    if not last:
        right_refs[0][...] = right
    right_product_upper(rinv_ref, right, held_ref)
    right_product(design_ref, held_ref[...], image_ref)


def turn_body(groups, last, *refs):
    left = tree([ref[...] for ref in refs[:groups]])
    before_ref, beta_ref, alpha_ref, *refs = refs[groups:]
    left = left - alpha_ref[...] * (before_ref[...] / beta_ref[...])
    square = splat(total(left * left))
    if last:
        left_ref, out_ref = refs
        out_ref[...] = jnp.broadcast_to(square, out_ref.shape)
    else:
        design_ref, left_ref, out_ref = refs
        tiles = design_ref.shape[1] // LANE
        out_ref[0] = jnp.zeros(out_ref.shape[1:], F32)
        left_product(left, design_ref, out_ref.at[0])
        out_ref[0, tiles : tiles + 1, :] = square
        copy_out(out_ref)
    left_ref[...] = left


def pieces(value):
    high = value.astype(jnp.bfloat16)
    return high, (value - high.astype(F32)).astype(jnp.bfloat16)


def weigh(mix, high, low):
    return jnp.dot(mix, high, preferred_element_type=F32) + jnp.dot(mix, low, preferred_element_type=F32)


def for_blocks(groups, step):
    if groups <= 8:
        for block in range(groups):
            step(block, 0)
    else:
        lax.fori_loop(0, groups, step, 0)


def mix_body(width, parts_ref, walsh_ref, mix_ref):
    groups, _, rows = mix_ref.shape
    me = lax.axis_index("row")
    local = lax.broadcasted_iota(jnp.int32, (LANE, rows), 1).astype(F32)
    per = LANE // PAIR

    def step(block, carry):
        parity = jnp.int32(0)
        for bit in range(groups.bit_length() - 1):
            parity = parity ^ ((block & me) >> bit)
        sign = (1 - 2 * (parity & 1)).astype(F32)
        for line in range(groups // per):
            start = picks_at(width) + line
            coded = across(parts_ref[block, start : start + 1, :])
            match = jnp.concatenate([coded] * (rows // LANE), axis=1) == local
            chosen = jnp.where(match, sign, 0.0).astype(jnp.bfloat16)
            for part in range(rows // HB):
                columns = slice(part * HB, (part + 1) * HB)
                mixed = jnp.dot(chosen[:, columns], walsh_ref[...], preferred_element_type=F32).astype(jnp.bfloat16)
                for index in range(per):
                    place = pl.multiple_of(((line * per + index) ^ me) * PAIR, PAIR)
                    mix_ref[block, pl.ds(place, PAIR), columns] = mixed[index * PAIR : (index + 1) * PAIR, :]
        return carry

    for_blocks(groups, step)


def sample_body(scale, start, design_ref, parts_ref, mix_ref, order_ref, *refs):
    near, (keep_ref, send_ref, token_ref, both) = refs[: NEAR - 1], refs[NEAR - 1 :]
    token_ref[...] = first_row(order_ref)
    rows, piece = near[-1].shape
    width = design_ref.shape[1]
    groups = mix_ref.shape[0]
    me = lax.axis_index("row")
    signs_start = signs_at(width, groups)
    for line in range(rows // LANE):
        part = slice(line * LANE, (line + 1) * LANE)
        signs = [across(parts_ref[me ^ mask, signs_start + line : signs_start + line + 1, :]) for mask in range(NEAR)]
        for tile in range(0, piece, LANE):
            column = pl.multiple_of(me % NEAR * (width // NEAR) + start + tile, LANE)
            here = slice(tile, tile + LANE)
            values = [design_ref[part, pl.ds(column, LANE)]] + [ref[part, here] for ref in near]
            values = [value * sign for value, sign in zip(values, signs)]
            apart = 1
            while apart < NEAR:
                for first in range(NEAR):
                    if not first & apart:
                        one, two = values[first], values[first | apart]
                        values[first], values[first | apart] = one + two, one - two
                apart *= 2
            for index, value in enumerate(values):
                both[index, 0, part, here], both[index, 1, part, here] = pieces(value)

    def step(block, carry):
        value = weigh(mix_ref[block], both[block % NEAR, 0], both[block % NEAR, 1]) / scale
        slot = pl.ds(block * PAIR, PAIR)
        for apart in range(groups):
            far, low = apart // NEAR, apart % NEAR
            out_ref = send_ref if far >= groups // NEAR // 2 else keep_ref
            out_ref[far % (groups // NEAR // 2), low, slot, :] = value[apart * PAIR : (apart + 1) * PAIR, :]
        return carry

    for_blocks(groups, step)


def halve_body(kept_ref, arrived_ref, order_ref, keep_ref, send_ref):
    half = keep_ref.shape[0]
    keep_ref[...] = kept_ref[:half] + arrived_ref[:half]
    send_ref[...] = kept_ref[half:] + arrived_ref[half:]


def first_row(ref):
    return ref[:1, :] if len(ref.shape) == 2 else ref[0, :1, :]


def join_body(kept_ref, arrived_ref, order_ref, out_ref, token_ref):
    token_ref[...] = first_row(order_ref)
    out_ref[...] = kept_ref[0] + arrived_ref[0]


def split_body(*refs):
    *joined, kept_ref, arrived_ref, order_ref = refs[:-NEAR]
    piece = kept_ref.shape[3]
    for index, rows_ref in enumerate(refs[-NEAR:]):
        for chunk, part_ref in enumerate(joined):
            rows_ref[:, chunk * piece : (chunk + 1) * piece] = part_ref[index]
        rows_ref[:, len(joined) * piece :] = kept_ref[0, index] + arrived_ref[0, index]


def pass_body(*refs):
    refs[-1][...] = refs[-2][...]


def last_body(parts_ref, left_ref, *refs):
    basis_ref, solution_ref, sketch_ref = refs[-3:]
    quarters = refs[3 * ITERS : 3 * ITERS + NEAR]
    place = lax.axis_index("row") % NEAR
    piece = quarters[0].shape[1]
    for mask, part_ref in enumerate(quarters):
        for tile in range(0, piece, LANE):
            column = pl.multiple_of((place ^ mask) * piece + tile, LANE)
            sketch_ref[:, pl.ds(column, LANE)] = part_ref[:, tile : tile + LANE]
    betas = [ref[...] for ref in refs[:ITERS]]
    alphas = [ref[...] for ref in refs[ITERS : 2 * ITERS]]
    held = [ref[...] for ref in refs[2 * ITERS : 3 * ITERS]]
    last = jnp.sqrt(tree([parts_ref[i] for i in range(parts_ref.shape[0])])[:1, :])
    basis_ref[...] = left_ref[...] / last
    betas.append(last)
    phibar, rhobar = betas[0], alphas[0]
    search, iterate = held[0], jnp.zeros_like(held[0])
    for step in range(ITERS):
        beta = betas[step + 1]
        rho = jnp.sqrt(rhobar * rhobar + beta * beta)
        cosine = rhobar / rho
        sine = beta / rho
        phi = cosine * phibar
        phibar = sine * phibar
        iterate = iterate + phi / rho * search
        if step + 1 < ITERS:
            alpha = alphas[step + 1]
            search = held[step + 1] - sine * alpha / rho * search
            rhobar = -cosine * alpha
    solution_ref[...] = iterate


def shape(*dims, dtype=F32):
    return jax.ShapeDtypeStruct(dims, dtype)


def shards(design, sign_bits, picks, counts, target, rinv):
    rows, width = design.shape
    whole = rinv.shape[1]
    row_groups = lax.axis_size("row")
    lines = rows // LANE
    scalar = shape(1, LANE)
    deep = message_rows(width)
    left = target.reshape(lines, LANE)
    bits = sign_bits.reshape(lines, LANE)
    chunks = min(CHUNKS, width // NEAR // LANE)
    piece = width // NEAR // chunks
    scale = float(np.sqrt(np.float32(rows * row_groups)))
    slots = row_groups * PAIR
    far = row_groups // NEAR

    sent = [(mask, chunk * piece) for chunk in range(chunks) for mask in range(1, NEAR)]

    message, *away = pl.pallas_call(
        functools.partial(first_body, sent),
        out_shape=(shape(row_groups, rounded(signs_at(width, row_groups) + lines, 8), LANE),)
        + (shape(rows, piece),) * len(sent),
        in_specs=[HBM] * 5,
        out_specs=(VMEM,) + (HBM,) * len(sent),
        scratch_shapes=[
            pltpu.VMEM((rows, width), F32),
            pltpu.VMEM((lines, LANE), F32),
            pltpu.VMEM((lines, LANE), jnp.int32),
            pltpu.VMEM((row_groups, PAIR), jnp.int32),
            pltpu.VMEM((1, row_groups), jnp.int32),
            pltpu.SemaphoreType.DMA((4 + lines * (1 + len(sent)),)),
        ],
        compiler_params=pltpu.CompilerParams(vmem_limit_bytes=58 << 20),
    )(design, left, bits, picks.reshape(row_groups, PAIR), counts.reshape(1, row_groups))

    def swap(array, mask):
        return lax.ppermute(array, "row", [(i, i ^ mask) for i in range(row_groups)])

    def mix(message):
        made = shape(row_groups, slots, rows, dtype=jnp.bfloat16)
        return call(functools.partial(mix_body, width), made, message, jnp.asarray(walsh(HB), jnp.bfloat16))

    def sample(chunk, mixed, order):
        return call(
            functools.partial(sample_body, scale, chunk * piece),
            (shape(far // 2, NEAR, slots, piece),) * 2 + (scalar,),
            design,
            picked,
            mixed,
            order,
            *near[chunk * (NEAR - 1) : (chunk + 1) * (NEAR - 1)],
            scratch=[pltpu.VMEM((NEAR, 2, rows, piece), jnp.bfloat16)],
        )

    def spread(indices, order):
        parts = [away[index] for index in indices]
        if order is not None:
            parts, _ = lax.optimization_barrier((parts, order))
        return [swap(part, sent[index][0]) for index, part in zip(indices, parts)]

    def halve(keep, come, order):
        bit = row_groups // 2
        while bit > NEAR:
            bit //= 2
            half = keep.shape[0] // 2
            keep, send = call(halve_body, (shape(half, *keep.shape[1:]),) * 2, keep, come, order)
            come = swap(send, bit)
        return keep, come

    def join(keep, come, order):
        keep, come = halve(keep, come, order)
        return call(join_body, (shape(*keep.shape[1:]), scalar), keep, come, order)

    def back(rinv, message, first):
        outs, scratch = (shape(whole // LANE, LANE), scalar), [pltpu.VMEM((width // LANE, LANE), F32)]
        if first:
            outs += (shape(*rinv.shape),)
            scratch += [pltpu.SemaphoreType.DMA((width // LANE,))]
        return pl.pallas_call(
            functools.partial(back_body, first),
            out_shape=outs,
            in_specs=[HBM if first else VMEM, VMEM],
            out_specs=(VMEM,) * len(outs),
            scratch_shapes=scratch,
            compiler_params=pltpu.CompilerParams(vmem_limit_bytes=(34 if first else 24) << 20),
            )(rinv, message)

    def forward(terms, token, last, *before):
        return call(
            functools.partial(forward_body, len(terms), not before, last),
            (shape(lines, LANE), shape(width // LANE, LANE), scalar)
            + (() if last else (shape(whole // LANE, LANE),)),
            here,
            design,
            token,
            *terms,
            *before,
        )

    def turn(images, left, beta, alpha, last):
        return call(
            functools.partial(turn_body, len(images), last),
            (shape(lines, LANE), shape(row_groups, 8 if last else deep, LANE)),
            *images,
            left,
            beta,
            alpha,
            *(() if last else (design,)),
        )

    betas, alphas, held, joined, right = [], [], [], [], []
    near = spread(range(NEAR - 2), None)
    message = picked = exchange(message, "row")
    late = len(sent) - (chunks > 1)
    near += spread(range(NEAR - 2, late), message)
    for step in range(ITERS):
        last = step + 1 == ITERS
        if step == 0:
            term, beta, here = back(rinv, message, True)
            term = pl.pallas_call(
                pass_body,
                out_shape=shape(*term.shape),
                in_specs=[ANY] * (NEAR - 2) + [VMEM],
                out_specs=VMEM,
                compiler_params=pltpu.CompilerParams(vmem_limit_bytes=2 << 20),
            )(*near[: NEAR - 2], term)
            mixed = mix(message)
        else:
            term, beta = back(here, message, False)
            token = beta
            if chunks > 1:
                part, token = join(keep, come, message)
                joined.append(part)
                keep, send, token = sample(1, mixed, token)
                come = swap(send, row_groups // 2)
        betas.append(beta)
        spare = chunks > 1 and step > 0
        terms = direct(term, "col") if spare else paired(term, "col")
        if step == 0:
            near += spread(range(late, len(sent)), terms[1])
            keep, send, token = sample(0, mixed, beta)
            come = swap(send, row_groups // 2)
        image, kept, alpha, *right = forward(terms, token, last, *right, *betas[1:])
        alphas.append(alpha)
        held.append(kept)
        images = direct(image, "col") if spare else paired(image, "col")
        left, message = turn(images, left, beta, alpha, last)
        message = exchange(message, "row")
    quarters = (shape(slots, width // NEAR),) * NEAR
    mine, *others = call(split_body, quarters, *joined, *halve(keep, come, beta), left)
    basis, answer, sketch = call(
        last_body,
        (shape(lines, LANE), shape(width // LANE, LANE), shape(slots, width)),
        message,
        left,
        *betas,
        *alphas,
        *held,
        mine,
        *(swap(part, mask + 1) for mask, part in enumerate(others)),
    )
    return (sketch, answer.reshape(-1), basis.reshape(-1))


def solution(mesh):
    placed = (
        P("row", "col"),
        P("row"),
        P(None, "row", None),
        P(None, "row"),
        P("row"),
        P("col", None),
    )
    return jax.shard_map(
        shards,
        mesh=mesh,
        in_specs=placed,
        out_specs=(P("row", "col"), P("col"), P("row")),
        check_vma=False,
    )
```

```python
import functools

import jax
import jax.numpy as jnp
import numpy as np
from jax import lax
from jax.experimental import pallas as pl
from jax.experimental.pallas import tpu as pltpu
from jax.sharding import PartitionSpec as P

HB = 256
PAIR = 16
ITERS = 2
LANE = 128
NEAR = 4
CHUNKS = 2
F32 = jnp.float32
VMEM = pl.BlockSpec(memory_space=pltpu.VMEM)
HBM = pl.BlockSpec(memory_space=pltpu.HBM)
ANY = pl.BlockSpec(memory_space=pl.ANY)


def exchange(copies, axis):
    return lax.all_to_all(copies, axis, split_axis=0, concat_axis=0, tiled=True)


def paired(array, axis):
    size = lax.axis_size(axis)
    mask = 1
    while True:
        come = lax.ppermute(array, axis, [(i, i ^ mask) for i in range(size)])
        mask *= 2
        if mask == size:
            return [array, come]
        array = array + come


def direct(array, axis):
    size = lax.axis_size(axis)
    return [array] + [
        lax.ppermute(array, axis, [(i, i ^ mask) for i in range(size)]) for mask in range(1, size)
    ]


def tree(values):
    while len(values) > 1:
        values = [values[i] + values[i + 1] for i in range(0, len(values), 2)]
    return values[0]


def walsh(size):
    index = np.arange(size)
    common = index[:, None] & index[None, :]
    parity = np.zeros((size, size), np.int64)
    for shift in range(size.bit_length()):
        parity ^= (common >> shift) & 1
    return (1 - 2 * parity).astype(np.float32)


def call(body, out_shape, *operands, scratch=()):
    return pl.pallas_call(
        body,
        out_shape=out_shape,
        in_specs=[VMEM] * len(operands),
        out_specs=jax.tree.map(lambda _: VMEM, out_shape),
        scratch_shapes=scratch,
        compiler_params=pltpu.CompilerParams(vmem_limit_bytes=24 << 20),
    )(*operands)


def fold_rows(block):
    return block.reshape(block.shape[0] // 8, 8, LANE).sum(axis=0)


def total(rows):
    return jnp.sum(jnp.sum(rows, axis=0, keepdims=True), axis=1, keepdims=True)


def splat(scalar):
    return jnp.broadcast_to(scalar, (1, LANE))


def left_product(vector, matrix_ref, out_ref):
    blocks, tiles = matrix_ref.shape[0] // LANE, matrix_ref.shape[1] // LANE
    sums = [jnp.zeros((8, LANE), F32) for _ in range(tiles)]
    for block in range(blocks):
        weight = across(vector[block : block + 1, :])
        for tile in range(tiles):
            part = matrix_ref[block * LANE : (block + 1) * LANE, tile * LANE : (tile + 1) * LANE]
            sums[tile] = sums[tile] + fold_rows(part * weight)
    for tile in range(tiles):
        out_ref[tile : tile + 1, :] = jnp.sum(sums[tile], axis=0, keepdims=True)


def left_product_upper(vector_ref, matrix_ref, out_ref, copies=()):
    blocks, tiles = matrix_ref.shape[0] // LANE, matrix_ref.shape[1] // LANE
    sums = [jnp.zeros((8, LANE), F32) for _ in range(tiles)]
    for block in range(blocks):
        if copies:
            copies[block].wait()
        weight = across(vector_ref[block : block + 1, :])
        for tile in range(block, tiles):
            part = matrix_ref[block * LANE : (block + 1) * LANE, tile * LANE : (tile + 1) * LANE]
            sums[tile] = sums[tile] + fold_rows(part * weight)
    for tile in range(tiles):
        out_ref[tile : tile + 1, :] = jnp.sum(sums[tile], axis=0, keepdims=True)


def right_product(matrix_ref, vector, out_ref):
    blocks, tiles = matrix_ref.shape[0] // LANE, matrix_ref.shape[1] // LANE

    def step(block, carry):
        rows = pl.ds(pl.multiple_of(block * LANE, LANE), LANE)
        sums = jnp.zeros((LANE, LANE), F32)
        for tile in range(tiles):
            sums = sums + matrix_ref[rows, tile * LANE : (tile + 1) * LANE] * vector[tile : tile + 1, :]
        out_ref[pl.ds(block, 1), :] = jnp.sum(fold_rows(sums.T), axis=0, keepdims=True)
        return carry

    lax.fori_loop(0, blocks, step, 0)


def right_product_upper(matrix_ref, vector, out_ref):
    blocks, tiles = matrix_ref.shape[0] // LANE, matrix_ref.shape[1] // LANE
    for block in range(blocks):
        rows = slice(block * LANE, (block + 1) * LANE)
        sums = jnp.zeros((LANE, LANE), F32)
        for tile in range(block, tiles):
            sums = sums + matrix_ref[rows, tile * LANE : (tile + 1) * LANE] * vector[tile : tile + 1, :]
        out_ref[block : block + 1, :] = jnp.sum(fold_rows(sums.T), axis=0, keepdims=True)


def rounded(count, unit):
    return -(-count // unit) * unit


def message_rows(width):
    return rounded(width // LANE + 1, 8)


def picks_at(width):
    return width // LANE + 1


def signs_at(width, groups):
    return picks_at(width) + groups * PAIR // LANE


def copy_out(out_ref):
    first = out_ref[0]
    for index in range(1, out_ref.shape[0]):
        out_ref[index] = first


def across(row):
    return jnp.broadcast_to(row, (LANE, LANE)).T


def first_body(sent, design_ref, target_ref, bits_ref, picks_ref, counts_ref, *refs):
    out_ref, away_refs = refs[0], refs[1:-6]
    design, target_here, bits, picks, counts, sems = refs[-6:]
    rows, width = design.shape
    lines, tiles = rows // LANE, width // LANE
    small = [
        pltpu.make_async_copy(source, place, sems.at[index])
        for index, (source, place) in enumerate(
            ((target_ref, target_here), (bits_ref, bits), (picks_ref, picks), (counts_ref, counts))
        )
    ]
    parts = [slice(line * LANE, (line + 1) * LANE) for line in range(lines)]
    large = [
        pltpu.make_async_copy(design_ref.at[part, :], design.at[part, :], sems.at[4 + line])
        for line, part in enumerate(parts)
    ]
    place = lax.axis_index("row") % NEAR
    away = []
    for index, away_ref in enumerate(away_refs):
        piece = away_ref.shape[1]
        mask, start = sent[index]
        column = pl.multiple_of((place ^ mask) * (width // NEAR) + start, LANE)
        for line, part in enumerate(parts):
            source = design.at[part, pl.ds(column, piece)]
            away.append(pltpu.make_async_copy(source, away_ref.at[part, :], sems.at[4 + lines * (index + 1) + line]))
    for copy in small + large:
        copy.start()
    for copy in small:
        copy.wait()
    out_ref[0] = jnp.zeros(out_ref.shape[1:], F32)
    groups = picks.shape[0]
    owner = lax.broadcasted_iota(jnp.int32, (groups, groups), 0)
    same = owner == lax.broadcasted_iota(jnp.int32, (groups, groups), 1)
    limit = jnp.sum(jnp.where(same, counts[...].astype(F32), 0.0), axis=1, keepdims=True)
    slot = lax.broadcasted_iota(jnp.int32, picks.shape, 1).astype(F32)
    coded = jnp.where(slot < limit, picks[...].astype(F32), -1.0)
    start = picks_at(width)
    for owner in range(0, groups, LANE // PAIR):
        line = jnp.concatenate([coded[i : i + 1, :] for i in range(owner, owner + LANE // PAIR)], axis=1)
        out_ref[0, start + owner * PAIR // LANE : start + owner * PAIR // LANE + 1, :] = line
    start = signs_at(width, groups)
    out_ref[0, start : start + lines, :] = (2 * bits[...] - 1).astype(F32)
    target = target_here[...]
    out_ref[0, tiles : tiles + 1, :] = splat(total(target * target))
    sums = [jnp.zeros((8, LANE), F32) for _ in range(tiles)]
    for line, part in enumerate(parts):
        weight = across(target[line : line + 1, :])
        large[line].wait()
        for copy in away[line::lines]:
            copy.start()
        for tile in range(tiles):
            sums[tile] = sums[tile] + fold_rows(design[part, tile * LANE : (tile + 1) * LANE] * weight)
    for tile in range(tiles):
        out_ref[0, tile : tile + 1, :] = jnp.sum(sums[tile], axis=0, keepdims=True)
    copy_out(out_ref)
    for copy in away:
        copy.wait()


def back_body(first, rinv_ref, parts_ref, term_ref, beta_ref, *refs):
    tiles = rinv_ref.shape[0] // LANE
    copies = []
    if first:
        rinv_here, scratch, sems = refs
        for block in range(tiles):
            part, right = slice(block * LANE, (block + 1) * LANE), slice(block * LANE, rinv_ref.shape[1])
            copies.append(pltpu.make_async_copy(rinv_ref.at[part, right], rinv_here.at[part, right], sems.at[block]))
            copies[-1].start()
    else:
        rinv_here, (scratch,) = rinv_ref, refs
    summed = tree([parts_ref[i, : tiles + 1, :] for i in range(parts_ref.shape[0])])
    beta = jnp.sqrt(summed[tiles : tiles + 1, :])
    beta_ref[...] = beta
    scratch[...] = summed[:tiles, :] / beta
    left_product_upper(scratch, rinv_here, term_ref, copies)


def forward_body(groups, first, last, rinv_ref, design_ref, token_ref, *refs):
    right = tree([ref[...] for ref in refs[:groups]])
    refs = refs[groups:]
    if not first:
        before_ref, beta_ref, *refs = refs
        right = right - beta_ref[...] * before_ref[...]
    image_ref, held_ref, alpha_ref, *right_refs = refs
    alpha = jnp.sqrt(total(right * right))
    alpha_ref[...] = splat(alpha)
    right = right / alpha
    if not last:
        right_refs[0][...] = right
    right_product_upper(rinv_ref, right, held_ref)
    right_product(design_ref, held_ref[...], image_ref)


def turn_body(groups, last, *refs):
    left = tree([ref[...] for ref in refs[:groups]])
    before_ref, beta_ref, alpha_ref, *refs = refs[groups:]
    left = left - alpha_ref[...] * (before_ref[...] / beta_ref[...])
    square = splat(total(left * left))
    if last:
        left_ref, out_ref = refs
        out_ref[...] = jnp.broadcast_to(square, out_ref.shape)
    else:
        design_ref, left_ref, out_ref = refs
        tiles = design_ref.shape[1] // LANE
        out_ref[0] = jnp.zeros(out_ref.shape[1:], F32)
        left_product(left, design_ref, out_ref.at[0])
        out_ref[0, tiles : tiles + 1, :] = square
        copy_out(out_ref)
    left_ref[...] = left


def pieces(value):
    high = value.astype(jnp.bfloat16)
    return high, (value - high.astype(F32)).astype(jnp.bfloat16)


def weigh(mix, high, low):
    return jnp.dot(mix, high, preferred_element_type=F32) + jnp.dot(mix, low, preferred_element_type=F32)


def for_blocks(groups, step):
    if groups <= 8:
        for block in range(groups):
            step(block, 0)
    else:
        lax.fori_loop(0, groups, step, 0)


def mix_body(width, parts_ref, walsh_ref, mix_ref):
    groups, _, rows = mix_ref.shape
    me = lax.axis_index("row")
    local = lax.broadcasted_iota(jnp.int32, (LANE, rows), 1).astype(F32)
    per = LANE // PAIR

    def step(block, carry):
        parity = jnp.int32(0)
        for bit in range(groups.bit_length() - 1):
            parity = parity ^ ((block & me) >> bit)
        sign = (1 - 2 * (parity & 1)).astype(F32)
        for line in range(groups // per):
            start = picks_at(width) + line
            coded = across(parts_ref[block, start : start + 1, :])
            match = jnp.concatenate([coded] * (rows // LANE), axis=1) == local
            chosen = jnp.where(match, sign, 0.0).astype(jnp.bfloat16)
            for part in range(rows // HB):
                columns = slice(part * HB, (part + 1) * HB)
                mixed = jnp.dot(chosen[:, columns], walsh_ref[...], preferred_element_type=F32).astype(jnp.bfloat16)
                for index in range(per):
                    place = pl.multiple_of(((line * per + index) ^ me) * PAIR, PAIR)
                    mix_ref[block, pl.ds(place, PAIR), columns] = mixed[index * PAIR : (index + 1) * PAIR, :]
        return carry

    for_blocks(groups, step)


def sample_body(scale, start, design_ref, parts_ref, mix_ref, order_ref, *refs):
    near, (keep_ref, send_ref, token_ref, both) = refs[: NEAR - 1], refs[NEAR - 1 :]
    token_ref[...] = first_row(order_ref)
    rows, piece = near[-1].shape
    width = design_ref.shape[1]
    groups = mix_ref.shape[0]
    me = lax.axis_index("row")
    signs_start = signs_at(width, groups)
    for line in range(rows // LANE):
        part = slice(line * LANE, (line + 1) * LANE)
        signs = [across(parts_ref[me ^ mask, signs_start + line : signs_start + line + 1, :]) for mask in range(NEAR)]
        for tile in range(0, piece, LANE):
            column = pl.multiple_of(me % NEAR * (width // NEAR) + start + tile, LANE)
            here = slice(tile, tile + LANE)
            values = [design_ref[part, pl.ds(column, LANE)]] + [ref[part, here] for ref in near]
            values = [value * sign for value, sign in zip(values, signs)]
            apart = 1
            while apart < NEAR:
                for first in range(NEAR):
                    if not first & apart:
                        one, two = values[first], values[first | apart]
                        values[first], values[first | apart] = one + two, one - two
                apart *= 2
            for index, value in enumerate(values):
                both[index, 0, part, here], both[index, 1, part, here] = pieces(value)

    def step(block, carry):
        value = weigh(mix_ref[block], both[block % NEAR, 0], both[block % NEAR, 1]) / scale
        slot = pl.ds(block * PAIR, PAIR)
        for apart in range(groups):
            far, low = apart // NEAR, apart % NEAR
            out_ref = send_ref if far >= groups // NEAR // 2 else keep_ref
            out_ref[far % (groups // NEAR // 2), low, slot, :] = value[apart * PAIR : (apart + 1) * PAIR, :]
        return carry

    for_blocks(groups, step)


def halve_body(kept_ref, arrived_ref, order_ref, keep_ref, send_ref):
    half = keep_ref.shape[0]
    keep_ref[...] = kept_ref[:half] + arrived_ref[:half]
    send_ref[...] = kept_ref[half:] + arrived_ref[half:]


def first_row(ref):
    return ref[:1, :] if len(ref.shape) == 2 else ref[0, :1, :]


def join_body(kept_ref, arrived_ref, order_ref, out_ref, token_ref):
    token_ref[...] = first_row(order_ref)
    out_ref[...] = kept_ref[0] + arrived_ref[0]


def split_body(*refs):
    *joined, kept_ref, arrived_ref, order_ref = refs[:-NEAR]
    piece = kept_ref.shape[3]
    for index, rows_ref in enumerate(refs[-NEAR:]):
        for chunk, part_ref in enumerate(joined):
            rows_ref[:, chunk * piece : (chunk + 1) * piece] = part_ref[index]
        rows_ref[:, len(joined) * piece :] = kept_ref[0, index] + arrived_ref[0, index]


def pass_body(*refs):
    refs[-1][...] = refs[-2][...]


def assemble_body(token_ref, *refs):
    quarters, sketch_ref = refs[:-1], refs[-1]
    place = lax.axis_index("row") % NEAR
    piece = quarters[0].shape[1]
    for mask, part_ref in enumerate(quarters):
        for tile in range(0, piece, LANE):
            column = pl.multiple_of((place ^ mask) * piece + tile, LANE)
            sketch_ref[:, pl.ds(column, LANE)] = part_ref[:, tile : tile + LANE]


def last_body(parts_ref, left_ref, *refs):
    basis_ref, solution_ref, token_ref = refs[-3:]
    betas = [ref[...] for ref in refs[:ITERS]]
    alphas = [ref[...] for ref in refs[ITERS : 2 * ITERS]]
    held = [ref[...] for ref in refs[2 * ITERS : 3 * ITERS]]
    last = jnp.sqrt(tree([parts_ref[i] for i in range(parts_ref.shape[0])])[:1, :])
    basis_ref[...] = left_ref[...] / last
    betas.append(last)
    phibar, rhobar = betas[0], alphas[0]
    search, iterate = held[0], jnp.zeros_like(held[0])
    for step in range(ITERS):
        beta = betas[step + 1]
        rho = jnp.sqrt(rhobar * rhobar + beta * beta)
        cosine = rhobar / rho
        sine = beta / rho
        phi = cosine * phibar
        phibar = sine * phibar
        iterate = iterate + phi / rho * search
        if step + 1 < ITERS:
            alpha = alphas[step + 1]
            search = held[step + 1] - sine * alpha / rho * search
            rhobar = -cosine * alpha
    solution_ref[...] = iterate
    token_ref[...] = last


def shape(*dims, dtype=F32):
    return jax.ShapeDtypeStruct(dims, dtype)


def shards(design, sign_bits, picks, counts, target, rinv):
    rows, width = design.shape
    whole = rinv.shape[1]
    row_groups = lax.axis_size("row")
    lines = rows // LANE
    scalar = shape(1, LANE)
    deep = message_rows(width)
    left = target.reshape(lines, LANE)
    bits = sign_bits.reshape(lines, LANE)
    chunks = min(CHUNKS, width // NEAR // LANE)
    piece = width // NEAR // chunks
    scale = float(np.sqrt(np.float32(rows * row_groups)))
    slots = row_groups * PAIR
    far = row_groups // NEAR

    sent = [(mask, chunk * piece) for chunk in range(chunks) for mask in range(1, NEAR)]

    message, *away = pl.pallas_call(
        functools.partial(first_body, sent),
        out_shape=(shape(row_groups, rounded(signs_at(width, row_groups) + lines, 8), LANE),)
        + (shape(rows, piece),) * len(sent),
        in_specs=[HBM] * 5,
        out_specs=(VMEM,) + (HBM,) * len(sent),
        scratch_shapes=[
            pltpu.VMEM((rows, width), F32),
            pltpu.VMEM((lines, LANE), F32),
            pltpu.VMEM((lines, LANE), jnp.int32),
            pltpu.VMEM((row_groups, PAIR), jnp.int32),
            pltpu.VMEM((1, row_groups), jnp.int32),
            pltpu.SemaphoreType.DMA((4 + lines * (1 + len(sent)),)),
        ],
        compiler_params=pltpu.CompilerParams(vmem_limit_bytes=58 << 20),
    )(design, left, bits, picks.reshape(row_groups, PAIR), counts.reshape(1, row_groups))

    def swap(array, mask):
        return lax.ppermute(array, "row", [(i, i ^ mask) for i in range(row_groups)])

    def mix(message):
        made = shape(row_groups, slots, rows, dtype=jnp.bfloat16)
        return call(functools.partial(mix_body, width), made, message, jnp.asarray(walsh(HB), jnp.bfloat16))

    def sample(chunk, mixed, order):
        return call(
            functools.partial(sample_body, scale, chunk * piece),
            (shape(far // 2, NEAR, slots, piece),) * 2 + (scalar,),
            design,
            picked,
            mixed,
            order,
            *near[chunk * (NEAR - 1) : (chunk + 1) * (NEAR - 1)],
            scratch=[pltpu.VMEM((NEAR, 2, rows, piece), jnp.bfloat16)],
        )

    def spread(indices, order):
        parts = [away[index] for index in indices]
        if order is not None:
            parts, _ = lax.optimization_barrier((parts, order))
        return [swap(part, sent[index][0]) for index, part in zip(indices, parts)]

    def halve(keep, come, order):
        bit = row_groups // 2
        while bit > NEAR:
            bit //= 2
            half = keep.shape[0] // 2
            keep, send = call(halve_body, (shape(half, *keep.shape[1:]),) * 2, keep, come, order)
            come = swap(send, bit)
        return keep, come

    def join(keep, come, order):
        keep, come = halve(keep, come, order)
        return call(join_body, (shape(*keep.shape[1:]), scalar), keep, come, order)

    def back(rinv, message, first):
        outs, scratch = (shape(whole // LANE, LANE), scalar), [pltpu.VMEM((width // LANE, LANE), F32)]
        if first:
            outs += (shape(*rinv.shape),)
            scratch += [pltpu.SemaphoreType.DMA((width // LANE,))]
        return pl.pallas_call(
            functools.partial(back_body, first),
            out_shape=outs,
            in_specs=[HBM if first else VMEM, VMEM],
            out_specs=(VMEM,) * len(outs),
            scratch_shapes=scratch,
            compiler_params=pltpu.CompilerParams(vmem_limit_bytes=(34 if first else 24) << 20),
            )(rinv, message)

    def forward(terms, token, last, *before):
        return call(
            functools.partial(forward_body, len(terms), not before, last),
            (shape(lines, LANE), shape(width // LANE, LANE), scalar)
            + (() if last else (shape(whole // LANE, LANE),)),
            here,
            design,
            token,
            *terms,
            *before,
        )

    def turn(images, left, beta, alpha, last):
        return call(
            functools.partial(turn_body, len(images), last),
            (shape(lines, LANE), shape(row_groups, 8 if last else deep, LANE)),
            *images,
            left,
            beta,
            alpha,
            *(() if last else (design,)),
        )

    betas, alphas, held, joined, right = [], [], [], [], []
    near = spread(range(NEAR - 2), None)
    message = picked = exchange(message, "row")
    late = len(sent) - (chunks > 1)
    near += spread(range(NEAR - 2, late), message)
    for step in range(ITERS):
        last = step + 1 == ITERS
        if step == 0:
            term, beta, here = back(rinv, message, True)
            term = pl.pallas_call(
                pass_body,
                out_shape=shape(*term.shape),
                in_specs=[ANY] * (NEAR - 2) + [VMEM],
                out_specs=VMEM,
                compiler_params=pltpu.CompilerParams(vmem_limit_bytes=2 << 20),
            )(*near[: NEAR - 2], term)
            mixed = mix(message)
        else:
            term, beta = back(here, message, False)
            token = beta
            if chunks > 1:
                part, token = join(keep, come, message)
                joined.append(part)
                keep, send, token = sample(1, mixed, token)
                come = swap(send, row_groups // 2)
        betas.append(beta)
        spare = chunks > 1 and step > 0
        terms = direct(term, "col") if spare else paired(term, "col")
        if step == 0:
            near += spread(range(late, len(sent)), terms[1])
            keep, send, token = sample(0, mixed, beta)
            come = swap(send, row_groups // 2)
        image, kept, alpha, *right = forward(terms, token, last, *right, *betas[1:])
        alphas.append(alpha)
        held.append(kept)
        images = direct(image, "col") if spare else paired(image, "col")
        left, message = turn(images, left, beta, alpha, last)
        message = exchange(message, "row")
    quarters = (shape(slots, width // NEAR),) * NEAR
    mine, *others = call(split_body, quarters, *joined, *halve(keep, come, beta), left)
    basis, answer, token = pl.pallas_call(
        last_body,
        out_shape=(shape(lines, LANE), shape(width // LANE, LANE), scalar),
        in_specs=[VMEM] * (2 + 3 * ITERS),
        out_specs=(VMEM,) * 3,
        compiler_params=pltpu.CompilerParams(vmem_limit_bytes=4 << 20),
        cost_estimate=pl.CostEstimate(flops=0, bytes_accessed=16000 << 10, transcendentals=0),
    )(message, left, *betas, *alphas, *held)
    others = [swap(part, mask + 1) for mask, part in enumerate(others)]
    sketch = call(assemble_body, shape(slots, width), token, mine, *others)
    return (sketch, answer.reshape(-1), basis.reshape(-1))


def solution(mesh):
    placed = (
        P("row", "col"),
        P("row"),
        P(None, "row", None),
        P(None, "row"),
        P("row"),
        P("col", None),
    )
    return jax.shard_map(
        shards,
        mesh=mesh,
        in_specs=placed,
        out_specs=(P("row", "col"), P("col"), P("row")),
        check_vma=False,
    )
```

```python
import functools

import jax
import jax.numpy as jnp
import numpy as np
from jax import lax
from jax.experimental import pallas as pl
from jax.experimental.pallas import tpu as pltpu
from jax.sharding import PartitionSpec as P

HB = 256
PAIR = 16
ITERS = 2
LANE = 128
NEAR = 4
CHUNKS = 2
F32 = jnp.float32
VMEM = pl.BlockSpec(memory_space=pltpu.VMEM)
HBM = pl.BlockSpec(memory_space=pltpu.HBM)
ANY = pl.BlockSpec(memory_space=pl.ANY)


def exchange(copies, axis):
    return lax.all_to_all(copies, axis, split_axis=0, concat_axis=0, tiled=True)


def paired(array, axis):
    size = lax.axis_size(axis)
    mask = 1
    while True:
        come = lax.ppermute(array, axis, [(i, i ^ mask) for i in range(size)])
        mask *= 2
        if mask == size:
            return [array, come]
        array = array + come


def direct(array, axis):
    size = lax.axis_size(axis)
    return [array] + [
        lax.ppermute(array, axis, [(i, i ^ mask) for i in range(size)]) for mask in range(1, size)
    ]


def tree(values):
    while len(values) > 1:
        values = [values[i] + values[i + 1] for i in range(0, len(values), 2)]
    return values[0]


def walsh(size):
    parity = lax.broadcasted_iota(jnp.int32, (size, size), 0) & lax.broadcasted_iota(jnp.int32, (size, size), 1)
    for shift in (4, 2, 1):
        parity = parity ^ (parity >> shift)
    return (1 - 2 * (parity & 1)).astype(F32).astype(jnp.bfloat16)


def call(body, out_shape, *operands, scratch=()):
    return pl.pallas_call(
        body,
        out_shape=out_shape,
        in_specs=[VMEM] * len(operands),
        out_specs=jax.tree.map(lambda _: VMEM, out_shape),
        scratch_shapes=scratch,
        compiler_params=pltpu.CompilerParams(vmem_limit_bytes=24 << 20),
    )(*operands)


def fold_rows(block):
    return block.reshape(block.shape[0] // 8, 8, LANE).sum(axis=0)


def total(rows):
    return jnp.sum(jnp.sum(rows, axis=0, keepdims=True), axis=1, keepdims=True)


def splat(scalar):
    return jnp.broadcast_to(scalar, (1, LANE))


def left_product(vector, matrix_ref, out_ref):
    blocks, tiles = matrix_ref.shape[0] // LANE, matrix_ref.shape[1] // LANE
    sums = [jnp.zeros((8, LANE), F32) for _ in range(tiles)]
    for block in range(blocks):
        weight = across(vector[block : block + 1, :])
        for tile in range(tiles):
            part = matrix_ref[block * LANE : (block + 1) * LANE, tile * LANE : (tile + 1) * LANE]
            sums[tile] = sums[tile] + fold_rows(part * weight)
    for tile in range(tiles):
        out_ref[tile : tile + 1, :] = jnp.sum(sums[tile], axis=0, keepdims=True)


def left_product_upper(vector_ref, matrix_ref, out_ref, copies=()):
    blocks, tiles = matrix_ref.shape[0] // LANE, matrix_ref.shape[1] // LANE
    sums = [jnp.zeros((8, LANE), F32) for _ in range(tiles)]
    for block in range(blocks):
        if copies:
            copies[block].wait()
        weight = across(vector_ref[block : block + 1, :])
        for tile in range(block, tiles):
            part = matrix_ref[block * LANE : (block + 1) * LANE, tile * LANE : (tile + 1) * LANE]
            sums[tile] = sums[tile] + fold_rows(part * weight)
    for tile in range(tiles):
        out_ref[tile : tile + 1, :] = jnp.sum(sums[tile], axis=0, keepdims=True)


def right_product(matrix_ref, vector, out_ref):
    blocks, tiles = matrix_ref.shape[0] // LANE, matrix_ref.shape[1] // LANE

    def step(block, carry):
        rows = pl.ds(pl.multiple_of(block * LANE, LANE), LANE)
        sums = jnp.zeros((LANE, LANE), F32)
        for tile in range(tiles):
            sums = sums + matrix_ref[rows, tile * LANE : (tile + 1) * LANE] * vector[tile : tile + 1, :]
        out_ref[pl.ds(block, 1), :] = jnp.sum(fold_rows(sums.T), axis=0, keepdims=True)
        return carry

    lax.fori_loop(0, blocks, step, 0)


def right_product_upper(matrix_ref, vector, out_ref):
    blocks, tiles = matrix_ref.shape[0] // LANE, matrix_ref.shape[1] // LANE
    for block in range(blocks):
        rows = slice(block * LANE, (block + 1) * LANE)
        sums = jnp.zeros((LANE, LANE), F32)
        for tile in range(block, tiles):
            sums = sums + matrix_ref[rows, tile * LANE : (tile + 1) * LANE] * vector[tile : tile + 1, :]
        out_ref[block : block + 1, :] = jnp.sum(fold_rows(sums.T), axis=0, keepdims=True)


def rounded(count, unit):
    return -(-count // unit) * unit


def message_rows(width):
    return rounded(width // LANE + 1, 8)


def picks_at(width):
    return width // LANE + 1


def signs_at(width, groups):
    return picks_at(width) + groups * PAIR // LANE


def copy_out(out_ref):
    first = out_ref[0]
    for index in range(1, out_ref.shape[0]):
        out_ref[index] = first


def across(row):
    return jnp.broadcast_to(row, (LANE, LANE)).T


def first_body(sent, design_ref, target_ref, bits_ref, picks_ref, counts_ref, *refs):
    out_ref, away_refs = refs[0], refs[1:-6]
    design, target_here, bits, picks, counts, sems = refs[-6:]
    rows, width = design.shape
    lines, tiles = rows // LANE, width // LANE
    small = [
        pltpu.make_async_copy(source, place, sems.at[index])
        for index, (source, place) in enumerate(
            ((target_ref, target_here), (bits_ref, bits), (picks_ref, picks), (counts_ref, counts))
        )
    ]
    parts = [slice(line * LANE, (line + 1) * LANE) for line in range(lines)]
    large = [
        pltpu.make_async_copy(design_ref.at[part, :], design.at[part, :], sems.at[4 + line])
        for line, part in enumerate(parts)
    ]
    place = lax.axis_index("row") % NEAR
    away = []
    for index, away_ref in enumerate(away_refs):
        piece = away_ref.shape[1]
        mask, start = sent[index]
        column = pl.multiple_of((place ^ mask) * (width // NEAR) + start, LANE)
        for line, part in enumerate(parts):
            source = design.at[part, pl.ds(column, piece)]
            away.append(pltpu.make_async_copy(source, away_ref.at[part, :], sems.at[4 + lines * (index + 1) + line]))
    for copy in small + large:
        copy.start()
    for copy in small:
        copy.wait()
    out_ref[0] = jnp.zeros(out_ref.shape[1:], F32)
    groups = picks.shape[0]
    owner = lax.broadcasted_iota(jnp.int32, (groups, groups), 0)
    same = owner == lax.broadcasted_iota(jnp.int32, (groups, groups), 1)
    limit = jnp.sum(jnp.where(same, counts[...].astype(F32), 0.0), axis=1, keepdims=True)
    slot = lax.broadcasted_iota(jnp.int32, picks.shape, 1).astype(F32)
    coded = jnp.where(slot < limit, picks[...].astype(F32), -1.0)
    start = picks_at(width)
    for owner in range(0, groups, LANE // PAIR):
        line = jnp.concatenate([coded[i : i + 1, :] for i in range(owner, owner + LANE // PAIR)], axis=1)
        out_ref[0, start + owner * PAIR // LANE : start + owner * PAIR // LANE + 1, :] = line
    start = signs_at(width, groups)
    out_ref[0, start : start + lines, :] = (2 * bits[...] - 1).astype(F32)
    target = target_here[...]
    out_ref[0, tiles : tiles + 1, :] = splat(total(target * target))
    sums = [jnp.zeros((8, LANE), F32) for _ in range(tiles)]
    for line, part in enumerate(parts):
        weight = across(target[line : line + 1, :])
        large[line].wait()
        for copy in away[line::lines]:
            copy.start()
        for tile in range(tiles):
            sums[tile] = sums[tile] + fold_rows(design[part, tile * LANE : (tile + 1) * LANE] * weight)
    for tile in range(tiles):
        out_ref[0, tile : tile + 1, :] = jnp.sum(sums[tile], axis=0, keepdims=True)
    copy_out(out_ref)
    for copy in away:
        copy.wait()


def back_body(first, rinv_ref, parts_ref, *refs):
    if first:
        term_ref, beta_ref, mix_ref, *refs, walsh_ref = refs
    else:
        term_ref, beta_ref, *refs = refs
    tiles = rinv_ref.shape[0] // LANE
    copies = []
    if first:
        rinv_here, scratch, sems = refs
        for block in range(tiles):
            part, right = slice(block * LANE, (block + 1) * LANE), slice(block * LANE, rinv_ref.shape[1])
            copies.append(pltpu.make_async_copy(rinv_ref.at[part, right], rinv_here.at[part, right], sems.at[block]))
            copies[-1].start()
        walsh_ref[...] = walsh(HB)
        mix_body(rinv_ref.shape[0], parts_ref, walsh_ref, mix_ref)
    else:
        rinv_here, (scratch,) = rinv_ref, refs
    summed = tree([parts_ref[i, : tiles + 1, :] for i in range(parts_ref.shape[0])])
    beta = jnp.sqrt(summed[tiles : tiles + 1, :])
    beta_ref[...] = beta
    scratch[...] = summed[:tiles, :] / beta
    left_product_upper(scratch, rinv_here, term_ref, copies)


def forward_body(groups, first, last, rinv_ref, design_ref, token_ref, *refs):
    right = tree([ref[...] for ref in refs[:groups]])
    refs = refs[groups:]
    if not first:
        before_ref, beta_ref, *refs = refs
        right = right - beta_ref[...] * before_ref[...]
    image_ref, held_ref, alpha_ref, *right_refs = refs
    alpha = jnp.sqrt(total(right * right))
    alpha_ref[...] = splat(alpha)
    right = right / alpha
    if not last:
        right_refs[0][...] = right
    right_product_upper(rinv_ref, right, held_ref)
    right_product(design_ref, held_ref[...], image_ref)


def turn_body(groups, last, *refs):
    left = tree([ref[...] for ref in refs[:groups]])
    before_ref, beta_ref, alpha_ref, *refs = refs[groups:]
    left = left - alpha_ref[...] * (before_ref[...] / beta_ref[...])
    square = splat(total(left * left))
    if last:
        left_ref, out_ref = refs
        out_ref[...] = jnp.broadcast_to(square, out_ref.shape)
    else:
        design_ref, left_ref, out_ref = refs
        tiles = design_ref.shape[1] // LANE
        out_ref[0] = jnp.zeros(out_ref.shape[1:], F32)
        left_product(left, design_ref, out_ref.at[0])
        out_ref[0, tiles : tiles + 1, :] = square
        copy_out(out_ref)
    left_ref[...] = left


def pieces(value):
    high = value.astype(jnp.bfloat16)
    return high, (value - high.astype(F32)).astype(jnp.bfloat16)


def weigh(mix, high, low):
    return jnp.dot(mix, high, preferred_element_type=F32) + jnp.dot(mix, low, preferred_element_type=F32)


def for_blocks(groups, step):
    if groups <= 8:
        for block in range(groups):
            step(block, 0)
    else:
        lax.fori_loop(0, groups, step, 0)


def mix_body(width, parts_ref, walsh_ref, mix_ref):
    groups, _, rows = mix_ref.shape
    me = lax.axis_index("row")
    local = lax.broadcasted_iota(jnp.int32, (LANE, rows), 1).astype(F32)
    per = LANE // PAIR

    def step(block, carry):
        parity = jnp.int32(0)
        for bit in range(groups.bit_length() - 1):
            parity = parity ^ ((block & me) >> bit)
        sign = (1 - 2 * (parity & 1)).astype(F32)
        for line in range(groups // per):
            start = picks_at(width) + line
            coded = across(parts_ref[block, start : start + 1, :])
            match = jnp.concatenate([coded] * (rows // LANE), axis=1) == local
            chosen = jnp.where(match, sign, 0.0).astype(jnp.bfloat16)
            for part in range(rows // HB):
                columns = slice(part * HB, (part + 1) * HB)
                mixed = jnp.dot(chosen[:, columns], walsh_ref[...], preferred_element_type=F32).astype(jnp.bfloat16)
                for index in range(per):
                    place = pl.multiple_of(((line * per + index) ^ me) * PAIR, PAIR)
                    mix_ref[block, pl.ds(place, PAIR), columns] = mixed[index * PAIR : (index + 1) * PAIR, :]
        return carry

    for_blocks(groups, step)


def sample_body(scale, start, design_ref, parts_ref, mix_ref, order_ref, *refs):
    near, (keep_ref, send_ref, token_ref, both) = refs[: NEAR - 1], refs[NEAR - 1 :]
    token_ref[...] = first_row(order_ref)
    rows, piece = near[-1].shape
    width = design_ref.shape[1]
    groups = mix_ref.shape[0]
    me = lax.axis_index("row")
    signs_start = signs_at(width, groups)
    for line in range(rows // LANE):
        part = slice(line * LANE, (line + 1) * LANE)
        signs = [across(parts_ref[me ^ mask, signs_start + line : signs_start + line + 1, :]) for mask in range(NEAR)]
        for tile in range(0, piece, LANE):
            column = pl.multiple_of(me % NEAR * (width // NEAR) + start + tile, LANE)
            here = slice(tile, tile + LANE)
            values = [design_ref[part, pl.ds(column, LANE)]] + [ref[part, here] for ref in near]
            values = [value * sign for value, sign in zip(values, signs)]
            apart = 1
            while apart < NEAR:
                for first in range(NEAR):
                    if not first & apart:
                        one, two = values[first], values[first | apart]
                        values[first], values[first | apart] = one + two, one - two
                apart *= 2
            for index, value in enumerate(values):
                both[index, 0, part, here], both[index, 1, part, here] = pieces(value)

    def step(block, carry):
        value = weigh(mix_ref[block], both[block % NEAR, 0], both[block % NEAR, 1]) / scale
        slot = pl.ds(block * PAIR, PAIR)
        for apart in range(groups):
            far, low = apart // NEAR, apart % NEAR
            out_ref = send_ref if far >= groups // NEAR // 2 else keep_ref
            out_ref[far % (groups // NEAR // 2), low, slot, :] = value[apart * PAIR : (apart + 1) * PAIR, :]
        return carry

    for_blocks(groups, step)


def halve_body(kept_ref, arrived_ref, order_ref, keep_ref, send_ref):
    half = keep_ref.shape[0]
    keep_ref[...] = kept_ref[:half] + arrived_ref[:half]
    send_ref[...] = kept_ref[half:] + arrived_ref[half:]


def first_row(ref):
    return ref[:1, :] if len(ref.shape) == 2 else ref[0, :1, :]


def join_body(kept_ref, arrived_ref, order_ref, out_ref, token_ref):
    token_ref[...] = first_row(order_ref)
    out_ref[...] = kept_ref[0] + arrived_ref[0]


def split_body(*refs):
    *joined, kept_ref, arrived_ref, order_ref = refs[:-NEAR]
    piece = kept_ref.shape[3]
    for index, rows_ref in enumerate(refs[-NEAR:]):
        for chunk, part_ref in enumerate(joined):
            rows_ref[:, chunk * piece : (chunk + 1) * piece] = part_ref[index]
        rows_ref[:, len(joined) * piece :] = kept_ref[0, index] + arrived_ref[0, index]


def pass_body(*refs):
    refs[-1][...] = refs[-2][...]


def last_body(parts_ref, left_ref, *refs):
    basis_ref, solution_ref, sketch_ref, sems = refs[-4:]
    quarters = refs[3 * ITERS : 3 * ITERS + NEAR]
    place = lax.axis_index("row") % NEAR
    piece = quarters[0].shape[1]
    copies = []
    for mask, part_ref in enumerate(quarters):
        columns = pl.ds(pl.multiple_of((place ^ mask) * piece, LANE), piece)
        copies.append(pltpu.make_async_copy(part_ref, sketch_ref.at[:, columns], sems.at[mask]))
        copies[-1].start()
    betas = [ref[...] for ref in refs[:ITERS]]
    alphas = [ref[...] for ref in refs[ITERS : 2 * ITERS]]
    held = [ref[...] for ref in refs[2 * ITERS : 3 * ITERS]]
    last = jnp.sqrt(tree([parts_ref[i] for i in range(parts_ref.shape[0])])[:1, :])
    basis_ref[...] = left_ref[...] / last
    betas.append(last)
    phibar, rhobar = betas[0], alphas[0]
    search, iterate = held[0], jnp.zeros_like(held[0])
    for step in range(ITERS):
        beta = betas[step + 1]
        rho = jnp.sqrt(rhobar * rhobar + beta * beta)
        cosine = rhobar / rho
        sine = beta / rho
        phi = cosine * phibar
        phibar = sine * phibar
        iterate = iterate + phi / rho * search
        if step + 1 < ITERS:
            alpha = alphas[step + 1]
            search = held[step + 1] - sine * alpha / rho * search
            rhobar = -cosine * alpha
    solution_ref[...] = iterate
    for copy in copies:
        copy.wait()


def shape(*dims, dtype=F32):
    return jax.ShapeDtypeStruct(dims, dtype)


def shards(design, sign_bits, picks, counts, target, rinv):
    rows, width = design.shape
    whole = rinv.shape[1]
    row_groups = lax.axis_size("row")
    lines = rows // LANE
    scalar = shape(1, LANE)
    deep = message_rows(width)
    left = target.reshape(lines, LANE)
    bits = sign_bits.reshape(lines, LANE)
    chunks = min(CHUNKS, width // NEAR // LANE)
    piece = width // NEAR // chunks
    scale = float(np.sqrt(np.float32(rows * row_groups)))
    slots = row_groups * PAIR
    far = row_groups // NEAR

    sent = [(mask, chunk * piece) for chunk in range(chunks) for mask in range(1, NEAR)]

    message, *away = pl.pallas_call(
        functools.partial(first_body, sent),
        out_shape=(shape(row_groups, rounded(signs_at(width, row_groups) + lines, 8), LANE),)
        + (shape(rows, piece),) * len(sent),
        in_specs=[HBM] * 5,
        out_specs=(VMEM,) + (HBM,) * len(sent),
        scratch_shapes=[
            pltpu.VMEM((rows, width), F32),
            pltpu.VMEM((lines, LANE), F32),
            pltpu.VMEM((lines, LANE), jnp.int32),
            pltpu.VMEM((row_groups, PAIR), jnp.int32),
            pltpu.VMEM((1, row_groups), jnp.int32),
            pltpu.SemaphoreType.DMA((4 + lines * (1 + len(sent)),)),
        ],
        compiler_params=pltpu.CompilerParams(vmem_limit_bytes=58 << 20),
    )(design, left, bits, picks.reshape(row_groups, PAIR), counts.reshape(1, row_groups))

    def swap(array, mask):
        return lax.ppermute(array, "row", [(i, i ^ mask) for i in range(row_groups)])

    def sample(chunk, mixed, order):
        return call(
            functools.partial(sample_body, scale, chunk * piece),
            (shape(far // 2, NEAR, slots, piece),) * 2 + (scalar,),
            design,
            picked,
            mixed,
            order,
            *near[chunk * (NEAR - 1) : (chunk + 1) * (NEAR - 1)],
            scratch=[pltpu.VMEM((NEAR, 2, rows, piece), jnp.bfloat16)],
        )

    def spread(indices, order):
        parts = [away[index] for index in indices]
        if order is not None:
            parts, _ = lax.optimization_barrier((parts, order))
        return [swap(part, sent[index][0]) for index, part in zip(indices, parts)]

    def halve(keep, come, order):
        bit = row_groups // 2
        while bit > NEAR:
            bit //= 2
            half = keep.shape[0] // 2
            keep, send = call(halve_body, (shape(half, *keep.shape[1:]),) * 2, keep, come, order)
            come = swap(send, bit)
        return keep, come

    def join(keep, come, order):
        keep, come = halve(keep, come, order)
        return call(join_body, (shape(*keep.shape[1:]), scalar), keep, come, order)

    def back(rinv, message, first):
        outs, scratch = (shape(whole // LANE, LANE), scalar), [pltpu.VMEM((width // LANE, LANE), F32)]
        operands = (rinv, message)
        if first:
            outs += (shape(row_groups, slots, rows, dtype=jnp.bfloat16), shape(*rinv.shape))
            scratch += [pltpu.SemaphoreType.DMA((width // LANE,))]
            scratch += [pltpu.VMEM((HB, HB), jnp.bfloat16)]
        return pl.pallas_call(
            functools.partial(back_body, first),
            out_shape=outs,
            in_specs=[HBM if first else VMEM] + [VMEM] * (len(operands) - 1),
            out_specs=(VMEM,) * len(outs),
            scratch_shapes=scratch,
            compiler_params=pltpu.CompilerParams(vmem_limit_bytes=(34 if first else 24) << 20),
        )(*operands)

    def forward(terms, token, last, *before):
        return call(
            functools.partial(forward_body, len(terms), not before, last),
            (shape(lines, LANE), shape(width // LANE, LANE), scalar)
            + (() if last else (shape(whole // LANE, LANE),)),
            here,
            design,
            token,
            *terms,
            *before,
        )

    def turn(images, left, beta, alpha, last):
        return call(
            functools.partial(turn_body, len(images), last),
            (shape(lines, LANE), shape(row_groups, 8 if last else deep, LANE)),
            *images,
            left,
            beta,
            alpha,
            *(() if last else (design,)),
        )

    betas, alphas, held, joined, right = [], [], [], [], []
    near = spread(range(NEAR - 2), None)
    message = picked = exchange(message, "row")
    late = len(sent) - (chunks > 1)
    near += spread(range(NEAR - 2, late), message)
    for step in range(ITERS):
        last = step + 1 == ITERS
        if step == 0:
            term, beta, mixed, here = back(rinv, message, True)
            term = pl.pallas_call(
                pass_body,
                out_shape=shape(*term.shape),
                in_specs=[ANY] * (NEAR - 2) + [VMEM],
                out_specs=VMEM,
                compiler_params=pltpu.CompilerParams(vmem_limit_bytes=2 << 20),
            )(*near[: NEAR - 2], term)
        else:
            term, beta = back(here, message, False)
            token = beta
            if chunks > 1:
                part, token = join(keep, come, message)
                joined.append(part)
                keep, send, token = sample(1, mixed, token)
                come = swap(send, row_groups // 2)
        betas.append(beta)
        spare = chunks > 1 and step > 0
        terms = direct(term, "col") if spare else paired(term, "col")
        if step == 0:
            near += spread(range(late, len(sent)), terms[1])
            keep, send, token = sample(0, mixed, beta)
            come = swap(send, row_groups // 2)
        image, kept, alpha, *right = forward(terms, token, last, *right, *betas[1:])
        alphas.append(alpha)
        held.append(kept)
        images = direct(image, "col") if spare else paired(image, "col")
        left, message = turn(images, left, beta, alpha, last)
        message = exchange(message, "row")
    quarters = (shape(slots, width // NEAR),) * NEAR
    mine, *others = call(split_body, quarters, *joined, *halve(keep, come, beta), left)
    quarters = [mine] + [swap(part, mask + 1) for mask, part in enumerate(others)]
    basis, answer, sketch = pl.pallas_call(
        last_body,
        out_shape=(shape(lines, LANE), shape(width // LANE, LANE), shape(slots, width)),
        in_specs=[VMEM] * (2 + 3 * ITERS + NEAR),
        out_specs=(VMEM, VMEM, HBM),
        scratch_shapes=[pltpu.SemaphoreType.DMA((NEAR,))],
        compiler_params=pltpu.CompilerParams(vmem_limit_bytes=24 << 20),
    )(message, left, *betas, *alphas, *held, *quarters)
    return (sketch, answer.reshape(-1), basis.reshape(-1))


def solution(mesh):
    placed = (
        P("row", "col"),
        P("row"),
        P(None, "row", None),
        P(None, "row"),
        P("row"),
        P("col", None),
    )
    return jax.shard_map(
        shards,
        mesh=mesh,
        in_specs=placed,
        out_specs=(P("row", "col"), P("col"), P("row")),
        check_vma=False,
    )
```

```python
import functools

import jax
import jax.numpy as jnp
import numpy as np
from jax import lax
from jax.experimental import pallas as pl
from jax.experimental.pallas import tpu as pltpu
from jax.sharding import PartitionSpec as P

HB = 256
PAIR = 16
ITERS = 2
LANE = 128
NEAR = 4
CHUNKS = 2
F32 = jnp.float32
VMEM = pl.BlockSpec(memory_space=pltpu.VMEM)
HBM = pl.BlockSpec(memory_space=pltpu.HBM)
ANY = pl.BlockSpec(memory_space=pl.ANY)


def exchange(copies, axis):
    return lax.all_to_all(copies, axis, split_axis=0, concat_axis=0, tiled=True)


def paired(array, axis):
    size = lax.axis_size(axis)
    mask = 1
    while True:
        come = lax.ppermute(array, axis, [(i, i ^ mask) for i in range(size)])
        mask *= 2
        if mask == size:
            return [array, come]
        array = array + come


def direct(array, axis):
    size = lax.axis_size(axis)
    return [array] + [
        lax.ppermute(array, axis, [(i, i ^ mask) for i in range(size)]) for mask in range(1, size)
    ]


def tree(values):
    while len(values) > 1:
        values = [values[i] + values[i + 1] for i in range(0, len(values), 2)]
    return values[0]


def walsh(size):
    parity = lax.broadcasted_iota(jnp.int32, (size, size), 0) & lax.broadcasted_iota(jnp.int32, (size, size), 1)
    for shift in (4, 2, 1):
        parity = parity ^ (parity >> shift)
    return (1 - 2 * (parity & 1)).astype(F32).astype(jnp.bfloat16)


def call(body, out_shape, *operands, scratch=()):
    return pl.pallas_call(
        body,
        out_shape=out_shape,
        in_specs=[VMEM] * len(operands),
        out_specs=jax.tree.map(lambda _: VMEM, out_shape),
        scratch_shapes=scratch,
        compiler_params=pltpu.CompilerParams(vmem_limit_bytes=24 << 20),
    )(*operands)


def fold_rows(block):
    return block.reshape(block.shape[0] // 8, 8, LANE).sum(axis=0)


def total(rows):
    return jnp.sum(jnp.sum(rows, axis=0, keepdims=True), axis=1, keepdims=True)


def splat(scalar):
    return jnp.broadcast_to(scalar, (1, LANE))


def left_product(vector, matrix_ref, out_ref):
    blocks, tiles = matrix_ref.shape[0] // LANE, matrix_ref.shape[1] // LANE
    sums = [jnp.zeros((8, LANE), F32) for _ in range(tiles)]
    for block in range(blocks):
        weight = across(vector[block : block + 1, :])
        for tile in range(tiles):
            part = matrix_ref[block * LANE : (block + 1) * LANE, tile * LANE : (tile + 1) * LANE]
            sums[tile] = sums[tile] + fold_rows(part * weight)
    for tile in range(tiles):
        out_ref[tile : tile + 1, :] = jnp.sum(sums[tile], axis=0, keepdims=True)


def left_product_upper(vector_ref, matrix_ref, out_ref, copies=()):
    blocks, tiles = matrix_ref.shape[0] // LANE, matrix_ref.shape[1] // LANE
    sums = [jnp.zeros((8, LANE), F32) for _ in range(tiles)]
    for block in range(blocks):
        if copies:
            copies[block].wait()
        weight = across(vector_ref[block : block + 1, :])
        for tile in range(block, tiles):
            part = matrix_ref[block * LANE : (block + 1) * LANE, tile * LANE : (tile + 1) * LANE]
            sums[tile] = sums[tile] + fold_rows(part * weight)
    for tile in range(tiles):
        out_ref[tile : tile + 1, :] = jnp.sum(sums[tile], axis=0, keepdims=True)


def right_product(matrix_ref, vector, out_ref):
    blocks, tiles = matrix_ref.shape[0] // LANE, matrix_ref.shape[1] // LANE

    def step(block, carry):
        rows = pl.ds(pl.multiple_of(block * LANE, LANE), LANE)
        sums = jnp.zeros((LANE, LANE), F32)
        for tile in range(tiles):
            sums = sums + matrix_ref[rows, tile * LANE : (tile + 1) * LANE] * vector[tile : tile + 1, :]
        out_ref[pl.ds(block, 1), :] = jnp.sum(fold_rows(sums.T), axis=0, keepdims=True)
        return carry

    lax.fori_loop(0, blocks, step, 0)


def right_product_upper(matrix_ref, vector, out_ref):
    blocks, tiles = matrix_ref.shape[0] // LANE, matrix_ref.shape[1] // LANE
    for block in range(blocks):
        rows = slice(block * LANE, (block + 1) * LANE)
        sums = jnp.zeros((LANE, LANE), F32)
        for tile in range(block, tiles):
            sums = sums + matrix_ref[rows, tile * LANE : (tile + 1) * LANE] * vector[tile : tile + 1, :]
        out_ref[block : block + 1, :] = jnp.sum(fold_rows(sums.T), axis=0, keepdims=True)


def rounded(count, unit):
    return -(-count // unit) * unit


def message_rows(width):
    return rounded(width // LANE + 1, 8)


def picks_at(width):
    return width // LANE + 1


def signs_at(width, groups):
    return picks_at(width) + groups * PAIR // LANE


def copy_out(out_ref):
    first = out_ref[0]
    for index in range(1, out_ref.shape[0]):
        out_ref[index] = first


def across(row):
    return jnp.broadcast_to(row, (LANE, LANE)).T


def first_body(sent, design_ref, target_ref, bits_ref, picks_ref, counts_ref, *refs):
    out_ref, away_refs = refs[0], refs[1:-6]
    design, target_here, bits, picks, counts, sems = refs[-6:]
    rows, width = design.shape
    lines, tiles = rows // LANE, width // LANE
    small = [
        pltpu.make_async_copy(source, place, sems.at[index])
        for index, (source, place) in enumerate(
            ((target_ref, target_here), (bits_ref, bits), (picks_ref, picks), (counts_ref, counts))
        )
    ]
    parts = [slice(line * LANE, (line + 1) * LANE) for line in range(lines)]
    large = [
        pltpu.make_async_copy(design_ref.at[part, :], design.at[part, :], sems.at[4 + line])
        for line, part in enumerate(parts)
    ]
    place = lax.axis_index("row") % NEAR
    away = []
    for index, away_ref in enumerate(away_refs):
        piece = away_ref.shape[1]
        mask, start = sent[index]
        column = pl.multiple_of((place ^ mask) * (width // NEAR) + start, LANE)
        for line, part in enumerate(parts):
            source = design.at[part, pl.ds(column, piece)]
            away.append(pltpu.make_async_copy(source, away_ref.at[part, :], sems.at[4 + lines * (index + 1) + line]))
    for copy in small + large:
        copy.start()
    for copy in small:
        copy.wait()
    out_ref[0] = jnp.zeros(out_ref.shape[1:], F32)
    groups = picks.shape[0]
    owner = lax.broadcasted_iota(jnp.int32, (groups, groups), 0)
    same = owner == lax.broadcasted_iota(jnp.int32, (groups, groups), 1)
    limit = jnp.sum(jnp.where(same, counts[...].astype(F32), 0.0), axis=1, keepdims=True)
    slot = lax.broadcasted_iota(jnp.int32, picks.shape, 1).astype(F32)
    coded = jnp.where(slot < limit, picks[...].astype(F32), -1.0)
    start = picks_at(width)
    for owner in range(0, groups, LANE // PAIR):
        line = jnp.concatenate([coded[i : i + 1, :] for i in range(owner, owner + LANE // PAIR)], axis=1)
        out_ref[0, start + owner * PAIR // LANE : start + owner * PAIR // LANE + 1, :] = line
    start = signs_at(width, groups)
    out_ref[0, start : start + lines, :] = (2 * bits[...] - 1).astype(F32)
    target = target_here[...]
    out_ref[0, tiles : tiles + 1, :] = splat(total(target * target))
    sums = [jnp.zeros((8, LANE), F32) for _ in range(tiles)]
    for line, part in enumerate(parts):
        weight = across(target[line : line + 1, :])
        large[line].wait()
        for copy in away[line::lines]:
            copy.start()
        for tile in range(tiles):
            sums[tile] = sums[tile] + fold_rows(design[part, tile * LANE : (tile + 1) * LANE] * weight)
    for tile in range(tiles):
        out_ref[0, tile : tile + 1, :] = jnp.sum(sums[tile], axis=0, keepdims=True)
    copy_out(out_ref)
    for copy in away:
        copy.wait()


def back_body(first, rinv_ref, parts_ref, *refs):
    if first:
        term_ref, beta_ref, mix_ref, *refs, walsh_ref = refs
    else:
        term_ref, beta_ref, *refs = refs
    tiles = rinv_ref.shape[0] // LANE
    copies = []
    if first:
        rinv_here, scratch, sems = refs
        for block in range(tiles):
            part, right = slice(block * LANE, (block + 1) * LANE), slice(block * LANE, rinv_ref.shape[1])
            copies.append(pltpu.make_async_copy(rinv_ref.at[part, right], rinv_here.at[part, right], sems.at[block]))
            copies[-1].start()
        walsh_ref[...] = walsh(HB)
        mix_body(rinv_ref.shape[0], parts_ref, walsh_ref, mix_ref)
    else:
        rinv_here, (scratch,) = rinv_ref, refs
    summed = tree([parts_ref[i, : tiles + 1, :] for i in range(parts_ref.shape[0])])
    beta = jnp.sqrt(summed[tiles : tiles + 1, :])
    beta_ref[...] = beta
    scratch[...] = summed[:tiles, :] / beta
    left_product_upper(scratch, rinv_here, term_ref, copies)


def forward_body(groups, first, last, rinv_ref, design_ref, token_ref, *refs):
    right = tree([ref[...] for ref in refs[:groups]])
    refs = refs[groups:]
    if not first:
        before_ref, beta_ref, *refs = refs
        right = right - beta_ref[...] * before_ref[...]
    image_ref, held_ref, alpha_ref, *right_refs = refs
    alpha = jnp.sqrt(total(right * right))
    alpha_ref[...] = splat(alpha)
    right = right / alpha
    if not last:
        right_refs[0][...] = right
    right_product_upper(rinv_ref, right, held_ref)
    right_product(design_ref, held_ref[...], image_ref)


def turn_body(groups, last, *refs):
    left = tree([ref[...] for ref in refs[:groups]])
    before_ref, beta_ref, alpha_ref, *refs = refs[groups:]
    left = left - alpha_ref[...] * (before_ref[...] / beta_ref[...])
    square = splat(total(left * left))
    if last:
        left_ref, out_ref = refs
        out_ref[...] = jnp.broadcast_to(square, out_ref.shape)
    else:
        design_ref, left_ref, out_ref = refs
        tiles = design_ref.shape[1] // LANE
        out_ref[0] = jnp.zeros(out_ref.shape[1:], F32)
        left_product(left, design_ref, out_ref.at[0])
        out_ref[0, tiles : tiles + 1, :] = square
        copy_out(out_ref)
    left_ref[...] = left


def pieces(value):
    high = value.astype(jnp.bfloat16)
    return high, (value - high.astype(F32)).astype(jnp.bfloat16)


def weigh(mix, high, low):
    return jnp.dot(mix, high, preferred_element_type=F32) + jnp.dot(mix, low, preferred_element_type=F32)


def for_blocks(groups, step):
    if groups <= 8:
        for block in range(groups):
            step(block, 0)
    else:
        lax.fori_loop(0, groups, step, 0)


def mix_body(width, parts_ref, walsh_ref, mix_ref):
    groups, _, rows = mix_ref.shape
    me = lax.axis_index("row")
    local = lax.broadcasted_iota(jnp.int32, (LANE, rows), 1).astype(F32)
    per = LANE // PAIR

    def step(block, carry):
        parity = jnp.int32(0)
        for bit in range(groups.bit_length() - 1):
            parity = parity ^ ((block & me) >> bit)
        sign = (1 - 2 * (parity & 1)).astype(F32)
        for line in range(groups // per):
            start = picks_at(width) + line
            coded = across(parts_ref[block, start : start + 1, :])
            match = jnp.concatenate([coded] * (rows // LANE), axis=1) == local
            chosen = jnp.where(match, sign, 0.0).astype(jnp.bfloat16)
            for part in range(rows // HB):
                columns = slice(part * HB, (part + 1) * HB)
                mixed = jnp.dot(chosen[:, columns], walsh_ref[...], preferred_element_type=F32).astype(jnp.bfloat16)
                for index in range(per):
                    place = pl.multiple_of(((line * per + index) ^ me) * PAIR, PAIR)
                    mix_ref[block, pl.ds(place, PAIR), columns] = mixed[index * PAIR : (index + 1) * PAIR, :]
        return carry

    for_blocks(groups, step)


def sample_body(scale, start, design_ref, parts_ref, mix_ref, order_ref, *refs):
    near, (keep_ref, send_ref, token_ref, both) = refs[: NEAR - 1], refs[NEAR - 1 :]
    token_ref[...] = first_row(order_ref)
    rows, piece = near[-1].shape
    width = design_ref.shape[1]
    groups = mix_ref.shape[0]
    me = lax.axis_index("row")
    signs_start = signs_at(width, groups)
    for line in range(rows // LANE):
        part = slice(line * LANE, (line + 1) * LANE)
        signs = [across(parts_ref[me ^ mask, signs_start + line : signs_start + line + 1, :]) for mask in range(NEAR)]
        for tile in range(0, piece, LANE):
            column = pl.multiple_of(me % NEAR * (width // NEAR) + start + tile, LANE)
            here = slice(tile, tile + LANE)
            values = [design_ref[part, pl.ds(column, LANE)]] + [ref[part, here] for ref in near]
            values = [value * sign for value, sign in zip(values, signs)]
            apart = 1
            while apart < NEAR:
                for first in range(NEAR):
                    if not first & apart:
                        one, two = values[first], values[first | apart]
                        values[first], values[first | apart] = one + two, one - two
                apart *= 2
            for index, value in enumerate(values):
                both[index, 0, part, here], both[index, 1, part, here] = pieces(value)

    def step(block, carry):
        value = weigh(mix_ref[block], both[block % NEAR, 0], both[block % NEAR, 1]) / scale
        slot = pl.ds(block * PAIR, PAIR)
        for apart in range(groups):
            far, low = apart // NEAR, apart % NEAR
            out_ref = send_ref if far >= groups // NEAR // 2 else keep_ref
            out_ref[far % (groups // NEAR // 2), low, slot, :] = value[apart * PAIR : (apart + 1) * PAIR, :]
        return carry

    for_blocks(groups, step)


def halve_body(kept_ref, arrived_ref, order_ref, keep_ref, send_ref):
    half = keep_ref.shape[0]
    keep_ref[...] = kept_ref[:half] + arrived_ref[:half]
    send_ref[...] = kept_ref[half:] + arrived_ref[half:]


def first_row(ref):
    return ref[:1, :] if len(ref.shape) == 2 else ref[0, :1, :]


def join_body(kept_ref, arrived_ref, order_ref, out_ref, token_ref):
    token_ref[...] = first_row(order_ref)
    out_ref[...] = kept_ref[0] + arrived_ref[0]


def split_body(*refs):
    *joined, kept_ref, arrived_ref, order_ref = refs[:-NEAR]
    piece = kept_ref.shape[3]
    for index, rows_ref in enumerate(refs[-NEAR:]):
        for chunk, part_ref in enumerate(joined):
            rows_ref[:, chunk * piece : (chunk + 1) * piece] = part_ref[index]
        rows_ref[:, len(joined) * piece :] = kept_ref[0, index] + arrived_ref[0, index]


def pass_body(*refs):
    refs[-1][...] = refs[-2][...]


def last_body(parts_ref, left_ref, *refs):
    basis_ref, solution_ref, sketch_ref = refs[-3:]
    quarters = refs[3 * ITERS : 3 * ITERS + NEAR]
    place = lax.axis_index("row") % NEAR
    piece = quarters[0].shape[1]
    for mask, part_ref in enumerate(quarters):
        for tile in range(0, piece, LANE):
            column = pl.multiple_of((place ^ mask) * piece + tile, LANE)
            sketch_ref[:, pl.ds(column, LANE)] = part_ref[:, tile : tile + LANE]
    betas = [ref[...] for ref in refs[:ITERS]]
    alphas = [ref[...] for ref in refs[ITERS : 2 * ITERS]]
    held = [ref[...] for ref in refs[2 * ITERS : 3 * ITERS]]
    last = jnp.sqrt(tree([parts_ref[i] for i in range(parts_ref.shape[0])])[:1, :])
    basis_ref[...] = left_ref[...] / last
    betas.append(last)
    phibar, rhobar = betas[0], alphas[0]
    search, iterate = held[0], jnp.zeros_like(held[0])
    for step in range(ITERS):
        beta = betas[step + 1]
        rho = jnp.sqrt(rhobar * rhobar + beta * beta)
        cosine = rhobar / rho
        sine = beta / rho
        phi = cosine * phibar
        phibar = sine * phibar
        iterate = iterate + phi / rho * search
        if step + 1 < ITERS:
            alpha = alphas[step + 1]
            search = held[step + 1] - sine * alpha / rho * search
            rhobar = -cosine * alpha
    solution_ref[...] = iterate


def shape(*dims, dtype=F32):
    return jax.ShapeDtypeStruct(dims, dtype)


def shards(design, sign_bits, picks, counts, target, rinv):
    rows, width = design.shape
    whole = rinv.shape[1]
    row_groups = lax.axis_size("row")
    lines = rows // LANE
    scalar = shape(1, LANE)
    deep = message_rows(width)
    left = target.reshape(lines, LANE)
    bits = sign_bits.reshape(lines, LANE)
    chunks = min(CHUNKS, width // NEAR // LANE)
    piece = width // NEAR // chunks
    scale = float(np.sqrt(np.float32(rows * row_groups)))
    slots = row_groups * PAIR
    far = row_groups // NEAR

    sent = [(mask, chunk * piece) for chunk in range(chunks) for mask in range(1, NEAR)]

    message, *away = pl.pallas_call(
        functools.partial(first_body, sent),
        out_shape=(shape(row_groups, rounded(signs_at(width, row_groups) + lines, 8), LANE),)
        + (shape(rows, piece),) * len(sent),
        in_specs=[HBM] * 5,
        out_specs=(VMEM,) + (HBM,) * len(sent),
        scratch_shapes=[
            pltpu.VMEM((rows, width), F32),
            pltpu.VMEM((lines, LANE), F32),
            pltpu.VMEM((lines, LANE), jnp.int32),
            pltpu.VMEM((row_groups, PAIR), jnp.int32),
            pltpu.VMEM((1, row_groups), jnp.int32),
            pltpu.SemaphoreType.DMA((4 + lines * (1 + len(sent)),)),
        ],
        compiler_params=pltpu.CompilerParams(vmem_limit_bytes=58 << 20),
    )(design, left, bits, picks.reshape(row_groups, PAIR), counts.reshape(1, row_groups))

    def swap(array, mask):
        return lax.ppermute(array, "row", [(i, i ^ mask) for i in range(row_groups)])

    def sample(chunk, mixed, order):
        return call(
            functools.partial(sample_body, scale, chunk * piece),
            (shape(far // 2, NEAR, slots, piece),) * 2 + (scalar,),
            design,
            picked,
            mixed,
            order,
            *near[chunk * (NEAR - 1) : (chunk + 1) * (NEAR - 1)],
            scratch=[pltpu.VMEM((NEAR, 2, rows, piece), jnp.bfloat16)],
        )

    def spread(indices, order):
        parts = [away[index] for index in indices]
        if order is not None:
            parts, _ = lax.optimization_barrier((parts, order))
        return [swap(part, sent[index][0]) for index, part in zip(indices, parts)]

    def halve(keep, come, order):
        bit = row_groups // 2
        while bit > NEAR:
            bit //= 2
            half = keep.shape[0] // 2
            keep, send = call(halve_body, (shape(half, *keep.shape[1:]),) * 2, keep, come, order)
            come = swap(send, bit)
        return keep, come

    def join(keep, come, order):
        keep, come = halve(keep, come, order)
        return call(join_body, (shape(*keep.shape[1:]), scalar), keep, come, order)

    def back(rinv, message, first):
        outs, scratch = (shape(whole // LANE, LANE), scalar), [pltpu.VMEM((width // LANE, LANE), F32)]
        operands = (rinv, message)
        if first:
            outs += (shape(row_groups, slots, rows, dtype=jnp.bfloat16), shape(*rinv.shape))
            scratch += [pltpu.SemaphoreType.DMA((width // LANE,))]
            scratch += [pltpu.VMEM((HB, HB), jnp.bfloat16)]
        return pl.pallas_call(
            functools.partial(back_body, first),
            out_shape=outs,
            in_specs=[HBM if first else VMEM] + [VMEM] * (len(operands) - 1),
            out_specs=(VMEM,) * len(outs),
            scratch_shapes=scratch,
            compiler_params=pltpu.CompilerParams(vmem_limit_bytes=(34 if first else 24) << 20),
        )(*operands)

    def forward(terms, token, last, *before):
        return call(
            functools.partial(forward_body, len(terms), not before, last),
            (shape(lines, LANE), shape(width // LANE, LANE), scalar)
            + (() if last else (shape(whole // LANE, LANE),)),
            here,
            design,
            token,
            *terms,
            *before,
        )

    def turn(images, left, beta, alpha, last):
        return call(
            functools.partial(turn_body, len(images), last),
            (shape(lines, LANE), shape(row_groups, 8 if last else deep, LANE)),
            *images,
            left,
            beta,
            alpha,
            *(() if last else (design,)),
        )

    betas, alphas, held, joined, right = [], [], [], [], []
    near = spread(range(NEAR - 1), None)
    message = picked = exchange(message, "row")
    late = len(sent) - (chunks > 1)
    near += spread(range(NEAR - 1, late), message)
    for step in range(ITERS):
        last = step + 1 == ITERS
        if step == 0:
            term, beta, mixed, here = back(rinv, message, True)
            term = pl.pallas_call(
                pass_body,
                out_shape=shape(*term.shape),
                in_specs=[ANY] * (NEAR - 1) + [VMEM],
                out_specs=VMEM,
                compiler_params=pltpu.CompilerParams(vmem_limit_bytes=2 << 20),
            )(*near[: NEAR - 1], term)
        else:
            term, beta = back(here, message, False)
            token = beta
            if chunks > 1:
                part, token = join(keep, come, message)
                joined.append(part)
                keep, send, token = sample(1, mixed, token)
                come = swap(send, row_groups // 2)
        betas.append(beta)
        spare = chunks > 1 and step > 0
        terms = direct(term, "col") if spare else paired(term, "col")
        if step == 0:
            near += spread(range(late, len(sent)), terms[1])
            keep, send, token = sample(0, mixed, beta)
            come = swap(send, row_groups // 2)
        image, kept, alpha, *right = forward(terms, token, last, *right, *betas[1:])
        alphas.append(alpha)
        held.append(kept)
        images = direct(image, "col") if spare else paired(image, "col")
        left, message = turn(images, left, beta, alpha, last)
        message = exchange(message, "row")
    quarters = (shape(slots, width // NEAR),) * NEAR
    mine, *others = call(split_body, quarters, *joined, *halve(keep, come, beta), left)
    basis, answer, sketch = call(
        last_body,
        (shape(lines, LANE), shape(width // LANE, LANE), shape(slots, width)),
        message,
        left,
        *betas,
        *alphas,
        *held,
        mine,
        *(swap(part, mask + 1) for mask, part in enumerate(others)),
    )
    return (sketch, answer.reshape(-1), basis.reshape(-1))


def solution(mesh):
    placed = (
        P("row", "col"),
        P("row"),
        P(None, "row", None),
        P(None, "row"),
        P("row"),
        P("col", None),
    )
    return jax.shard_map(
        shards,
        mesh=mesh,
        in_specs=placed,
        out_specs=(P("row", "col"), P("col"), P("row")),
        check_vma=False,
    )
```

```python
import functools

import jax
import jax.numpy as jnp
import numpy as np
from jax import lax
from jax.experimental import pallas as pl
from jax.experimental.pallas import tpu as pltpu
from jax.sharding import PartitionSpec as P

HB = 256
PAIR = 16
ITERS = 2
LANE = 128
NEAR = 4
CHUNKS = 2
F32 = jnp.float32
VMEM = pl.BlockSpec(memory_space=pltpu.VMEM)
HBM = pl.BlockSpec(memory_space=pltpu.HBM)
ANY = pl.BlockSpec(memory_space=pl.ANY)


def exchange(copies, axis):
    return lax.all_to_all(copies, axis, split_axis=0, concat_axis=0, tiled=True)


def paired(array, axis):
    size = lax.axis_size(axis)
    mask = 1
    while True:
        come = lax.ppermute(array, axis, [(i, i ^ mask) for i in range(size)])
        mask *= 2
        if mask == size:
            return [array, come]
        array = array + come


def direct(array, axis):
    size = lax.axis_size(axis)
    return [array] + [
        lax.ppermute(array, axis, [(i, i ^ mask) for i in range(size)]) for mask in range(1, size)
    ]


def tree(values):
    while len(values) > 1:
        values = [values[i] + values[i + 1] for i in range(0, len(values), 2)]
    return values[0]


def walsh(size):
    parity = lax.broadcasted_iota(jnp.int32, (size, size), 0) & lax.broadcasted_iota(jnp.int32, (size, size), 1)
    for shift in (4, 2, 1):
        parity = parity ^ (parity >> shift)
    return (1 - 2 * (parity & 1)).astype(F32).astype(jnp.bfloat16)


def call(body, out_shape, *operands, scratch=()):
    return pl.pallas_call(
        body,
        out_shape=out_shape,
        in_specs=[VMEM] * len(operands),
        out_specs=jax.tree.map(lambda _: VMEM, out_shape),
        scratch_shapes=scratch,
        compiler_params=pltpu.CompilerParams(vmem_limit_bytes=24 << 20),
    )(*operands)


def fold_rows(block):
    return block.reshape(block.shape[0] // 8, 8, LANE).sum(axis=0)


def total(rows):
    return jnp.sum(jnp.sum(rows, axis=0, keepdims=True), axis=1, keepdims=True)


def splat(scalar):
    return jnp.broadcast_to(scalar, (1, LANE))


def left_product(vector, matrix_ref, out_ref):
    blocks, tiles = matrix_ref.shape[0] // LANE, matrix_ref.shape[1] // LANE
    sums = [jnp.zeros((8, LANE), F32) for _ in range(tiles)]
    for block in range(blocks):
        weight = across(vector[block : block + 1, :])
        for tile in range(tiles):
            part = matrix_ref[block * LANE : (block + 1) * LANE, tile * LANE : (tile + 1) * LANE]
            sums[tile] = sums[tile] + fold_rows(part * weight)
    for tile in range(tiles):
        out_ref[tile : tile + 1, :] = jnp.sum(sums[tile], axis=0, keepdims=True)


def left_product_upper(vector_ref, matrix_ref, out_ref, copies=()):
    blocks, tiles = matrix_ref.shape[0] // LANE, matrix_ref.shape[1] // LANE
    sums = [jnp.zeros((8, LANE), F32) for _ in range(tiles)]
    for block in range(blocks):
        if copies:
            copies[block].wait()
        weight = across(vector_ref[block : block + 1, :])
        for tile in range(block, tiles):
            part = matrix_ref[block * LANE : (block + 1) * LANE, tile * LANE : (tile + 1) * LANE]
            sums[tile] = sums[tile] + fold_rows(part * weight)
    for tile in range(tiles):
        out_ref[tile : tile + 1, :] = jnp.sum(sums[tile], axis=0, keepdims=True)


def right_product(matrix_ref, vector, out_ref):
    blocks, tiles = matrix_ref.shape[0] // LANE, matrix_ref.shape[1] // LANE

    def step(block, carry):
        rows = pl.ds(pl.multiple_of(block * LANE, LANE), LANE)
        sums = jnp.zeros((LANE, LANE), F32)
        for tile in range(tiles):
            sums = sums + matrix_ref[rows, tile * LANE : (tile + 1) * LANE] * vector[tile : tile + 1, :]
        out_ref[pl.ds(block, 1), :] = jnp.sum(fold_rows(sums.T), axis=0, keepdims=True)
        return carry

    lax.fori_loop(0, blocks, step, 0)


def right_product_upper(matrix_ref, vector, out_ref):
    blocks, tiles = matrix_ref.shape[0] // LANE, matrix_ref.shape[1] // LANE
    for block in range(blocks):
        rows = slice(block * LANE, (block + 1) * LANE)
        sums = jnp.zeros((LANE, LANE), F32)
        for tile in range(block, tiles):
            sums = sums + matrix_ref[rows, tile * LANE : (tile + 1) * LANE] * vector[tile : tile + 1, :]
        out_ref[block : block + 1, :] = jnp.sum(fold_rows(sums.T), axis=0, keepdims=True)


def rounded(count, unit):
    return -(-count // unit) * unit


def message_rows(width):
    return rounded(width // LANE + 1, 8)


def picks_at(width):
    return width // LANE + 1


def signs_at(width, groups):
    return picks_at(width) + groups * PAIR // LANE


def copy_out(out_ref):
    first = out_ref[0]
    for index in range(1, out_ref.shape[0]):
        out_ref[index] = first


def across(row):
    return jnp.broadcast_to(row, (LANE, LANE)).T


def first_body(sent, design_ref, target_ref, bits_ref, picks_ref, counts_ref, *refs):
    out_ref, away_refs = refs[0], refs[1:-6]
    design, target_here, bits, picks, counts, sems = refs[-6:]
    rows, width = design.shape
    lines, tiles = rows // LANE, width // LANE
    small = [
        pltpu.make_async_copy(source, place, sems.at[index])
        for index, (source, place) in enumerate(
            ((target_ref, target_here), (bits_ref, bits), (picks_ref, picks), (counts_ref, counts))
        )
    ]
    parts = [slice(line * LANE, (line + 1) * LANE) for line in range(lines)]
    large = [
        pltpu.make_async_copy(design_ref.at[part, :], design.at[part, :], sems.at[4 + line])
        for line, part in enumerate(parts)
    ]
    place = lax.axis_index("row") % NEAR
    away = []
    for index, away_ref in enumerate(away_refs):
        piece = away_ref.shape[1]
        mask, start = sent[index]
        column = pl.multiple_of((place ^ mask) * (width // NEAR) + start, LANE)
        for line, part in enumerate(parts):
            source = design.at[part, pl.ds(column, piece)]
            away.append(pltpu.make_async_copy(source, away_ref.at[part, :], sems.at[4 + lines * (index + 1) + line]))
    for copy in small + large:
        copy.start()
    for copy in small:
        copy.wait()
    out_ref[0] = jnp.zeros(out_ref.shape[1:], F32)
    groups = picks.shape[0]
    owner = lax.broadcasted_iota(jnp.int32, (groups, groups), 0)
    same = owner == lax.broadcasted_iota(jnp.int32, (groups, groups), 1)
    limit = jnp.sum(jnp.where(same, counts[...].astype(F32), 0.0), axis=1, keepdims=True)
    slot = lax.broadcasted_iota(jnp.int32, picks.shape, 1).astype(F32)
    coded = jnp.where(slot < limit, picks[...].astype(F32), -1.0)
    start = picks_at(width)
    for owner in range(0, groups, LANE // PAIR):
        line = jnp.concatenate([coded[i : i + 1, :] for i in range(owner, owner + LANE // PAIR)], axis=1)
        out_ref[0, start + owner * PAIR // LANE : start + owner * PAIR // LANE + 1, :] = line
    start = signs_at(width, groups)
    out_ref[0, start : start + lines, :] = (2 * bits[...] - 1).astype(F32)
    target = target_here[...]
    out_ref[0, tiles : tiles + 1, :] = splat(total(target * target))
    sums = [jnp.zeros((8, LANE), F32) for _ in range(tiles)]
    for line, part in enumerate(parts):
        weight = across(target[line : line + 1, :])
        large[line].wait()
        for copy in away[line::lines]:
            copy.start()
        for tile in range(tiles):
            sums[tile] = sums[tile] + fold_rows(design[part, tile * LANE : (tile + 1) * LANE] * weight)
    for tile in range(tiles):
        out_ref[0, tile : tile + 1, :] = jnp.sum(sums[tile], axis=0, keepdims=True)
    copy_out(out_ref)
    for copy in away:
        copy.wait()


def back_body(first, rinv_ref, parts_ref, *refs):
    if first:
        term_ref, beta_ref, mix_ref, *refs, walsh_ref = refs
    else:
        term_ref, beta_ref, *refs = refs
    tiles = rinv_ref.shape[0] // LANE
    copies = []
    if first:
        rinv_here, scratch, sems = refs
        for block in range(tiles):
            part, right = slice(block * LANE, (block + 1) * LANE), slice(block * LANE, rinv_ref.shape[1])
            copies.append(pltpu.make_async_copy(rinv_ref.at[part, right], rinv_here.at[part, right], sems.at[block]))
            copies[-1].start()
        walsh_ref[...] = walsh(HB)
        mix_body(rinv_ref.shape[0], parts_ref, walsh_ref, mix_ref)
    else:
        rinv_here, (scratch,) = rinv_ref, refs
    summed = tree([parts_ref[i, : tiles + 1, :] for i in range(parts_ref.shape[0])])
    beta = jnp.sqrt(summed[tiles : tiles + 1, :])
    beta_ref[...] = beta
    scratch[...] = summed[:tiles, :] / beta
    left_product_upper(scratch, rinv_here, term_ref, copies)


def forward_body(groups, first, last, rinv_ref, design_ref, token_ref, *refs):
    right = tree([ref[...] for ref in refs[:groups]])
    refs = refs[groups:]
    if not first:
        before_ref, beta_ref, *refs = refs
        right = right - beta_ref[...] * before_ref[...]
    image_ref, held_ref, alpha_ref, *right_refs = refs
    alpha = jnp.sqrt(total(right * right))
    alpha_ref[...] = splat(alpha)
    right = right / alpha
    if not last:
        right_refs[0][...] = right
    right_product_upper(rinv_ref, right, held_ref)
    right_product(design_ref, held_ref[...], image_ref)


def turn_body(groups, last, *refs):
    left = tree([ref[...] for ref in refs[:groups]])
    before_ref, beta_ref, alpha_ref, *refs = refs[groups:]
    left = left - alpha_ref[...] * (before_ref[...] / beta_ref[...])
    square = splat(total(left * left))
    if last:
        left_ref, out_ref = refs
        out_ref[...] = jnp.broadcast_to(square, out_ref.shape)
    else:
        design_ref, left_ref, out_ref = refs
        tiles = design_ref.shape[1] // LANE
        out_ref[0] = jnp.zeros(out_ref.shape[1:], F32)
        left_product(left, design_ref, out_ref.at[0])
        out_ref[0, tiles : tiles + 1, :] = square
        copy_out(out_ref)
    left_ref[...] = left


def pieces(value):
    high = value.astype(jnp.bfloat16)
    return high, (value - high.astype(F32)).astype(jnp.bfloat16)


def weigh(mix, high, low):
    return jnp.dot(mix, high, preferred_element_type=F32) + jnp.dot(mix, low, preferred_element_type=F32)


def for_blocks(groups, step):
    if groups <= 8:
        for block in range(groups):
            step(block, 0)
    else:
        lax.fori_loop(0, groups, step, 0)


def mix_body(width, parts_ref, walsh_ref, mix_ref):
    groups, _, rows = mix_ref.shape
    me = lax.axis_index("row")
    local = lax.broadcasted_iota(jnp.int32, (LANE, rows), 1).astype(F32)
    per = LANE // PAIR

    def step(block, carry):
        parity = jnp.int32(0)
        for bit in range(groups.bit_length() - 1):
            parity = parity ^ ((block & me) >> bit)
        sign = (1 - 2 * (parity & 1)).astype(F32)
        for line in range(groups // per):
            start = picks_at(width) + line
            coded = across(parts_ref[block, start : start + 1, :])
            match = jnp.concatenate([coded] * (rows // LANE), axis=1) == local
            chosen = jnp.where(match, sign, 0.0).astype(jnp.bfloat16)
            for part in range(rows // HB):
                columns = slice(part * HB, (part + 1) * HB)
                mixed = jnp.dot(chosen[:, columns], walsh_ref[...], preferred_element_type=F32).astype(jnp.bfloat16)
                for index in range(per):
                    place = pl.multiple_of(((line * per + index) ^ me) * PAIR, PAIR)
                    mix_ref[block, pl.ds(place, PAIR), columns] = mixed[index * PAIR : (index + 1) * PAIR, :]
        return carry

    for_blocks(groups, step)


def sample_body(scale, start, design_ref, parts_ref, mix_ref, order_ref, *refs):
    near, (keep_ref, send_ref, token_ref, both) = refs[: NEAR - 1], refs[NEAR - 1 :]
    token_ref[...] = first_row(order_ref)
    rows, piece = near[-1].shape
    width = design_ref.shape[1]
    groups = mix_ref.shape[0]
    me = lax.axis_index("row")
    signs_start = signs_at(width, groups)
    for line in range(rows // LANE):
        part = slice(line * LANE, (line + 1) * LANE)
        signs = [across(parts_ref[me ^ mask, signs_start + line : signs_start + line + 1, :]) for mask in range(NEAR)]
        for tile in range(0, piece, LANE):
            column = pl.multiple_of(me % NEAR * (width // NEAR) + start + tile, LANE)
            here = slice(tile, tile + LANE)
            values = [design_ref[part, pl.ds(column, LANE)]] + [ref[part, here] for ref in near]
            values = [value * sign for value, sign in zip(values, signs)]
            apart = 1
            while apart < NEAR:
                for first in range(NEAR):
                    if not first & apart:
                        one, two = values[first], values[first | apart]
                        values[first], values[first | apart] = one + two, one - two
                apart *= 2
            for index, value in enumerate(values):
                both[index, 0, part, here], both[index, 1, part, here] = pieces(value)

    def step(block, carry):
        value = weigh(mix_ref[block], both[block % NEAR, 0], both[block % NEAR, 1]) / scale
        slot = pl.ds(block * PAIR, PAIR)
        for apart in range(groups):
            far, low = apart // NEAR, apart % NEAR
            out_ref = send_ref if far >= groups // NEAR // 2 else keep_ref
            out_ref[far % (groups // NEAR // 2), low, slot, :] = value[apart * PAIR : (apart + 1) * PAIR, :]
        return carry

    for_blocks(groups, step)


def halve_body(kept_ref, arrived_ref, order_ref, keep_ref, send_ref):
    half = keep_ref.shape[0]
    keep_ref[...] = kept_ref[:half] + arrived_ref[:half]
    send_ref[...] = kept_ref[half:] + arrived_ref[half:]


def first_row(ref):
    return ref[:1, :] if len(ref.shape) == 2 else ref[0, :1, :]


def join_body(kept_ref, arrived_ref, order_ref, out_ref, token_ref):
    token_ref[...] = first_row(order_ref)
    out_ref[...] = kept_ref[0] + arrived_ref[0]


def split_body(*refs):
    *joined, kept_ref, arrived_ref, order_ref = refs[:-NEAR]
    piece = kept_ref.shape[3]
    for index, rows_ref in enumerate(refs[-NEAR:]):
        for chunk, part_ref in enumerate(joined):
            rows_ref[:, chunk * piece : (chunk + 1) * piece] = part_ref[index]
        rows_ref[:, len(joined) * piece :] = kept_ref[0, index] + arrived_ref[0, index]


def pass_body(*refs):
    refs[-1][...] = refs[-2][...]


def last_body(parts_ref, left_ref, *refs):
    basis_ref, solution_ref, sketch_ref = refs[-3:]
    quarters = refs[3 * ITERS : 3 * ITERS + NEAR]
    place = lax.axis_index("row") % NEAR
    piece = quarters[0].shape[1]
    for mask, part_ref in enumerate(quarters):
        for tile in range(0, piece, LANE):
            column = pl.multiple_of((place ^ mask) * piece + tile, LANE)
            sketch_ref[:, pl.ds(column, LANE)] = part_ref[:, tile : tile + LANE]
    betas = [ref[...] for ref in refs[:ITERS]]
    alphas = [ref[...] for ref in refs[ITERS : 2 * ITERS]]
    held = [ref[...] for ref in refs[2 * ITERS : 3 * ITERS]]
    last = jnp.sqrt(tree([parts_ref[i] for i in range(parts_ref.shape[0])])[:1, :])
    basis_ref[...] = left_ref[...] / last
    betas.append(last)
    phibar, rhobar = betas[0], alphas[0]
    search, iterate = held[0], jnp.zeros_like(held[0])
    for step in range(ITERS):
        beta = betas[step + 1]
        rho = jnp.sqrt(rhobar * rhobar + beta * beta)
        cosine = rhobar / rho
        sine = beta / rho
        phi = cosine * phibar
        phibar = sine * phibar
        iterate = iterate + phi / rho * search
        if step + 1 < ITERS:
            alpha = alphas[step + 1]
            search = held[step + 1] - sine * alpha / rho * search
            rhobar = -cosine * alpha
    solution_ref[...] = iterate


def shape(*dims, dtype=F32):
    return jax.ShapeDtypeStruct(dims, dtype)


def shards(design, sign_bits, picks, counts, target, rinv):
    rows, width = design.shape
    whole = rinv.shape[1]
    row_groups = lax.axis_size("row")
    lines = rows // LANE
    scalar = shape(1, LANE)
    deep = message_rows(width)
    left = target.reshape(lines, LANE)
    bits = sign_bits.reshape(lines, LANE)
    chunks = min(CHUNKS, width // NEAR // LANE)
    piece = width // NEAR // chunks
    scale = float(np.sqrt(np.float32(rows * row_groups)))
    slots = row_groups * PAIR
    far = row_groups // NEAR

    sent = [(mask, chunk * piece) for chunk in range(chunks) for mask in range(1, NEAR)]

    message, *away = pl.pallas_call(
        functools.partial(first_body, sent),
        out_shape=(shape(row_groups, rounded(signs_at(width, row_groups) + lines, 8), LANE),)
        + (shape(rows, piece),) * len(sent),
        in_specs=[HBM] * 5,
        out_specs=(VMEM,) + (HBM,) * len(sent),
        scratch_shapes=[
            pltpu.VMEM((rows, width), F32),
            pltpu.VMEM((lines, LANE), F32),
            pltpu.VMEM((lines, LANE), jnp.int32),
            pltpu.VMEM((row_groups, PAIR), jnp.int32),
            pltpu.VMEM((1, row_groups), jnp.int32),
            pltpu.SemaphoreType.DMA((4 + lines * (1 + len(sent)),)),
        ],
        compiler_params=pltpu.CompilerParams(vmem_limit_bytes=58 << 20),
    )(design, left, bits, picks.reshape(row_groups, PAIR), counts.reshape(1, row_groups))

    def swap(array, mask):
        return lax.ppermute(array, "row", [(i, i ^ mask) for i in range(row_groups)])

    def sample(chunk, mixed, order):
        return call(
            functools.partial(sample_body, scale, chunk * piece),
            (shape(far // 2, NEAR, slots, piece),) * 2 + (scalar,),
            design,
            picked,
            mixed,
            order,
            *near[chunk * (NEAR - 1) : (chunk + 1) * (NEAR - 1)],
            scratch=[pltpu.VMEM((NEAR, 2, rows, piece), jnp.bfloat16)],
        )

    def spread(indices, order):
        parts = [away[index] for index in indices]
        if order is not None:
            parts, _ = lax.optimization_barrier((parts, order))
        return [swap(part, sent[index][0]) for index, part in zip(indices, parts)]

    def halve(keep, come, order):
        bit = row_groups // 2
        while bit > NEAR:
            bit //= 2
            half = keep.shape[0] // 2
            keep, send = call(halve_body, (shape(half, *keep.shape[1:]),) * 2, keep, come, order)
            come = swap(send, bit)
        return keep, come

    def join(keep, come, order):
        keep, come = halve(keep, come, order)
        return call(join_body, (shape(*keep.shape[1:]), scalar), keep, come, order)

    def back(rinv, message, first):
        outs, scratch = (shape(whole // LANE, LANE), scalar), [pltpu.VMEM((width // LANE, LANE), F32)]
        operands = (rinv, message)
        if first:
            outs += (shape(row_groups, slots, rows, dtype=jnp.bfloat16), shape(*rinv.shape))
            scratch += [pltpu.SemaphoreType.DMA((width // LANE,))]
            scratch += [pltpu.VMEM((HB, HB), jnp.bfloat16)]
        return pl.pallas_call(
            functools.partial(back_body, first),
            out_shape=outs,
            in_specs=[HBM if first else VMEM] + [VMEM] * (len(operands) - 1),
            out_specs=(VMEM,) * len(outs),
            scratch_shapes=scratch,
            compiler_params=pltpu.CompilerParams(vmem_limit_bytes=(34 if first else 24) << 20),
        )(*operands)

    def forward(terms, token, last, *before):
        return call(
            functools.partial(forward_body, len(terms), not before, last),
            (shape(lines, LANE), shape(width // LANE, LANE), scalar)
            + (() if last else (shape(whole // LANE, LANE),)),
            here,
            design,
            token,
            *terms,
            *before,
        )

    def turn(images, left, beta, alpha, last):
        return call(
            functools.partial(turn_body, len(images), last),
            (shape(lines, LANE), shape(row_groups, 8 if last else deep, LANE)),
            *images,
            left,
            beta,
            alpha,
            *(() if last else (design,)),
        )

    betas, alphas, held, joined, right = [], [], [], [], []
    near = spread(range(NEAR - 2), None)
    message = picked = exchange(message, "row")
    late = len(sent) - (chunks > 1)
    near += spread(range(NEAR - 2, late), message)
    for step in range(ITERS):
        last = step + 1 == ITERS
        if step == 0:
            term, beta, mixed, here = back(rinv, message, True)
            term = pl.pallas_call(
                pass_body,
                out_shape=shape(*term.shape),
                in_specs=[ANY] * (NEAR - 2) + [VMEM],
                out_specs=VMEM,
                compiler_params=pltpu.CompilerParams(vmem_limit_bytes=2 << 20),
            )(*near[: NEAR - 2], term)
        else:
            term, beta = back(here, message, False)
            token = beta
            if chunks > 1:
                part, token = join(keep, come, message)
                joined.append(part)
                keep, send, token = sample(1, mixed, token)
                come = swap(send, row_groups // 2)
        betas.append(beta)
        spare = chunks > 1 and step > 0
        terms = direct(term, "col") if spare else paired(term, "col")
        if step == 0:
            near += spread(range(late, len(sent)), terms[1])
            keep, send, token = sample(0, mixed, beta)
            come = swap(send, row_groups // 2)
        image, kept, alpha, *right = forward(terms, token, last, *right, *betas[1:])
        alphas.append(alpha)
        held.append(kept)
        images = direct(image, "col") if spare else paired(image, "col")
        left, message = turn(images, left, beta, alpha, last)
        message = exchange(message, "row")
    quarters = (shape(slots, width // NEAR),) * NEAR
    mine, *others = call(split_body, quarters, *joined, *halve(keep, come, beta), left)
    basis, answer, sketch = call(
        last_body,
        (shape(lines, LANE), shape(width // LANE, LANE), shape(slots, width)),
        message,
        left,
        *betas,
        *alphas,
        *held,
        mine,
        *(swap(part, mask + 1) for mask, part in enumerate(others)),
    )
    return (sketch, answer.reshape(-1), basis.reshape(-1))


def solution(mesh):
    placed = (
        P("row", "col"),
        P("row"),
        P(None, "row", None),
        P(None, "row"),
        P("row"),
        P("col", None),
    )
    return jax.shard_map(
        shards,
        mesh=mesh,
        in_specs=placed,
        out_specs=(P("row", "col"), P("col"), P("row")),
        check_vma=False,
    )
```

```python
import functools

import jax
import jax.numpy as jnp
import numpy as np
from jax import lax
from jax.experimental import pallas as pl
from jax.experimental.pallas import tpu as pltpu
from jax.sharding import PartitionSpec as P

HB = 256
PAIR = 16
ITERS = 2
LANE = 128
NEAR = 4
CHUNKS = 2
F32 = jnp.float32
VMEM = pl.BlockSpec(memory_space=pltpu.VMEM)
HBM = pl.BlockSpec(memory_space=pltpu.HBM)
ANY = pl.BlockSpec(memory_space=pl.ANY)


def exchange(copies, axis):
    return lax.all_to_all(copies, axis, split_axis=0, concat_axis=0, tiled=True)


def paired(array, axis):
    size = lax.axis_size(axis)
    mask = 1
    while True:
        come = lax.ppermute(array, axis, [(i, i ^ mask) for i in range(size)])
        mask *= 2
        if mask == size:
            return [array, come]
        array = array + come


def direct(array, axis):
    size = lax.axis_size(axis)
    return [array] + [
        lax.ppermute(array, axis, [(i, i ^ mask) for i in range(size)]) for mask in range(1, size)
    ]


def tree(values):
    while len(values) > 1:
        values = [values[i] + values[i + 1] for i in range(0, len(values), 2)]
    return values[0]


def walsh(size):
    parity = lax.broadcasted_iota(jnp.int32, (size, size), 0) & lax.broadcasted_iota(jnp.int32, (size, size), 1)
    for shift in (4, 2, 1):
        parity = parity ^ (parity >> shift)
    return (1 - 2 * (parity & 1)).astype(F32).astype(jnp.bfloat16)


def call(body, out_shape, *operands, scratch=()):
    return pl.pallas_call(
        body,
        out_shape=out_shape,
        in_specs=[VMEM] * len(operands),
        out_specs=jax.tree.map(lambda _: VMEM, out_shape),
        scratch_shapes=scratch,
        compiler_params=pltpu.CompilerParams(vmem_limit_bytes=24 << 20),
    )(*operands)


def fold_rows(block):
    return block.reshape(block.shape[0] // 8, 8, LANE).sum(axis=0)


def total(rows):
    return jnp.sum(jnp.sum(rows, axis=0, keepdims=True), axis=1, keepdims=True)


def splat(scalar):
    return jnp.broadcast_to(scalar, (1, LANE))


def left_product(vector, matrix_ref, out_ref):
    blocks, tiles = matrix_ref.shape[0] // LANE, matrix_ref.shape[1] // LANE
    sums = [jnp.zeros((8, LANE), F32) for _ in range(tiles)]
    for block in range(blocks):
        weight = across(vector[block : block + 1, :])
        for tile in range(tiles):
            part = matrix_ref[block * LANE : (block + 1) * LANE, tile * LANE : (tile + 1) * LANE]
            sums[tile] = sums[tile] + fold_rows(part * weight)
    for tile in range(tiles):
        out_ref[tile : tile + 1, :] = jnp.sum(sums[tile], axis=0, keepdims=True)


def left_product_upper(vector_ref, matrix_ref, out_ref, copies=()):
    blocks, tiles = matrix_ref.shape[0] // LANE, matrix_ref.shape[1] // LANE
    sums = [jnp.zeros((8, LANE), F32) for _ in range(tiles)]
    for block in range(blocks):
        if copies:
            copies[block].wait()
        weight = across(vector_ref[block : block + 1, :])
        for tile in range(block, tiles):
            part = matrix_ref[block * LANE : (block + 1) * LANE, tile * LANE : (tile + 1) * LANE]
            sums[tile] = sums[tile] + fold_rows(part * weight)
    for tile in range(tiles):
        out_ref[tile : tile + 1, :] = jnp.sum(sums[tile], axis=0, keepdims=True)


def right_product(matrix_ref, vector, out_ref):
    blocks, tiles = matrix_ref.shape[0] // LANE, matrix_ref.shape[1] // LANE

    def step(block, carry):
        rows = pl.ds(pl.multiple_of(block * LANE, LANE), LANE)
        sums = jnp.zeros((LANE, LANE), F32)
        for tile in range(tiles):
            sums = sums + matrix_ref[rows, tile * LANE : (tile + 1) * LANE] * vector[tile : tile + 1, :]
        out_ref[pl.ds(block, 1), :] = jnp.sum(fold_rows(sums.T), axis=0, keepdims=True)
        return carry

    lax.fori_loop(0, blocks, step, 0)


def right_product_upper(matrix_ref, vector, out_ref):
    blocks, tiles = matrix_ref.shape[0] // LANE, matrix_ref.shape[1] // LANE
    for block in range(blocks):
        rows = slice(block * LANE, (block + 1) * LANE)
        sums = jnp.zeros((LANE, LANE), F32)
        for tile in range(block, tiles):
            sums = sums + matrix_ref[rows, tile * LANE : (tile + 1) * LANE] * vector[tile : tile + 1, :]
        out_ref[block : block + 1, :] = jnp.sum(fold_rows(sums.T), axis=0, keepdims=True)


def rounded(count, unit):
    return -(-count // unit) * unit


def message_rows(width):
    return rounded(width // LANE + 1, 8)


def picks_at(width):
    return width // LANE + 1


def signs_at(width, groups):
    return picks_at(width) + groups * PAIR // LANE


def copy_out(out_ref):
    first = out_ref[0]
    for index in range(1, out_ref.shape[0]):
        out_ref[index] = first


def across(row):
    return jnp.broadcast_to(row, (LANE, LANE)).T


def first_body(sent, design_ref, target_ref, bits_ref, picks_ref, counts_ref, *refs):
    out_ref, away_refs = refs[0], refs[1:-6]
    design, target_here, bits, picks, counts, sems = refs[-6:]
    rows, width = design.shape
    lines, tiles = rows // LANE, width // LANE
    small = [
        pltpu.make_async_copy(source, place, sems.at[index])
        for index, (source, place) in enumerate(
            ((target_ref, target_here), (bits_ref, bits), (picks_ref, picks), (counts_ref, counts))
        )
    ]
    parts = [slice(line * LANE, (line + 1) * LANE) for line in range(lines)]
    large = [
        pltpu.make_async_copy(design_ref.at[part, :], design.at[part, :], sems.at[4 + line])
        for line, part in enumerate(parts)
    ]
    place = lax.axis_index("row") % NEAR
    away = []
    for index, away_ref in enumerate(away_refs):
        piece = away_ref.shape[1]
        mask, start = sent[index]
        column = pl.multiple_of((place ^ mask) * (width // NEAR) + start, LANE)
        for line, part in enumerate(parts):
            source = design.at[part, pl.ds(column, piece)]
            away.append(pltpu.make_async_copy(source, away_ref.at[part, :], sems.at[4 + lines * (index + 1) + line]))
    for copy in small + large:
        copy.start()
    for copy in small:
        copy.wait()
    out_ref[0] = jnp.zeros(out_ref.shape[1:], F32)
    groups = picks.shape[0]
    owner = lax.broadcasted_iota(jnp.int32, (groups, groups), 0)
    same = owner == lax.broadcasted_iota(jnp.int32, (groups, groups), 1)
    limit = jnp.sum(jnp.where(same, counts[...].astype(F32), 0.0), axis=1, keepdims=True)
    slot = lax.broadcasted_iota(jnp.int32, picks.shape, 1).astype(F32)
    coded = jnp.where(slot < limit, picks[...].astype(F32), -1.0)
    start = picks_at(width)
    for owner in range(0, groups, LANE // PAIR):
        line = jnp.concatenate([coded[i : i + 1, :] for i in range(owner, owner + LANE // PAIR)], axis=1)
        out_ref[0, start + owner * PAIR // LANE : start + owner * PAIR // LANE + 1, :] = line
    start = signs_at(width, groups)
    out_ref[0, start : start + lines, :] = (2 * bits[...] - 1).astype(F32)
    target = target_here[...]
    out_ref[0, tiles : tiles + 1, :] = splat(total(target * target))
    sums = [jnp.zeros((8, LANE), F32) for _ in range(tiles)]
    for line, part in enumerate(parts):
        weight = across(target[line : line + 1, :])
        large[line].wait()
        for copy in away[line::lines]:
            copy.start()
        for tile in range(tiles):
            sums[tile] = sums[tile] + fold_rows(design[part, tile * LANE : (tile + 1) * LANE] * weight)
    for tile in range(tiles):
        out_ref[0, tile : tile + 1, :] = jnp.sum(sums[tile], axis=0, keepdims=True)
    copy_out(out_ref)
    for copy in away:
        copy.wait()


def back_body(first, rinv_ref, parts_ref, *refs):
    if first:
        term_ref, beta_ref, mix_ref, *refs, walsh_ref = refs
    else:
        term_ref, beta_ref, *refs = refs
    tiles = rinv_ref.shape[0] // LANE
    copies = []
    if first:
        rinv_here, scratch, sems = refs
        for block in range(tiles):
            part, right = slice(block * LANE, (block + 1) * LANE), slice(block * LANE, rinv_ref.shape[1])
            copies.append(pltpu.make_async_copy(rinv_ref.at[part, right], rinv_here.at[part, right], sems.at[block]))
            copies[-1].start()
        walsh_ref[...] = walsh(HB)
        mix_body(rinv_ref.shape[0], parts_ref, walsh_ref, mix_ref)
    else:
        rinv_here, (scratch,) = rinv_ref, refs
    summed = tree([parts_ref[i, : tiles + 1, :] for i in range(parts_ref.shape[0])])
    beta = jnp.sqrt(summed[tiles : tiles + 1, :])
    beta_ref[...] = beta
    scratch[...] = summed[:tiles, :] / beta
    left_product_upper(scratch, rinv_here, term_ref, copies)


def forward_body(groups, first, last, rinv_ref, design_ref, token_ref, *refs):
    right = tree([ref[...] for ref in refs[:groups]])
    refs = refs[groups:]
    if not first:
        before_ref, beta_ref, *refs = refs
        right = right - beta_ref[...] * before_ref[...]
    image_ref, held_ref, alpha_ref, *right_refs = refs
    alpha = jnp.sqrt(total(right * right))
    alpha_ref[...] = splat(alpha)
    right = right / alpha
    if not last:
        right_refs[0][...] = right
    right_product_upper(rinv_ref, right, held_ref)
    right_product(design_ref, held_ref[...], image_ref)


def turn_body(groups, last, *refs):
    left = tree([ref[...] for ref in refs[:groups]])
    before_ref, beta_ref, alpha_ref, *refs = refs[groups:]
    left = left - alpha_ref[...] * (before_ref[...] / beta_ref[...])
    square = splat(total(left * left))
    if last:
        left_ref, out_ref = refs
        out_ref[...] = jnp.broadcast_to(square, out_ref.shape)
    else:
        design_ref, left_ref, out_ref = refs
        tiles = design_ref.shape[1] // LANE
        out_ref[0] = jnp.zeros(out_ref.shape[1:], F32)
        left_product(left, design_ref, out_ref.at[0])
        out_ref[0, tiles : tiles + 1, :] = square
        copy_out(out_ref)
    left_ref[...] = left


def pieces(value):
    high = value.astype(jnp.bfloat16)
    return high, (value - high.astype(F32)).astype(jnp.bfloat16)


def weigh(mix, high, low):
    return jnp.dot(mix, high, preferred_element_type=F32) + jnp.dot(mix, low, preferred_element_type=F32)


def for_blocks(groups, step):
    if groups <= 8:
        for block in range(groups):
            step(block, 0)
    else:
        lax.fori_loop(0, groups, step, 0)


def mix_body(width, parts_ref, walsh_ref, mix_ref):
    groups, _, rows = mix_ref.shape
    me = lax.axis_index("row")
    local = lax.broadcasted_iota(jnp.int32, (LANE, rows), 1).astype(F32)
    per = LANE // PAIR

    def step(block, carry):
        parity = jnp.int32(0)
        for bit in range(groups.bit_length() - 1):
            parity = parity ^ ((block & me) >> bit)
        sign = (1 - 2 * (parity & 1)).astype(F32)
        for line in range(groups // per):
            start = picks_at(width) + line
            coded = across(parts_ref[block, start : start + 1, :])
            match = jnp.concatenate([coded] * (rows // LANE), axis=1) == local
            chosen = jnp.where(match, sign, 0.0).astype(jnp.bfloat16)
            for part in range(rows // HB):
                columns = slice(part * HB, (part + 1) * HB)
                mixed = jnp.dot(chosen[:, columns], walsh_ref[...], preferred_element_type=F32).astype(jnp.bfloat16)
                for index in range(per):
                    place = pl.multiple_of(((line * per + index) ^ me) * PAIR, PAIR)
                    mix_ref[block, pl.ds(place, PAIR), columns] = mixed[index * PAIR : (index + 1) * PAIR, :]
        return carry

    for_blocks(groups, step)


def sample_body(scale, start, design_ref, parts_ref, mix_ref, order_ref, *refs):
    near, (keep_ref, send_ref, token_ref, both) = refs[: NEAR - 1], refs[NEAR - 1 :]
    token_ref[...] = first_row(order_ref)
    rows, piece = near[-1].shape
    width = design_ref.shape[1]
    groups = mix_ref.shape[0]
    me = lax.axis_index("row")
    signs_start = signs_at(width, groups)
    for line in range(rows // LANE):
        part = slice(line * LANE, (line + 1) * LANE)
        signs = [across(parts_ref[me ^ mask, signs_start + line : signs_start + line + 1, :]) for mask in range(NEAR)]
        for tile in range(0, piece, LANE):
            column = pl.multiple_of(me % NEAR * (width // NEAR) + start + tile, LANE)
            here = slice(tile, tile + LANE)
            values = [design_ref[part, pl.ds(column, LANE)]] + [ref[part, here] for ref in near]
            values = [value * sign for value, sign in zip(values, signs)]
            apart = 1
            while apart < NEAR:
                for first in range(NEAR):
                    if not first & apart:
                        one, two = values[first], values[first | apart]
                        values[first], values[first | apart] = one + two, one - two
                apart *= 2
            for index, value in enumerate(values):
                both[index, 0, part, here], both[index, 1, part, here] = pieces(value)

    def step(block, carry):
        value = weigh(mix_ref[block], both[block % NEAR, 0], both[block % NEAR, 1]) / scale
        slot = pl.ds(block * PAIR, PAIR)
        for apart in range(groups):
            far, low = apart // NEAR, apart % NEAR
            out_ref = send_ref if far >= groups // NEAR // 2 else keep_ref
            out_ref[far % (groups // NEAR // 2), low, slot, :] = value[apart * PAIR : (apart + 1) * PAIR, :]
        return carry

    for_blocks(groups, step)


def halve_body(kept_ref, arrived_ref, order_ref, keep_ref, send_ref):
    half = keep_ref.shape[0]
    keep_ref[...] = kept_ref[:half] + arrived_ref[:half]
    send_ref[...] = kept_ref[half:] + arrived_ref[half:]


def first_row(ref):
    return ref[:1, :] if len(ref.shape) == 2 else ref[0, :1, :]


def join_body(kept_ref, arrived_ref, order_ref, out_ref, token_ref):
    token_ref[...] = first_row(order_ref)
    out_ref[...] = kept_ref[0] + arrived_ref[0]


def split_body(*refs):
    *joined, kept_ref, arrived_ref, order_ref = refs[:-NEAR]
    piece = kept_ref.shape[3]
    for index, rows_ref in enumerate(refs[-NEAR:]):
        for chunk, part_ref in enumerate(joined):
            rows_ref[:, chunk * piece : (chunk + 1) * piece] = part_ref[index]
        rows_ref[:, len(joined) * piece :] = kept_ref[0, index] + arrived_ref[0, index]


def pass_body(*refs):
    refs[-1][...] = refs[-2][...]


def last_body(parts_ref, left_ref, *refs):
    basis_ref, solution_ref, sketch_ref = refs[-3:]
    quarters = refs[3 * ITERS : 3 * ITERS + NEAR]
    place = lax.axis_index("row") % NEAR
    piece = quarters[0].shape[1]
    for mask, part_ref in enumerate(quarters):
        for tile in range(0, piece, LANE):
            column = pl.multiple_of((place ^ mask) * piece + tile, LANE)
            sketch_ref[:, pl.ds(column, LANE)] = part_ref[:, tile : tile + LANE]
    betas = [ref[...] for ref in refs[:ITERS]]
    alphas = [ref[...] for ref in refs[ITERS : 2 * ITERS]]
    held = [ref[...] for ref in refs[2 * ITERS : 3 * ITERS]]
    last = jnp.sqrt(tree([parts_ref[i] for i in range(parts_ref.shape[0])])[:1, :])
    basis_ref[...] = left_ref[...] / last
    betas.append(last)
    phibar, rhobar = betas[0], alphas[0]
    search, iterate = held[0], jnp.zeros_like(held[0])
    for step in range(ITERS):
        beta = betas[step + 1]
        rho = jnp.sqrt(rhobar * rhobar + beta * beta)
        cosine = rhobar / rho
        sine = beta / rho
        phi = cosine * phibar
        phibar = sine * phibar
        iterate = iterate + phi / rho * search
        if step + 1 < ITERS:
            alpha = alphas[step + 1]
            search = held[step + 1] - sine * alpha / rho * search
            rhobar = -cosine * alpha
    solution_ref[...] = iterate


def shape(*dims, dtype=F32):
    return jax.ShapeDtypeStruct(dims, dtype)


def shards(design, sign_bits, picks, counts, target, rinv):
    rows, width = design.shape
    whole = rinv.shape[1]
    row_groups = lax.axis_size("row")
    lines = rows // LANE
    scalar = shape(1, LANE)
    deep = message_rows(width)
    left = target.reshape(lines, LANE)
    bits = sign_bits.reshape(lines, LANE)
    chunks = min(CHUNKS, width // NEAR // LANE)
    piece = width // NEAR // chunks
    scale = float(np.sqrt(np.float32(rows * row_groups)))
    slots = row_groups * PAIR
    far = row_groups // NEAR

    sent = [(mask, chunk * piece) for chunk in range(chunks) for mask in range(1, NEAR)]

    message, *away = pl.pallas_call(
        functools.partial(first_body, sent),
        out_shape=(shape(row_groups, rounded(signs_at(width, row_groups) + lines, 8), LANE),)
        + (shape(rows, piece),) * len(sent),
        in_specs=[HBM] * 5,
        out_specs=(VMEM,) + (HBM,) * len(sent),
        scratch_shapes=[
            pltpu.VMEM((rows, width), F32),
            pltpu.VMEM((lines, LANE), F32),
            pltpu.VMEM((lines, LANE), jnp.int32),
            pltpu.VMEM((row_groups, PAIR), jnp.int32),
            pltpu.VMEM((1, row_groups), jnp.int32),
            pltpu.SemaphoreType.DMA((4 + lines * (1 + len(sent)),)),
        ],
        compiler_params=pltpu.CompilerParams(vmem_limit_bytes=58 << 20),
    )(design, left, bits, picks.reshape(row_groups, PAIR), counts.reshape(1, row_groups))

    def swap(array, mask):
        return lax.ppermute(array, "row", [(i, i ^ mask) for i in range(row_groups)])

    def sample(chunk, mixed, order):
        return call(
            functools.partial(sample_body, scale, chunk * piece),
            (shape(far // 2, NEAR, slots, piece),) * 2 + (scalar,),
            design,
            picked,
            mixed,
            order,
            *near[chunk * (NEAR - 1) : (chunk + 1) * (NEAR - 1)],
            scratch=[pltpu.VMEM((NEAR, 2, rows, piece), jnp.bfloat16)],
        )

    def spread(indices, order):
        parts = [away[index] for index in indices]
        if order is not None:
            parts, _ = lax.optimization_barrier((parts, order))
        return [swap(part, sent[index][0]) for index, part in zip(indices, parts)]

    def halve(keep, come, order):
        bit = row_groups // 2
        while bit > NEAR:
            bit //= 2
            half = keep.shape[0] // 2
            keep, send = call(halve_body, (shape(half, *keep.shape[1:]),) * 2, keep, come, order)
            come = swap(send, bit)
        return keep, come

    def join(keep, come, order):
        keep, come = halve(keep, come, order)
        return call(join_body, (shape(*keep.shape[1:]), scalar), keep, come, order)

    def back(rinv, message, first):
        outs, scratch = (shape(whole // LANE, LANE), scalar), [pltpu.VMEM((width // LANE, LANE), F32)]
        operands = (rinv, message)
        if first:
            outs += (shape(row_groups, slots, rows, dtype=jnp.bfloat16), shape(*rinv.shape))
            scratch += [pltpu.SemaphoreType.DMA((width // LANE,))]
            scratch += [pltpu.VMEM((HB, HB), jnp.bfloat16)]
        return pl.pallas_call(
            functools.partial(back_body, first),
            out_shape=outs,
            in_specs=[HBM if first else VMEM] + [VMEM] * (len(operands) - 1),
            out_specs=(VMEM,) * len(outs),
            scratch_shapes=scratch,
            compiler_params=pltpu.CompilerParams(vmem_limit_bytes=(34 if first else 24) << 20),
        )(*operands)

    def forward(terms, token, last, *before):
        return call(
            functools.partial(forward_body, len(terms), not before, last),
            (shape(lines, LANE), shape(width // LANE, LANE), scalar)
            + (() if last else (shape(whole // LANE, LANE),)),
            here,
            design,
            token,
            *terms,
            *before,
        )

    def turn(images, left, beta, alpha, last):
        return call(
            functools.partial(turn_body, len(images), last),
            (shape(lines, LANE), shape(row_groups, 8 if last else deep, LANE)),
            *images,
            left,
            beta,
            alpha,
            *(() if last else (design,)),
        )

    def after(arrays, value):
        return pl.pallas_call(
            pass_body,
            out_shape=shape(*value.shape),
            in_specs=[ANY] * len(arrays) + [VMEM],
            out_specs=VMEM,
            compiler_params=pltpu.CompilerParams(vmem_limit_bytes=2 << 20),
        )(*arrays, value)

    betas, alphas, held, joined, right = [], [], [], [], []
    near = spread(range(NEAR - 2), None)
    message = picked = exchange(message, "row")
    late = len(sent) - (chunks > 1)
    near += spread(range(NEAR - 2, late), message)
    for step in range(ITERS):
        last = step + 1 == ITERS
        if step == 0:
            term, beta, mixed, here = back(rinv, message, True)
            term = after(near[: NEAR - 2], term)
        else:
            term, beta = back(here, message, False)
            token = beta
            if chunks > 1:
                part, token = join(keep, come, message)
                joined.append(part)
                keep, send, token = sample(1, mixed, token)
                come = swap(send, row_groups // 2)
        betas.append(beta)
        spare = chunks > 1 and step > 0
        terms = direct(term, "col") if spare else paired(term, "col")
        if step == 0:
            near += spread(range(late, len(sent)), terms[1])
            keep, send, token = sample(0, mixed, after([near[NEAR - 2], *near[NEAR:late]], beta) if chunks > 1 else beta)
            come = swap(send, row_groups // 2)
        image, kept, alpha, *right = forward(terms, token, last, *right, *betas[1:])
        alphas.append(alpha)
        held.append(kept)
        images = direct(image, "col") if spare else paired(image, "col")
        left, message = turn(images, left, beta, alpha, last)
        message = exchange(message, "row")
    quarters = (shape(slots, width // NEAR),) * NEAR
    mine, *others = call(split_body, quarters, *joined, *halve(keep, come, beta), left)
    basis, answer, sketch = call(
        last_body,
        (shape(lines, LANE), shape(width // LANE, LANE), shape(slots, width)),
        message,
        left,
        *betas,
        *alphas,
        *held,
        mine,
        *(swap(part, mask + 1) for mask, part in enumerate(others)),
    )
    return (sketch, answer.reshape(-1), basis.reshape(-1))


def solution(mesh):
    placed = (
        P("row", "col"),
        P("row"),
        P(None, "row", None),
        P(None, "row"),
        P("row"),
        P("col", None),
    )
    return jax.shard_map(
        shards,
        mesh=mesh,
        in_specs=placed,
        out_specs=(P("row", "col"), P("col"), P("row")),
        check_vma=False,
    )
```

```python
import functools

import jax
import jax.numpy as jnp
import numpy as np
from jax import lax
from jax.experimental import pallas as pl
from jax.experimental.pallas import tpu as pltpu
from jax.sharding import PartitionSpec as P

HB = 256
PAIR = 16
ITERS = 2
LANE = 128
NEAR = 4
CHUNKS = 2
F32 = jnp.float32
VMEM = pl.BlockSpec(memory_space=pltpu.VMEM)
HBM = pl.BlockSpec(memory_space=pltpu.HBM)
ANY = pl.BlockSpec(memory_space=pl.ANY)


def exchange(copies, axis):
    return lax.all_to_all(copies, axis, split_axis=0, concat_axis=0, tiled=True)


def paired(array, axis):
    size = lax.axis_size(axis)
    mask = 1
    while True:
        come = lax.ppermute(array, axis, [(i, i ^ mask) for i in range(size)])
        mask *= 2
        if mask == size:
            return [array, come]
        array = array + come


def direct(array, axis):
    size = lax.axis_size(axis)
    return [array] + [
        lax.ppermute(array, axis, [(i, i ^ mask) for i in range(size)]) for mask in range(1, size)
    ]


def tree(values):
    while len(values) > 1:
        values = [values[i] + values[i + 1] for i in range(0, len(values), 2)]
    return values[0]


def walsh(size):
    parity = lax.broadcasted_iota(jnp.int32, (size, size), 0) & lax.broadcasted_iota(jnp.int32, (size, size), 1)
    for shift in (4, 2, 1):
        parity = parity ^ (parity >> shift)
    return (1 - 2 * (parity & 1)).astype(F32).astype(jnp.bfloat16)


def call(body, out_shape, *operands, scratch=()):
    return pl.pallas_call(
        body,
        out_shape=out_shape,
        in_specs=[VMEM] * len(operands),
        out_specs=jax.tree.map(lambda _: VMEM, out_shape),
        scratch_shapes=scratch,
        compiler_params=pltpu.CompilerParams(vmem_limit_bytes=24 << 20),
    )(*operands)


def fold_rows(block):
    return block.reshape(block.shape[0] // 8, 8, LANE).sum(axis=0)


def total(rows):
    return jnp.sum(jnp.sum(rows, axis=0, keepdims=True), axis=1, keepdims=True)


def splat(scalar):
    return jnp.broadcast_to(scalar, (1, LANE))


def left_product(vector, matrix_ref, out_ref):
    blocks, tiles = matrix_ref.shape[0] // LANE, matrix_ref.shape[1] // LANE
    sums = [jnp.zeros((8, LANE), F32) for _ in range(tiles)]
    for block in range(blocks):
        weight = across(vector[block : block + 1, :])
        for tile in range(tiles):
            part = matrix_ref[block * LANE : (block + 1) * LANE, tile * LANE : (tile + 1) * LANE]
            sums[tile] = sums[tile] + fold_rows(part * weight)
    for tile in range(tiles):
        out_ref[tile : tile + 1, :] = jnp.sum(sums[tile], axis=0, keepdims=True)


def left_product_upper(vector_ref, matrix_ref, out_ref, copies=()):
    blocks, tiles = matrix_ref.shape[0] // LANE, matrix_ref.shape[1] // LANE
    sums = [jnp.zeros((8, LANE), F32) for _ in range(tiles)]
    for block in range(blocks):
        if copies:
            copies[block].wait()
        weight = across(vector_ref[block : block + 1, :])
        for tile in range(block, tiles):
            part = matrix_ref[block * LANE : (block + 1) * LANE, tile * LANE : (tile + 1) * LANE]
            sums[tile] = sums[tile] + fold_rows(part * weight)
    for tile in range(tiles):
        out_ref[tile : tile + 1, :] = jnp.sum(sums[tile], axis=0, keepdims=True)


def right_product(matrix_ref, vector, out_ref):
    blocks, tiles = matrix_ref.shape[0] // LANE, matrix_ref.shape[1] // LANE

    def step(block, carry):
        rows = pl.ds(pl.multiple_of(block * LANE, LANE), LANE)
        sums = jnp.zeros((LANE, LANE), F32)
        for tile in range(tiles):
            sums = sums + matrix_ref[rows, tile * LANE : (tile + 1) * LANE] * vector[tile : tile + 1, :]
        out_ref[pl.ds(block, 1), :] = jnp.sum(fold_rows(sums.T), axis=0, keepdims=True)
        return carry

    lax.fori_loop(0, blocks, step, 0)


def right_product_upper(matrix_ref, vector, out_ref):
    blocks, tiles = matrix_ref.shape[0] // LANE, matrix_ref.shape[1] // LANE
    for block in range(blocks):
        rows = slice(block * LANE, (block + 1) * LANE)
        sums = jnp.zeros((LANE, LANE), F32)
        for tile in range(block, tiles):
            sums = sums + matrix_ref[rows, tile * LANE : (tile + 1) * LANE] * vector[tile : tile + 1, :]
        out_ref[block : block + 1, :] = jnp.sum(fold_rows(sums.T), axis=0, keepdims=True)


def rounded(count, unit):
    return -(-count // unit) * unit


def message_rows(width):
    return rounded(width // LANE + 1, 8)


def picks_at(width):
    return width // LANE + 1


def signs_at(width, groups):
    return picks_at(width) + groups * PAIR // LANE


def copy_out(out_ref):
    first = out_ref[0]
    for index in range(1, out_ref.shape[0]):
        out_ref[index] = first


def across(row):
    return jnp.broadcast_to(row, (LANE, LANE)).T


def first_body(sent, design_ref, target_ref, bits_ref, picks_ref, counts_ref, *refs):
    out_ref, away_refs = refs[0], refs[1:-6]
    design, target_here, bits, picks, counts, sems = refs[-6:]
    rows, width = design.shape
    lines, tiles = rows // LANE, width // LANE
    small = [
        pltpu.make_async_copy(source, place, sems.at[index])
        for index, (source, place) in enumerate(
            ((target_ref, target_here), (bits_ref, bits), (picks_ref, picks), (counts_ref, counts))
        )
    ]
    parts = [slice(line * LANE, (line + 1) * LANE) for line in range(lines)]
    large = [
        pltpu.make_async_copy(design_ref.at[part, :], design.at[part, :], sems.at[4 + line])
        for line, part in enumerate(parts)
    ]
    place = lax.axis_index("row") % NEAR
    away = []
    for index, away_ref in enumerate(away_refs):
        piece = away_ref.shape[1]
        mask, start = sent[index]
        column = pl.multiple_of((place ^ mask) * (width // NEAR) + start, LANE)
        for line, part in enumerate(parts):
            source = design.at[part, pl.ds(column, piece)]
            away.append(pltpu.make_async_copy(source, away_ref.at[part, :], sems.at[4 + lines * (index + 1) + line]))
    for copy in small + large:
        copy.start()
    for copy in small:
        copy.wait()
    out_ref[0] = jnp.zeros(out_ref.shape[1:], F32)
    groups = picks.shape[0]
    owner = lax.broadcasted_iota(jnp.int32, (groups, groups), 0)
    same = owner == lax.broadcasted_iota(jnp.int32, (groups, groups), 1)
    limit = jnp.sum(jnp.where(same, counts[...].astype(F32), 0.0), axis=1, keepdims=True)
    slot = lax.broadcasted_iota(jnp.int32, picks.shape, 1).astype(F32)
    coded = jnp.where(slot < limit, picks[...].astype(F32), -1.0)
    start = picks_at(width)
    for owner in range(0, groups, LANE // PAIR):
        line = jnp.concatenate([coded[i : i + 1, :] for i in range(owner, owner + LANE // PAIR)], axis=1)
        out_ref[0, start + owner * PAIR // LANE : start + owner * PAIR // LANE + 1, :] = line
    start = signs_at(width, groups)
    out_ref[0, start : start + lines, :] = (2 * bits[...] - 1).astype(F32)
    target = target_here[...]
    out_ref[0, tiles : tiles + 1, :] = splat(total(target * target))
    sums = [jnp.zeros((8, LANE), F32) for _ in range(tiles)]
    for line, part in enumerate(parts):
        weight = across(target[line : line + 1, :])
        large[line].wait()
        for copy in away[line::lines]:
            copy.start()
        for tile in range(tiles):
            sums[tile] = sums[tile] + fold_rows(design[part, tile * LANE : (tile + 1) * LANE] * weight)
    for tile in range(tiles):
        out_ref[0, tile : tile + 1, :] = jnp.sum(sums[tile], axis=0, keepdims=True)
    copy_out(out_ref)
    for copy in away:
        copy.wait()


def back_body(first, rinv_ref, parts_ref, *refs):
    if first:
        term_ref, beta_ref, mix_ref, *refs, walsh_ref = refs
    else:
        term_ref, beta_ref, *refs = refs
    tiles = rinv_ref.shape[0] // LANE
    copies = []
    if first:
        rinv_here, scratch, sems = refs
        for block in range(tiles):
            part, right = slice(block * LANE, (block + 1) * LANE), slice(block * LANE, rinv_ref.shape[1])
            copies.append(pltpu.make_async_copy(rinv_ref.at[part, right], rinv_here.at[part, right], sems.at[block]))
            copies[-1].start()
        walsh_ref[...] = walsh(HB)
        mix_body(rinv_ref.shape[0], parts_ref, walsh_ref, mix_ref)
    else:
        rinv_here, (scratch,) = rinv_ref, refs
    summed = tree([parts_ref[i, : tiles + 1, :] for i in range(parts_ref.shape[0])])
    beta = jnp.sqrt(summed[tiles : tiles + 1, :])
    beta_ref[...] = beta
    scratch[...] = summed[:tiles, :] / beta
    left_product_upper(scratch, rinv_here, term_ref, copies)


def forward_body(groups, first, last, rinv_ref, design_ref, token_ref, *refs):
    right = tree([ref[...] for ref in refs[:groups]])
    refs = refs[groups:]
    if not first:
        before_ref, beta_ref, *refs = refs
        right = right - beta_ref[...] * before_ref[...]
    image_ref, held_ref, alpha_ref, *right_refs = refs
    alpha = jnp.sqrt(total(right * right))
    alpha_ref[...] = splat(alpha)
    right = right / alpha
    if not last:
        right_refs[0][...] = right
    right_product_upper(rinv_ref, right, held_ref)
    right_product(design_ref, held_ref[...], image_ref)


def turn_body(groups, last, *refs):
    left = tree([ref[...] for ref in refs[:groups]])
    before_ref, beta_ref, alpha_ref, *refs = refs[groups:]
    left = left - alpha_ref[...] * (before_ref[...] / beta_ref[...])
    square = splat(total(left * left))
    if last:
        left_ref, out_ref = refs
        out_ref[...] = jnp.broadcast_to(square, out_ref.shape)
    else:
        design_ref, left_ref, out_ref = refs
        tiles = design_ref.shape[1] // LANE
        out_ref[0] = jnp.zeros(out_ref.shape[1:], F32)
        left_product(left, design_ref, out_ref.at[0])
        out_ref[0, tiles : tiles + 1, :] = square
        copy_out(out_ref)
    left_ref[...] = left


def pieces(value):
    high = value.astype(jnp.bfloat16)
    return high, (value - high.astype(F32)).astype(jnp.bfloat16)


def weigh(mix, high, low):
    return jnp.dot(mix, high, preferred_element_type=F32) + jnp.dot(mix, low, preferred_element_type=F32)


def for_blocks(groups, step):
    if groups <= 8:
        for block in range(groups):
            step(block, 0)
    else:
        lax.fori_loop(0, groups, step, 0)


def mix_body(width, parts_ref, walsh_ref, mix_ref):
    groups, _, rows = mix_ref.shape
    me = lax.axis_index("row")
    local = lax.broadcasted_iota(jnp.int32, (LANE, rows), 1).astype(F32)
    per = LANE // PAIR

    def step(block, carry):
        parity = jnp.int32(0)
        for bit in range(groups.bit_length() - 1):
            parity = parity ^ ((block & me) >> bit)
        sign = (1 - 2 * (parity & 1)).astype(F32)
        for line in range(groups // per):
            start = picks_at(width) + line
            coded = across(parts_ref[block, start : start + 1, :])
            match = jnp.concatenate([coded] * (rows // LANE), axis=1) == local
            chosen = jnp.where(match, sign, 0.0).astype(jnp.bfloat16)
            for part in range(rows // HB):
                columns = slice(part * HB, (part + 1) * HB)
                mixed = jnp.dot(chosen[:, columns], walsh_ref[...], preferred_element_type=F32).astype(jnp.bfloat16)
                for index in range(per):
                    place = pl.multiple_of(((line * per + index) ^ me) * PAIR, PAIR)
                    mix_ref[block, pl.ds(place, PAIR), columns] = mixed[index * PAIR : (index + 1) * PAIR, :]
        return carry

    for_blocks(groups, step)


def sample_body(scale, start, design_ref, parts_ref, mix_ref, order_ref, *refs):
    near, (keep_ref, send_ref, token_ref, both) = refs[: NEAR - 1], refs[NEAR - 1 :]
    token_ref[...] = first_row(order_ref)
    rows, piece = near[-1].shape
    width = design_ref.shape[1]
    groups = mix_ref.shape[0]
    me = lax.axis_index("row")
    signs_start = signs_at(width, groups)
    for line in range(rows // LANE):
        part = slice(line * LANE, (line + 1) * LANE)
        signs = [across(parts_ref[me ^ mask, signs_start + line : signs_start + line + 1, :]) for mask in range(NEAR)]
        for tile in range(0, piece, LANE):
            column = pl.multiple_of(me % NEAR * (width // NEAR) + start + tile, LANE)
            here = slice(tile, tile + LANE)
            values = [design_ref[part, pl.ds(column, LANE)]] + [ref[part, here] for ref in near]
            values = [value * sign for value, sign in zip(values, signs)]
            apart = 1
            while apart < NEAR:
                for first in range(NEAR):
                    if not first & apart:
                        one, two = values[first], values[first | apart]
                        values[first], values[first | apart] = one + two, one - two
                apart *= 2
            for index, value in enumerate(values):
                both[index, 0, part, here], both[index, 1, part, here] = pieces(value)

    def step(block, carry):
        value = weigh(mix_ref[block], both[block % NEAR, 0], both[block % NEAR, 1]) / scale
        slot = pl.ds(block * PAIR, PAIR)
        for apart in range(groups):
            far, low = apart // NEAR, apart % NEAR
            out_ref = send_ref if far >= groups // NEAR // 2 else keep_ref
            out_ref[far % (groups // NEAR // 2), low, slot, :] = value[apart * PAIR : (apart + 1) * PAIR, :]
        return carry

    for_blocks(groups, step)


def halve_body(kept_ref, arrived_ref, order_ref, keep_ref, send_ref):
    half = keep_ref.shape[0]
    keep_ref[...] = kept_ref[:half] + arrived_ref[:half]
    send_ref[...] = kept_ref[half:] + arrived_ref[half:]


def first_row(ref):
    return ref[:1, :] if len(ref.shape) == 2 else ref[0, :1, :]


def join_body(kept_ref, arrived_ref, order_ref, out_ref, token_ref):
    token_ref[...] = first_row(order_ref)
    out_ref[...] = kept_ref[0] + arrived_ref[0]


def split_body(*refs):
    *joined, kept_ref, arrived_ref, order_ref = refs[:-NEAR]
    piece = kept_ref.shape[3]
    for index, rows_ref in enumerate(refs[-NEAR:]):
        for chunk, part_ref in enumerate(joined):
            rows_ref[:, chunk * piece : (chunk + 1) * piece] = part_ref[index]
        rows_ref[:, len(joined) * piece :] = kept_ref[0, index] + arrived_ref[0, index]


def pass_body(*refs):
    refs[-1][...] = refs[-2][...]


def last_body(parts_ref, left_ref, *refs):
    basis_ref, solution_ref, sketch_ref = refs[-3:]
    quarters = refs[3 * ITERS : 3 * ITERS + NEAR]
    place = lax.axis_index("row") % NEAR
    piece = quarters[0].shape[1]
    for mask, part_ref in enumerate(quarters):
        for tile in range(0, piece, LANE):
            column = pl.multiple_of((place ^ mask) * piece + tile, LANE)
            sketch_ref[:, pl.ds(column, LANE)] = part_ref[:, tile : tile + LANE]
    betas = [ref[...] for ref in refs[:ITERS]]
    alphas = [ref[...] for ref in refs[ITERS : 2 * ITERS]]
    held = [ref[...] for ref in refs[2 * ITERS : 3 * ITERS]]
    last = jnp.sqrt(tree([parts_ref[i] for i in range(parts_ref.shape[0])])[:1, :])
    basis_ref[...] = left_ref[...] / last
    betas.append(last)
    phibar, rhobar = betas[0], alphas[0]
    search, iterate = held[0], jnp.zeros_like(held[0])
    for step in range(ITERS):
        beta = betas[step + 1]
        rho = jnp.sqrt(rhobar * rhobar + beta * beta)
        cosine = rhobar / rho
        sine = beta / rho
        phi = cosine * phibar
        phibar = sine * phibar
        iterate = iterate + phi / rho * search
        if step + 1 < ITERS:
            alpha = alphas[step + 1]
            search = held[step + 1] - sine * alpha / rho * search
            rhobar = -cosine * alpha
    solution_ref[...] = iterate


def shape(*dims, dtype=F32):
    return jax.ShapeDtypeStruct(dims, dtype)


def shards(design, sign_bits, picks, counts, target, rinv):
    rows, width = design.shape
    whole = rinv.shape[1]
    row_groups = lax.axis_size("row")
    lines = rows // LANE
    scalar = shape(1, LANE)
    deep = message_rows(width)
    left = target.reshape(lines, LANE)
    bits = sign_bits.reshape(lines, LANE)
    chunks = min(CHUNKS, width // NEAR // LANE)
    piece = width // NEAR // chunks
    scale = float(np.sqrt(np.float32(rows * row_groups)))
    slots = row_groups * PAIR
    far = row_groups // NEAR

    sent = [(mask, chunk * piece) for chunk in range(chunks) for mask in range(1, NEAR)]

    message, *away = pl.pallas_call(
        functools.partial(first_body, sent),
        out_shape=(shape(row_groups, rounded(signs_at(width, row_groups) + lines, 8), LANE),)
        + (shape(rows, piece),) * len(sent),
        in_specs=[HBM] * 5,
        out_specs=(VMEM,) + (HBM,) * len(sent),
        scratch_shapes=[
            pltpu.VMEM((rows, width), F32),
            pltpu.VMEM((lines, LANE), F32),
            pltpu.VMEM((lines, LANE), jnp.int32),
            pltpu.VMEM((row_groups, PAIR), jnp.int32),
            pltpu.VMEM((1, row_groups), jnp.int32),
            pltpu.SemaphoreType.DMA((4 + lines * (1 + len(sent)),)),
        ],
        compiler_params=pltpu.CompilerParams(vmem_limit_bytes=58 << 20),
    )(design, left, bits, picks.reshape(row_groups, PAIR), counts.reshape(1, row_groups))

    def swap(array, mask):
        return lax.ppermute(array, "row", [(i, i ^ mask) for i in range(row_groups)])

    def sample(chunk, mixed, order):
        return call(
            functools.partial(sample_body, scale, chunk * piece),
            (shape(far // 2, NEAR, slots, piece),) * 2 + (scalar,),
            design,
            picked,
            mixed,
            order,
            *near[chunk * (NEAR - 1) : (chunk + 1) * (NEAR - 1)],
            scratch=[pltpu.VMEM((NEAR, 2, rows, piece), jnp.bfloat16)],
        )

    def spread(indices, order):
        parts = [away[index] for index in indices]
        if order is not None:
            parts, _ = lax.optimization_barrier((parts, order))
        return [swap(part, sent[index][0]) for index, part in zip(indices, parts)]

    def halve(keep, come, order):
        bit = row_groups // 2
        while bit > NEAR:
            bit //= 2
            half = keep.shape[0] // 2
            keep, send = call(halve_body, (shape(half, *keep.shape[1:]),) * 2, keep, come, order)
            come = swap(send, bit)
        return keep, come

    def join(keep, come, order):
        keep, come = halve(keep, come, order)
        return call(join_body, (shape(*keep.shape[1:]), scalar), keep, come, order)

    def back(rinv, message, first):
        outs, scratch = (shape(whole // LANE, LANE), scalar), [pltpu.VMEM((width // LANE, LANE), F32)]
        operands = (rinv, message)
        if first:
            outs += (shape(row_groups, slots, rows, dtype=jnp.bfloat16), shape(*rinv.shape))
            scratch += [pltpu.SemaphoreType.DMA((width // LANE,))]
            scratch += [pltpu.VMEM((HB, HB), jnp.bfloat16)]
        return pl.pallas_call(
            functools.partial(back_body, first),
            out_shape=outs,
            in_specs=[HBM if first else VMEM] + [VMEM] * (len(operands) - 1),
            out_specs=(VMEM,) * len(outs),
            scratch_shapes=scratch,
            compiler_params=pltpu.CompilerParams(vmem_limit_bytes=(34 if first else 24) << 20),
        )(*operands)

    def forward(terms, token, last, *before):
        return call(
            functools.partial(forward_body, len(terms), not before, last),
            (shape(lines, LANE), shape(width // LANE, LANE), scalar)
            + (() if last else (shape(whole // LANE, LANE),)),
            here,
            design,
            token,
            *terms,
            *before,
        )

    def turn(images, left, beta, alpha, last):
        return call(
            functools.partial(turn_body, len(images), last),
            (shape(lines, LANE), shape(row_groups, 8 if last else deep, LANE)),
            *images,
            left,
            beta,
            alpha,
            *(() if last else (design,)),
        )

    def after(arrays, value):
        return pl.pallas_call(
            pass_body,
            out_shape=shape(*value.shape),
            in_specs=[ANY] * len(arrays) + [VMEM],
            out_specs=VMEM,
            compiler_params=pltpu.CompilerParams(vmem_limit_bytes=2 << 20),
        )(*arrays, value)

    betas, alphas, held, joined, right = [], [], [], [], []
    near = spread(range(NEAR - 2), None)
    message = picked = exchange(message, "row")
    late = len(sent) - (chunks > 1)
    near += spread(range(NEAR - 2, late), message)
    for step in range(ITERS):
        last = step + 1 == ITERS
        if step == 0:
            term, beta, mixed, here = back(rinv, message, True)
            term = after(near[: NEAR - 2], term)
        else:
            term, beta = back(here, message, False)
            token = beta
            if chunks > 1:
                part, token = join(keep, come, message)
                joined.append(part)
                keep, send, token = sample(1, mixed, token)
                come = swap(send, row_groups // 2)
        betas.append(beta)
        spare = chunks > 1 and step > 0
        terms = direct(term, "col") if spare else paired(term, "col")
        if step == 0:
            near += spread(range(late, len(sent)), terms[1])
            keep, send, token = sample(0, mixed, beta)
            come = swap(send, row_groups // 2)
        image, kept, alpha, *right = forward(terms, token, last, *right, *betas[1:])
        alphas.append(alpha)
        held.append(kept)
        if step == 0 and chunks > 1:
            image = after(near[NEAR:late], image)
        images = direct(image, "col") if spare else paired(image, "col")
        left, message = turn(images, left, beta, alpha, last)
        message = exchange(message, "row")
    quarters = (shape(slots, width // NEAR),) * NEAR
    mine, *others = call(split_body, quarters, *joined, *halve(keep, come, beta), left)
    basis, answer, sketch = call(
        last_body,
        (shape(lines, LANE), shape(width // LANE, LANE), shape(slots, width)),
        message,
        left,
        *betas,
        *alphas,
        *held,
        mine,
        *(swap(part, mask + 1) for mask, part in enumerate(others)),
    )
    return (sketch, answer.reshape(-1), basis.reshape(-1))


def solution(mesh):
    placed = (
        P("row", "col"),
        P("row"),
        P(None, "row", None),
        P(None, "row"),
        P("row"),
        P("col", None),
    )
    return jax.shard_map(
        shards,
        mesh=mesh,
        in_specs=placed,
        out_specs=(P("row", "col"), P("col"), P("row")),
        check_vma=False,
    )
```
